32 devices in a mesh: bucket: 8 (over y, x, core), seq: 4 (over z).
Axes of the slice: x: 2, y: 2, z: 4, core: 2. Of those that a mesh axis runs over, the one named last changes fastest.
Arguments:
- tokens: bfloat16 [4096, 1536], P(('bucket', 'seq')), may hold values from -6 to 6
- captions: bfloat16 [2048, 4096], P(('bucket', 'seq')), may hold values from -6 to 6
- cotangent: bfloat16 [4096, 1536], P(('bucket', 'seq')), may hold values from -6 to 6
- counts: int32 [8], replicated, may hold values from 128 to 512, as said below
- cap_lens: int32 [8], replicated, may hold values from 8 to 256, as said below
- steps_t: int32 [8], replicated, may hold values from 0 to 999
- w_query: bfloat16 [1536, 1536], P(('bucket', 'seq')), may hold values from -0.15625 to 0.15625
- w_key: bfloat16 [1536, 1536], P(('bucket', 'seq')), may hold values from -0.15625 to 0.15625
- w_value: bfloat16 [1536, 1536], P(('bucket', 'seq')), may hold values from -0.15625 to 0.15625
- w_out: bfloat16 [1536, 1536], P(('bucket', 'seq')), may hold values from -0.15625 to 0.15625
- w_cap_key: bfloat16 [4096, 1536], P(('bucket', 'seq')), may hold values from -0.09375 to 0.09375
- w_cap_value: bfloat16 [4096, 1536], P(('bucket', 'seq')), may hold values from -0.09375 to 0.09375
- w_gate: bfloat16 [1536, 4096], P(('bucket', 'seq')), may hold values from -0.15625 to 0.15625
- w_up: bfloat16 [1536, 4096], P(('bucket', 'seq')), may hold values from -0.15625 to 0.15625
- w_down: bfloat16 [4096, 1536], P(('bucket', 'seq')), may hold values from -0.09375 to 0.09375
- w_mod: bfloat16 [1024, 6144], P(('bucket', 'seq')), may hold values from -0.1875 to 0.1875
- gains: bfloat16 [7, 1536], P(None, ('bucket', 'seq')), may hold values from 0.099609375 to 1.8984375
- cross_gate: bfloat16 [1536], P(('bucket', 'seq')), may hold values from -1.5 to 1.5
Outputs:
- block_out: bfloat16 [4096, 1536], P(('bucket', 'seq'))
- tokens_grad: float32 [4096, 1536], P(('bucket', 'seq'))
- w_query_grad: float32 [1536, 1536], P('bucket', 'seq')
- w_key_grad: float32 [1536, 1536], P('bucket', 'seq')
- w_value_grad: float32 [1536, 1536], P('bucket', 'seq')
- w_out_grad: float32 [1536, 1536], P('bucket', 'seq')
- w_cap_key_grad: float32 [4096, 1536], P('bucket', 'seq')
- w_cap_value_grad: float32 [4096, 1536], P('bucket', 'seq')
- w_gate_grad: float32 [1536, 4096], P('bucket', 'seq')
- w_up_grad: float32 [1536, 4096], P('bucket', 'seq')
- w_down_grad: float32 [4096, 1536], P('bucket', 'seq')
- w_mod_grad: float32 [1024, 6144], P('bucket', 'seq')
- gains_grad: float32 [7, 1536], P(None, ('bucket', 'seq'))
- cross_gate_grad: float32 [1536], P(('bucket', 'seq'))
The draws below stay inside these ranges and needn't reach their ends.
Inputs may be any that keep to these rules, and one draw needn't show every extreme that they name: `counts`: each bucket has 128, 288 or 512 live rows, at its start; some bucket has 512. `cap_lens`: live caption tokens lie at the start of a bucket's slots; some bucket has 256.
All inputs are finite; a program needn't handle non-finite values.
Results may differ from the reference program's by a relative error of at most 0.029.
Values may be sent and summed in bfloat16 or wider, within the bound.
A program may use at most 256 MiB of HBM per device.

```python
import math
import jax
import jax.numpy as jnp
from jax import lax

D = 1536
HEAD_DIM = 64
FF = 4096
COND = 1024
CAP_DIM = 4096
CAPS = 256
HEADS = 24
CAP = 512
ROWS = 4096
CAPTIONS = 2048
N_BUCKET = 8


def draw_counts(key, part):
    bucket_key, forced_key = jax.random.split(jax.random.fold_in(key, 11))
    bucket_pick = jax.random.randint(bucket_key, (N_BUCKET,), 0, 3)
    lengths_all = jnp.where(bucket_pick == 0, CAP // 4, jnp.where(bucket_pick == 1, 9 * CAP // 16, CAP))
    forced_at = jax.random.randint(forced_key, (), 0, N_BUCKET)
    return jnp.where(jnp.arange(N_BUCKET) == forced_at, CAP, lengths_all).astype(jnp.int32)


def draw_cap_lens(key, part):
    length_key, forced_key = jax.random.split(jax.random.fold_in(key, 23))
    drawn = jax.random.randint(length_key, (N_BUCKET,), 8, CAPS + 1)
    forced_at = jax.random.randint(forced_key, (), 0, N_BUCKET)
    return jnp.where(jnp.arange(N_BUCKET) == forced_at, CAPS, drawn).astype(jnp.int32)


def set_ends(array, key, smallest, largest):
    dims = array.shape
    spot = [jax.random.randint(jax.random.fold_in(key, axis), (), 0, dims[axis]) for axis in range(len(dims))]
    array = array.at[tuple(spot)].set(smallest)
    longest = dims.index(max(dims))
    spot[longest] = (spot[longest] + 1) % dims[longest]
    return array.at[tuple(spot)].set(largest)


def block_scale(key, shape, cuts, smallest, largest):
    gain, own = 1.0, jax.random.fold_in(key, 6)
    for axis_at, shards_of in cuts:
        heights = jnp.exp(jax.random.uniform(jax.random.fold_in(own, axis_at), (shards_of,), jnp.float32, smallest / len(cuts), largest / len(cuts)))
        gain = gain * jnp.repeat(heights, shape[axis_at] // shards_of).reshape([-1 if axis == axis_at else 1 for axis in range(len(shape))])
    return gain


def centred(own_key, dims, scale, reach, cuts=(), kind=jnp.bfloat16):
    level = block_scale(own_key, dims, cuts, -0.22, 0.18) if cuts else 1.0
    result = jax.random.normal(own_key, dims, jnp.float32) * scale * level
    return jnp.minimum(jnp.maximum(result, -reach), reach).astype(kind)


def setup_inputs(seed: int = 0) -> dict:
    streams_of = jax.random.split(jax.random.key(seed), 19)
    tokens = centred(streams_of[0], (ROWS, D), 1.0, 6.0, ((0, 32),))
    captions = centred(streams_of[1], (CAPTIONS, CAP_DIM), 1.0, 6.0, ((0, 32),))
    cotangent = centred(streams_of[2], (ROWS, D), 1.0, 6.0, ((0, 32),))
    counts = draw_counts(jax.random.fold_in(streams_of[18], 71), 0)
    cap_lens = draw_cap_lens(jax.random.fold_in(streams_of[18], 71), 0)
    steps_t = set_ends(jax.random.randint(streams_of[5], (N_BUCKET,), 0, 1000), jax.random.fold_in(streams_of[5], 1), 0, 999).astype(jnp.int32)
    w_query = centred(streams_of[6], (D, D), D ** -0.5, 0.15625, ((0, 32),))
    w_key = centred(streams_of[7], (D, D), D ** -0.5, 0.15625, ((0, 32),))
    w_value = centred(streams_of[8], (D, D), D ** -0.5, 0.15625, ((0, 32),))
    w_out = centred(streams_of[9], (D, D), D ** -0.5, 0.15625, ((0, 32),))
    w_cap_key = centred(streams_of[10], (CAP_DIM, D), CAP_DIM ** -0.5, 0.09375, ((0, 32),))
    w_cap_value = centred(streams_of[11], (CAP_DIM, D), CAP_DIM ** -0.5, 0.09375, ((0, 32),))
    w_gate = centred(streams_of[12], (D, FF), D ** -0.5, 0.15625, ((0, 32),))
    w_up = centred(streams_of[13], (D, FF), D ** -0.5, 0.15625, ((0, 32),))
    w_down = centred(streams_of[14], (FF, D), FF ** -0.5, 0.09375, ((0, 32),))
    w_mod = centred(streams_of[15], (COND, 4 * D), COND ** -0.5, 0.1875, ((0, 32),))
    gains = jnp.clip(1.0 + 0.18 * jax.random.normal(streams_of[16], (7, D), jnp.float32), 0.099609375, 1.8984375).astype(jnp.bfloat16)
    cross_gate = jnp.clip(jax.random.uniform(streams_of[17], (D,), jnp.float32, -1.5, 1.5) * block_scale(streams_of[17], (D,), ((0, 32),), -0.4, 0.0), -1.5, 1.5).astype(jnp.bfloat16)
    return dict(tokens=tokens, captions=captions, cotangent=cotangent, counts=counts, cap_lens=cap_lens, steps_t=steps_t, w_query=w_query, w_key=w_key, w_value=w_value, w_out=w_out, w_cap_key=w_cap_key, w_cap_value=w_cap_value, w_gate=w_gate, w_up=w_up, w_down=w_down, w_mod=w_mod, gains=gains, cross_gate=cross_gate)


@jax.custom_vjp
def low(v):
    return lax.optimization_barrier(v.astype(jnp.bfloat16)).astype(jnp.float32)

@jax.custom_vjp
def low_back(v):
    return v

def low_keep(v):
    return (low(v), None)

def low_pass(kept, grad):
    return (grad,)

def back_keep(v):
    return (v, None)

def back_low(kept, grad):
    return (low(grad),)
low.defvjp(low_keep, low_pass)
low_back.defvjp(back_keep, back_low)

def high_dot(left, right):
    return jnp.dot(left, right, precision=lax.Precision.HIGHEST, preferred_element_type=jnp.float32)

def rms_rows(values):
    return values * lax.rsqrt(lax.optimization_barrier(jnp.mean(values * values, axis=-1, keepdims=True)) + 1e-05)

def head_rms(values):
    shaped = values.reshape(values.shape[:-1] + (HEADS, HEAD_DIM))
    shaped = shaped * lax.rsqrt(lax.optimization_barrier(jnp.mean(shaped * shaped, axis=-1, keepdims=True)) + 1e-06)
    return shaped.reshape(values.shape)

def time_embed(step_value, width):
    half_width = width // 2
    freqs = jnp.exp(-math.log(10000.0) * jnp.arange(half_width, dtype=jnp.float32) / half_width)
    angles = step_value.astype(jnp.float32) * freqs
    return jnp.concatenate([jnp.cos(angles), jnp.sin(angles)])

def attend(queries, keys, values, key_live):
    query_rows = queries.shape[0]
    query_heads = queries.reshape(query_rows, HEADS, HEAD_DIM)
    key_heads = keys.reshape(keys.shape[0], HEADS, HEAD_DIM)
    value_heads = values.reshape(values.shape[0], HEADS, HEAD_DIM)
    scores = jnp.einsum('qhd,khd->hqk', query_heads, key_heads, precision=lax.Precision.HIGHEST) * HEAD_DIM ** (-0.5)
    scores = low_back(scores)
    scores = jnp.where(key_live[None, None, :], scores, -1e+30)
    probs = jax.nn.softmax(scores, axis=-1)
    mixed = jnp.einsum('hqk,khd->qhd', low(probs), value_heads, precision=lax.Precision.HIGHEST)
    return mixed.reshape(query_rows, HEADS * HEAD_DIM)

def group_forward(params, x_group, y_group, live_rows, cap_len, step_value):
    w_query, w_key, w_value, w_out, w_cap_key, w_cap_value, w_gate, w_up, w_down, w_mod, gains, cross_gate = params
    cond = low(jax.nn.silu(time_embed(step_value, COND)))
    modulation = high_dot(cond[None, :], w_mod)[0]
    scale_attn = modulation[0:D]
    gate_attn = modulation[D:2 * D]
    scale_ffn = modulation[2 * D:3 * D]
    gate_ffn = modulation[3 * D:4 * D]
    hidden_in = low(rms_rows(x_group) * gains[0] * (1.0 + scale_attn))
    query_proj = low_back(high_dot(hidden_in, w_query))
    key_proj = low_back(high_dot(hidden_in, w_key))
    value_proj = low_back(high_dot(hidden_in, w_value))
    query_norm = low(head_rms(query_proj) * gains[4])
    key_norm = low(head_rms(key_proj) * gains[5])
    value_low = low(value_proj)
    cap_keys = low(head_rms(low_back(high_dot(y_group, w_cap_key))) * gains[6])
    cap_values = low(low_back(high_dot(y_group, w_cap_value)))
    key_live = jnp.arange(CAP) < live_rows
    cap_live = jnp.arange(CAPS) < cap_len
    gate_cross = jnp.tanh(cross_gate)
    block_rows = min(512, CAP)

    def one_block(query_block):
        own_part = attend(query_block, key_norm, value_low, key_live)
        cross_part = low_back(attend(query_block, cap_keys, cap_values, cap_live))
        return low_back(own_part + gate_cross * cross_part)
    mixed = lax.map(jax.checkpoint(one_block), query_norm.reshape(CAP // block_rows, block_rows, D)).reshape(CAP, D)
    attn_out = low_back(high_dot(low(mixed), w_out))
    resid_one = x_group + jnp.tanh(gate_attn) * rms_rows(attn_out) * gains[1]
    hidden_ffn = low(rms_rows(resid_one) * gains[2] * (1.0 + scale_ffn))
    gate_proj = low_back(high_dot(hidden_ffn, w_gate))
    up_proj = low_back(high_dot(hidden_ffn, w_up))
    act_low = low(jax.nn.silu(gate_proj) * up_proj)
    ffn_out = low_back(high_dot(act_low, w_down))
    return resid_one + jnp.tanh(gate_ffn) * rms_rows(ffn_out) * gains[3]

def reference(tokens, captions, cotangent, counts, cap_lens, steps_t, w_query, w_key, w_value, w_out, w_cap_key, w_cap_value, w_gate, w_up, w_down, w_mod, gains, cross_gate):
    params = tuple((weight.astype(jnp.float32) for weight in (w_query, w_key, w_value, w_out, w_cap_key, w_cap_value, w_gate, w_up, w_down, w_mod, gains, cross_gate)))
    tokens_f = tokens.astype(jnp.float32)
    caps_f = captions.astype(jnp.float32).reshape(N_BUCKET, CAPS, CAP_DIM)
    checked = jax.checkpoint(group_forward)

    def forward(tokens_in, params_in):

        def scan_step(carry, item):
            x_group, y_group, live_rows, cap_len, step_value = item
            return (carry, checked(params_in, x_group, y_group, live_rows, cap_len, step_value))
        unused, outputs = lax.scan(scan_step, jnp.zeros((), jnp.float32), (tokens_in.reshape(N_BUCKET, CAP, D), caps_f, counts, cap_lens, steps_t))
        return outputs.reshape(N_BUCKET * CAP, D)
    block_out, pull_back = jax.vjp(forward, tokens_f, params)
    row_live = (jnp.arange(CAP)[None, :] < counts[:, None]).reshape(N_BUCKET * CAP).astype(jnp.float32)
    token_total = jnp.sum(counts).astype(jnp.float32)
    weighted = cotangent.astype(jnp.float32) * row_live[:, None] * (N_BUCKET * CAP / token_total)
    tokens_grad, param_grads = pull_back(weighted)
    return (block_out.astype(jnp.bfloat16), tokens_grad, param_grads[0], param_grads[1], param_grads[2], param_grads[3], param_grads[4], param_grads[5], param_grads[6], param_grads[7], param_grads[8], param_grads[9], param_grads[10], param_grads[11])
```

```python
import functools
import math

import jax
import jax.numpy as jnp
from jax import lax
from jax.experimental import pallas as pl
from jax.experimental.pallas import tpu as pltpu
from jax.sharding import PartitionSpec as P

HEAD_DIM = 64
MESH = pl.DeviceIdType.MESH
F32, BF16 = jnp.float32, jnp.bfloat16


def rms_rows(values):
    return values * lax.rsqrt(jnp.mean(values * values, axis=-1, keepdims=True) + 1e-05)


def head_rms(values):
    shaped = values.reshape(values.shape[:-1] + (values.shape[-1] // HEAD_DIM, HEAD_DIM))
    shaped = shaped * lax.rsqrt(jnp.mean(shaped * shaped, axis=-1, keepdims=True) + 1e-06)
    return shaped.reshape(values.shape)


def time_embed(steps, width):
    half_width = width // 2
    freqs = jnp.exp(-math.log(10000.0) * jnp.arange(half_width, dtype=F32) / half_width)
    angles = steps.astype(F32)[:, None] * freqs
    return jnp.concatenate([jnp.cos(angles), jnp.sin(angles)], axis=1)


def pick_entry(table, index):
    return jnp.sum(jnp.where(jnp.arange(table.shape[0]) == index, table, 0))


def bf_dot(left, right):
    return jnp.dot(left, right, preferred_element_type=F32)


def left_dot(rows_left, rows_right):
    return lax.dot_general(
        rows_left, rows_right, (((0,), (0,)), ((), ())), preferred_element_type=F32
    )


def right_dot(left, right):
    return lax.dot_general(left, right, (((1,), (1,)), ((), ())), preferred_element_type=F32)


def pre_attn(tokens_in, gain_pre, scale_attn):
    return rms_rows(tokens_in) * gain_pre * (1.0 + scale_attn)


def qk_norm(query_in, key_in, gain_query, gain_key):
    return (head_rms(query_in) * gain_query, head_rms(key_in) * gain_key)


def cap_norm(key_in, gain_cap):
    return head_rms(key_in) * gain_cap


def middle(tokens_in, attn_out, gain_post, gate_attn, gain_ffn, scale_ffn):
    resid_one = tokens_in + jnp.tanh(gate_attn) * rms_rows(attn_out) * gain_post
    return (resid_one, rms_rows(resid_one) * gain_ffn * (1.0 + scale_ffn))


def activate(gate_proj, up_proj):
    return jax.nn.silu(gate_proj) * up_proj


def finish(resid_one, ffn_out, gain_last, gate_ffn):
    return resid_one + jnp.tanh(gate_ffn) * rms_rows(ffn_out) * gain_last


def flip(index, bit):
    return index + bit - 2 * bit * lax.rem(lax.div(index, bit), 2)


class Copies:
    def __init__(self, send, recv):
        self.send, self.recv, self.used = send, recv, 0

    def take(self, count=1):
        first = self.used
        self.used += count
        assert self.used <= self.send.shape[0], self.used
        return first

    def remote(self, src, dst, b, s, at=None):
        at = self.take() if at is None else at
        return pltpu.make_async_remote_copy(
            src_ref=src,
            dst_ref=dst,
            send_sem=self.send.at[at],
            recv_sem=self.recv.at[at],
            device_id={"bucket": b, "seq": s},
            device_id_type=MESH,
        )

    def local(self, src, dst):
        return pltpu.make_async_copy(src, dst, self.send.at[self.take()])


def greet(b, s):
    pl.semaphore_signal(
        pltpu.get_barrier_semaphore(),
        inc=1,
        device_id={"bucket": b, "seq": s},
        device_id_type=MESH,
    )


class Relay:
    def __init__(self, copies, own, out, b, s, seq):
        self.copies, self.own, self.out, self.b, self.s, self.seq = copies, own, out, b, s, seq
        self.base = {1: copies.take(seq - 1), -1: copies.take(seq - 1)}
        self.up = jnp.where(s < seq - 1, s + 1, s - 1)
        self.down = jnp.where(s > 0, s - 1, s + 1)
        self.kept = copies.local(own, out.at[s])

    def packet(self, way, j):
        block = self.out.at[self.s - way * j]
        return self.copies.remote(
            self.own if j == 0 else block,
            block,
            self.b,
            self.up if way > 0 else self.down,
            self.base[way] + j,
        )

    def sends(self, way):
        return self.s < self.seq - 1 if way > 0 else self.s > 0

    def has(self, way, j):
        return self.s >= j if way > 0 else self.s + j <= self.seq - 1

    def start(self, j):
        if j == 0:
            self.kept.start()
        for way in (1, -1):
            if j > 0:

                @pl.when(self.has(way, j))
                def _():
                    self.packet(way, j - 1).wait_recv()

            if j <= self.seq - 2:

                @pl.when(jnp.logical_and(self.sends(way), self.has(way, j)))
                def _():
                    self.packet(way, j).start()

    def sent(self, j):
        for way in (1, -1):

            @pl.when(jnp.logical_and(self.sends(way), self.has(way, j)))
            def _():
                self.packet(way, j).wait_send()

        if j == 0:
            self.kept.wait()


def greet_line(b, s, seq):
    @pl.when(s > 0)
    def _():
        greet(b, s - 1)

    @pl.when(s < seq - 1)
    def _():
        greet(b, s + 1)

    peers = jnp.where(s > 0, 1, 0) + jnp.where(s < seq - 1, 1, 0)
    pl.semaphore_wait(pltpu.get_barrier_semaphore(), peers)


def halves_of(shape):
    if len(shape) == 3:
        return shape[0] // 2
    return (shape[0] // 32) * 16 if shape[0] >= 32 else shape[0] // 2


def gather_kernel(buckets, seq, kinds, *refs):
    count = len(kinds)
    tokens, captions, small, cond, w_mod = refs[:5]
    shards = refs[5 : 5 + count]
    tok_all, cap_all, small_all, mod_out = refs[5 + count : 9 + count]
    fulls = refs[9 + count : 9 + 2 * count]
    part, got_bucket, got_seq, mod_sum, send, recv = refs[9 + 2 * count :]
    b, s = lax.axis_index("bucket"), lax.axis_index("seq")
    copies = Copies(send, recv)
    chips = buckets // 2
    place = b * seq + s
    to_b, to_s = lax.rem(place, buckets), lax.div(place, buckets)
    back = s * buckets + b
    from_b, from_s = lax.div(back, seq), lax.rem(back, seq)
    stays = jnp.logical_and(to_b == b, to_s == s)

    lanes = part.shape[2]
    for j in range(part.shape[1]):
        part[:, j, :] = bf_dot(cond[...], w_mod[:, j * lanes : (j + 1) * lanes])

    for k in range(1, buckets):
        greet(lax.rem(b + k, buckets), s)
    for k in range(1, seq):
        greet(b, lax.rem(s + k, seq))

    @pl.when(jnp.logical_not(stays))
    def _():
        greet(from_b, from_s)

    peers = buckets - 1 + seq - 1 + jnp.where(stays, 0, 1)
    pl.semaphore_wait(pltpu.get_barrier_semaphore(), peers)

    sent = []

    def go(copy):
        copy.start()
        sent.append(copy)
        return copy

    mod_moves = []
    for k in range(1, buckets):
        peer = lax.rem(b + k, buckets)
        mod_moves.append(go(copies.remote(part.at[peer], got_bucket.at[k], peer, s)))
    small_moves = []
    for k in range(1, seq):
        peer = lax.rem(s + k, seq)
        small_moves.append(go(copies.remote(small, small_all.at[b, s], b, peer)))
    small_own = copies.local(small, small_all.at[b, s])
    small_own.start()

    tok = Relay(copies, tokens, tok_all, b, s, seq)
    cap = Relay(copies, captions, cap_all, b, s, seq)
    queue = [(tok, j) for j in range(seq)] + [(cap, j) for j in range(seq)]
    ahead = [(None, at) for at in range(count)]
    items = []
    while queue or ahead:
        items += queue[:1] + ahead[:1]
        queue, ahead = queue[1:], ahead[1:]

    first = [None] * count

    def depart(at):
        kind, shard, full = kinds[at], shards[at], fulls[at]
        if kind == "row":
            move = copies.remote(shard, full.at[to_b], to_b, to_s)
            keep = copies.local(shard, full.at[b])

            @pl.when(jnp.logical_not(stays))
            def _():
                move.start()

            @pl.when(stays)
            def _():
                keep.start()

            first[at] = (move, keep)
            return
        wide = full.shape[-1]

        def columns(peer):
            if kind == "cut":
                return shard.at[peer]
            return shard.at[:, pl.ds(pl.multiple_of(peer * wide, 128), wide)]

        moves = []
        for k in range(1, seq):
            peer = lax.rem(s + k, seq)
            move = copies.remote(columns(peer), full.at[b, s], b, peer)
            move.start()
            moves.append(move)
        keep = copies.local(columns(s), full.at[b, s])
        keep.start()
        first[at] = (moves, keep)

    def arrived(at):
        moves, keep = first[at]
        if kinds[at] == "row":

            @pl.when(jnp.logical_not(stays))
            def _():
                moves.wait()

            @pl.when(stays)
            def _():
                keep.wait()

            return
        for move in moves:
            move.wait()
        keep.wait()

    twin = flip(b, 1)
    second = [None] * count
    if chips == 4:
        near_x, near_y = flip(b, 2), flip(b, 4)
        far = flip(near_x, 4)

        def stage_a(at):
            full = fulls[at]
            second[at] = {
                "x": go(copies.remote(full.at[b], full.at[b], near_x, s)),
                "y": go(copies.remote(full.at[b], full.at[b], near_y, s)),
                "twin": [go(copies.remote(full.at[b], full.at[b], twin, s))],
            }

        def stage_b(at):
            full, now = fulls[at], second[at]
            cut = halves_of(full.shape[1:])
            now["x"].wait_recv()
            block = full.at[near_x, pl.ds(0, cut)]
            now["dy"] = go(copies.remote(block, block, near_y, s))
            block = full.at[near_x]
            now["twin"].append(go(copies.remote(block, block, twin, s)))
            now["y"].wait_recv()
            block = full.at[near_y, pl.ds(cut, full.shape[1] - cut)]
            now["dx"] = go(copies.remote(block, block, near_x, s))
            block = full.at[near_y]
            now["twin"].append(go(copies.remote(block, block, twin, s)))

        def stage_c(at):
            full, now = fulls[at], second[at]
            now["dy"].wait_recv()
            now["dx"].wait_recv()
            block = full.at[far]
            now["twin"].append(go(copies.remote(block, block, twin, s)))

    else:

        def stage_a(at):
            full = fulls[at]
            second[at] = {"far": [], "twin": []}
            for k in range(1, chips):
                peer = lax.rem(b + 2 * k, buckets)
                second[at]["far"].append(go(copies.remote(full.at[b], full.at[b], peer, s)))
            second[at]["twin"].append(go(copies.remote(full.at[b], full.at[b], twin, s)))

        def stage_b(at):
            full = fulls[at]
            for k, copy in enumerate(second[at]["far"], 1):
                copy.wait_recv()
                block = full.at[lax.rem(b + buckets - 2 * k, buckets)]
                second[at]["twin"].append(go(copies.remote(block, block, twin, s)))

        def stage_c(at):
            pass

    def begin(i):
        relay, j = items[i]
        if relay is None:
            depart(j)
        else:
            relay.start(j)

    begin(0)
    begin(1)
    for move in small_moves:
        move.wait_recv()
    small_own.wait()
    small_next = []
    for k in range(1, buckets):
        peer = lax.rem(b + k, buckets)
        small_next.append(go(copies.remote(small_all.at[b], small_all.at[b], peer, s)))
    total = part[b]
    for k, move in enumerate(mod_moves, 1):
        move.wait_recv()
        total = total + got_bucket[k]
    mod_sum[...] = total
    mod_next = []
    for k in range(1, seq):
        peer = lax.rem(s + k, seq)
        mod_next.append(go(copies.remote(mod_sum, got_seq.at[k], b, peer)))

    for i, (relay, j) in enumerate(items):
        if relay is None:
            arrived(j)
        elif j <= seq - 2:
            relay.sent(j)
        if i + 2 < len(items):
            begin(i + 2)
        if relay is None:
            stage_a(j)
            if j >= 1:
                stage_b(j - 1)
            if j >= 2:
                stage_c(j - 2)
    stage_b(count - 1)
    if count >= 2:
        stage_c(count - 2)
    stage_c(count - 1)

    total = mod_sum[...]
    for k, move in enumerate(mod_next, 1):
        move.wait_recv()
        total = total + got_seq[k]
    mod_out[...] = total
    for move in small_next:
        move.wait_recv()
    for now in second:
        for move in now["twin"]:
            move.wait_recv()
    for move in sent:
        move.wait_send()


def gather_all(buckets, seq, tokens, captions, small, cond, w_mod, shards, kinds):
    any_spec = pl.BlockSpec(memory_space=pl.ANY)
    vmem = pl.BlockSpec(memory_space=pltpu.VMEM)
    fulls, inputs, names = [], [], []
    for shard, kind in zip(shards, kinds, strict=True):
        rows, wide = shard.shape
        if kind == "row":
            fulls.append(jax.ShapeDtypeStruct((buckets, rows, wide), BF16))
        else:
            part = wide // seq
            fulls.append(jax.ShapeDtypeStruct((buckets, seq, rows, part), BF16))
            if part % 128:
                kind = "cut"
                shard = shard.reshape(rows, seq, part).transpose(1, 0, 2)
        inputs.append(shard)
        names.append(kind)
    mod_lanes = w_mod.shape[1] // 8
    n_sems = 64 + 16 * buckets + len(shards) * (seq + 2 * buckets)
    outs = pl.pallas_call(
        functools.partial(gather_kernel, buckets, seq, tuple(names)),
        out_shape=[
            jax.ShapeDtypeStruct((seq,) + tokens.shape, BF16),
            jax.ShapeDtypeStruct((seq,) + captions.shape, BF16),
            jax.ShapeDtypeStruct((buckets, seq) + small.shape, F32),
            jax.ShapeDtypeStruct((8, mod_lanes), F32),
            *fulls,
        ],
        in_specs=[any_spec, any_spec, any_spec, vmem, vmem] + [any_spec] * len(shards),
        out_specs=[any_spec, any_spec, any_spec, vmem] + [any_spec] * len(shards),
        scratch_shapes=[
            pltpu.VMEM((buckets, 8, mod_lanes), F32),
            pltpu.VMEM((buckets, 8, mod_lanes), F32),
            pltpu.VMEM((seq, 8, mod_lanes), F32),
            pltpu.VMEM((8, mod_lanes), F32),
            pltpu.SemaphoreType.DMA((n_sems,)),
            pltpu.SemaphoreType.DMA((n_sems,)),
        ],
        compiler_params=pltpu.CompilerParams(
            collective_id=0, has_side_effects=True, vmem_limit_bytes=24 * 2**20
        ),
    )(tokens, captions, small, cond, w_mod, *inputs)
    weights = []
    for full, kind in zip(outs[4:], names, strict=True):
        weights.append(full.reshape(-1, full.shape[-1]))
    return outs[0], outs[1], outs[2], outs[3], weights


def line_gather_kernel(seq, own, out, send, recv):
    b, s = lax.axis_index("bucket"), lax.axis_index("seq")
    greet_line(b, s, seq)
    relay = Relay(Copies(send, recv), own, out, b, s, seq)
    for j in range(seq):
        relay.start(j)
    for j in range(seq - 1):
        relay.sent(j)


def line_gather(seq, own, collective_id):
    return pl.pallas_call(
        functools.partial(line_gather_kernel, seq),
        out_shape=jax.ShapeDtypeStruct((seq,) + own.shape, own.dtype),
        in_specs=[pl.BlockSpec(memory_space=pl.ANY)],
        out_specs=pl.BlockSpec(memory_space=pl.ANY),
        scratch_shapes=[pltpu.SemaphoreType.DMA((2 * seq + 2,))] * 2,
        compiler_params=pltpu.CompilerParams(collective_id=collective_id, has_side_effects=True),
    )(own).reshape(-1, own.shape[-1])


def add_rows(out, terms):
    rows = out.shape[0]
    step = 16 if rows % 16 == 0 else rows

    def body(i, carry):
        at = pl.ds(pl.multiple_of(i * step, step), step)
        total = terms[0][at, :].astype(F32)
        for term in terms[1:]:
            total = total + term[at, :].astype(F32)
        out[at, :] = total.astype(out.dtype)
        return carry

    lax.fori_loop(0, rows // step, body, 0)


def line_scatter_kernel(seq, parts, out, from_left, from_right, send, recv):
    b, s = lax.axis_index("bucket"), lax.axis_index("seq")
    greet_line(b, s, seq)
    copies = Copies(send, recv)
    rows = parts.shape[1]
    cuts = 2 if rows % 32 == 0 else 1
    thin = rows // cuts
    steps = (seq - 1) * cuts
    base_r, base_l = copies.take(steps), copies.take(steps)
    up, down = jnp.where(s < seq - 1, s + 1, s - 1), jnp.where(s > 0, s - 1, s + 1)

    def to_right(q):
        j, at = q // cuts, pl.ds(q % cuts * thin, thin)
        return copies.remote(parts.at[seq - 1 - j, at], from_left.at[j, at], b, up, base_r + q)

    def to_left(q):
        j, at = q // cuts, pl.ds(q % cuts * thin, thin)
        return copies.remote(parts.at[j, at], from_right.at[j, at], b, down, base_l + q)

    def right_on(q):
        return s < seq - 1 - q // cuts

    def left_on(q):
        return s > q // cuts

    def right_step(q):
        j, at = q // cuts, pl.ds(q % cuts * thin, thin)
        block = parts.at[seq - 1 - j, at]

        @pl.when(jnp.logical_and(s > 0, right_on(q)))
        def _():
            to_right(q).wait_recv()
            add_rows(block, [block, from_left.at[j, at]])

        @pl.when(right_on(q))
        def _():
            if q >= 2:
                to_right(q - 2).wait_send()
            to_right(q).start()

    def left_step(q):
        j, at = q // cuts, pl.ds(q % cuts * thin, thin)
        block = parts.at[j, at]

        @pl.when(jnp.logical_and(s < seq - 1, left_on(q)))
        def _():
            to_left(q).wait_recv()
            add_rows(block, [block, from_right.at[j, at]])

        @pl.when(left_on(q))
        def _():
            if q >= 2:
                to_left(q - 2).wait_send()
            to_left(q).start()

    @pl.when(s < seq // 2)
    def _():
        for q in range(steps):
            right_step(q)
            left_step(q)

    @pl.when(s >= seq // 2)
    def _():
        for q in range(steps):
            left_step(q)
            right_step(q)

    for t in range(seq):

        @pl.when(s == t)
        def _():
            terms = [parts.at[t]]
            if t > 0:
                for c in range(cuts):
                    to_right((seq - 1 - t) * cuts + c).wait_recv()
                terms.append(from_left.at[seq - 1 - t])
            if t < seq - 1:
                for c in range(cuts):
                    to_left(t * cuts + c).wait_recv()
                terms.append(from_right.at[t])
            add_rows(out, terms)

    for q in range(steps):
        more = q + 2 < steps

        @pl.when(jnp.logical_and(right_on(q), jnp.logical_not(right_on(q + 2)) if more else True))
        def _():
            to_right(q).wait_send()

        @pl.when(jnp.logical_and(left_on(q), jnp.logical_not(left_on(q + 2)) if more else True))
        def _():
            to_left(q).wait_send()


def line_scatter(seq, parts, collective_id):
    rows, wide = parts.shape[0] // seq, parts.shape[1]
    vmem = pl.BlockSpec(memory_space=pltpu.VMEM)
    return pl.pallas_call(
        functools.partial(line_scatter_kernel, seq),
        out_shape=jax.ShapeDtypeStruct((rows, wide), F32),
        in_specs=[vmem],
        out_specs=vmem,
        input_output_aliases={},
        scratch_shapes=[
            pltpu.VMEM((seq - 1, rows, wide), BF16),
            pltpu.VMEM((seq - 1, rows, wide), BF16),
            pltpu.SemaphoreType.DMA((4 * seq,)),
            pltpu.SemaphoreType.DMA((4 * seq,)),
        ],
        compiler_params=pltpu.CompilerParams(
            collective_id=collective_id, has_side_effects=True, vmem_limit_bytes=24 * 2**20
        ),
    )(parts.astype(BF16).reshape(seq, rows, wide))


def scatter_kernel(buckets, seq, kinds, *refs):
    count = len(kinds)
    vec, grads = refs[0], refs[1 : 1 + count]
    vec_all, outs = refs[1 + count], refs[2 + count : 2 + 2 * count]
    at = 2 + 2 * count
    vec_seq, vec_sum, send, recv = refs[at : at + 4]
    scratch = refs[at + 4 :]
    b, s = lax.axis_index("bucket"), lax.axis_index("seq")
    copies = Copies(send, recv)
    chips = buckets // 2
    chip, core = lax.div(b, 2), lax.rem(b, 2)
    place = s * buckets + b
    to_b = lax.div(place, seq)
    twin = flip(b, 1)
    sent = []

    def go(copy):
        copy.start()
        sent.append(copy)
        return copy

    for k in range(1, buckets):
        greet(lax.rem(b + k, buckets), s)
    for k in range(1, seq):
        greet(b, lax.rem(s + k, seq))
    for j in range(seq):
        d = b * seq + j
        src_b, src_s = lax.rem(d, buckets), lax.div(d, buckets)

        @pl.when(jnp.logical_not(jnp.logical_and(src_b == b, src_s == s)))
        def _():
            greet(src_b, src_s)

    peers = buckets - 1 + seq - 1 + seq - jnp.where(to_b == b, 1, 0)
    pl.semaphore_wait(pltpu.get_barrier_semaphore(), peers)

    vec_moves = []
    for k in range(1, seq):
        vec_moves.append(go(copies.remote(vec, vec_seq.at[k], b, lax.rem(s + k, seq))))

    begun = []

    def begin(w):
        own, other = scratch[6 * w], scratch[6 * w + 1]
        swap = copies.remote(grads[w].at[:, 1 - core], other, twin, s)
        keep = copies.local(grads[w].at[:, core], own)
        swap.start()
        keep.start()
        begun.append((swap, keep))

    begin(0)
    if count > 1:
        begin(1)

    for move in vec_moves:
        move.wait_recv()
    add_rows(vec_sum, [vec] + [vec_seq.at[k] for k in range(1, seq)])
    vec_next = []
    for k in range(1, buckets):
        peer = lax.rem(b + k, buckets)
        vec_next.append(go(copies.remote(vec_sum, vec_all.at[b], peer, s)))
    vec_own = copies.local(vec_sum, vec_all.at[b])
    vec_own.start()

    state = [None] * count
    if chips == 4:
        mx, my = flip(chip, 1), flip(chip, 2)
        far = flip(mx, 2)
        near_x, near_y = flip(b, 2), flip(b, 4)

        def stage_a(w):
            own, other, half_x, half_y, _, _ = scratch[6 * w : 6 * w + 6]
            swap, keep = begun[w]
            swap.wait()
            keep.wait()
            if w + 2 < count:
                begin(w + 2)
            add_rows(own.at[far], [own.at[far], other.at[far]])
            rows = own.shape[1]
            cut = halves_of(own.shape[1:])
            state[w] = [
                go(copies.remote(own.at[far, pl.ds(0, cut)], half_x, near_x, s)),
                go(copies.remote(own.at[far, pl.ds(cut, rows - cut)], half_y, near_y, s)),
            ]

        def stage_b(w):
            own, other, half_x, half_y, got_x, got_y = scratch[6 * w : 6 * w + 6]
            rows = own.shape[1]
            cut = halves_of(own.shape[1:])
            top, low = pl.ds(0, cut), pl.ds(cut, rows - cut)
            move_x, move_y = state[w]
            move_x.wait_recv()
            add_rows(own.at[my, top], [own.at[my, top], other.at[my, top], half_x])
            add_rows(own.at[my, low], [own.at[my, low], other.at[my, low]])
            next_y = go(copies.remote(own.at[my], got_y, near_y, s))
            move_y.wait_recv()
            add_rows(own.at[mx, low], [own.at[mx, low], other.at[mx, low], half_y])
            add_rows(own.at[mx, top], [own.at[mx, top], other.at[mx, top]])
            next_x = go(copies.remote(own.at[mx], got_x, near_x, s))
            state[w] = [next_x, next_y]

        def terms_of(w):
            own, other, _, _, got_x, got_y = scratch[6 * w : 6 * w + 6]
            return [own.at[chip], other.at[chip], got_x, got_y]

    else:

        def stage_a(w):
            own, other, got = scratch[6 * w], scratch[6 * w + 1], scratch[6 * w + 4]
            swap, keep = begun[w]
            swap.wait()
            keep.wait()
            if w + 2 < count:
                begin(w + 2)
            state[w] = []
            for k in range(1, chips):
                to = lax.rem(chip + k, chips)
                add_rows(own.at[to], [own.at[to], other.at[to]])
                state[w].append(go(copies.remote(own.at[to], got.at[k], 2 * to + core, s)))

        def stage_b(w):
            pass

        def terms_of(w):
            own, other, got = scratch[6 * w], scratch[6 * w + 1], scratch[6 * w + 4]
            return [own.at[chip], other.at[chip]] + [got.at[k] for k in range(1, chips)]

    last = [None] * count

    def stage_c(w):
        for move in state[w]:
            move.wait_recv()
        add_rows(outs[w], terms_of(w))

    row_base = {w: copies.take(2 * seq) for w in range(count) if kinds[w] == "row"}

    def stage_c_row(w):
        for move in state[w]:
            move.wait_recv()
        out, terms = outs[w], terms_of(w)
        done, landed = scratch[6 * count + 2 * w], scratch[6 * count + 2 * w + 1]
        wide = out.shape[-1]
        me = lax.rem(place, seq)
        base = row_base[w]
        rows = terms[0].shape[0]
        step = 16 if rows % 16 == 0 else rows

        def body(i, carry):
            at = pl.ds(pl.multiple_of(i * step, step), step)
            total = terms[0][at, :].astype(F32)
            for term in terms[1:]:
                total = total + term[at, :].astype(F32)
            for t in range(seq):
                done[t, at, :] = total[:, t * wide : (t + 1) * wide].astype(BF16)
            return carry

        lax.fori_loop(0, rows // step, body, 0)
        moves = []
        for t in range(seq):
            move = pltpu.make_async_remote_copy(
                src_ref=done.at[t],
                dst_ref=landed.at[me],
                send_sem=send.at[base + t],
                recv_sem=recv.at[base + me],
                device_id={"bucket": to_b, "seq": t},
                device_id_type=MESH,
            )
            keep = pltpu.make_async_copy(done.at[t], landed.at[me], send.at[base + seq + t])
            here = jnp.logical_and(to_b == b, s == t)

            @pl.when(jnp.logical_not(here))
            def _():
                move.start()

            @pl.when(here)
            def _():
                keep.start()

            moves.append((move, keep, here))
        last[w] = moves

    def stage_d(w):
        if kinds[w] != "row":
            return
        out = outs[w]
        done, landed = scratch[6 * count + 2 * w], scratch[6 * count + 2 * w + 1]
        base = row_base[w]
        for j in range(seq):
            d = b * seq + j
            here = jnp.logical_and(lax.rem(d, buckets) == b, lax.div(d, buckets) == s)

            @pl.when(jnp.logical_not(here))
            def _():
                pltpu.make_async_remote_copy(
                    src_ref=done.at[j],
                    dst_ref=landed.at[j],
                    send_sem=send.at[base + j],
                    recv_sem=recv.at[base + j],
                    device_id={"bucket": twin, "seq": s},
                    device_id_type=MESH,
                ).wait_recv()

        for move, keep, here in last[w]:

            @pl.when(jnp.logical_not(here))
            def _():
                move.wait_send()

            @pl.when(here)
            def _():
                keep.wait()

        for j in range(seq):
            add_rows(out.at[j], [landed.at[j]])

    for w in range(count + 2):
        if w < count:
            stage_a(w)
        if 1 <= w <= count:
            stage_b(w - 1)
        if w >= 2:
            if kinds[w - 2] == "row":
                stage_c_row(w - 2)
            else:
                stage_c(w - 2)
    for w in range(count):
        stage_d(w)
    for move in vec_next:
        move.wait_recv()
    vec_own.wait()
    for move in sent:
        move.wait_send()


def scatter_all(buckets, seq, vec, grads, kinds):
    chips = buckets // 2
    any_spec = pl.BlockSpec(memory_space=pl.ANY)
    vmem = pl.BlockSpec(memory_space=pltpu.VMEM)
    inputs, outs, scratch, tail = [], [], [], []
    for grad, kind in zip(grads, kinds, strict=True):
        rows, wide = grad.shape[0] // buckets, grad.shape[1]
        inputs.append(grad.astype(BF16).reshape(chips, 2, rows, wide))
        cut = halves_of((rows, wide))
        scratch += [
            pltpu.VMEM((chips, rows, wide), BF16),
            pltpu.VMEM((chips, rows, wide), BF16),
            pltpu.VMEM((cut, wide), BF16),
            pltpu.VMEM((rows - cut, wide), BF16),
            pltpu.VMEM((rows, wide) if chips == 4 else (chips, rows, wide), BF16),
            pltpu.VMEM((rows, wide) if chips == 4 else (16, 128), BF16),
        ]
        if kind == "row":
            shape = (seq, rows, wide // seq)
            outs.append(jax.ShapeDtypeStruct(shape, F32))
            tail += [pltpu.VMEM(shape, BF16)] * 2
        else:
            outs.append(jax.ShapeDtypeStruct((rows, wide), F32))
            tail += [pltpu.VMEM((16, 128), BF16)] * 2
    n_sems = 32 + 2 * buckets + len(grads) * (8 + 3 * seq + buckets)
    results = pl.pallas_call(
        functools.partial(scatter_kernel, buckets, seq, tuple(kinds)),
        out_shape=[jax.ShapeDtypeStruct((buckets,) + vec.shape, F32), *outs],
        in_specs=[vmem] + [any_spec] * len(grads),
        out_specs=[any_spec] + [vmem] * len(grads),
        scratch_shapes=[
            pltpu.VMEM((seq,) + vec.shape, F32),
            pltpu.VMEM(vec.shape, F32),
            pltpu.SemaphoreType.DMA((n_sems,)),
            pltpu.SemaphoreType.DMA((n_sems,)),
            *scratch,
            *tail,
        ],
        compiler_params=pltpu.CompilerParams(
            collective_id=1, has_side_effects=True, vmem_limit_bytes=60 * 2**20
        ),
    )(vec, *inputs)
    return results[0], [out.reshape(-1, out.shape[-1]) for out in results[1:]]


def attention(queries, keys, values, live, scale):
    scores = jnp.einsum("qhd,khd->hqk", queries, keys, preferred_element_type=F32) * scale
    scores = jnp.where(live[None, None, :], scores, -1e30)
    probs = jax.nn.softmax(scores, axis=-1)
    mixed = jnp.einsum("hqk,khd->qhd", probs.astype(BF16), values, preferred_element_type=F32)
    return probs, mixed


def attention_back(probs, queries, keys, values, d_out, scale):
    d_probs = jnp.einsum("qhd,khd->hqk", d_out, values, preferred_element_type=F32)
    d_scores = probs * (d_probs - jnp.sum(probs * d_probs, axis=-1, keepdims=True))
    d_low = d_scores.astype(BF16)
    d_query = jnp.einsum("hqk,khd->qhd", d_low, keys, preferred_element_type=F32) * scale
    d_key = jnp.einsum("hqk,qhd->khd", d_low, queries, preferred_element_type=F32) * scale
    d_value = jnp.einsum("hqk,qhd->khd", probs.astype(BF16), d_out, preferred_element_type=F32)
    return d_query, d_key, d_value


def on_device(
    tokens,
    captions,
    cotangent,
    counts,
    cap_lens,
    steps_t,
    w_query,
    w_key,
    w_value,
    w_out,
    w_cap_key,
    w_cap_value,
    w_gate,
    w_up,
    w_down,
    w_mod,
    gains,
    cross_gate,
):
    buckets, seq = lax.axis_size("bucket"), lax.axis_size("seq")
    b, s = lax.axis_index("bucket"), lax.axis_index("seq")
    place = b * seq + s
    rows, width = tokens.shape
    span = rows * seq
    share = width // seq
    heads = share // HEAD_DIM
    scale = HEAD_DIM ** (-0.5)
    live_rows, cap_len = pick_entry(counts, b), pick_entry(cap_lens, b)
    token_total = jnp.sum(counts).astype(F32)

    cond_size = w_mod.shape[0] * buckets * seq
    cond = jax.nn.silu(time_embed(steps_t, cond_size)).astype(BF16)
    cond_part = lax.dynamic_slice_in_dim(cond, place * w_mod.shape[0], w_mod.shape[0], 1)
    slim = gains.shape[1]
    small = jnp.concatenate([gains, cross_gate[None]], axis=0).astype(F32)
    small = jnp.pad(small, ((0, 0), (0, 128 - slim)))
    tok_all, cap_all, small_all, mod, weights = gather_all(
        buckets,
        seq,
        tokens,
        captions,
        small,
        cond_part,
        w_mod,
        [w_query, w_key, w_value, w_cap_key, w_cap_value, w_out, w_gate, w_up, w_down],
        ["col", "col", "col", "col", "col", "row", "col", "col", "row"],
    )
    wq, wk, wv, wck, wcv, wo, wg, wu, wd = weights
    caps = cap_all.reshape(-1, captions.shape[1])
    small_rows = small_all[..., :slim].transpose(2, 0, 1, 3).reshape(8, width)
    gain_f = small_rows[:7]
    own_cols = lax.dynamic_slice_in_dim(small_rows, s * share, share, 1)
    gate_cross = jnp.tanh(own_cols[7])
    scale_attn, gate_attn, scale_ffn, gate_ffn = mod.reshape(4, width)

    hidden = pre_attn(tok_all.astype(F32), gain_f[0], scale_attn).astype(BF16).reshape(span, width)
    query_proj, key_proj = bf_dot(hidden, wq), bf_dot(hidden, wk)
    value_low = bf_dot(hidden, wv).astype(BF16)
    (query_f, key_f), norm_back = jax.vjp(qk_norm, query_proj, key_proj, own_cols[4], own_cols[5])
    cap_key_f, cap_back = jax.vjp(cap_norm, bf_dot(caps, wck), own_cols[6])

    def by_head(values):
        return values.astype(BF16).reshape(values.shape[0], heads, HEAD_DIM)

    query, key, value = by_head(query_f), by_head(key_f), by_head(value_low)
    cap_key, cap_value = by_head(cap_key_f), by_head(bf_dot(caps, wcv))
    probs, self_out = attention(query, key, value, jnp.arange(span) < live_rows, scale)
    cap_live = jnp.arange(caps.shape[0]) < cap_len
    cap_probs, cross_out = attention(query, cap_key, cap_value, cap_live, scale)
    self_out, cross_out = self_out.reshape(span, share), cross_out.reshape(span, share)
    mixed_low = (self_out + gate_cross * cross_out).astype(BF16)
    attn_out = line_scatter(seq, bf_dot(mixed_low, wo), 2)

    tokens_f = tokens.astype(F32)
    (resid_one, ffn_pre), middle_back = jax.vjp(
        middle, tokens_f, attn_out, gain_f[1], gate_attn, gain_f[2], scale_ffn
    )
    ffn_all = line_gather(seq, ffn_pre.astype(BF16), 3)
    act_pre, act_back = jax.vjp(activate, bf_dot(ffn_all, wg), bf_dot(ffn_all, wu))
    act_low = act_pre.astype(BF16)
    ffn_out = line_scatter(seq, bf_dot(act_low, wd), 4)
    out_f, finish_back = jax.vjp(finish, resid_one, ffn_out, gain_f[3], gate_ffn)
    block_out = out_f.astype(BF16)

    row_live = (s * rows + jnp.arange(rows) < live_rows).astype(F32)
    weighted = cotangent.astype(F32) * row_live[:, None] * (buckets * span / token_total)
    d_resid, d_ffn_out, d_gain_last, d_gate_ffn = finish_back(weighted)
    d_ffn_all = line_gather(seq, d_ffn_out.astype(BF16), 5)
    d_gate, d_up = act_back(right_dot(d_ffn_all, wd))
    d_gate, d_up = d_gate.astype(BF16), d_up.astype(BF16)
    d_hidden_ffn = line_scatter(seq, right_dot(d_gate, wg) + right_dot(d_up, wu), 6)
    d_tokens_one, d_attn_out, d_gain_post, d_gate_attn, d_gain_ffn, d_scale_ffn = middle_back(
        (d_resid, d_hidden_ffn)
    )
    d_attn_all = line_gather(seq, d_attn_out.astype(BF16), 7)
    d_mixed_low = right_dot(d_attn_all, wo).astype(BF16)
    d_mixed = d_mixed_low.astype(F32)
    d_cross_low = (gate_cross * d_mixed).astype(BF16)
    grad_cross = jnp.sum(d_mixed * cross_out, axis=0) * (1.0 - gate_cross * gate_cross)

    d_query_cross, d_cap_key, d_cap_value = attention_back(
        cap_probs, query, cap_key, cap_value, by_head(d_cross_low), scale
    )
    d_query, d_key, d_value = attention_back(probs, query, key, value, by_head(d_mixed_low), scale)
    d_cap_key, d_gain_cap = cap_back(d_cap_key.reshape(-1, share))
    d_query, d_key, d_gain_query, d_gain_key = norm_back(
        ((d_query + d_query_cross).reshape(span, share), d_key.reshape(span, share))
    )
    d_query, d_key, d_cap_key = d_query.astype(BF16), d_key.astype(BF16), d_cap_key.astype(BF16)
    d_value = d_value.reshape(span, share).astype(BF16)
    d_cap_value = d_cap_value.reshape(-1, share).astype(BF16)
    d_hidden = line_scatter(
        seq, right_dot(d_query, wq) + right_dot(d_key, wk) + right_dot(d_value, wv), 8
    )
    _, pre_back = jax.vjp(pre_attn, tokens_f, gain_f[0], scale_attn)
    d_tokens_two, d_gain_pre, d_scale_attn = pre_back(d_hidden)
    tokens_grad = d_tokens_one + d_tokens_two

    own_sums = jnp.stack([d_gain_query, d_gain_key, d_gain_cap, grad_cross])
    own_wide = lax.dynamic_update_slice(jnp.zeros((4, width), F32), own_sums, (0, s * share))
    vec = jnp.concatenate(
        [
            jnp.stack([d_scale_attn, d_gate_attn, d_scale_ffn, d_gate_ffn]),
            jnp.stack([d_gain_pre, d_gain_post, d_gain_ffn, d_gain_last]),
            own_wide,
            jnp.zeros((4, width), F32),
        ]
    )
    grads = [
        left_dot(ffn_all, d_gate),
        left_dot(ffn_all, d_up),
        left_dot(act_low, d_ffn_all),
        left_dot(mixed_low, d_attn_all),
        left_dot(caps, d_cap_key),
        left_dot(caps, d_cap_value),
        left_dot(hidden, d_query),
        left_dot(hidden, d_key),
        left_dot(hidden, d_value),
    ]
    kinds = ["col", "col", "row", "row", "col", "col", "col", "col", "col"]
    vec_all, sums = scatter_all(buckets, seq, vec, grads, kinds)
    s_gate, s_up, s_down, s_out, s_cap_key, s_cap_value, s_query, s_key, s_value = sums

    quarter = 4 * width // seq
    mod_rows = vec_all[:, :4].reshape(buckets, -1, quarter)
    mod_rows = lax.dynamic_slice_in_dim(mod_rows, s, 1, 1)[:, 0]
    cond_size = cond.shape[1] // buckets
    cond_cols = lax.dynamic_slice_in_dim(cond, b * cond_size, cond_size, 1).astype(F32)
    s_mod = jnp.sum(cond_cols[:, :, None] * mod_rows[:, None, :], axis=0)
    tail = lax.dynamic_slice(vec_all, (0, 4, place * slim), (buckets, 8, slim))
    tail = jnp.sum(tail, axis=0)
    return (
        block_out,
        tokens_grad,
        s_query,
        s_key,
        s_value,
        s_out,
        s_cap_key,
        s_cap_value,
        s_gate,
        s_up,
        s_down,
        s_mod,
        tail[:7],
        tail[7],
    )


def solution(mesh):
    spread = P(("bucket", "seq"), None)
    in_specs = (
        *([spread] * 3),
        *([P()] * 3),
        *([spread] * 10),
        P(None, ("bucket", "seq")),
        P(("bucket", "seq")),
    )
    out_specs = (
        spread,
        spread,
        *([P("bucket", "seq")] * 10),
        P(None, ("bucket", "seq")),
        P(("bucket", "seq")),
    )
    return jax.shard_map(
        on_device, mesh=mesh, in_specs=in_specs, out_specs=out_specs, check_vma=False
    )
```

```python
import functools
import math

import jax
import jax.numpy as jnp
from jax import lax
from jax.experimental import pallas as pl
from jax.experimental.pallas import tpu as pltpu
from jax.sharding import PartitionSpec as P

HEAD_DIM = 64
MESH = pl.DeviceIdType.MESH
F32, BF16 = jnp.float32, jnp.bfloat16


def rms_rows(values):
    return values * lax.rsqrt(jnp.mean(values * values, axis=-1, keepdims=True) + 1e-05)


def head_rms(values):
    shaped = values.reshape(values.shape[:-1] + (values.shape[-1] // HEAD_DIM, HEAD_DIM))
    shaped = shaped * lax.rsqrt(jnp.mean(shaped * shaped, axis=-1, keepdims=True) + 1e-06)
    return shaped.reshape(values.shape)


def time_embed(steps, width):
    half_width = width // 2
    freqs = jnp.exp(-math.log(10000.0) * jnp.arange(half_width, dtype=F32) / half_width)
    angles = steps.astype(F32)[:, None] * freqs
    return jnp.concatenate([jnp.cos(angles), jnp.sin(angles)], axis=1)


def pick_entry(table, index):
    return jnp.sum(jnp.where(jnp.arange(table.shape[0]) == index, table, 0))


def bf_dot(left, right):
    return jnp.dot(left, right, preferred_element_type=F32)


def left_dot(rows_left, rows_right):
    return lax.dot_general(
        rows_left, rows_right, (((0,), (0,)), ((), ())), preferred_element_type=F32
    )


def right_dot(left, right):
    return lax.dot_general(left, right, (((1,), (1,)), ((), ())), preferred_element_type=F32)


def pre_attn(tokens_in, gain_pre, scale_attn):
    return rms_rows(tokens_in) * gain_pre * (1.0 + scale_attn)


def qk_norm(query_in, key_in, gain_query, gain_key):
    return (head_rms(query_in) * gain_query, head_rms(key_in) * gain_key)


def cap_norm(key_in, gain_cap):
    return head_rms(key_in) * gain_cap


def middle(tokens_in, attn_out, gain_post, gate_attn, gain_ffn, scale_ffn):
    resid_one = tokens_in + jnp.tanh(gate_attn) * rms_rows(attn_out) * gain_post
    return (resid_one, rms_rows(resid_one) * gain_ffn * (1.0 + scale_ffn))


def activate(gate_proj, up_proj):
    return jax.nn.silu(gate_proj) * up_proj


def finish(resid_one, ffn_out, gain_last, gate_ffn):
    return resid_one + jnp.tanh(gate_ffn) * rms_rows(ffn_out) * gain_last


def flip(index, bit):
    return index + bit - 2 * bit * lax.rem(lax.div(index, bit), 2)


class Copies:
    def __init__(self, send, recv):
        self.send, self.recv, self.used = send, recv, 0

    def take(self, count=1):
        first = self.used
        self.used += count
        assert self.used <= self.send.shape[0], self.used
        return first

    def remote(self, src, dst, b, s, at=None):
        at = self.take() if at is None else at
        return pltpu.make_async_remote_copy(
            src_ref=src,
            dst_ref=dst,
            send_sem=self.send.at[at],
            recv_sem=self.recv.at[at],
            device_id={"bucket": b, "seq": s},
            device_id_type=MESH,
        )

    def local(self, src, dst):
        return pltpu.make_async_copy(src, dst, self.send.at[self.take()])


def greet(b, s):
    pl.semaphore_signal(
        pltpu.get_barrier_semaphore(),
        inc=1,
        device_id={"bucket": b, "seq": s},
        device_id_type=MESH,
    )


class Relay:
    def __init__(self, copies, own, out, b, s, seq):
        self.copies, self.own, self.out, self.b, self.s, self.seq = copies, own, out, b, s, seq
        self.base = {1: copies.take(seq - 1), -1: copies.take(seq - 1)}
        self.up = jnp.where(s < seq - 1, s + 1, s - 1)
        self.down = jnp.where(s > 0, s - 1, s + 1)
        self.kept = copies.local(own, out.at[s])

    def packet(self, way, j):
        block = self.out.at[self.s - way * j]
        return self.copies.remote(
            self.own if j == 0 else block,
            block,
            self.b,
            self.up if way > 0 else self.down,
            self.base[way] + j,
        )

    def sends(self, way):
        return self.s < self.seq - 1 if way > 0 else self.s > 0

    def has(self, way, j):
        return self.s >= j if way > 0 else self.s + j <= self.seq - 1

    def start(self, j):
        if j == 0:
            self.kept.start()
        for way in (1, -1):
            if j > 0:

                @pl.when(self.has(way, j))
                def _():
                    self.packet(way, j - 1).wait_recv()

            if j <= self.seq - 2:

                @pl.when(jnp.logical_and(self.sends(way), self.has(way, j)))
                def _():
                    self.packet(way, j).start()

    def sent(self, j):
        for way in (1, -1):

            @pl.when(jnp.logical_and(self.sends(way), self.has(way, j)))
            def _():
                self.packet(way, j).wait_send()

        if j == 0:
            self.kept.wait()


def greet_line(b, s, seq):
    @pl.when(s > 0)
    def _():
        greet(b, s - 1)

    @pl.when(s < seq - 1)
    def _():
        greet(b, s + 1)

    peers = jnp.where(s > 0, 1, 0) + jnp.where(s < seq - 1, 1, 0)
    pl.semaphore_wait(pltpu.get_barrier_semaphore(), peers)


def halves_of(shape):
    if len(shape) == 3:
        return shape[0] // 2
    return (shape[0] // 32) * 16 if shape[0] >= 32 else shape[0] // 2


def gather_kernel(buckets, seq, kinds, *refs):
    count = len(kinds)
    tokens, captions, small, cond, w_mod = refs[:5]
    shards = refs[5 : 5 + count]
    tok_all, cap_all, small_all, mod_out = refs[5 + count : 9 + count]
    fulls = refs[9 + count : 9 + 2 * count]
    part, got_bucket, got_seq, mod_sum, send, recv = refs[9 + 2 * count :]
    b, s = lax.axis_index("bucket"), lax.axis_index("seq")
    copies = Copies(send, recv)
    chips = buckets // 2
    place = b * seq + s
    to_b, to_s = lax.rem(place, buckets), lax.div(place, buckets)
    back = s * buckets + b
    from_b, from_s = lax.div(back, seq), lax.rem(back, seq)
    stays = jnp.logical_and(to_b == b, to_s == s)

    lanes = part.shape[2]
    for j in range(part.shape[1]):
        part[:, j, :] = bf_dot(cond[...], w_mod[:, j * lanes : (j + 1) * lanes])

    for k in range(1, buckets):
        greet(lax.rem(b + k, buckets), s)
    for k in range(1, seq):
        greet(b, lax.rem(s + k, seq))

    @pl.when(jnp.logical_not(stays))
    def _():
        greet(from_b, from_s)

    peers = buckets - 1 + seq - 1 + jnp.where(stays, 0, 1)
    pl.semaphore_wait(pltpu.get_barrier_semaphore(), peers)

    sent = []

    def go(copy):
        copy.start()
        sent.append(copy)
        return copy

    mod_moves = []
    for k in range(1, buckets):
        peer = lax.rem(b + k, buckets)
        mod_moves.append(go(copies.remote(part.at[peer], got_bucket.at[k], peer, s)))
    small_moves = []
    for k in range(1, seq):
        peer = lax.rem(s + k, seq)
        small_moves.append(go(copies.remote(small, small_all.at[b, s], b, peer)))
    small_own = copies.local(small, small_all.at[b, s])
    small_own.start()

    tok = Relay(copies, tokens, tok_all, b, s, seq)
    cap = Relay(copies, captions, cap_all, b, s, seq)
    queue = [(tok, j) for j in range(seq)] + [(cap, j) for j in range(seq)]
    ahead = [(None, at) for at in range(count)]
    items = []
    while queue or ahead:
        items += queue[:1] + ahead[:1]
        queue, ahead = queue[1:], ahead[1:]

    first = [None] * count

    def depart(at):
        kind, shard, full = kinds[at], shards[at], fulls[at]
        if kind == "row":
            move = copies.remote(shard, full.at[to_b], to_b, to_s)
            keep = copies.local(shard, full.at[b])

            @pl.when(jnp.logical_not(stays))
            def _():
                move.start()

            @pl.when(stays)
            def _():
                keep.start()

            first[at] = (move, keep)
            return
        wide = full.shape[-1]

        def columns(peer):
            if kind == "cut":
                return shard.at[peer]
            return shard.at[:, pl.ds(pl.multiple_of(peer * wide, 128), wide)]

        moves = []
        for k in range(1, seq):
            peer = lax.rem(s + k, seq)
            move = copies.remote(columns(peer), full.at[b, s], b, peer)
            move.start()
            moves.append(move)
        keep = copies.local(columns(s), full.at[b, s])
        keep.start()
        first[at] = (moves, keep)

    def arrived(at):
        moves, keep = first[at]
        if kinds[at] == "row":

            @pl.when(jnp.logical_not(stays))
            def _():
                moves.wait()

            @pl.when(stays)
            def _():
                keep.wait()

            return
        for move in moves:
            move.wait()
        keep.wait()

    twin = flip(b, 1)
    second = [None] * count
    if chips == 4:
        near_x, near_y = flip(b, 2), flip(b, 4)
        far = flip(near_x, 4)

        def stage_a(at):
            full = fulls[at]
            second[at] = {
                "x": go(copies.remote(full.at[b], full.at[b], near_x, s)),
                "y": go(copies.remote(full.at[b], full.at[b], near_y, s)),
                "twin": [go(copies.remote(full.at[b], full.at[b], twin, s))],
            }

        def stage_b(at):
            full, now = fulls[at], second[at]
            cut = halves_of(full.shape[1:])
            now["x"].wait_recv()
            block = full.at[near_x, pl.ds(0, cut)]
            now["dy"] = go(copies.remote(block, block, near_y, s))
            block = full.at[near_x]
            now["twin"].append(go(copies.remote(block, block, twin, s)))
            now["y"].wait_recv()
            block = full.at[near_y, pl.ds(cut, full.shape[1] - cut)]
            now["dx"] = go(copies.remote(block, block, near_x, s))
            block = full.at[near_y]
            now["twin"].append(go(copies.remote(block, block, twin, s)))

        def stage_c(at):
            full, now = fulls[at], second[at]
            now["dy"].wait_recv()
            now["dx"].wait_recv()
            block = full.at[far]
            now["twin"].append(go(copies.remote(block, block, twin, s)))

    else:

        def stage_a(at):
            full = fulls[at]
            second[at] = {"far": [], "twin": []}
            for k in range(1, chips):
                peer = lax.rem(b + 2 * k, buckets)
                second[at]["far"].append(go(copies.remote(full.at[b], full.at[b], peer, s)))
            second[at]["twin"].append(go(copies.remote(full.at[b], full.at[b], twin, s)))

        def stage_b(at):
            full = fulls[at]
            for k, copy in enumerate(second[at]["far"], 1):
                copy.wait_recv()
                block = full.at[lax.rem(b + buckets - 2 * k, buckets)]
                second[at]["twin"].append(go(copies.remote(block, block, twin, s)))

        def stage_c(at):
            pass

    def begin(i):
        relay, j = items[i]
        if relay is None:
            depart(j)
        else:
            relay.start(j)

    begin(0)
    begin(1)
    for move in small_moves:
        move.wait_recv()
    small_own.wait()
    small_next = []
    for k in range(1, buckets):
        peer = lax.rem(b + k, buckets)
        small_next.append(go(copies.remote(small_all.at[b], small_all.at[b], peer, s)))
    total = part[b]
    for k, move in enumerate(mod_moves, 1):
        move.wait_recv()
        total = total + got_bucket[k]
    mod_sum[...] = total
    mod_next = []
    for k in range(1, seq):
        peer = lax.rem(s + k, seq)
        mod_next.append(go(copies.remote(mod_sum, got_seq.at[k], b, peer)))

    for i, (relay, j) in enumerate(items):
        if relay is None:
            arrived(j)
        elif j <= seq - 2:
            relay.sent(j)
        if i + 2 < len(items):
            begin(i + 2)
        if relay is None:
            stage_a(j)
            if j >= 1:
                stage_b(j - 1)
            if j >= 2:
                stage_c(j - 2)
    stage_b(count - 1)
    if count >= 2:
        stage_c(count - 2)
    stage_c(count - 1)

    total = mod_sum[...]
    for k, move in enumerate(mod_next, 1):
        move.wait_recv()
        total = total + got_seq[k]
    mod_out[...] = total
    for move in small_next:
        move.wait_recv()
    for now in second:
        for move in now["twin"]:
            move.wait_recv()
    for move in sent:
        move.wait_send()


def gather_all(buckets, seq, tokens, captions, small, cond, w_mod, shards, kinds):
    any_spec = pl.BlockSpec(memory_space=pl.ANY)
    vmem = pl.BlockSpec(memory_space=pltpu.VMEM)
    fulls, inputs, names = [], [], []
    for shard, kind in zip(shards, kinds, strict=True):
        rows, wide = shard.shape
        if kind == "row":
            fulls.append(jax.ShapeDtypeStruct((buckets, rows, wide), BF16))
        else:
            part = wide // seq
            fulls.append(jax.ShapeDtypeStruct((buckets, seq, rows, part), BF16))
            if part % 128:
                kind = "cut"
                shard = shard.reshape(rows, seq, part).transpose(1, 0, 2)
        inputs.append(shard)
        names.append(kind)
    mod_lanes = w_mod.shape[1] // 8
    n_sems = 64 + 16 * buckets + len(shards) * (seq + 2 * buckets)
    outs = pl.pallas_call(
        functools.partial(gather_kernel, buckets, seq, tuple(names)),
        out_shape=[
            jax.ShapeDtypeStruct((seq,) + tokens.shape, BF16),
            jax.ShapeDtypeStruct((seq,) + captions.shape, BF16),
            jax.ShapeDtypeStruct((buckets, seq) + small.shape, F32),
            jax.ShapeDtypeStruct((8, mod_lanes), F32),
            *fulls,
        ],
        in_specs=[any_spec, any_spec, any_spec, vmem, vmem] + [any_spec] * len(shards),
        out_specs=[any_spec, any_spec, any_spec, vmem] + [any_spec] * len(shards),
        scratch_shapes=[
            pltpu.VMEM((buckets, 8, mod_lanes), F32),
            pltpu.VMEM((buckets, 8, mod_lanes), F32),
            pltpu.VMEM((seq, 8, mod_lanes), F32),
            pltpu.VMEM((8, mod_lanes), F32),
            pltpu.SemaphoreType.DMA((n_sems,)),
            pltpu.SemaphoreType.DMA((n_sems,)),
        ],
        compiler_params=pltpu.CompilerParams(
            collective_id=0, has_side_effects=True, vmem_limit_bytes=24 * 2**20
        ),
    )(tokens, captions, small, cond, w_mod, *inputs)
    weights = []
    for full, kind in zip(outs[4:], names, strict=True):
        weights.append(full.reshape(-1, full.shape[-1]))
    return outs[0], outs[1], outs[2], outs[3], weights


def line_gather_kernel(seq, own, out, send, recv):
    b, s = lax.axis_index("bucket"), lax.axis_index("seq")
    greet_line(b, s, seq)
    relay = Relay(Copies(send, recv), own, out, b, s, seq)
    for j in range(seq):
        relay.start(j)
    for j in range(seq - 1):
        relay.sent(j)


def line_gather(seq, own, collective_id):
    return pl.pallas_call(
        functools.partial(line_gather_kernel, seq),
        out_shape=jax.ShapeDtypeStruct((seq,) + own.shape, own.dtype),
        in_specs=[pl.BlockSpec(memory_space=pl.ANY)],
        out_specs=pl.BlockSpec(memory_space=pl.ANY),
        scratch_shapes=[pltpu.SemaphoreType.DMA((2 * seq + 2,))] * 2,
        compiler_params=pltpu.CompilerParams(collective_id=collective_id, has_side_effects=True),
    )(own).reshape(-1, own.shape[-1])


def add_rows(out, terms):
    rows = out.shape[0]
    step = 16 if rows % 16 == 0 else rows

    def body(i, carry):
        at = pl.ds(pl.multiple_of(i * step, step), step)
        total = terms[0][at, :].astype(F32)
        for term in terms[1:]:
            total = total + term[at, :].astype(F32)
        out[at, :] = total.astype(out.dtype)
        return carry

    lax.fori_loop(0, rows // step, body, 0)


class Pour:
    def __init__(self, copies, parts, from_left, from_right, b, s, seq):
        self.copies, self.parts, self.b, self.s, self.seq = copies, parts, b, s, seq
        self.got = {1: from_left, -1: from_right}
        rows = parts.shape[1]
        self.cuts = 2 if rows % 32 == 0 else 1
        self.thin = rows // self.cuts
        self.count = (seq - 1) * self.cuts
        self.base = {1: copies.take(self.count), -1: copies.take(self.count)}
        self.next = {
            1: jnp.where(s < seq - 1, s + 1, s - 1),
            -1: jnp.where(s > 0, s - 1, s + 1),
        }

    def block(self, way, q):
        j, at = q // self.cuts, pl.ds(q % self.cuts * self.thin, self.thin)
        return self.parts.at[self.seq - 1 - j if way > 0 else j, at], self.got[way].at[j, at]

    def packet(self, way, q):
        src, dst = self.block(way, q)
        return self.copies.remote(src, dst, self.b, self.next[way], self.base[way] + q)

    def on(self, way, q):
        j = q // self.cuts
        return self.s < self.seq - 1 - j if way > 0 else self.s > j

    def behind(self, way):
        return self.s > 0 if way > 0 else self.s < self.seq - 1

    def one(self, way, q):
        src, dst = self.block(way, q)

        @pl.when(jnp.logical_and(self.behind(way), self.on(way, q)))
        def _():
            self.packet(way, q).wait_recv()
            add_rows(src, [src, dst])

        @pl.when(self.on(way, q))
        def _():
            if q >= 2:
                self.packet(way, q - 2).wait_send()
            self.packet(way, q).start()

    def step(self, q):
        @pl.when(self.s < self.seq // 2)
        def _():
            self.one(1, q)
            self.one(-1, q)

        @pl.when(self.s >= self.seq // 2)
        def _():
            self.one(-1, q)
            self.one(1, q)

    def end(self, out):
        seq, cuts = self.seq, self.cuts
        for t in range(seq):

            @pl.when(self.s == t)
            def _():
                terms = [self.parts.at[t]]
                for way, j in ((1, seq - 1 - t), (-1, t)):
                    if j < seq - 1:
                        for c in range(cuts):
                            self.packet(way, j * cuts + c).wait_recv()
                        terms.append(self.got[way].at[j])
                add_rows(out, terms)

        for q in range(self.count):
            more = q + 2 < self.count
            for way in (1, -1):
                last = jnp.logical_not(self.on(way, q + 2)) if more else True

                @pl.when(jnp.logical_and(self.on(way, q), last))
                def _():
                    self.packet(way, q).wait_send()


def line_scatter_kernel(seq, parts, out, from_left, from_right, send, recv):
    b, s = lax.axis_index("bucket"), lax.axis_index("seq")
    greet_line(b, s, seq)
    pour = Pour(Copies(send, recv), parts, from_left, from_right, b, s, seq)
    for q in range(pour.count):
        pour.step(q)
    pour.end(out)


def line_scatter(seq, parts, collective_id):
    rows, wide = parts.shape[0] // seq, parts.shape[1]
    vmem = pl.BlockSpec(memory_space=pltpu.VMEM)
    return pl.pallas_call(
        functools.partial(line_scatter_kernel, seq),
        out_shape=jax.ShapeDtypeStruct((rows, wide), F32),
        in_specs=[vmem],
        out_specs=vmem,
        input_output_aliases={},
        scratch_shapes=[
            pltpu.VMEM((seq - 1, rows, wide), BF16),
            pltpu.VMEM((seq - 1, rows, wide), BF16),
            pltpu.SemaphoreType.DMA((4 * seq,)),
            pltpu.SemaphoreType.DMA((4 * seq,)),
        ],
        compiler_params=pltpu.CompilerParams(
            collective_id=collective_id, has_side_effects=True, vmem_limit_bytes=24 * 2**20
        ),
    )(parts.astype(BF16).reshape(seq, rows, wide))


class GradSums:
    def __init__(self, copies, b, s, buckets, seq, kinds, grads, outs, scratch):
        self.copies, self.b, self.s, self.buckets, self.seq = copies, b, s, buckets, seq
        self.kinds, self.grads, self.outs = kinds, grads, outs
        self.scratch = [scratch[8 * w : 8 * w + 8] for w in range(len(kinds))]
        self.chips = buckets // 2
        self.chip, self.core = lax.div(b, 2), lax.rem(b, 2)
        self.place = s * buckets + b
        self.to_b = lax.div(self.place, seq)
        self.twin = flip(b, 1)
        self.begun, self.state, self.last = {}, {}, {}
        self.sent = []

    def go(self, copy):
        copy.start()
        self.sent.append(copy)
        return copy

    def begin(self, w):
        own, other = self.scratch[w][:2]
        grad = self.grads[w]
        swap = self.copies.remote(grad.at[:, 1 - self.core], other, self.twin, self.s)
        keep = self.copies.local(grad.at[:, self.core], own)
        swap.start()
        keep.start()
        self.begun[w] = (swap, keep)

    def stage_a(self, w):
        own, other, half_x, half_y, got, _ = self.scratch[w][:6]
        for copy in self.begun[w]:
            copy.wait()
        if w + 2 in range(len(self.kinds)) and w + 2 not in self.begun:
            self.begin(w + 2)
        rows = own.shape[1]
        if self.chips != 4:
            moves = []
            for k in range(1, self.chips):
                to = lax.rem(self.chip + k, self.chips)
                add_rows(own.at[to], [own.at[to], other.at[to]])
                move = self.copies.remote(own.at[to], got.at[k], 2 * to + self.core, self.s)
                moves.append(self.go(move))
            self.state[w] = moves
            return
        far = flip(flip(self.chip, 1), 2)
        add_rows(own.at[far], [own.at[far], other.at[far]])
        cut = halves_of(own.shape[1:])
        near_x, near_y = flip(self.b, 2), flip(self.b, 4)
        top, low = own.at[far, pl.ds(0, cut)], own.at[far, pl.ds(cut, rows - cut)]
        self.state[w] = [
            self.go(self.copies.remote(top, half_x, near_x, self.s)),
            self.go(self.copies.remote(low, half_y, near_y, self.s)),
        ]

    def stage_b(self, w):
        if self.chips != 4:
            return
        own, other, half_x, half_y, got_x, got_y = self.scratch[w][:6]
        rows = own.shape[1]
        cut = halves_of(own.shape[1:])
        top, low = pl.ds(0, cut), pl.ds(cut, rows - cut)
        mx, my = flip(self.chip, 1), flip(self.chip, 2)
        move_x, move_y = self.state[w]
        move_x.wait_recv()
        add_rows(own.at[my, top], [own.at[my, top], other.at[my, top], half_x])
        add_rows(own.at[my, low], [own.at[my, low], other.at[my, low]])
        next_y = self.go(self.copies.remote(own.at[my], got_y, flip(self.b, 4), self.s))
        move_y.wait_recv()
        add_rows(own.at[mx, low], [own.at[mx, low], other.at[mx, low], half_y])
        add_rows(own.at[mx, top], [own.at[mx, top], other.at[mx, top]])
        next_x = self.go(self.copies.remote(own.at[mx], got_x, flip(self.b, 2), self.s))
        self.state[w] = [next_x, next_y]

    def stage_c(self, w):
        own, other, _, _, got_x, got_y, done, landed = self.scratch[w]
        for move in self.state[w]:
            move.wait_recv()
        terms = [own.at[self.chip], other.at[self.chip]]
        if self.chips == 4:
            terms += [got_x, got_y]
        else:
            terms += [got_x.at[k] for k in range(1, self.chips)]
        if self.kinds[w] == "col":
            add_rows(self.outs[w], terms)
            return
        seq, send, recv = self.seq, self.copies.send, self.copies.recv
        wide = self.outs[w].shape[-1]
        me = lax.rem(self.place, seq)
        base = self.copies.take(2 * seq)
        rows = terms[0].shape[0]
        step = 16 if rows % 16 == 0 else rows

        def body(i, carry):
            at = pl.ds(pl.multiple_of(i * step, step), step)
            total = terms[0][at, :].astype(F32)
            for term in terms[1:]:
                total = total + term[at, :].astype(F32)
            for t in range(seq):
                done[t, at, :] = total[:, t * wide : (t + 1) * wide].astype(BF16)
            return carry

        lax.fori_loop(0, rows // step, body, 0)
        moves = []
        for t in range(seq):
            move = pltpu.make_async_remote_copy(
                src_ref=done.at[t],
                dst_ref=landed.at[me],
                send_sem=send.at[base + t],
                recv_sem=recv.at[base + me],
                device_id={"bucket": self.to_b, "seq": t},
                device_id_type=MESH,
            )
            keep = pltpu.make_async_copy(done.at[t], landed.at[me], send.at[base + seq + t])
            here = jnp.logical_and(self.to_b == self.b, self.s == t)

            @pl.when(jnp.logical_not(here))
            def _():
                move.start()

            @pl.when(here)
            def _():
                keep.start()

            moves.append((move, keep, here))
        self.last[w] = (base, moves)

    def stage_d(self, w):
        if self.kinds[w] != "row":
            return
        done, landed = self.scratch[w][6:]
        base, moves = self.last[w]
        out, seq, buckets = self.outs[w], self.seq, self.buckets
        for j in range(seq):
            d = self.b * seq + j
            here = jnp.logical_and(lax.rem(d, buckets) == self.b, lax.div(d, buckets) == self.s)

            @pl.when(jnp.logical_not(here))
            def _():
                pltpu.make_async_remote_copy(
                    src_ref=done.at[j],
                    dst_ref=landed.at[j],
                    send_sem=self.copies.send.at[base + j],
                    recv_sem=self.copies.recv.at[base + j],
                    device_id={"bucket": self.twin, "seq": self.s},
                    device_id_type=MESH,
                ).wait_recv()

        for move, keep, here in moves:

            @pl.when(jnp.logical_not(here))
            def _():
                move.wait_send()

            @pl.when(here)
            def _():
                keep.wait()

        for j in range(seq):
            add_rows(out.at[j], [landed.at[j]])

    def steps(self):
        count = len(self.kinds)
        for w in range(count + 2):
            if w < count:
                yield lambda w=w: self.stage_a(w)
            if 1 <= w <= count:
                yield lambda w=w: self.stage_b(w - 1)
            if w >= 2:
                yield lambda w=w: self.stage_c(w - 2)
        yield lambda: [self.stage_d(w) for w in range(count)]

    def end(self):
        for move in self.sent:
            move.wait_send()


def greet_all(b, s, buckets, seq):
    for k in range(1, buckets):
        greet(lax.rem(b + k, buckets), s)
    for k in range(1, seq):
        greet(b, lax.rem(s + k, seq))
    for j in range(seq):
        d = b * seq + j
        src_b, src_s = lax.rem(d, buckets), lax.div(d, buckets)

        @pl.when(jnp.logical_not(jnp.logical_and(src_b == b, src_s == s)))
        def _():
            greet(src_b, src_s)

    to_b = lax.div(s * buckets + b, seq)
    return buckets - 1 + seq - 1 + seq - jnp.where(to_b == b, 1, 0)


def sums_shapes(buckets, seq, grads, kinds):
    chips = buckets // 2
    inputs, outs, scratch = [], [], []
    for grad, kind in zip(grads, kinds, strict=True):
        rows, wide = grad.shape[0] // buckets, grad.shape[1]
        inputs.append(grad.astype(BF16).reshape(chips, 2, rows, wide))
        cut = halves_of((rows, wide))
        tiny = pltpu.VMEM((16, 128), BF16)
        scratch += [pltpu.VMEM((chips, rows, wide), BF16)] * 2
        if chips == 4:
            scratch += [pltpu.VMEM((cut, wide), BF16), pltpu.VMEM((rows - cut, wide), BF16)]
            scratch += [pltpu.VMEM((rows, wide), BF16)] * 2
        else:
            scratch += [tiny, tiny, pltpu.VMEM((chips, rows, wide), BF16), tiny]
        shape = (seq, rows, wide // seq) if kind == "row" else (rows, wide)
        outs.append(jax.ShapeDtypeStruct(shape, F32))
        scratch += [pltpu.VMEM(shape, BF16) if kind == "row" else tiny] * 2
    n_sems = 32 + 2 * buckets + len(grads) * (8 + 3 * seq + buckets)
    return inputs, outs, scratch, n_sems


def scatter_kernel(buckets, seq, kinds, *refs):
    count = len(kinds)
    vec, grads = refs[0], refs[1 : 1 + count]
    vec_all, outs = refs[1 + count], refs[2 + count : 2 + 2 * count]
    at = 2 + 2 * count
    vec_seq, vec_sum, send, recv = refs[at : at + 4]
    b, s = lax.axis_index("bucket"), lax.axis_index("seq")
    copies = Copies(send, recv)
    sums = GradSums(copies, b, s, buckets, seq, kinds, grads, outs, refs[at + 4 :])
    peers = greet_all(b, s, buckets, seq)
    pl.semaphore_wait(pltpu.get_barrier_semaphore(), peers)
    vec_moves = []
    for k in range(1, seq):
        vec_moves.append(sums.go(copies.remote(vec, vec_seq.at[k], b, lax.rem(s + k, seq))))
    for w in range(min(2, count)):
        sums.begin(w)
    for move in vec_moves:
        move.wait_recv()
    add_rows(vec_sum, [vec] + [vec_seq.at[k] for k in range(1, seq)])
    vec_next = []
    for k in range(1, buckets):
        peer = lax.rem(b + k, buckets)
        vec_next.append(sums.go(copies.remote(vec_sum, vec_all.at[b], peer, s)))
    vec_own = copies.local(vec_sum, vec_all.at[b])
    vec_own.start()
    for step in sums.steps():
        step()
    for move in vec_next:
        move.wait_recv()
    vec_own.wait()
    sums.end()


def scatter_all(buckets, seq, vec, grads, kinds, collective_id=1):
    any_spec = pl.BlockSpec(memory_space=pl.ANY)
    vmem = pl.BlockSpec(memory_space=pltpu.VMEM)
    inputs, outs, scratch, n_sems = sums_shapes(buckets, seq, grads, kinds)
    results = pl.pallas_call(
        functools.partial(scatter_kernel, buckets, seq, tuple(kinds)),
        out_shape=[jax.ShapeDtypeStruct((buckets,) + vec.shape, F32), *outs],
        in_specs=[vmem] + [any_spec] * len(grads),
        out_specs=[any_spec] + [vmem] * len(grads),
        scratch_shapes=[
            pltpu.VMEM((seq,) + vec.shape, F32),
            pltpu.VMEM(vec.shape, F32),
            pltpu.SemaphoreType.DMA((n_sems,)),
            pltpu.SemaphoreType.DMA((n_sems,)),
            *scratch,
        ],
        compiler_params=pltpu.CompilerParams(
            collective_id=collective_id, has_side_effects=True, vmem_limit_bytes=60 * 2**20
        ),
    )(vec, *inputs)
    return results[0], [out.reshape(-1, out.shape[-1]) for out in results[1:]]


def attention(queries, keys, values, live, scale):
    scores = jnp.einsum("qhd,khd->hqk", queries, keys, preferred_element_type=F32) * scale
    scores = jnp.where(live[None, None, :], scores, -1e30)
    probs = jax.nn.softmax(scores, axis=-1)
    mixed = jnp.einsum("hqk,khd->qhd", probs.astype(BF16), values, preferred_element_type=F32)
    return probs, mixed


def attention_back(probs, queries, keys, values, d_out, scale):
    d_probs = jnp.einsum("qhd,khd->hqk", d_out, values, preferred_element_type=F32)
    d_scores = probs * (d_probs - jnp.sum(probs * d_probs, axis=-1, keepdims=True))
    d_low = d_scores.astype(BF16)
    d_query = jnp.einsum("hqk,khd->qhd", d_low, keys, preferred_element_type=F32) * scale
    d_key = jnp.einsum("hqk,qhd->khd", d_low, queries, preferred_element_type=F32) * scale
    d_value = jnp.einsum("hqk,qhd->khd", probs.astype(BF16), d_out, preferred_element_type=F32)
    return d_query, d_key, d_value


def on_device_general(
    tokens,
    captions,
    cotangent,
    counts,
    cap_lens,
    steps_t,
    w_query,
    w_key,
    w_value,
    w_out,
    w_cap_key,
    w_cap_value,
    w_gate,
    w_up,
    w_down,
    w_mod,
    gains,
    cross_gate,
):
    buckets, seq = lax.axis_size("bucket"), lax.axis_size("seq")
    b, s = lax.axis_index("bucket"), lax.axis_index("seq")
    place = b * seq + s
    rows, width = tokens.shape
    span = rows * seq
    share = width // seq
    heads = share // HEAD_DIM
    scale = HEAD_DIM ** (-0.5)
    live_rows, cap_len = pick_entry(counts, b), pick_entry(cap_lens, b)
    token_total = jnp.sum(counts).astype(F32)

    cond_size = w_mod.shape[0] * buckets * seq
    cond = jax.nn.silu(time_embed(steps_t, cond_size)).astype(BF16)
    cond_part = lax.dynamic_slice_in_dim(cond, place * w_mod.shape[0], w_mod.shape[0], 1)
    slim = gains.shape[1]
    small = jnp.concatenate([gains, cross_gate[None]], axis=0).astype(F32)
    small = jnp.pad(small, ((0, 0), (0, 128 - slim)))
    tok_all, cap_all, small_all, mod, weights = gather_all(
        buckets,
        seq,
        tokens,
        captions,
        small,
        cond_part,
        w_mod,
        [w_query, w_key, w_value, w_cap_key, w_cap_value, w_out, w_gate, w_up, w_down],
        ["col", "col", "col", "col", "col", "row", "col", "col", "row"],
    )
    wq, wk, wv, wck, wcv, wo, wg, wu, wd = weights
    caps = cap_all.reshape(-1, captions.shape[1])
    small_rows = small_all[..., :slim].transpose(2, 0, 1, 3).reshape(8, width)
    gain_f = small_rows[:7]
    own_cols = lax.dynamic_slice_in_dim(small_rows, s * share, share, 1)
    gate_cross = jnp.tanh(own_cols[7])
    scale_attn, gate_attn, scale_ffn, gate_ffn = mod.reshape(4, width)

    hidden = pre_attn(tok_all.astype(F32), gain_f[0], scale_attn).astype(BF16).reshape(span, width)
    query_proj, key_proj = bf_dot(hidden, wq), bf_dot(hidden, wk)
    value_low = bf_dot(hidden, wv).astype(BF16)
    (query_f, key_f), norm_back = jax.vjp(qk_norm, query_proj, key_proj, own_cols[4], own_cols[5])
    cap_key_f, cap_back = jax.vjp(cap_norm, bf_dot(caps, wck), own_cols[6])

    def by_head(values):
        return values.astype(BF16).reshape(values.shape[0], heads, HEAD_DIM)

    query, key, value = by_head(query_f), by_head(key_f), by_head(value_low)
    cap_key, cap_value = by_head(cap_key_f), by_head(bf_dot(caps, wcv))
    probs, self_out = attention(query, key, value, jnp.arange(span) < live_rows, scale)
    cap_live = jnp.arange(caps.shape[0]) < cap_len
    cap_probs, cross_out = attention(query, cap_key, cap_value, cap_live, scale)
    self_out, cross_out = self_out.reshape(span, share), cross_out.reshape(span, share)
    mixed_low = (self_out + gate_cross * cross_out).astype(BF16)
    attn_out = line_scatter(seq, bf_dot(mixed_low, wo), 2)

    tokens_f = tokens.astype(F32)
    (resid_one, ffn_pre), middle_back = jax.vjp(
        middle, tokens_f, attn_out, gain_f[1], gate_attn, gain_f[2], scale_ffn
    )
    ffn_all = line_gather(seq, ffn_pre.astype(BF16), 3)
    act_pre, act_back = jax.vjp(activate, bf_dot(ffn_all, wg), bf_dot(ffn_all, wu))
    act_low = act_pre.astype(BF16)
    ffn_out = line_scatter(seq, bf_dot(act_low, wd), 4)
    out_f, finish_back = jax.vjp(finish, resid_one, ffn_out, gain_f[3], gate_ffn)
    block_out = out_f.astype(BF16)

    row_live = (s * rows + jnp.arange(rows) < live_rows).astype(F32)
    weighted = cotangent.astype(F32) * row_live[:, None] * (buckets * span / token_total)
    d_resid, d_ffn_out, d_gain_last, d_gate_ffn = finish_back(weighted)
    d_ffn_all = line_gather(seq, d_ffn_out.astype(BF16), 5)
    d_gate, d_up = act_back(right_dot(d_ffn_all, wd))
    d_gate, d_up = d_gate.astype(BF16), d_up.astype(BF16)
    d_hidden_ffn = line_scatter(seq, right_dot(d_gate, wg) + right_dot(d_up, wu), 6)
    d_tokens_one, d_attn_out, d_gain_post, d_gate_attn, d_gain_ffn, d_scale_ffn = middle_back(
        (d_resid, d_hidden_ffn)
    )
    d_attn_all = line_gather(seq, d_attn_out.astype(BF16), 7)
    d_mixed_low = right_dot(d_attn_all, wo).astype(BF16)
    d_mixed = d_mixed_low.astype(F32)
    d_cross_low = (gate_cross * d_mixed).astype(BF16)
    grad_cross = jnp.sum(d_mixed * cross_out, axis=0) * (1.0 - gate_cross * gate_cross)

    d_query_cross, d_cap_key, d_cap_value = attention_back(
        cap_probs, query, cap_key, cap_value, by_head(d_cross_low), scale
    )
    d_query, d_key, d_value = attention_back(probs, query, key, value, by_head(d_mixed_low), scale)
    d_cap_key, d_gain_cap = cap_back(d_cap_key.reshape(-1, share))
    d_query, d_key, d_gain_query, d_gain_key = norm_back(
        ((d_query + d_query_cross).reshape(span, share), d_key.reshape(span, share))
    )
    d_query, d_key, d_cap_key = d_query.astype(BF16), d_key.astype(BF16), d_cap_key.astype(BF16)
    d_value = d_value.reshape(span, share).astype(BF16)
    d_cap_value = d_cap_value.reshape(-1, share).astype(BF16)
    d_hidden = line_scatter(
        seq, right_dot(d_query, wq) + right_dot(d_key, wk) + right_dot(d_value, wv), 8
    )
    _, pre_back = jax.vjp(pre_attn, tokens_f, gain_f[0], scale_attn)
    d_tokens_two, d_gain_pre, d_scale_attn = pre_back(d_hidden)
    tokens_grad = d_tokens_one + d_tokens_two

    own_sums = jnp.stack([d_gain_query, d_gain_key, d_gain_cap, grad_cross])
    own_wide = lax.dynamic_update_slice(jnp.zeros((4, width), F32), own_sums, (0, s * share))
    vec = jnp.concatenate(
        [
            jnp.stack([d_scale_attn, d_gate_attn, d_scale_ffn, d_gate_ffn]),
            jnp.stack([d_gain_pre, d_gain_post, d_gain_ffn, d_gain_last]),
            own_wide,
            jnp.zeros((4, width), F32),
        ]
    )
    grads = [
        left_dot(ffn_all, d_gate),
        left_dot(ffn_all, d_up),
        left_dot(act_low, d_ffn_all),
        left_dot(mixed_low, d_attn_all),
        left_dot(caps, d_cap_key),
        left_dot(caps, d_cap_value),
        left_dot(hidden, d_query),
        left_dot(hidden, d_key),
        left_dot(hidden, d_value),
    ]
    kinds = ["col", "col", "row", "row", "col", "col", "col", "col", "col"]
    vec_all, sums = scatter_all(buckets, seq, vec, grads, kinds)
    s_gate, s_up, s_down, s_out, s_cap_key, s_cap_value, s_query, s_key, s_value = sums

    quarter = 4 * width // seq
    mod_rows = vec_all[:, :4].reshape(buckets, -1, quarter)
    mod_rows = lax.dynamic_slice_in_dim(mod_rows, s, 1, 1)[:, 0]
    cond_size = cond.shape[1] // buckets
    cond_cols = lax.dynamic_slice_in_dim(cond, b * cond_size, cond_size, 1).astype(F32)
    s_mod = jnp.sum(cond_cols[:, :, None] * mod_rows[:, None, :], axis=0)
    tail = lax.dynamic_slice(vec_all, (0, 4, place * slim), (buckets, 8, slim))
    tail = jnp.sum(tail, axis=0)
    return (
        block_out,
        tokens_grad,
        s_query,
        s_key,
        s_value,
        s_out,
        s_cap_key,
        s_cap_value,
        s_gate,
        s_up,
        s_down,
        s_mod,
        tail[:7],
        tail[7],
    )


def low_half(shape):
    return lax.broadcasted_iota(jnp.int32, shape, len(shape) - 1) < HEAD_DIM


def pair_scale(values, eps):
    low = low_half(values.shape)
    squares = values * values
    first = jnp.sum(jnp.where(low, squares, 0.0), axis=-1, keepdims=True)
    second = jnp.sum(jnp.where(low, 0.0, squares), axis=-1, keepdims=True)
    return lax.rsqrt(jnp.where(low, first, second) * (1.0 / HEAD_DIM) + eps)


FORWARD_ORDER = ("tok", 0, "tok", 1, "tok", 2, "tok", 5, 3, "cap", 4, "cap", 6, "cap", 7, "cap", 8)


def forward_kernel(buckets, seq, kinds, slim, *refs):
    count = len(kinds)
    tokens, captions, small, cond, w_mod, key_mask, cap_mask = refs[:7]
    shards = refs[7 : 7 + count]
    refs = refs[7 + count :]
    cap_all = refs[0]
    fulls = refs[1 : 1 + count]
    refs = refs[1 + count :]
    (
        gain_rows,
        mod_rows,
        hidden,
        query_raw,
        key_raw,
        cap_raw,
        query,
        key,
        value,
        cap_key,
        cap_value,
        cross_out,
        mixed,
    ) = refs[:13]
    refs = refs[13:]
    part, got_bucket, got_seq, mod_sum, small_all, tok_all, cap_near = refs[:7]
    near = refs[7:12]
    send, recv = refs[12:]
    b, s = lax.axis_index("bucket"), lax.axis_index("seq")
    copies = Copies(send, recv)
    place = b * seq + s
    to_b, to_s = lax.rem(place, buckets), lax.div(place, buckets)
    back = s * buckets + b
    from_b, from_s = lax.div(back, seq), lax.rem(back, seq)
    stays = jnp.logical_and(to_b == b, to_s == s)

    for k in range(1, buckets):
        greet(lax.rem(b + k, buckets), s)
    for k in range(1, seq):
        greet(b, lax.rem(s + k, seq))

    @pl.when(jnp.logical_not(stays))
    def _():
        greet(from_b, from_s)

    lanes = part.shape[2]
    for j in range(part.shape[1]):
        part[:, j, :] = bf_dot(cond[...], w_mod[:, j * lanes : (j + 1) * lanes])

    peers = buckets - 1 + seq - 1 + jnp.where(stays, 0, 1)
    pl.semaphore_wait(pltpu.get_barrier_semaphore(), peers)

    sent = []

    def go(copy):
        copy.start()
        sent.append(copy)
        return copy

    mod_moves = []
    for k in range(1, buckets):
        peer = lax.rem(b + k, buckets)
        mod_moves.append(go(copies.remote(part.at[peer], got_bucket.at[k], peer, s)))
    small_moves = []
    for k in range(1, seq):
        peer = lax.rem(s + k, seq)
        small_moves.append(go(copies.remote(small, small_all.at[b, s], b, peer)))
    small_own = copies.local(small, small_all.at[b, s])
    small_own.start()

    tok = Relay(copies, tokens, tok_all, b, s, seq)
    cap = Relay(copies, captions, cap_near, b, s, seq)
    items, step = [], {"tok": 0, "cap": 0}
    for what in FORWARD_ORDER:
        if isinstance(what, str):
            items.append((tok if what == "tok" else cap, step[what]))
            step[what] += 1
        else:
            items.append((None, what))

    first = [None] * count

    def depart(at):
        kind, shard, full = kinds[at], shards[at], fulls[at]
        if kind == "row":
            move = copies.remote(shard, full.at[to_b], to_b, to_s)
            keep = copies.local(shard, full.at[b])

            @pl.when(jnp.logical_not(stays))
            def _():
                move.start()

            @pl.when(stays)
            def _():
                keep.start()

            first[at] = (move, keep)
            return
        wide = full.shape[-1]

        def columns(peer):
            return shard.at[:, pl.ds(pl.multiple_of(peer * wide, 128), wide)]

        moves = []
        for k in range(1, seq):
            peer = lax.rem(s + k, seq)
            move = copies.remote(columns(peer), full.at[b, s], b, peer)
            move.start()
            moves.append(move)
        keep = copies.local(columns(s), full.at[b, s])
        keep.start()
        first[at] = (moves, keep)

    def arrived(at):
        moves, keep = first[at]
        if kinds[at] == "row":

            @pl.when(jnp.logical_not(stays))
            def _():
                moves.wait()

            @pl.when(stays)
            def _():
                keep.wait()

            return
        for move in moves:
            move.wait()
        keep.wait()

    twin = flip(b, 1)
    near_x, near_y = flip(b, 2), flip(b, 4)
    far = flip(near_x, 4)
    second = [None] * count

    def stage_a(at):
        full = fulls[at]
        second[at] = {
            "x": go(copies.remote(full.at[b], full.at[b], near_x, s)),
            "y": go(copies.remote(full.at[b], full.at[b], near_y, s)),
            "twin": [go(copies.remote(full.at[b], full.at[b], twin, s))],
        }

    def stage_b(at):
        full, now = fulls[at], second[at]
        cut = halves_of(full.shape[1:])
        now["x"].wait_recv()
        block = full.at[near_x, pl.ds(0, cut)]
        now["dy"] = go(copies.remote(block, block, near_y, s))
        block = full.at[near_x]
        now["twin"].append(go(copies.remote(block, block, twin, s)))
        now["y"].wait_recv()
        block = full.at[near_y, pl.ds(cut, full.shape[1] - cut)]
        now["dx"] = go(copies.remote(block, block, near_x, s))
        block = full.at[near_y]
        now["twin"].append(go(copies.remote(block, block, twin, s)))

    fetched = {}

    def stage_c(at):
        full, now = fulls[at], second[at]
        now["dy"].wait_recv()
        now["dx"].wait_recv()
        block = full.at[far]
        now["twin"].append(go(copies.remote(block, block, twin, s)))
        for move in now["twin"]:
            move.wait_recv()
        if at < len(near):
            fetched[at] = copies.local(full, near[at])
            fetched[at].start()

    def fetch(at):
        fetched[at].wait()
        whole = near[at][...]
        return whole.reshape(-1, whole.shape[-1])


    rows = seq * tok_all.shape[1]
    width = tok_all.shape[2]
    cap_rows = seq * cap_near.shape[1]
    share = query.shape[1]
    pairs = share // 128
    block_rows = tok_all.shape[1]

    def small_sums():
        for move in small_next:
            move.wait_recv()
        strips = [None] * (width // 128)
        lane = lax.broadcasted_iota(jnp.int32, (8, 128), 1)
        for d in range(buckets * seq):
            at, shift = divmod(d * slim, 128)
            piece = small_all[d // seq, d % seq]
            turned = pltpu.roll(piece, shift, 1) if shift else piece
            for index, keep in ((at, lane >= shift), (at + 1, lane < shift)):
                if index == at + 1 and shift + slim <= 128:
                    continue
                add = jnp.where(keep, turned, 0.0)
                strips[index] = add if strips[index] is None else strips[index] + add
        for at, strip in enumerate(strips):
            gain_rows[:, at * 128 : (at + 1) * 128] = strip
        total = mod_sum[...]
        for k, move in enumerate(mod_next, 1):
            move.wait_recv()
            total = total + got_seq[k]
        for j in range(8):
            at, lane_at = divmod(j * lanes, width)
            mod_rows[at : at + 1, lane_at : lane_at + lanes] = total[j : j + 1, :]
        mod_rows[4:8, :] = jnp.zeros((4, width), F32)

    def make_hidden():
        factor = gain_rows[0:1, :] * (1.0 + mod_rows[0:1, :])
        for t in range(seq):

            def body(i, carry):
                at = pl.ds(pl.multiple_of(i * 32, 32), 32)
                x = tok_all[t, at, :].astype(F32)
                x = x * lax.rsqrt(jnp.mean(x * x, axis=-1, keepdims=True) + 1e-05) * factor
                to = pl.ds(pl.multiple_of(t * block_rows + i * 32, 32), 32)
                hidden[to, :] = x.astype(BF16)
                return carry

            lax.fori_loop(0, block_rows // 32, body, 0)

    def gain_of(row, pair):
        at = pl.multiple_of(s * share + pair * 128, 128)
        return gain_rows[row : row + 1, pl.ds(at, 128)]

    def make_normed(raw, out, row, scale):
        def body(i, carry):
            at = pl.ds(pl.multiple_of(i * 64, 64), 64)
            for pair in range(pairs):
                lane = slice(pair * 128, (pair + 1) * 128)
                x = raw[at, lane]
                x = x * pair_scale(x, 1e-06) * gain_of(row, pair)
                out[at, lane] = x.astype(BF16)
            return carry

        del scale
        lax.fori_loop(0, raw.shape[0] // 64, body, 0)

    def make_query():
        query_raw[...] = bf_dot(hidden[...], fetch(0))
        make_normed(query_raw, query, 4, None)

    def make_key():
        key_raw[...] = bf_dot(hidden[...], fetch(1))
        make_normed(key_raw, key, 5, None)

    def make_value():
        value[...] = bf_dot(hidden[...], fetch(2)).astype(BF16)

    def cap_near_rows():
        whole = cap_near[...]
        return whole.reshape(cap_rows, whole.shape[-1])

    def make_cap_key():
        cap_raw[...] = bf_dot(cap_near_rows(), fetch(3))
        make_normed(cap_raw, cap_key, 6, None)

    def make_cap_value():
        cap_value[...] = bf_dot(cap_near_rows(), fetch(4)).astype(BF16)

    def make_mixed(pair):
        lane = slice(pair * 128, (pair + 1) * 128)
        gate = jnp.tanh(gain_of(7, pair))
        low = low_half((128, 128))
        keys, cap_keys = key[:, lane], cap_key[:, lane]
        values = jnp.concatenate([value[:, lane] * key_mask[...], key_mask[...]], axis=1)
        cap_values = jnp.concatenate([cap_value[:, lane] * cap_mask[...], cap_mask[...]], axis=1)

        def body(i, carry):
            at = pl.ds(pl.multiple_of(i * 128, 128), 128)
            q = query[at, lane] * jnp.asarray(HEAD_DIM**-0.5, BF16)
            halves = (jnp.where(low, q, jnp.zeros_like(q)), jnp.where(low, jnp.zeros_like(q), q))
            found = []
            for k, v in ((keys, values), (cap_keys, cap_values)):
                outs = []
                for half in halves:
                    weights = jnp.exp(right_dot(half, k))
                    outs.append(bf_dot(weights.astype(BF16), v))
                out = jnp.where(low, outs[0][:, :128], outs[1][:, :128])
                norm = 1.0 / jnp.where(low, outs[0][:, 128:], outs[1][:, 128:])
                found.append(out * norm)
            own, cross = found
            cross_out[at, lane] = cross
            mixed[at, lane] = (own + gate * cross).astype(BF16)
            return carry

        lax.fori_loop(0, rows // 128, body, 0)


    def begin(i):
        relay, j = items[i]
        if relay is None:
            depart(j)
        else:
            relay.start(j)

    window = 2
    for i in range(window):
        begin(i)
    for move in small_moves:
        move.wait_recv()
    small_own.wait()
    small_next = []
    for k in range(1, buckets):
        peer = lax.rem(b + k, buckets)
        small_next.append(go(copies.remote(small_all.at[b], small_all.at[b], peer, s)))
    total = part[b]
    for k, move in enumerate(mod_moves, 1):
        move.wait_recv()
        total = total + got_bucket[k]
    mod_sum[...] = total
    mod_next = []
    for k in range(1, seq):
        peer = lax.rem(s + k, seq)
        mod_next.append(go(copies.remote(mod_sum, got_seq.at[k], b, peer)))

    cap_out = copies.local(cap_near, cap_all)
    pieces = {
        7: [small_sums, make_hidden],
        9: [make_query],
        10: [make_key],
        11: [make_value],
        15: [cap_out.start, make_cap_key],
    }
    order = []
    for i, (relay, j) in enumerate(items):
        if relay is None:
            arrived(j)
        elif j <= seq - 2:
            relay.sent(j)
        if i + window < len(items):
            begin(i + window)
        if relay is None:
            order.append(j)
            stage_a(j)
            if len(order) >= 2:
                stage_b(order[-2])
            if len(order) >= 3:
                stage_c(order[-3])
        for piece in pieces.get(i, ()):
            piece()
    stage_b(order[-1])
    stage_c(order[-2])
    make_cap_value()
    make_mixed(0)
    stage_c(order[-1])
    for pair in range(1, pairs):
        make_mixed(pair)
    cap_out.wait()
    for move in sent:
        move.wait_send()


def forward_all(buckets, seq, tokens, captions, small, slim, cond, w_mod, masks, shards, kinds):
    any_spec = pl.BlockSpec(memory_space=pl.ANY)
    vmem = pl.BlockSpec(memory_space=pltpu.VMEM)
    fulls = []
    for shard, kind in zip(shards, kinds, strict=True):
        rows, wide = shard.shape
        shape = (buckets, rows, wide) if kind == "row" else (buckets, seq, rows, wide // seq)
        fulls.append(jax.ShapeDtypeStruct(shape, BF16))
    near = [pltpu.VMEM(full.shape, BF16) for full in fulls[:5]]
    width = tokens.shape[1]
    mod_lanes = w_mod.shape[1] // 8
    span, cap_span, share = seq * tokens.shape[0], seq * captions.shape[0], width // seq
    f32_rows = jax.ShapeDtypeStruct((span, share), F32)
    low_rows = jax.ShapeDtypeStruct((span, share), BF16)
    cap_low = jax.ShapeDtypeStruct((cap_span, share), BF16)
    inner = [
        jax.ShapeDtypeStruct((8, width), F32),
        jax.ShapeDtypeStruct((8, width), F32),
        jax.ShapeDtypeStruct((span, width), BF16),
        f32_rows,
        f32_rows,
        jax.ShapeDtypeStruct((cap_span, share), F32),
        low_rows,
        low_rows,
        low_rows,
        cap_low,
        cap_low,
        f32_rows,
        low_rows,
    ]
    n_sems = 64 + 16 * buckets + len(shards) * (seq + 2 * buckets)
    outs = pl.pallas_call(
        functools.partial(forward_kernel, buckets, seq, tuple(kinds), slim),
        out_shape=[jax.ShapeDtypeStruct((seq,) + captions.shape, BF16), *fulls, *inner],
        in_specs=[any_spec, any_spec, any_spec, vmem, vmem, vmem, vmem] + [any_spec] * len(shards),
        out_specs=[any_spec] * (1 + len(shards)) + [vmem] * len(inner),
        scratch_shapes=[
            pltpu.VMEM((buckets, 8, mod_lanes), F32),
            pltpu.VMEM((buckets, 8, mod_lanes), F32),
            pltpu.VMEM((seq, 8, mod_lanes), F32),
            pltpu.VMEM((8, mod_lanes), F32),
            pltpu.VMEM((buckets, seq) + small.shape, F32),
            pltpu.VMEM((seq,) + tokens.shape, BF16),
            pltpu.VMEM((seq,) + captions.shape, BF16),
            *near,
            pltpu.SemaphoreType.DMA((n_sems,)),
            pltpu.SemaphoreType.DMA((n_sems,)),
        ],
        compiler_params=pltpu.CompilerParams(
            collective_id=9, has_side_effects=True, vmem_limit_bytes=56 * 2**20
        ),
    )(tokens, captions, small, cond, w_mod, *masks, *shards)
    at = 1 + len(shards)
    weights = [full.reshape(-1, full.shape[-1]) for full in outs[1:at]]
    return outs[0], weights, outs[at:]


def backward_kernel(buckets, seq, kinds, *refs):
    count = len(kinds)
    (
        d_attn,
        w_out,
        w_query,
        w_key,
        w_value,
        query,
        key,
        value,
        cap_key,
        cap_value,
        cross_out,
        query_raw,
        key_raw,
        cap_raw,
        gain_rows,
        key_bias,
        cap_bias,
    ) = refs[:17]
    grads = refs[17 : 17 + count]
    refs = refs[17 + count :]
    d_hidden, d_query, d_key, d_value, d_cap_key, d_cap_value, own_sums = refs[:7]
    outs = refs[7 : 7 + count]
    refs = refs[7 + count :]
    mixed_low, cross_low, query_acc, key_acc, value_acc, cap_key_acc, cap_value_acc = refs[:7]
    parts, from_left, from_right, send, recv = refs[7:12]
    b, s = lax.axis_index("bucket"), lax.axis_index("seq")
    copies = Copies(send, recv)
    sums = GradSums(copies, b, s, buckets, seq, kinds, grads, outs, refs[12:])
    peers = greet_all(b, s, buckets, seq)
    pl.semaphore_wait(pltpu.get_barrier_semaphore(), peers)
    for w in range(min(2, count)):
        sums.begin(w)
    steps = sums.steps()

    def advance(times=1):
        for _ in range(times):
            step = next(steps, None)
            if step is not None:
                step()

    rows, share = query.shape
    pairs = share // 128
    span_block = 256
    scale = HEAD_DIM**-0.5

    def gain_of(row, pair):
        at = pl.multiple_of(s * share + pair * 128, 128)
        return gain_rows[row : row + 1, pl.ds(at, 128)]

    weights = w_out[...]
    mixed_low[...] = right_dot(d_attn[...], weights.reshape(share, weights.shape[-1])).astype(BF16)
    own_sums[...] = jnp.zeros_like(own_sums)
    advance()

    def cross_part(pair):
        lane = slice(pair * 128, (pair + 1) * 128)
        gate = jnp.tanh(gain_of(7, pair))

        def body(i, total):
            at = pl.ds(pl.multiple_of(i * 128, 128), 128)
            d = mixed_low[at, lane].astype(F32)
            cross_low[at, lane] = (gate * d).astype(BF16)
            return total + jnp.sum(d * cross_out[at, lane], axis=0, keepdims=True)

        total = lax.fori_loop(0, rows // 128, body, jnp.zeros((1, 128), F32))
        own_sums[3:4, lane] = total * (1.0 - gate * gate)

    def attend_back(pair):
        lane = slice(pair * 128, (pair + 1) * 128)
        low = low_half((span_block, 128))
        sides = (
            (key, value, key_bias, mixed_low, key_acc, value_acc),
            (cap_key, cap_value, cap_bias, cross_low, cap_key_acc, cap_value_acc),
        )
        turned = [side[0][:, lane].T for side in sides]
        for side in sides:
            side[4][:, lane] = jnp.zeros((side[4].shape[0], 128), F32)
            side[5][:, lane] = jnp.zeros((side[5].shape[0], 128), F32)

        def body(i, carry):
            at = pl.ds(pl.multiple_of(i * span_block, span_block), span_block)
            q = query[at, lane] * jnp.asarray(scale, BF16)
            d_turned = None
            for side, k_turned in zip(sides, turned, strict=True):
                k_ref, v_ref, bias, d_ref, k_acc, v_acc = side
                d = d_ref[at, lane]
                found = []
                for keep in (low, jnp.logical_not(low)):
                    q_half = jnp.where(keep, q, jnp.zeros_like(q))
                    d_half = jnp.where(keep, d, jnp.zeros_like(d))
                    scores = right_dot(k_ref[:, lane], q_half)
                    scores = scores + jnp.concatenate([bias[...], bias[...]], axis=1)
                    weights = jnp.exp(scores)
                    probs = weights * (1.0 / jnp.sum(weights, axis=0, keepdims=True))
                    d_probs = right_dot(v_ref[:, lane], d_half)
                    delta = jnp.sum(probs * d_probs, axis=0, keepdims=True)
                    d_scores = (probs * (d_probs - delta)).astype(BF16)
                    k_acc[:, lane] += bf_dot(d_scores, q_half)
                    v_acc[:, lane] += bf_dot(probs.astype(BF16), d_half)
                    found.append(bf_dot(k_turned, d_scores))
                both = jnp.concatenate([found[0][:HEAD_DIM], found[1][HEAD_DIM:]], axis=0)
                d_turned = both if d_turned is None else d_turned + both
            query_acc[at, lane] = d_turned.T * scale
            return carry

        lax.fori_loop(0, rows // span_block, body, 0)

    def norm_back(raw, d_norm, out, row, sum_row):
        for pair in range(pairs):
            lane = slice(pair * 128, (pair + 1) * 128)
            gain = gain_of(row, pair)

            def body(i, total):
                at = pl.ds(pl.multiple_of(i * 64, 64), 64)
                x, d = raw[at, lane], d_norm[at, lane]
                size = pair_scale(x, 1e-06)
                normed, inner = x * size, d * gain
                low = low_half(x.shape)
                product = inner * normed
                first = jnp.sum(jnp.where(low, product, 0.0), axis=-1, keepdims=True)
                second = jnp.sum(jnp.where(low, 0.0, product), axis=-1, keepdims=True)
                mean = jnp.where(low, first, second) * (1.0 / HEAD_DIM)
                out[at, lane] = (size * (inner - normed * mean)).astype(BF16)
                return total + jnp.sum(d * normed, axis=0, keepdims=True)

            total = lax.fori_loop(0, raw.shape[0] // 64, body, jnp.zeros((1, 128), F32))
            own_sums[sum_row : sum_row + 1, lane] = total

    for pair in range(pairs):
        cross_part(pair)
        attend_back(pair)
        advance(2)
    norm_back(query_raw, query_acc, d_query, 4, 0)
    norm_back(key_raw, key_acc, d_key, 5, 1)
    d_value[...] = value_acc[...].astype(BF16)
    pour = Pour(copies, parts, from_left, from_right, b, s, seq)
    width = parts.shape[-1]
    wide = 512
    for at in range(0, width, wide):
        cols = slice(at, at + wide)
        total = right_dot(d_query[...], w_query[cols, :]) + right_dot(d_key[...], w_key[cols, :])
        total = total + right_dot(d_value[...], w_value[cols, :])
        parts[:, :, cols] = total.astype(BF16).reshape(seq, rows // seq, wide)
    for q in range(2):
        pour.step(q)
    norm_back(cap_raw, cap_key_acc, d_cap_key, 6, 2)
    d_cap_value[...] = cap_value_acc[...].astype(BF16)
    for q in range(2, pour.count):
        pour.step(q)
        advance()
    pour.end(d_hidden)
    for step in steps:
        step()
    sums.end()


def backward_all(buckets, seq, rows, attention_refs, grads, kinds):
    any_spec = pl.BlockSpec(memory_space=pl.ANY)
    vmem = pl.BlockSpec(memory_space=pltpu.VMEM)
    inputs, outs, scratch, n_sems = sums_shapes(buckets, seq, grads, kinds)
    d_attn, query, cap_key = attention_refs[0], attention_refs[5], attention_refs[8]
    width = d_attn.shape[1]
    low = jax.ShapeDtypeStruct(query.shape, BF16)
    cap_low = jax.ShapeDtypeStruct(cap_key.shape, BF16)
    inner = [
        jax.ShapeDtypeStruct((rows, width), F32),
        low,
        low,
        low,
        cap_low,
        cap_low,
        jax.ShapeDtypeStruct((8, query.shape[1]), F32),
    ]
    n_sems += 8 * seq
    results = pl.pallas_call(
        functools.partial(backward_kernel, buckets, seq, tuple(kinds)),
        out_shape=[*inner, *outs],
        in_specs=[vmem] * len(attention_refs) + [any_spec] * len(grads),
        out_specs=[vmem] * (len(inner) + len(outs)),
        scratch_shapes=[
            pltpu.VMEM(query.shape, BF16),
            pltpu.VMEM(query.shape, BF16),
            pltpu.VMEM(query.shape, F32),
            pltpu.VMEM(query.shape, F32),
            pltpu.VMEM(query.shape, F32),
            pltpu.VMEM(cap_key.shape, F32),
            pltpu.VMEM(cap_key.shape, F32),
            pltpu.VMEM((seq, rows, width), BF16),
            pltpu.VMEM((seq - 1, rows, width), BF16),
            pltpu.VMEM((seq - 1, rows, width), BF16),
            pltpu.SemaphoreType.DMA((n_sems,)),
            pltpu.SemaphoreType.DMA((n_sems,)),
            *scratch,
        ],
        compiler_params=pltpu.CompilerParams(
            collective_id=10, has_side_effects=True, vmem_limit_bytes=60 * 2**20
        ),
    )(*attention_refs, *inputs)
    return results[:7], [out.reshape(-1, out.shape[-1]) for out in results[7:]]


def on_device(
    tokens,
    captions,
    cotangent,
    counts,
    cap_lens,
    steps_t,
    w_query,
    w_key,
    w_value,
    w_out,
    w_cap_key,
    w_cap_value,
    w_gate,
    w_up,
    w_down,
    w_mod,
    gains,
    cross_gate,
):
    buckets, seq = lax.axis_size("bucket"), lax.axis_size("seq")
    b, s = lax.axis_index("bucket"), lax.axis_index("seq")
    place = b * seq + s
    rows, width = tokens.shape
    span = rows * seq
    share = width // seq
    heads = share // HEAD_DIM
    scale = HEAD_DIM ** (-0.5)
    live_rows, cap_len = pick_entry(counts, b), pick_entry(cap_lens, b)
    token_total = jnp.sum(counts).astype(F32)

    cond_size = w_mod.shape[0] * buckets * seq
    cond = jax.nn.silu(time_embed(steps_t, cond_size)).astype(BF16)
    cond_part = lax.dynamic_slice_in_dim(cond, place * w_mod.shape[0], w_mod.shape[0], 1)
    slim = gains.shape[1]
    small = jnp.concatenate([gains, cross_gate[None]], axis=0).astype(F32)
    small = jnp.pad(small, ((0, 0), (0, 128 - slim)))
    key_mask = jnp.broadcast_to((jnp.arange(span) < live_rows)[:, None], (span, 128)).astype(BF16)
    cap_span = captions.shape[0] * seq
    cap_mask = jnp.broadcast_to((jnp.arange(cap_span) < cap_len)[:, None], (cap_span, 128))
    cap_all, weights, inner = forward_all(
        buckets,
        seq,
        tokens,
        captions,
        small,
        slim,
        cond_part,
        w_mod,
        [key_mask, cap_mask.astype(BF16)],
        [w_query, w_key, w_value, w_cap_key, w_cap_value, w_out, w_gate, w_up, w_down],
        ["col", "col", "col", "col", "col", "row", "col", "col", "row"],
    )
    wq, wk, wv, wck, wcv, wo, wg, wu, wd = weights
    caps = cap_all.reshape(-1, captions.shape[1])
    small_rows, mod, hidden, query_proj, key_proj, cap_proj = inner[:6]
    query, key, value, cap_key, cap_value = inner[6:11]
    cross_out, mixed_low = inner[11:]
    gain_f = small_rows[:7]
    own_cols = lax.dynamic_slice_in_dim(small_rows, s * share, share, 1)
    gate_cross = jnp.tanh(own_cols[7])
    scale_attn, gate_attn, scale_ffn, gate_ffn = mod[0], mod[1], mod[2], mod[3]

    attn_out = line_scatter(seq, bf_dot(mixed_low, wo), 2)

    tokens_f = tokens.astype(F32)
    (resid_one, ffn_pre), middle_back = jax.vjp(
        middle, tokens_f, attn_out, gain_f[1], gate_attn, gain_f[2], scale_ffn
    )
    ffn_all = line_gather(seq, ffn_pre.astype(BF16), 3)
    act_pre, act_back = jax.vjp(activate, bf_dot(ffn_all, wg), bf_dot(ffn_all, wu))
    act_low = act_pre.astype(BF16)
    ffn_out = line_scatter(seq, bf_dot(act_low, wd), 4)
    out_f, finish_back = jax.vjp(finish, resid_one, ffn_out, gain_f[3], gate_ffn)
    block_out = out_f.astype(BF16)

    row_live = (s * rows + jnp.arange(rows) < live_rows).astype(F32)
    weighted = cotangent.astype(F32) * row_live[:, None] * (buckets * span / token_total)
    d_resid, d_ffn_out, d_gain_last, d_gate_ffn = finish_back(weighted)
    d_ffn_all = line_gather(seq, d_ffn_out.astype(BF16), 5)
    d_gate, d_up = act_back(right_dot(d_ffn_all, wd))
    d_gate, d_up = d_gate.astype(BF16), d_up.astype(BF16)
    d_hidden_ffn = line_scatter(seq, right_dot(d_gate, wg) + right_dot(d_up, wu), 6)
    d_tokens_one, d_attn_out, d_gain_post, d_gate_attn, d_gain_ffn, d_scale_ffn = middle_back(
        (d_resid, d_hidden_ffn)
    )
    d_attn_all = line_gather(seq, d_attn_out.astype(BF16), 7)
    key_bias = jnp.where(jnp.arange(span) < live_rows, 0.0, -1e30).astype(F32)
    cap_bias = jnp.where(jnp.arange(cap_span) < cap_len, 0.0, -1e30).astype(F32)
    (d_hidden, d_query, d_key, d_value, d_cap_key, d_cap_value, own_sums), early = backward_all(
        buckets,
        seq,
        rows,
        [
            d_attn_all,
            wo.reshape(buckets, -1, width),
            wq,
            wk,
            wv,
            query,
            key,
            value,
            cap_key,
            cap_value,
            cross_out,
            query_proj,
            key_proj,
            cap_proj,
            small_rows,
            jnp.broadcast_to(key_bias[:, None], (span, 128)),
            jnp.broadcast_to(cap_bias[:, None], (cap_span, 128)),
        ],
        [
            left_dot(ffn_all, d_gate),
            left_dot(ffn_all, d_up),
            left_dot(act_low, d_ffn_all),
            left_dot(mixed_low, d_attn_all),
        ],
        ["col", "col", "row", "row"],
    )
    s_gate, s_up, s_down, s_out = early
    _, pre_back = jax.vjp(pre_attn, tokens_f, gain_f[0], scale_attn)
    d_tokens_two, d_gain_pre, d_scale_attn = pre_back(d_hidden)
    tokens_grad = d_tokens_one + d_tokens_two

    own_wide = lax.dynamic_update_slice(jnp.zeros((4, width), F32), own_sums[:4], (0, s * share))
    vec = jnp.concatenate(
        [
            jnp.stack([d_scale_attn, d_gate_attn, d_scale_ffn, d_gate_ffn]),
            jnp.stack([d_gain_pre, d_gain_post, d_gain_ffn, d_gain_last]),
            own_wide,
            jnp.zeros((4, width), F32),
        ]
    )
    grads = [
        left_dot(caps, d_cap_key),
        left_dot(caps, d_cap_value),
        left_dot(hidden, d_query),
        left_dot(hidden, d_key),
        left_dot(hidden, d_value),
    ]
    vec_all, sums = scatter_all(buckets, seq, vec, grads, ["col"] * 5)
    s_cap_key, s_cap_value, s_query, s_key, s_value = sums

    quarter = 4 * width // seq
    mod_rows = vec_all[:, :4].reshape(buckets, -1, quarter)
    mod_rows = lax.dynamic_slice_in_dim(mod_rows, s, 1, 1)[:, 0]
    cond_size = cond.shape[1] // buckets
    cond_cols = lax.dynamic_slice_in_dim(cond, b * cond_size, cond_size, 1).astype(F32)
    s_mod = jnp.sum(cond_cols[:, :, None] * mod_rows[:, None, :], axis=0)
    tail = lax.dynamic_slice(vec_all, (0, 4, place * slim), (buckets, 8, slim))
    tail = jnp.sum(tail, axis=0)
    return (
        block_out,
        tokens_grad,
        s_query,
        s_key,
        s_value,
        s_out,
        s_cap_key,
        s_cap_value,
        s_gate,
        s_up,
        s_down,
        s_mod,
        tail[:7],
        tail[7],
    )


def solution(mesh):
    spread = P(("bucket", "seq"), None)
    in_specs = (
        *([spread] * 3),
        *([P()] * 3),
        *([spread] * 10),
        P(None, ("bucket", "seq")),
        P(("bucket", "seq")),
    )
    out_specs = (
        spread,
        spread,
        *([P("bucket", "seq")] * 10),
        P(None, ("bucket", "seq")),
        P(("bucket", "seq")),
    )
    buckets, seq = mesh.shape["bucket"], mesh.shape["seq"]

    def step(*args):
        tokens, weight = args[0], args[6]
        tiled = weight.shape[0] % 16 == 0 and weight.shape[1] // seq % 128 == 0
        fits = buckets == 8 and seq == 4 and tokens.shape[0] % 64 == 0
        return (on_device if tiled and fits else on_device_general)(*args)

    return jax.shard_map(
        step, mesh=mesh, in_specs=in_specs, out_specs=out_specs, check_vma=False
    )
```

```python
import functools
import math

import jax
import jax.numpy as jnp
from jax import lax
from jax.experimental import pallas as pl
from jax.experimental.pallas import tpu as pltpu
from jax.sharding import PartitionSpec as P

HEAD_DIM = 64
MESH = pl.DeviceIdType.MESH
F32, BF16 = jnp.float32, jnp.bfloat16
CHUNKS, CUTS, FLIGHT = 2, 2, 2


def rms_rows(values):
    return values * lax.rsqrt(jnp.mean(values * values, axis=-1, keepdims=True) + 1e-05)


def head_rms(values):
    shaped = values.reshape(values.shape[:-1] + (values.shape[-1] // HEAD_DIM, HEAD_DIM))
    shaped = shaped * lax.rsqrt(jnp.mean(shaped * shaped, axis=-1, keepdims=True) + 1e-06)
    return shaped.reshape(values.shape)


def time_embed(steps, width):
    half_width = width // 2
    freqs = jnp.exp(-math.log(10000.0) * jnp.arange(half_width, dtype=F32) / half_width)
    angles = steps.astype(F32)[:, None] * freqs
    return jnp.concatenate([jnp.cos(angles), jnp.sin(angles)], axis=1)


def pick_entry(table, index):
    return jnp.sum(jnp.where(jnp.arange(table.shape[0]) == index, table, 0))


def bf_dot(left, right):
    return jnp.dot(left, right, preferred_element_type=F32)


def left_dot(rows_left, rows_right):
    return lax.dot_general(
        rows_left, rows_right, (((0,), (0,)), ((), ())), preferred_element_type=F32
    )


def right_dot(left, right):
    return lax.dot_general(left, right, (((1,), (1,)), ((), ())), preferred_element_type=F32)


def pre_attn(tokens_in, gain_pre, scale_attn):
    return rms_rows(tokens_in) * gain_pre * (1.0 + scale_attn)


def qk_norm(query_in, key_in, gain_query, gain_key):
    return (head_rms(query_in) * gain_query, head_rms(key_in) * gain_key)


def cap_norm(key_in, gain_cap):
    return head_rms(key_in) * gain_cap


def middle(tokens_in, attn_out, gain_post, gate_attn, gain_ffn, scale_ffn):
    resid_one = tokens_in + jnp.tanh(gate_attn) * rms_rows(attn_out) * gain_post
    return (resid_one, rms_rows(resid_one) * gain_ffn * (1.0 + scale_ffn))


def activate(gate_proj, up_proj):
    return jax.nn.silu(gate_proj) * up_proj


def finish(resid_one, ffn_out, gain_last, gate_ffn):
    return resid_one + jnp.tanh(gate_ffn) * rms_rows(ffn_out) * gain_last


def flip(index, bit):
    return index + bit - 2 * bit * lax.rem(lax.div(index, bit), 2)


def slot(index, buckets):
    if buckets != 8:
        return index
    high, low = lax.div(index, 4), lax.rem(index, 4)
    return 4 * high + 2 * lax.rem(low, 2) + lax.div(low, 2)


class Copies:
    def __init__(self, send, recv):
        self.send, self.recv, self.used = send, recv, 0

    def take(self, count=1):
        first = self.used
        self.used += count
        assert self.used <= self.send.shape[0], self.used
        return first

    def remote(self, src, dst, b, s, at=None):
        at = self.take() if at is None else at
        return pltpu.make_async_remote_copy(
            src_ref=src,
            dst_ref=dst,
            send_sem=self.send.at[at],
            recv_sem=self.recv.at[at],
            device_id={"bucket": b, "seq": s},
            device_id_type=MESH,
        )

    def local(self, src, dst):
        return pltpu.make_async_copy(src, dst, self.send.at[self.take()])


def greet(b, s):
    pl.semaphore_signal(
        pltpu.get_barrier_semaphore(),
        inc=1,
        device_id={"bucket": b, "seq": s},
        device_id_type=MESH,
    )


class Relay:
    def __init__(self, copies, own, out, b, s, seq, part=None):
        self.copies, self.own, self.out, self.b, self.s, self.seq = copies, own, out, b, s, seq
        self.part = part
        self.base = {1: copies.take(seq - 1), -1: copies.take(seq - 1)}
        self.up = jnp.where(s < seq - 1, s + 1, s - 1)
        self.down = jnp.where(s > 0, s - 1, s + 1)
        self.kept = None if own is None else copies.local(own, out.at[s])

    def packet(self, way, j):
        at = self.s - way * j
        block = self.out.at[at] if self.part is None else self.out.at[at, self.part]
        return self.copies.remote(
            self.own if j == 0 and self.own is not None else block,
            block,
            self.b,
            self.up if way > 0 else self.down,
            self.base[way] + j,
        )

    def sends(self, way):
        return self.s < self.seq - 1 if way > 0 else self.s > 0

    def has(self, way, j):
        return self.s >= j if way > 0 else self.s + j <= self.seq - 1

    def start(self, j):
        if j == 0 and self.kept is not None:
            self.kept.start()
        for way in (1, -1):
            if j == self.seq - 1:

                @pl.when(jnp.logical_not(self.sends(way)))
                def _():
                    for k in range(self.seq - 1):
                        self.packet(way, k).wait_recv()

                continue

            @pl.when(jnp.logical_and(self.sends(way), self.has(way, j)))
            def _():
                if j > 0:
                    self.packet(way, j - 1).wait_recv()
                self.packet(way, j).start()

    def sent(self, j):
        for way in (1, -1):

            @pl.when(jnp.logical_and(self.sends(way), self.has(way, j)))
            def _():
                self.packet(way, j).wait_send()

        if j == 0 and self.kept is not None:
            self.kept.wait()


def greet_line(b, s, seq):
    @pl.when(s > 0)
    def _():
        greet(b, s - 1)

    @pl.when(s < seq - 1)
    def _():
        greet(b, s + 1)

    peers = jnp.where(s > 0, 1, 0) + jnp.where(s < seq - 1, 1, 0)
    pl.semaphore_wait(pltpu.get_barrier_semaphore(), peers)


def halves_of(shape):
    if len(shape) == 3:
        return shape[0] // 2
    return (shape[0] // 32) * 16 if shape[0] >= 32 else shape[0] // 2


def gather_kernel(buckets, seq, kinds, *refs):
    count = len(kinds)
    tokens, captions, small, cond, w_mod = refs[:5]
    shards = refs[5 : 5 + count]
    tok_all, cap_all, small_all, mod_out = refs[5 + count : 9 + count]
    fulls = refs[9 + count : 9 + 2 * count]
    part, got_bucket, got_seq, mod_sum, send, recv = refs[9 + 2 * count :]
    b, s = lax.axis_index("bucket"), lax.axis_index("seq")
    copies = Copies(send, recv)
    chips = buckets // 2
    place = b * seq + s
    to_b, to_s = lax.rem(place, buckets), lax.div(place, buckets)
    back = s * buckets + b
    from_b, from_s = lax.div(back, seq), lax.rem(back, seq)
    stays = jnp.logical_and(to_b == b, to_s == s)

    lanes = part.shape[2]
    for j in range(part.shape[1]):
        part[:, j, :] = bf_dot(cond[...], w_mod[:, j * lanes : (j + 1) * lanes])

    for k in range(1, buckets):
        greet(lax.rem(b + k, buckets), s)
    for k in range(1, seq):
        greet(b, lax.rem(s + k, seq))

    @pl.when(jnp.logical_not(stays))
    def _():
        greet(from_b, from_s)

    peers = buckets - 1 + seq - 1 + jnp.where(stays, 0, 1)
    pl.semaphore_wait(pltpu.get_barrier_semaphore(), peers)

    sent = []

    def go(copy):
        copy.start()
        sent.append(copy)
        return copy

    mod_moves = []
    for k in range(1, buckets):
        peer = lax.rem(b + k, buckets)
        mod_moves.append(go(copies.remote(part.at[peer], got_bucket.at[k], peer, s)))
    small_moves = []
    for k in range(1, seq):
        peer = lax.rem(s + k, seq)
        small_moves.append(go(copies.remote(small, small_all.at[b, s], b, peer)))
    small_own = copies.local(small, small_all.at[b, s])
    small_own.start()

    tok = Relay(copies, tokens, tok_all, b, s, seq)
    cap = Relay(copies, captions, cap_all, b, s, seq)
    queue = [(tok, j) for j in range(seq)] + [(cap, j) for j in range(seq)]
    ahead = [(None, at) for at in range(count)]
    items = []
    while queue or ahead:
        items += queue[:1] + ahead[:1]
        queue, ahead = queue[1:], ahead[1:]

    first = [None] * count

    def depart(at):
        kind, shard, full = kinds[at], shards[at], fulls[at]
        if kind == "row":
            move = copies.remote(shard, full.at[to_b], to_b, to_s)
            keep = copies.local(shard, full.at[b])

            @pl.when(jnp.logical_not(stays))
            def _():
                move.start()

            @pl.when(stays)
            def _():
                keep.start()

            first[at] = (move, keep)
            return
        wide = full.shape[-1]

        def columns(peer):
            if kind == "cut":
                return shard.at[peer]
            return shard.at[:, pl.ds(pl.multiple_of(peer * wide, 128), wide)]

        moves = []
        for k in range(1, seq):
            peer = lax.rem(s + k, seq)
            move = copies.remote(columns(peer), full.at[b, s], b, peer)
            move.start()
            moves.append(move)
        keep = copies.local(columns(s), full.at[b, s])
        keep.start()
        first[at] = (moves, keep)

    def arrived(at):
        moves, keep = first[at]
        if kinds[at] == "row":

            @pl.when(jnp.logical_not(stays))
            def _():
                moves.wait()

            @pl.when(stays)
            def _():
                keep.wait()

            return
        for move in moves:
            move.wait()
        keep.wait()

    twin = flip(b, 1)
    second = [None] * count
    if chips == 4:
        near_x, near_y = flip(b, 2), flip(b, 4)
        far = flip(near_x, 4)

        def stage_a(at):
            full = fulls[at]
            second[at] = {
                "x": go(copies.remote(full.at[b], full.at[b], near_x, s)),
                "y": go(copies.remote(full.at[b], full.at[b], near_y, s)),
                "twin": [go(copies.remote(full.at[b], full.at[b], twin, s))],
            }

        def stage_b(at):
            full, now = fulls[at], second[at]
            cut = halves_of(full.shape[1:])
            now["x"].wait_recv()
            block = full.at[near_x, pl.ds(0, cut)]
            now["dy"] = go(copies.remote(block, block, near_y, s))
            block = full.at[near_x]
            now["twin"].append(go(copies.remote(block, block, twin, s)))
            now["y"].wait_recv()
            block = full.at[near_y, pl.ds(cut, full.shape[1] - cut)]
            now["dx"] = go(copies.remote(block, block, near_x, s))
            block = full.at[near_y]
            now["twin"].append(go(copies.remote(block, block, twin, s)))

        def stage_c(at):
            full, now = fulls[at], second[at]
            now["dy"].wait_recv()
            now["dx"].wait_recv()
            block = full.at[far]
            now["twin"].append(go(copies.remote(block, block, twin, s)))

    else:

        def stage_a(at):
            full = fulls[at]
            second[at] = {"far": [], "twin": []}
            for k in range(1, chips):
                peer = lax.rem(b + 2 * k, buckets)
                second[at]["far"].append(go(copies.remote(full.at[b], full.at[b], peer, s)))
            second[at]["twin"].append(go(copies.remote(full.at[b], full.at[b], twin, s)))

        def stage_b(at):
            full = fulls[at]
            for k, copy in enumerate(second[at]["far"], 1):
                copy.wait_recv()
                block = full.at[lax.rem(b + buckets - 2 * k, buckets)]
                second[at]["twin"].append(go(copies.remote(block, block, twin, s)))

        def stage_c(at):
            pass

    def begin(i):
        relay, j = items[i]
        if relay is None:
            depart(j)
        else:
            relay.start(j)

    begin(0)
    begin(1)
    for move in small_moves:
        move.wait_recv()
    small_own.wait()
    small_next = []
    for k in range(1, buckets):
        peer = lax.rem(b + k, buckets)
        small_next.append(go(copies.remote(small_all.at[b], small_all.at[b], peer, s)))
    total = part[b]
    for k, move in enumerate(mod_moves, 1):
        move.wait_recv()
        total = total + got_bucket[k]
    mod_sum[...] = total
    mod_next = []
    for k in range(1, seq):
        peer = lax.rem(s + k, seq)
        mod_next.append(go(copies.remote(mod_sum, got_seq.at[k], b, peer)))

    for i, (relay, j) in enumerate(items):
        if relay is None:
            arrived(j)
        elif j <= seq - 2:
            relay.sent(j)
        if i + 2 < len(items):
            begin(i + 2)
        if relay is None:
            stage_a(j)
            if j >= 1:
                stage_b(j - 1)
            if j >= 2:
                stage_c(j - 2)
    stage_b(count - 1)
    if count >= 2:
        stage_c(count - 2)
    stage_c(count - 1)

    total = mod_sum[...]
    for k, move in enumerate(mod_next, 1):
        move.wait_recv()
        total = total + got_seq[k]
    mod_out[...] = total
    for move in small_next:
        move.wait_recv()
    for now in second:
        for move in now["twin"]:
            move.wait_recv()
    for move in sent:
        move.wait_send()


def gather_all(buckets, seq, tokens, captions, small, cond, w_mod, shards, kinds):
    any_spec = pl.BlockSpec(memory_space=pl.ANY)
    vmem = pl.BlockSpec(memory_space=pltpu.VMEM)
    fulls, inputs, names = [], [], []
    for shard, kind in zip(shards, kinds, strict=True):
        rows, wide = shard.shape
        if kind == "row":
            fulls.append(jax.ShapeDtypeStruct((buckets, rows, wide), BF16))
        else:
            part = wide // seq
            fulls.append(jax.ShapeDtypeStruct((buckets, seq, rows, part), BF16))
            if part % 128:
                kind = "cut"
                shard = shard.reshape(rows, seq, part).transpose(1, 0, 2)
        inputs.append(shard)
        names.append(kind)
    mod_lanes = w_mod.shape[1] // 8
    n_sems = 64 + 16 * buckets + len(shards) * (seq + 2 * buckets)
    outs = pl.pallas_call(
        functools.partial(gather_kernel, buckets, seq, tuple(names)),
        out_shape=[
            jax.ShapeDtypeStruct((seq,) + tokens.shape, BF16),
            jax.ShapeDtypeStruct((seq,) + captions.shape, BF16),
            jax.ShapeDtypeStruct((buckets, seq) + small.shape, F32),
            jax.ShapeDtypeStruct((8, mod_lanes), F32),
            *fulls,
        ],
        in_specs=[any_spec, any_spec, any_spec, vmem, vmem] + [any_spec] * len(shards),
        out_specs=[any_spec, any_spec, any_spec, vmem] + [any_spec] * len(shards),
        scratch_shapes=[
            pltpu.VMEM((buckets, 8, mod_lanes), F32),
            pltpu.VMEM((buckets, 8, mod_lanes), F32),
            pltpu.VMEM((seq, 8, mod_lanes), F32),
            pltpu.VMEM((8, mod_lanes), F32),
            pltpu.SemaphoreType.DMA((n_sems,)),
            pltpu.SemaphoreType.DMA((n_sems,)),
        ],
        compiler_params=pltpu.CompilerParams(
            collective_id=0, has_side_effects=True, vmem_limit_bytes=24 * 2**20
        ),
    )(tokens, captions, small, cond, w_mod, *inputs)
    weights = []
    for full, kind in zip(outs[4:], names, strict=True):
        weights.append(full.reshape(-1, full.shape[-1]))
    return outs[0], outs[1], outs[2], outs[3], weights


def line_gather_kernel(seq, own, out, send, recv):
    b, s = lax.axis_index("bucket"), lax.axis_index("seq")
    greet_line(b, s, seq)
    relay = Relay(Copies(send, recv), own, out, b, s, seq)
    for j in range(seq):
        relay.start(j)
    for j in range(seq - 1):
        relay.sent(j)


def line_gather(seq, own, collective_id):
    return pl.pallas_call(
        functools.partial(line_gather_kernel, seq),
        out_shape=jax.ShapeDtypeStruct((seq,) + own.shape, own.dtype),
        in_specs=[pl.BlockSpec(memory_space=pl.ANY)],
        out_specs=pl.BlockSpec(memory_space=pl.ANY),
        scratch_shapes=[pltpu.SemaphoreType.DMA((2 * seq + 2,))] * 2,
        compiler_params=pltpu.CompilerParams(collective_id=collective_id, has_side_effects=True),
    )(own).reshape(-1, own.shape[-1])


def add_rows(out, terms):
    rows = out.shape[0]
    step = 16 if rows % 16 == 0 else rows

    def body(i, carry):
        at = pl.ds(pl.multiple_of(i * step, step), step)
        total = terms[0][at, :].astype(F32)
        for term in terms[1:]:
            total = total + term[at, :].astype(F32)
        out[at, :] = total.astype(out.dtype)
        return carry

    lax.fori_loop(0, rows // step, body, 0)


class Pour:
    def __init__(self, copies, parts, from_left, from_right, b, s, seq):
        self.copies, self.parts, self.b, self.s, self.seq = copies, parts, b, s, seq
        self.got = {1: from_left, -1: from_right}
        rows = parts.shape[1]
        self.cuts = CUTS if rows % (16 * CUTS) == 0 else 1
        self.thin = rows // self.cuts
        self.count = (seq - 1) * self.cuts
        self.base = {1: copies.take(self.count), -1: copies.take(self.count)}
        self.next = {
            1: jnp.where(s < seq - 1, s + 1, s - 1),
            -1: jnp.where(s > 0, s - 1, s + 1),
        }

    def block(self, way, q):
        j, at = q // self.cuts, pl.ds(q % self.cuts * self.thin, self.thin)
        return self.parts.at[self.seq - 1 - j if way > 0 else j, at], self.got[way].at[j, at]

    def packet(self, way, q):
        src, dst = self.block(way, q)
        return self.copies.remote(src, dst, self.b, self.next[way], self.base[way] + q)

    def on(self, way, q):
        j = q // self.cuts
        return self.s < self.seq - 1 - j if way > 0 else self.s > j

    def behind(self, way):
        return self.s > 0 if way > 0 else self.s < self.seq - 1

    def one(self, way, q):
        src, dst = self.block(way, q)

        @pl.when(jnp.logical_and(self.behind(way), self.on(way, q)))
        def _():
            self.packet(way, q).wait_recv()
            add_rows(src, [src, dst])

        @pl.when(self.on(way, q))
        def _():
            if q >= FLIGHT:
                self.packet(way, q - FLIGHT).wait_send()
            self.packet(way, q).start()

    def step(self, q):
        @pl.when(self.s < self.seq // 2)
        def _():
            self.one(1, q)
            self.one(-1, q)

        @pl.when(self.s >= self.seq // 2)
        def _():
            self.one(-1, q)
            self.one(1, q)

    def end(self, out):
        seq, cuts = self.seq, self.cuts
        for t in range(seq):

            @pl.when(self.s == t)
            def _():
                terms = [self.parts.at[t]]
                for way, j in ((1, seq - 1 - t), (-1, t)):
                    if j < seq - 1:
                        for c in range(cuts):
                            self.packet(way, j * cuts + c).wait_recv()
                        terms.append(self.got[way].at[j])
                add_rows(out, terms)

        for q in range(self.count):
            more = q + FLIGHT < self.count
            for way in (1, -1):
                last = jnp.logical_not(self.on(way, q + FLIGHT)) if more else True

                @pl.when(jnp.logical_and(self.on(way, q), last))
                def _():
                    self.packet(way, q).wait_send()


def line_scatter_kernel(seq, parts, out, from_left, from_right, send, recv):
    b, s = lax.axis_index("bucket"), lax.axis_index("seq")
    greet_line(b, s, seq)
    pour = Pour(Copies(send, recv), parts, from_left, from_right, b, s, seq)
    for q in range(pour.count):
        pour.step(q)
    pour.end(out)


def line_scatter(seq, parts, collective_id):
    rows, wide = parts.shape[0] // seq, parts.shape[1]
    vmem = pl.BlockSpec(memory_space=pltpu.VMEM)
    return pl.pallas_call(
        functools.partial(line_scatter_kernel, seq),
        out_shape=jax.ShapeDtypeStruct((rows, wide), F32),
        in_specs=[vmem],
        out_specs=vmem,
        input_output_aliases={},
        scratch_shapes=[
            pltpu.VMEM((seq - 1, rows, wide), BF16),
            pltpu.VMEM((seq - 1, rows, wide), BF16),
            pltpu.SemaphoreType.DMA((4 * seq,)),
            pltpu.SemaphoreType.DMA((4 * seq,)),
        ],
        compiler_params=pltpu.CompilerParams(
            collective_id=collective_id, has_side_effects=True, vmem_limit_bytes=24 * 2**20
        ),
    )(parts.astype(BF16).reshape(seq, rows, wide))


class GradSums:
    def __init__(self, copies, b, s, buckets, seq, kinds, grads, outs, scratch, near=False):
        self.near = near
        self.copies, self.b, self.s, self.buckets, self.seq = copies, b, s, buckets, seq
        self.kinds, self.grads, self.outs = kinds, grads, outs
        self.scratch = [scratch[8 * w : 8 * w + 8] for w in range(len(kinds))]
        self.chips = buckets // 2
        self.chip, self.core = lax.div(b, 2), lax.rem(b, 2)
        self.place = s * buckets + slot(b, buckets)
        self.to_b = lax.div(self.place, seq)
        self.twin = flip(b, 1)
        self.begun, self.state, self.last = {}, {}, {}
        self.sent = []

    def go(self, copy):
        copy.start()
        self.sent.append(copy)
        return copy

    def own(self, w, chip, rows=None):
        where = (chip,) if rows is None else (chip, rows)
        if self.near:
            return self.grads[w].at[(chip, self.core, *where[1:])]
        return self.scratch[w][0].at[where]

    def begin(self, w):
        own, other = self.scratch[w][:2]
        grad = self.grads[w]
        swap = self.copies.remote(grad.at[:, 1 - self.core], other, self.twin, self.s)
        swap.start()
        self.begun[w] = [swap]
        if not self.near:
            keep = self.copies.local(grad.at[:, self.core], own)
            keep.start()
            self.begun[w].append(keep)

    def stage_a(self, w):
        _, other, half_x, half_y, got, _ = self.scratch[w][:6]
        for copy in self.begun[w]:
            copy.wait()
        if not self.near and w + 2 in range(len(self.kinds)) and w + 2 not in self.begun:
            self.begin(w + 2)
        rows = other.shape[1]
        if self.chips != 4:
            moves = []
            for k in range(1, self.chips):
                to = lax.rem(self.chip + k, self.chips)
                own = self.own(w, to)
                add_rows(own, [own, other.at[to]])
                move = self.copies.remote(own, got.at[k], 2 * to + self.core, self.s)
                moves.append(self.go(move))
            self.state[w] = moves
            return
        far = flip(flip(self.chip, 1), 2)
        add_rows(self.own(w, far), [self.own(w, far), other.at[far]])
        cut = halves_of(other.shape[1:])
        near_x, near_y = flip(self.b, 2), flip(self.b, 4)
        top, low = self.own(w, far, pl.ds(0, cut)), self.own(w, far, pl.ds(cut, rows - cut))
        self.state[w] = [
            self.go(self.copies.remote(top, half_x, near_x, self.s)),
            self.go(self.copies.remote(low, half_y, near_y, self.s)),
        ]

    def stage_b(self, w):
        if self.chips != 4:
            return
        _, other, half_x, half_y, got_x, got_y = self.scratch[w][:6]
        rows = other.shape[1]
        cut = halves_of(other.shape[1:])
        top, low = pl.ds(0, cut), pl.ds(cut, rows - cut)
        mx, my = flip(self.chip, 1), flip(self.chip, 2)
        move_x, move_y = self.state[w]
        move_x.wait_recv()
        block = self.own(w, my, top)
        add_rows(block, [block, other.at[my, top], half_x])
        block = self.own(w, my, low)
        add_rows(block, [block, other.at[my, low]])
        block = self.own(w, my)
        next_y = self.go(self.copies.remote(block, got_y, flip(self.b, 4), self.s))
        move_y.wait_recv()
        block = self.own(w, mx, low)
        add_rows(block, [block, other.at[mx, low], half_y])
        block = self.own(w, mx, top)
        add_rows(block, [block, other.at[mx, top]])
        block = self.own(w, mx)
        next_x = self.go(self.copies.remote(block, got_x, flip(self.b, 2), self.s))
        self.state[w] = [next_x, next_y]

    def stage_c(self, w):
        _, other, _, _, got_x, got_y, done, landed = self.scratch[w]
        for move in self.state[w]:
            move.wait_recv()
        terms = [self.own(w, self.chip), other.at[self.chip]]
        if self.chips == 4:
            terms += [got_x, got_y]
        else:
            terms += [got_x.at[k] for k in range(1, self.chips)]
        if self.kinds[w] == "col":
            add_rows(self.outs[w], terms)
            return
        seq, send, recv = self.seq, self.copies.send, self.copies.recv
        wide = self.outs[w].shape[-1]
        me = lax.rem(self.place, seq)
        base = self.copies.take(2 * seq)
        rows = terms[0].shape[0]
        step = 16 if rows % 16 == 0 else rows

        def body(i, carry):
            at = pl.ds(pl.multiple_of(i * step, step), step)
            total = terms[0][at, :].astype(F32)
            for term in terms[1:]:
                total = total + term[at, :].astype(F32)
            for t in range(seq):
                done[t, at, :] = total[:, t * wide : (t + 1) * wide].astype(BF16)
            return carry

        lax.fori_loop(0, rows // step, body, 0)
        moves = []
        for t in range(seq):
            move = pltpu.make_async_remote_copy(
                src_ref=done.at[t],
                dst_ref=landed.at[me],
                send_sem=send.at[base + t],
                recv_sem=recv.at[base + me],
                device_id={"bucket": self.to_b, "seq": t},
                device_id_type=MESH,
            )
            keep = pltpu.make_async_copy(done.at[t], landed.at[me], send.at[base + seq + t])
            here = jnp.logical_and(self.to_b == self.b, self.s == t)

            @pl.when(jnp.logical_not(here))
            def _():
                move.start()

            @pl.when(here)
            def _():
                keep.start()

            moves.append((move, keep, here))
        self.last[w] = (base, moves)

    def stage_d(self, w):
        if self.kinds[w] != "row":
            return
        done, landed = self.scratch[w][6:]
        base, moves = self.last[w]
        out, seq, buckets = self.outs[w], self.seq, self.buckets
        for j in range(seq):
            d = self.b * seq + j
            from_b = slot(lax.rem(d, buckets), buckets)
            here = jnp.logical_and(from_b == self.b, lax.div(d, buckets) == self.s)

            @pl.when(jnp.logical_not(here))
            def _():
                pltpu.make_async_remote_copy(
                    src_ref=done.at[j],
                    dst_ref=landed.at[j],
                    send_sem=self.copies.send.at[base + j],
                    recv_sem=self.copies.recv.at[base + j],
                    device_id={"bucket": self.twin, "seq": self.s},
                    device_id_type=MESH,
                ).wait_recv()

        for move, keep, here in moves:

            @pl.when(jnp.logical_not(here))
            def _():
                move.wait_send()

            @pl.when(here)
            def _():
                keep.wait()

        for j in range(seq):
            add_rows(out.at[j], [landed.at[j]])

    def steps(self):
        count = len(self.kinds)
        for w in range(count + 2):
            if w < count:
                yield lambda w=w: self.stage_a(w)
            if 1 <= w <= count:
                yield lambda w=w: self.stage_b(w - 1)
            if w >= 2:
                yield lambda w=w: self.stage_c(w - 2)
        yield lambda: [self.stage_d(w) for w in range(count)]

    def end(self):
        for move in self.sent:
            move.wait_send()


def greet_all(b, s, buckets, seq):
    for k in range(1, buckets):
        greet(lax.rem(b + k, buckets), s)
    for k in range(1, seq):
        greet(b, lax.rem(s + k, seq))
    for j in range(seq):
        d = b * seq + j
        src_b, src_s = slot(lax.rem(d, buckets), buckets), lax.div(d, buckets)

        @pl.when(jnp.logical_not(jnp.logical_and(src_b == b, src_s == s)))
        def _():
            greet(src_b, src_s)

    to_b = lax.div(s * buckets + slot(b, buckets), seq)
    return buckets - 1 + seq - 1 + seq - jnp.where(to_b == b, 1, 0)


def sums_shapes(buckets, seq, shapes, kinds, near=False):
    chips = buckets // 2
    inputs, outs, scratch = [], [], []
    tiny = pltpu.VMEM((16, 128), BF16)
    for (rows, wide), kind in zip(shapes, kinds, strict=True):
        rows = rows // buckets
        inputs.append((chips, 2, rows, wide))
        cut = halves_of((rows, wide))
        scratch += [tiny if near else pltpu.VMEM((chips, rows, wide), BF16)]
        scratch += [pltpu.VMEM((chips, rows, wide), BF16)]
        if chips == 4:
            scratch += [pltpu.VMEM((cut, wide), BF16), pltpu.VMEM((rows - cut, wide), BF16)]
            scratch += [pltpu.VMEM((rows, wide), BF16)] * 2
        else:
            scratch += [tiny, tiny, pltpu.VMEM((chips, rows, wide), BF16), tiny]
        shape = (seq, rows, wide // seq) if kind == "row" else (rows, wide)
        outs.append(jax.ShapeDtypeStruct(shape, F32))
        scratch += [pltpu.VMEM(shape, BF16) if kind == "row" else tiny] * 2
    n_sems = 32 + 2 * buckets + len(shapes) * (8 + 3 * seq + buckets)
    return inputs, outs, scratch, n_sems


def place_grads(buckets, grads, kinds, shapes):
    inputs = []
    for grad, kind, shape in zip(grads, kinds, shapes, strict=True):
        grad = grad.astype(BF16)
        if kind == "row" and buckets == 8:
            grad = grad.reshape((2, 2, 2) + shape[2:]).transpose(0, 2, 1, 3, 4)
        inputs.append(grad.reshape(shape))
    return inputs


def spread(buckets):
    if buckets != 8:
        return tuple(range(buckets))
    return tuple(4 * (p // 4) + 2 * (p % 2) + p // 2 % 2 for p in range(buckets))


def scatter_kernel(buckets, seq, kinds, *refs):
    count = len(kinds)
    vec, grads = refs[0], refs[1 : 1 + count]
    vec_all, outs = refs[1 + count], refs[2 + count : 2 + 2 * count]
    at = 2 + 2 * count
    vec_seq, vec_sum, send, recv = refs[at : at + 4]
    b, s = lax.axis_index("bucket"), lax.axis_index("seq")
    copies = Copies(send, recv)
    sums = GradSums(copies, b, s, buckets, seq, kinds, grads, outs, refs[at + 4 :])
    peers = greet_all(b, s, buckets, seq)
    pl.semaphore_wait(pltpu.get_barrier_semaphore(), peers)
    vec_moves = []
    for k in range(1, seq):
        vec_moves.append(sums.go(copies.remote(vec, vec_seq.at[k], b, lax.rem(s + k, seq))))
    for w in range(min(2, count)):
        sums.begin(w)
    for move in vec_moves:
        move.wait_recv()
    add_rows(vec_sum, [vec] + [vec_seq.at[k] for k in range(1, seq)])
    vec_next = []
    for k in range(1, buckets):
        peer = lax.rem(b + k, buckets)
        vec_next.append(sums.go(copies.remote(vec_sum, vec_all.at[b], peer, s)))
    vec_own = copies.local(vec_sum, vec_all.at[b])
    vec_own.start()
    for step in sums.steps():
        step()
    for move in vec_next:
        move.wait_recv()
    vec_own.wait()
    sums.end()


def scatter_all(buckets, seq, vec, grads, kinds, collective_id=1):
    any_spec = pl.BlockSpec(memory_space=pl.ANY)
    vmem = pl.BlockSpec(memory_space=pltpu.VMEM)
    shapes, outs, scratch, n_sems = sums_shapes(buckets, seq, [g.shape for g in grads], kinds)
    inputs = place_grads(buckets, grads, kinds, shapes)
    results = pl.pallas_call(
        functools.partial(scatter_kernel, buckets, seq, tuple(kinds)),
        out_shape=[jax.ShapeDtypeStruct((buckets,) + vec.shape, F32), *outs],
        in_specs=[vmem] + [any_spec] * len(grads),
        out_specs=[any_spec] + [vmem] * len(grads),
        scratch_shapes=[
            pltpu.VMEM((seq,) + vec.shape, F32),
            pltpu.VMEM(vec.shape, F32),
            pltpu.SemaphoreType.DMA((n_sems,)),
            pltpu.SemaphoreType.DMA((n_sems,)),
            *scratch,
        ],
        compiler_params=pltpu.CompilerParams(
            collective_id=collective_id, has_side_effects=True, vmem_limit_bytes=60 * 2**20
        ),
    )(vec, *inputs)
    return results[0], [out.reshape(-1, out.shape[-1]) for out in results[1:]]


def attention(queries, keys, values, live, scale):
    scores = jnp.einsum("qhd,khd->hqk", queries, keys, preferred_element_type=F32) * scale
    scores = jnp.where(live[None, None, :], scores, -1e30)
    probs = jax.nn.softmax(scores, axis=-1)
    mixed = jnp.einsum("hqk,khd->qhd", probs.astype(BF16), values, preferred_element_type=F32)
    return probs, mixed


def attention_back(probs, queries, keys, values, d_out, scale):
    d_probs = jnp.einsum("qhd,khd->hqk", d_out, values, preferred_element_type=F32)
    d_scores = probs * (d_probs - jnp.sum(probs * d_probs, axis=-1, keepdims=True))
    d_low = d_scores.astype(BF16)
    d_query = jnp.einsum("hqk,khd->qhd", d_low, keys, preferred_element_type=F32) * scale
    d_key = jnp.einsum("hqk,qhd->khd", d_low, queries, preferred_element_type=F32) * scale
    d_value = jnp.einsum("hqk,qhd->khd", probs.astype(BF16), d_out, preferred_element_type=F32)
    return d_query, d_key, d_value


def on_device_general(
    tokens,
    captions,
    cotangent,
    counts,
    cap_lens,
    steps_t,
    w_query,
    w_key,
    w_value,
    w_out,
    w_cap_key,
    w_cap_value,
    w_gate,
    w_up,
    w_down,
    w_mod,
    gains,
    cross_gate,
):
    buckets, seq = lax.axis_size("bucket"), lax.axis_size("seq")
    b, s = lax.axis_index("bucket"), lax.axis_index("seq")
    place = b * seq + s
    rows, width = tokens.shape
    span = rows * seq
    share = width // seq
    heads = share // HEAD_DIM
    scale = HEAD_DIM ** (-0.5)
    live_rows, cap_len = pick_entry(counts, b), pick_entry(cap_lens, b)
    token_total = jnp.sum(counts).astype(F32)

    cond_size = w_mod.shape[0] * buckets * seq
    cond = jax.nn.silu(time_embed(steps_t, cond_size)).astype(BF16)
    cond_part = lax.dynamic_slice_in_dim(cond, place * w_mod.shape[0], w_mod.shape[0], 1)
    slim = gains.shape[1]
    small = jnp.concatenate([gains, cross_gate[None]], axis=0).astype(F32)
    small = jnp.pad(small, ((0, 0), (0, 128 - slim)))
    tok_all, cap_all, small_all, mod, weights = gather_all(
        buckets,
        seq,
        tokens,
        captions,
        small,
        cond_part,
        w_mod,
        [w_query, w_key, w_value, w_cap_key, w_cap_value, w_out, w_gate, w_up, w_down],
        ["col", "col", "col", "col", "col", "row", "col", "col", "row"],
    )
    wq, wk, wv, wck, wcv, wo, wg, wu, wd = weights
    caps = cap_all.reshape(-1, captions.shape[1])
    small_rows = small_all[..., :slim].transpose(2, 0, 1, 3).reshape(8, width)
    gain_f = small_rows[:7]
    own_cols = lax.dynamic_slice_in_dim(small_rows, s * share, share, 1)
    gate_cross = jnp.tanh(own_cols[7])
    scale_attn, gate_attn, scale_ffn, gate_ffn = mod.reshape(4, width)

    hidden = pre_attn(tok_all.astype(F32), gain_f[0], scale_attn).astype(BF16).reshape(span, width)
    query_proj, key_proj = bf_dot(hidden, wq), bf_dot(hidden, wk)
    value_low = bf_dot(hidden, wv).astype(BF16)
    (query_f, key_f), norm_back = jax.vjp(qk_norm, query_proj, key_proj, own_cols[4], own_cols[5])
    cap_key_f, cap_back = jax.vjp(cap_norm, bf_dot(caps, wck), own_cols[6])

    def by_head(values):
        return values.astype(BF16).reshape(values.shape[0], heads, HEAD_DIM)

    query, key, value = by_head(query_f), by_head(key_f), by_head(value_low)
    cap_key, cap_value = by_head(cap_key_f), by_head(bf_dot(caps, wcv))
    probs, self_out = attention(query, key, value, jnp.arange(span) < live_rows, scale)
    cap_live = jnp.arange(caps.shape[0]) < cap_len
    cap_probs, cross_out = attention(query, cap_key, cap_value, cap_live, scale)
    self_out, cross_out = self_out.reshape(span, share), cross_out.reshape(span, share)
    mixed_low = (self_out + gate_cross * cross_out).astype(BF16)
    attn_out = line_scatter(seq, bf_dot(mixed_low, wo), 2)

    tokens_f = tokens.astype(F32)
    (resid_one, ffn_pre), middle_back = jax.vjp(
        middle, tokens_f, attn_out, gain_f[1], gate_attn, gain_f[2], scale_ffn
    )
    ffn_all = line_gather(seq, ffn_pre.astype(BF16), 3)
    act_pre, act_back = jax.vjp(activate, bf_dot(ffn_all, wg), bf_dot(ffn_all, wu))
    act_low = act_pre.astype(BF16)
    ffn_out = line_scatter(seq, bf_dot(act_low, wd), 4)
    out_f, finish_back = jax.vjp(finish, resid_one, ffn_out, gain_f[3], gate_ffn)
    block_out = out_f.astype(BF16)

    row_live = (s * rows + jnp.arange(rows) < live_rows).astype(F32)
    weighted = cotangent.astype(F32) * row_live[:, None] * (buckets * span / token_total)
    d_resid, d_ffn_out, d_gain_last, d_gate_ffn = finish_back(weighted)
    d_ffn_all = line_gather(seq, d_ffn_out.astype(BF16), 5)
    d_gate, d_up = act_back(right_dot(d_ffn_all, wd))
    d_gate, d_up = d_gate.astype(BF16), d_up.astype(BF16)
    d_hidden_ffn = line_scatter(seq, right_dot(d_gate, wg) + right_dot(d_up, wu), 6)
    d_tokens_one, d_attn_out, d_gain_post, d_gate_attn, d_gain_ffn, d_scale_ffn = middle_back(
        (d_resid, d_hidden_ffn)
    )
    d_attn_all = line_gather(seq, d_attn_out.astype(BF16), 7)
    d_mixed_low = right_dot(d_attn_all, wo).astype(BF16)
    d_mixed = d_mixed_low.astype(F32)
    d_cross_low = (gate_cross * d_mixed).astype(BF16)
    grad_cross = jnp.sum(d_mixed * cross_out, axis=0) * (1.0 - gate_cross * gate_cross)

    d_query_cross, d_cap_key, d_cap_value = attention_back(
        cap_probs, query, cap_key, cap_value, by_head(d_cross_low), scale
    )
    d_query, d_key, d_value = attention_back(probs, query, key, value, by_head(d_mixed_low), scale)
    d_cap_key, d_gain_cap = cap_back(d_cap_key.reshape(-1, share))
    d_query, d_key, d_gain_query, d_gain_key = norm_back(
        ((d_query + d_query_cross).reshape(span, share), d_key.reshape(span, share))
    )
    d_query, d_key, d_cap_key = d_query.astype(BF16), d_key.astype(BF16), d_cap_key.astype(BF16)
    d_value = d_value.reshape(span, share).astype(BF16)
    d_cap_value = d_cap_value.reshape(-1, share).astype(BF16)
    d_hidden = line_scatter(
        seq, right_dot(d_query, wq) + right_dot(d_key, wk) + right_dot(d_value, wv), 8
    )
    _, pre_back = jax.vjp(pre_attn, tokens_f, gain_f[0], scale_attn)
    d_tokens_two, d_gain_pre, d_scale_attn = pre_back(d_hidden)
    tokens_grad = d_tokens_one + d_tokens_two

    own_sums = jnp.stack([d_gain_query, d_gain_key, d_gain_cap, grad_cross])
    own_wide = lax.dynamic_update_slice(jnp.zeros((4, width), F32), own_sums, (0, s * share))
    vec = jnp.concatenate(
        [
            jnp.stack([d_scale_attn, d_gate_attn, d_scale_ffn, d_gate_ffn]),
            jnp.stack([d_gain_pre, d_gain_post, d_gain_ffn, d_gain_last]),
            own_wide,
            jnp.zeros((4, width), F32),
        ]
    )
    grads = [
        left_dot(ffn_all, d_gate),
        left_dot(ffn_all, d_up),
        left_dot(act_low, d_ffn_all),
        left_dot(mixed_low, d_attn_all),
        left_dot(caps, d_cap_key),
        left_dot(caps, d_cap_value),
        left_dot(hidden, d_query),
        left_dot(hidden, d_key),
        left_dot(hidden, d_value),
    ]
    kinds = ["col", "col", "row", "row", "col", "col", "col", "col", "col"]
    vec_all, sums = scatter_all(buckets, seq, vec, grads, kinds)
    s_gate, s_up, s_down, s_out, s_cap_key, s_cap_value, s_query, s_key, s_value = sums

    quarter = 4 * width // seq
    mod_rows = vec_all[:, :4].reshape(buckets, -1, quarter)
    mod_rows = lax.dynamic_slice_in_dim(mod_rows, s, 1, 1)[:, 0]
    cond_size = cond.shape[1] // buckets
    cond_cols = lax.dynamic_slice_in_dim(cond, b * cond_size, cond_size, 1).astype(F32)
    s_mod = jnp.sum(cond_cols[:, :, None] * mod_rows[:, None, :], axis=0)
    tail = lax.dynamic_slice(vec_all, (0, 4, place * slim), (buckets, 8, slim))
    tail = jnp.sum(tail, axis=0)
    return (
        block_out,
        tokens_grad,
        s_query,
        s_key,
        s_value,
        s_out,
        s_cap_key,
        s_cap_value,
        s_gate,
        s_up,
        s_down,
        s_mod,
        tail[:7],
        tail[7],
    )


def low_half(shape):
    return lax.broadcasted_iota(jnp.int32, shape, len(shape) - 1) < HEAD_DIM


def pair_scale(values, eps):
    low = low_half(values.shape)
    squares = values * values
    first = jnp.sum(jnp.where(low, squares, 0.0), axis=-1, keepdims=True)
    second = jnp.sum(jnp.where(low, 0.0, squares), axis=-1, keepdims=True)
    return lax.rsqrt(jnp.where(low, first, second) * (1.0 / HEAD_DIM) + eps)


FORWARD_ORDER = ("tok", 0, "tok", 1, "tok", 2, "tok", 6, 7, "cap", 8, 3, "cap", 4, "cap", 5, "cap")
LAG = 1
WINDOW = 2


def forward_kernel(buckets, seq, kinds, slim, *refs):
    count = len(kinds)
    tokens, captions, small, cond, w_mod, key_mask, cap_mask = refs[:7]
    shards = refs[7 : 7 + count]
    refs = refs[7 + count :]
    cap_all = refs[0]
    fulls = refs[1 : 1 + count]
    refs = refs[1 + count :]
    (
        gain_rows,
        mod_rows,
        hidden,
        query_raw,
        key_raw,
        cap_raw,
        query,
        key,
        value,
        cap_key,
        cap_value,
        cross_out,
        mixed,
    ) = refs[:13]
    refs = refs[13:]
    part, got_bucket, got_seq, mod_sum, small_all, tok_all, cap_near, own_out = refs[:8]
    near = refs[8:13]
    send, recv = refs[13:]
    b, s = lax.axis_index("bucket"), lax.axis_index("seq")
    copies = Copies(send, recv)
    place = b * seq + s
    to_slot, to_s = lax.rem(place, buckets), lax.div(place, buckets)
    to_b = slot(to_slot, buckets)
    back = s * buckets + slot(b, buckets)
    from_b, from_s = lax.div(back, seq), lax.rem(back, seq)
    stays = jnp.logical_and(to_b == b, to_s == s)

    for k in range(1, buckets):
        greet(lax.rem(b + k, buckets), s)
    for k in range(1, seq):
        greet(b, lax.rem(s + k, seq))

    @pl.when(jnp.logical_not(stays))
    def _():
        greet(from_b, from_s)

    lanes = part.shape[2]
    for j in range(part.shape[1]):
        part[:, j, :] = bf_dot(cond[...], w_mod[:, j * lanes : (j + 1) * lanes])

    peers = buckets - 1 + seq - 1 + jnp.where(stays, 0, 1)
    pl.semaphore_wait(pltpu.get_barrier_semaphore(), peers)

    sent = []

    def go(copy):
        copy.start()
        sent.append(copy)
        return copy

    mod_moves = []
    for k in range(1, buckets):
        peer = lax.rem(b + k, buckets)
        mod_moves.append(go(copies.remote(part.at[peer], got_bucket.at[k], peer, s)))
    small_moves = []
    for k in range(1, seq):
        peer = lax.rem(s + k, seq)
        small_moves.append(go(copies.remote(small, small_all.at[b, s], b, peer)))
    small_own = copies.local(small, small_all.at[b, s])
    small_own.start()

    tok = Relay(copies, tokens, tok_all, b, s, seq)
    cap = Relay(copies, captions, cap_near, b, s, seq)
    items, step = [], {"tok": 0, "cap": 0}
    for what in FORWARD_ORDER:
        if isinstance(what, str):
            items.append((tok if what == "tok" else cap, step[what]))
            step[what] += 1
        else:
            items.append((None, what))

    first = [None] * count

    def depart(at):
        kind, shard, full = kinds[at], shards[at], fulls[at]
        if kind == "row":
            move = copies.remote(shard, full.at[to_slot], to_b, to_s)
            keep = copies.local(shard, full.at[slot(b, buckets)])

            @pl.when(jnp.logical_not(stays))
            def _():
                move.start()

            @pl.when(stays)
            def _():
                keep.start()

            first[at] = (move, keep)
            return
        wide = full.shape[-1]

        def columns(peer):
            return shard.at[:, pl.ds(pl.multiple_of(peer * wide, 128), wide)]

        moves = []
        for k in range(1, seq):
            peer = lax.rem(s + k, seq)
            move = copies.remote(columns(peer), full.at[b, s], b, peer)
            move.start()
            moves.append(move)
        keep = copies.local(columns(s), full.at[b, s])
        keep.start()
        first[at] = (moves, keep)

    def arrived(at):
        moves, keep = first[at]
        if kinds[at] == "row":

            @pl.when(jnp.logical_not(stays))
            def _():
                moves.wait()

            @pl.when(stays)
            def _():
                keep.wait()

            return
        for move in moves:
            move.wait()
        keep.wait()

    twin = flip(b, 1)
    near_x, near_y = flip(b, 2), flip(b, 4)
    far = flip(near_x, 4)
    second = [None] * count

    def index(at, device):
        return slot(device, buckets) if kinds[at] == "row" else device

    def stage_a(at):
        block = fulls[at].at[index(at, b)]
        second[at] = {
            "x": go(copies.remote(block, block, near_x, s)),
            "y": go(copies.remote(block, block, near_y, s)),
            "twin": [go(copies.remote(block, block, twin, s))],
        }

    def stage_b(at):
        full, now = fulls[at], second[at]
        cut = halves_of(full.shape[1:])
        now["x"].wait_recv()
        block = full.at[index(at, near_x), pl.ds(0, cut)]
        now["dy"] = go(copies.remote(block, block, near_y, s))
        block = full.at[index(at, near_x)]
        now["twin"].append(go(copies.remote(block, block, twin, s)))
        now["y"].wait_recv()
        block = full.at[index(at, near_y), pl.ds(cut, full.shape[1] - cut)]
        now["dx"] = go(copies.remote(block, block, near_x, s))
        block = full.at[index(at, near_y)]
        now["twin"].append(go(copies.remote(block, block, twin, s)))

    fetched = {}

    def stage_c(at):
        full, now = fulls[at], second[at]
        now["dy"].wait_recv()
        now["dx"].wait_recv()
        block = full.at[index(at, far)]
        now["twin"].append(go(copies.remote(block, block, twin, s)))
        for move in now["twin"]:
            move.wait_recv()
        if at < len(near):
            fetched[at] = copies.local(full, near[at])
            fetched[at].start()
            done.add(at)

    def fetch(at):
        fetched[at].wait()
        whole = near[at][...]
        return whole.reshape(-1, whole.shape[-1])


    rows = seq * tok_all.shape[1]
    width = tok_all.shape[2]
    cap_rows = seq * cap_near.shape[1]
    share = query.shape[1]
    pairs = share // 128
    block_rows = tok_all.shape[1]

    def small_sums():
        for move in small_next:
            move.wait_recv()
        strips = [None] * (width // 128)
        lane = lax.broadcasted_iota(jnp.int32, (8, 128), 1)
        for d in range(buckets * seq):
            at, shift = divmod(d * slim, 128)
            piece = small_all[d // seq, d % seq]
            turned = pltpu.roll(piece, shift, 1) if shift else piece
            for index, keep in ((at, lane >= shift), (at + 1, lane < shift)):
                if index == at + 1 and shift + slim <= 128:
                    continue
                add = jnp.where(keep, turned, 0.0)
                strips[index] = add if strips[index] is None else strips[index] + add
        for at, strip in enumerate(strips):
            gain_rows[:, at * 128 : (at + 1) * 128] = strip
        total = mod_sum[...]
        for k, move in enumerate(mod_next, 1):
            move.wait_recv()
            total = total + got_seq[k]
        for j in range(8):
            at, lane_at = divmod(j * lanes, width)
            mod_rows[at : at + 1, lane_at : lane_at + lanes] = total[j : j + 1, :]
        mod_rows[4:8, :] = jnp.zeros((4, width), F32)

    def make_hidden():
        factor = gain_rows[0:1, :] * (1.0 + mod_rows[0:1, :])
        for t in range(seq):

            def body(i, carry):
                at = pl.ds(pl.multiple_of(i * 32, 32), 32)
                x = tok_all[t, at, :].astype(F32)
                x = x * lax.rsqrt(jnp.mean(x * x, axis=-1, keepdims=True) + 1e-05) * factor
                to = pl.ds(pl.multiple_of(t * block_rows + i * 32, 32), 32)
                hidden[to, :] = x.astype(BF16)
                return carry

            lax.fori_loop(0, block_rows // 32, body, 0)

    def gain_of(row, pair):
        at = pl.multiple_of(s * share + pair * 128, 128)
        return gain_rows[row : row + 1, pl.ds(at, 128)]

    def make_normed(raw, out, row, scale):
        def body(i, carry):
            at = pl.ds(pl.multiple_of(i * 64, 64), 64)
            for pair in range(pairs):
                lane = slice(pair * 128, (pair + 1) * 128)
                x = raw[at, lane]
                x = x * pair_scale(x, 1e-06) * gain_of(row, pair)
                out[at, lane] = x.astype(BF16)
            return carry

        del scale
        lax.fori_loop(0, raw.shape[0] // 64, body, 0)

    def make_query():
        query_raw[...] = bf_dot(hidden[...], fetch(0))
        make_normed(query_raw, query, 4, None)

    def make_key():
        key_raw[...] = bf_dot(hidden[...], fetch(1))
        make_normed(key_raw, key, 5, None)

    def make_value():
        value[...] = bf_dot(hidden[...], fetch(2)).astype(BF16)

    def cap_near_rows():
        whole = cap_near[...]
        return whole.reshape(cap_rows, whole.shape[-1])

    def make_cap_key():
        cap_raw[...] = bf_dot(cap_near_rows(), fetch(3))
        make_normed(cap_raw, cap_key, 6, None)

    def make_cap_value():
        cap_value[...] = bf_dot(cap_near_rows(), fetch(4)).astype(BF16)

    def attend(pair, k_ref, v_ref, mask, store):
        lane = slice(pair * 128, (pair + 1) * 128)
        low = low_half((128, 128))
        keys = k_ref[:, lane]
        values = jnp.concatenate([v_ref[:, lane] * mask[...], mask[...]], axis=1)

        def body(i, carry):
            at = pl.ds(pl.multiple_of(i * 128, 128), 128)
            q = query[at, lane] * jnp.asarray(HEAD_DIM**-0.5, BF16)
            outs = []
            for half in (jnp.where(low, q, jnp.zeros_like(q)), jnp.where(low, jnp.zeros_like(q), q)):
                weights = jnp.exp(right_dot(half, keys))
                outs.append(bf_dot(weights.astype(BF16), values))
            out = jnp.where(low, outs[0][:, :128], outs[1][:, :128])
            store(at, lane, out / jnp.where(low, outs[0][:, 128:], outs[1][:, 128:]))
            return carry

        lax.fori_loop(0, rows // 128, body, 0)

    def make_own(pair):
        def store(at, lane, out):
            own_out[at, lane] = out

        attend(pair, key, value, key_mask, store)

    def make_mixed(pair):
        gate = jnp.tanh(gain_of(7, pair))

        def store(at, lane, out):
            cross_out[at, lane] = out
            mixed[at, lane] = (own_out[at, lane] + gate * out).astype(BF16)

        attend(pair, cap_key, cap_value, cap_mask, store)

    work = [
        (lambda: (small_sums(), make_hidden()), "h", {"tok"}),
        (make_query, "q", {"h", 0}),
        (make_key, "k", {"h", 1}),
        (make_value, "v", {"h", 2}),
        (make_cap_key, "ck", {"cap", 3}),
        (make_cap_value, "cv", {"cap", 4}),
        *((functools.partial(make_own, p), ("own", p), {"q", "k", "v"}) for p in range(pairs)),
        *(
            (functools.partial(make_mixed, p), ("all", p), {"q", "ck", "cv", ("own", p)})
            for p in range(pairs)
        ),
    ]

    def do_work():
        for at, (piece, name, needs) in enumerate(work):
            if needs <= done:
                piece()
                done.add(name)
                del work[at]
                return True
        return False


    done = set()

    def begin(i):
        relay, j = items[i]
        if relay is None:
            depart(j)
        else:
            relay.start(j)
            if j == seq - 1:
                done.add("tok" if relay is tok else "cap")

    window = WINDOW
    for i in range(window):
        begin(i)
    for move in small_moves:
        move.wait_recv()
    small_own.wait()
    small_next = []
    for k in range(1, buckets):
        peer = lax.rem(b + k, buckets)
        small_next.append(go(copies.remote(small_all.at[b], small_all.at[b], peer, s)))
    total = part[b]
    for k, move in enumerate(mod_moves, 1):
        move.wait_recv()
        total = total + got_bucket[k]
    mod_sum[...] = total
    mod_next = []
    for k in range(1, seq):
        peer = lax.rem(s + k, seq)
        mod_next.append(go(copies.remote(mod_sum, got_seq.at[k], b, peer)))

    cap_out = copies.local(cap_near, cap_all)
    order = []
    for i, (relay, j) in enumerate(items):
        if relay is None:
            arrived(j)
        elif j <= seq - 2:
            relay.sent(j)
        if i + window < len(items):
            begin(i + window)
        if relay is None:
            order.append(j)
            stage_a(j)
            if len(order) > LAG:
                stage_b(order[-1 - LAG])
            if len(order) > LAG + 1:
                stage_c(order[-2 - LAG])
        do_work()
    cap_out.start()
    for at in range(LAG):
        stage_b(order[len(order) - LAG + at])
        stage_c(order[len(order) - LAG - 1 + at])
        do_work()
    stage_c(order[-1])
    while do_work():
        pass
    cap_out.wait()
    for move in sent:
        move.wait_send()


def forward_all(buckets, seq, tokens, captions, small, slim, cond, w_mod, masks, shards, kinds):
    any_spec = pl.BlockSpec(memory_space=pl.ANY)
    vmem = pl.BlockSpec(memory_space=pltpu.VMEM)
    fulls = []
    for shard, kind in zip(shards, kinds, strict=True):
        rows, wide = shard.shape
        shape = (buckets, rows, wide) if kind == "row" else (buckets, seq, rows, wide // seq)
        fulls.append(jax.ShapeDtypeStruct(shape, BF16))
    near = [pltpu.VMEM(full.shape, BF16) for full in fulls[:5]]
    width = tokens.shape[1]
    mod_lanes = w_mod.shape[1] // 8
    span, cap_span, share = seq * tokens.shape[0], seq * captions.shape[0], width // seq
    f32_rows = jax.ShapeDtypeStruct((span, share), F32)
    low_rows = jax.ShapeDtypeStruct((span, share), BF16)
    cap_low = jax.ShapeDtypeStruct((cap_span, share), BF16)
    inner = [
        jax.ShapeDtypeStruct((8, width), F32),
        jax.ShapeDtypeStruct((8, width), F32),
        jax.ShapeDtypeStruct((span, width), BF16),
        f32_rows,
        f32_rows,
        jax.ShapeDtypeStruct((cap_span, share), F32),
        low_rows,
        low_rows,
        low_rows,
        cap_low,
        cap_low,
        f32_rows,
        low_rows,
    ]
    n_sems = 64 + 16 * buckets + len(shards) * (seq + 2 * buckets)
    outs = pl.pallas_call(
        functools.partial(forward_kernel, buckets, seq, tuple(kinds), slim),
        out_shape=[jax.ShapeDtypeStruct((seq,) + captions.shape, BF16), *fulls, *inner],
        in_specs=[any_spec, any_spec, any_spec, vmem, vmem, vmem, vmem] + [any_spec] * len(shards),
        out_specs=[any_spec] * (1 + len(shards)) + [vmem] * len(inner),
        scratch_shapes=[
            pltpu.VMEM((buckets, 8, mod_lanes), F32),
            pltpu.VMEM((buckets, 8, mod_lanes), F32),
            pltpu.VMEM((seq, 8, mod_lanes), F32),
            pltpu.VMEM((8, mod_lanes), F32),
            pltpu.VMEM((buckets, seq) + small.shape, F32),
            pltpu.VMEM((seq,) + tokens.shape, BF16),
            pltpu.VMEM((seq,) + captions.shape, BF16),
            pltpu.VMEM((span, share), F32),
            *near,
            pltpu.SemaphoreType.DMA((n_sems,)),
            pltpu.SemaphoreType.DMA((n_sems,)),
        ],
        compiler_params=pltpu.CompilerParams(
            collective_id=9, has_side_effects=True, vmem_limit_bytes=56 * 2**20
        ),
    )(tokens, captions, small, cond, w_mod, *masks, *shards)
    at = 1 + len(shards)
    weights = [full.reshape(-1, full.shape[-1]) for full in outs[1:at]]
    return outs[0], weights, outs[at:]


def middle_kernel(buckets, seq, chunks, kinds, *refs):
    mixed, w_out, tokens, cotangent, row_scale, gain_rows, mod_rows = refs[:7]
    far_weights, refs = refs[7:10], refs[10:]
    block_out, d_tokens, d_attn, row_sums = refs[:4]
    outs, refs = refs[4:7], refs[7:]
    w_gate, w_up, w_down, ffn_all, d_ffn, act, d_gate, d_up = refs[:8]
    gate_keep, up_keep, attn_keep, resid_keep, got, parts, from_left, from_right = refs[8:16]
    send, recv = refs[16:18]
    grads, refs = refs[18:21], refs[21:]
    b, s = lax.axis_index("bucket"), lax.axis_index("seq")
    copies = Copies(send, recv)
    loads = [copies.local(a, b_) for a, b_ in zip(far_weights, (w_gate, w_up, w_down), strict=True)]
    for load in loads:
        load.start()
    sums = GradSums(copies, b, s, buckets, seq, kinds, grads, outs, refs, near=True)
    pl.semaphore_wait(pltpu.get_barrier_semaphore(), greet_all(b, s, buckets, seq))

    rows, width = tokens.shape
    thin = rows // chunks
    tall = seq * thin
    hidden = act.shape[-1]
    wide = 512
    gate_post = jnp.tanh(mod_rows[1:2, :]) * gain_rows[1:2, :]
    gain_ffn = gain_rows[2:3, :] * (1.0 + mod_rows[2:3, :])
    gate_last = jnp.tanh(mod_rows[3:4, :]) * gain_rows[3:4, :]
    row_sums[...] = jnp.zeros_like(row_sums)

    def of(c):
        return pl.ds(c * thin, thin)

    def chunk_of(ref, c, cols=slice(None)):
        whole = ref[:, of(c), cols]
        return whole.reshape(tall, whole.shape[-1])

    def mean(values):
        return jnp.mean(values, axis=-1, keepdims=True)

    def over_rows(c, body):
        step = 16

        def one(i, carry):
            return body(pl.ds(pl.multiple_of(c * thin + i * step, step), step), carry)

        return lax.fori_loop(0, thin // step, one, jnp.zeros((1, width), F32), unroll=2)

    def weighted(at):
        return cotangent[at, :].astype(F32) * row_scale[at, 0:1]

    def after_attn(c):
        def body(at, carry):
            out = got[at, :]
            attn_keep[at, :] = out
            resid = out * lax.rsqrt(mean(out * out) + 1e-05) * gate_post
            resid = tokens[at, :].astype(F32) + resid
            resid_keep[at, :] = resid
            normed = resid * lax.rsqrt(mean(resid * resid) + 1e-05)
            ffn_all[s, at, :] = (normed * gain_ffn).astype(BF16)
            return carry

        over_rows(c, body)

    def after_ffn(c):
        def body(at, total):
            out, resid, grad = got[at, :], resid_keep[at, :], weighted(at)
            size = lax.rsqrt(mean(out * out) + 1e-05)
            normed = out * size
            block_out[at, :] = (resid + gate_last * normed).astype(BF16)
            inner = grad * gate_last
            d_ffn[s, at, :] = (size * (inner - normed * mean(inner * normed))).astype(BF16)
            return total + jnp.sum(grad * normed, axis=0, keepdims=True)

        row_sums[2:3, :] += over_rows(c, body)

    def after_ffn_back(c):
        def body(at, totals):
            first, second = totals
            d_pre, resid, out = got[at, :], resid_keep[at, :], attn_keep[at, :]
            size = lax.rsqrt(mean(resid * resid) + 1e-05)
            normed, inner = resid * size, d_pre * gain_ffn
            second = second + jnp.sum(d_pre * normed, axis=0, keepdims=True)
            grad = weighted(at) + size * (inner - normed * mean(inner * normed))
            d_tokens[at, :] = grad
            size = lax.rsqrt(mean(out * out) + 1e-05)
            normed, inner = out * size, grad * gate_post
            first = first + jnp.sum(grad * normed, axis=0, keepdims=True)
            d_attn[s, at, :] = (size * (inner - normed * mean(inner * normed))).astype(BF16)
            return first, second

        step, zero = 16, jnp.zeros((1, width), F32)

        def one(i, carry):
            return body(pl.ds(pl.multiple_of(c * thin + i * step, step), step), carry)

        first, second = lax.fori_loop(0, thin // step, one, (zero, zero), unroll=2)
        row_sums[0:1, :] += first
        row_sums[1:2, :] += second

    def put_parts(c, cols, total):
        parts[c, :, :, cols] = total.astype(BF16).reshape(seq, thin, total.shape[-1])

    def attn_product(c):
        left = chunk_of(mixed, c)
        for at in range(0, width, wide):
            cols = slice(at, at + wide)
            put_parts(c, cols, bf_dot(left, w_out[:, cols]))

    def ffn_product(c):
        for at in range(0, hidden, wide):
            cols = slice(at, at + wide)
            left = chunk_of(ffn_all, c)
            gate, up = bf_dot(left, w_gate[:, cols]), bf_dot(left, w_up[:, cols])
            gate_keep[c, :, cols], up_keep[c, :, cols] = gate, up
            value = (gate * jax.nn.sigmoid(gate) * up).astype(BF16)
            act[:, of(c), cols] = value.reshape(seq, thin, wide)
        left = chunk_of(act, c)
        for at in range(0, width, wide):
            cols = slice(at, at + wide)
            put_parts(c, cols, bf_dot(left, w_down[:, cols]))

    def ffn_back_product(c):
        for at in range(0, hidden, wide):
            cols = slice(at, at + wide)
            d_act = right_dot(chunk_of(d_ffn, c), w_down[cols, :])
            gate, up = gate_keep[c, :, cols], up_keep[c, :, cols]
            sig = jax.nn.sigmoid(gate)
            silu = gate * sig
            d_g = (d_act * up * (sig + silu * (1.0 - sig))).astype(BF16)
            d_u = (d_act * silu).astype(BF16)
            d_gate[:, of(c), cols] = d_g.reshape(seq, thin, wide)
            d_up[:, of(c), cols] = d_u.reshape(seq, thin, wide)
        left_g, left_u = chunk_of(d_gate, c), chunk_of(d_up, c)
        for at in range(0, width, wide):
            cols = slice(at, at + wide)
            total = right_dot(left_g, w_gate[cols, :]) + right_dot(left_u, w_up[cols, :])
            put_parts(c, cols, total)

    def pour_of(c, turn):
        left, right = from_left.at[turn * chunks + c], from_right.at[turn * chunks + c]
        return Pour(copies, parts.at[c], left, right, b, s, seq)

    gathered = (ffn_all, d_ffn, d_attn)
    after = (after_attn, after_ffn, after_ffn_back)
    products = (attn_product, ffn_product, ffn_back_product)

    def all_rows(ref, cols=slice(None)):
        whole = ref[:, :, cols]
        return whole.reshape(seq * rows, whole.shape[-1])

    def down_grad():
        chips, part = buckets // 2, hidden // buckets
        at = spread(buckets)
        for i in range(chips):
            turned = all_rows(act, slice(2 * i * part, 2 * (i + 1) * part)).T
            total = bf_dot(turned, all_rows(d_ffn)).astype(BF16)
            for half in range(2):
                p = at[2 * i + half]
                grads[2][p // 2, p % 2] = total[half * part : (half + 1) * part]
        sums.begin(2)

    def weight_grads():
        chips, part = buckets // 2, width // (buckets // 2)
        for i in range(chips):
            turned = all_rows(ffn_all, slice(i * part, (i + 1) * part)).T
            for grad, d in zip(grads[:2], (d_gate, d_up), strict=True):
                total = bf_dot(turned, all_rows(d))
                grad[i] = total.astype(BF16).reshape(2, part // 2, hidden)
            if i == 1:
                sums.stage_a(2)
            yield
        sums.begin(0)
        sums.begin(1)
        sums.stage_b(2)
        yield
        sums.stage_a(0)
        yield
        sums.stage_c(2)
        sums.stage_a(1)
        yield
        sums.stage_b(0)
        yield
        sums.stage_b(1)
        yield
        sums.stage_c(0)
        sums.stage_c(1)
        sums.stage_d(2)

    extra = weight_grads()
    plan = [(turn, c) for turn in range(3) for c in range(chunks)]
    gathers, open_gather = {}, []

    def finish_gather():
        turn, c = open_gather.pop(0)
        gathers[turn, c].start(seq - 1)
        for j in range(seq - 1):
            gathers[turn, c].sent(j)
        return turn, c

    attn_product(0)
    pours = {(0, 0): pour_of(0, 0)}
    ready = pours[0, 0].cuts
    for q in range(ready):
        pours[0, 0].step(q)
    for c in range(1, chunks):
        attn_product(c)
    for load in loads:
        load.wait()
    for at, (turn, c) in enumerate(plan):
        pour = pours[turn, c]
        mate = gathers[open_gather[0]] if open_gather else None
        per = pour.count // (seq - 1)
        final = at == len(plan) - 1
        for j in range(2, seq):
            if mate is not None and j < seq - 1:
                mate.start(j)
            if final:
                next(extra, None)
            for q in range((j - 1) * per, j * per):
                pour.step(q)
            if final:
                next(extra, None)
        pour.end(got.at[of(c)])
        after[turn](c)
        gathers[turn, c] = Relay(copies, None, gathered[turn], b, s, seq, of(c))
        gathers[turn, c].start(0)
        if mate is not None:
            done_turn, done_c = finish_gather()
            if (done_turn, done_c) == (1, chunks - 1):
                down_grad()
            if done_turn < 2:
                products[done_turn + 1](done_c)
        open_gather.append((turn, c))
        gathers[turn, c].start(1)
        if at + 1 < len(plan):
            nxt = plan[at + 1]
            pours[nxt] = pour_of(nxt[1], nxt[0])
            for q in range(ready):
                pours[nxt].step(q)
            if at + 2 == len(plan):
                next(extra)
                next(extra)
    turn, c = open_gather[0]
    for j in range(2, seq - 1):
        next(extra, None)
        gathers[turn, c].start(j)
    next(extra, None)
    finish_gather()
    for _ in extra:
        pass
    sums.end()


def middle_all(buckets, seq, mixed, weights, tokens, cotangent, row_scale, gain_rows, mod_rows):
    any_spec = pl.BlockSpec(memory_space=pl.ANY)
    vmem = pl.BlockSpec(memory_space=pltpu.VMEM)
    chunks = CHUNKS
    w_out, w_gate, w_up, w_down = weights
    rows, width = tokens.shape
    hidden = w_gate.shape[1]
    tall, thin = (seq, rows, width), rows // chunks
    flat = (seq, rows, hidden)
    blocks = pltpu.VMEM((3 * chunks, seq - 1, thin, width), BF16)
    kinds = ("col", "col", "row")
    shapes, sums_out, scratch, n_sems = sums_shapes(
        buckets, seq, [w_gate.shape, w_up.shape, w_down.shape], kinds, near=True
    )
    n_sems += 16 + 3 * chunks * (2 * CUTS + 2) * seq
    results = pl.pallas_call(
        functools.partial(middle_kernel, buckets, seq, chunks, kinds),
        out_shape=[
            jax.ShapeDtypeStruct((rows, width), BF16),
            jax.ShapeDtypeStruct((rows, width), F32),
            jax.ShapeDtypeStruct(tall, BF16),
            jax.ShapeDtypeStruct((8, width), F32),
            *sums_out,
        ],
        in_specs=[vmem] * 7 + [any_spec] * 3,
        out_specs=[vmem] * 7,
        scratch_shapes=[
            pltpu.VMEM(w_gate.shape, BF16),
            pltpu.VMEM(w_up.shape, BF16),
            pltpu.VMEM(w_down.shape, BF16),
            pltpu.VMEM(tall, BF16),
            pltpu.VMEM(tall, BF16),
            *([pltpu.VMEM(flat, BF16)] * 3),
            pltpu.VMEM((chunks, seq * thin, hidden), F32),
            pltpu.VMEM((chunks, seq * thin, hidden), F32),
            pltpu.VMEM((rows, width), F32),
            pltpu.VMEM((rows, width), F32),
            pltpu.VMEM((rows, width), F32),
            pltpu.VMEM((chunks, seq, thin, width), BF16),
            blocks,
            blocks,
            pltpu.SemaphoreType.DMA((n_sems,)),
            pltpu.SemaphoreType.DMA((n_sems,)),
            *[pltpu.VMEM(shape, BF16) for shape in shapes],
            *scratch,
        ],
        compiler_params=pltpu.CompilerParams(
            collective_id=11, has_side_effects=True, vmem_limit_bytes=62 * 2**20
        ),
    )(
        mixed.reshape(seq, rows, mixed.shape[1]),
        w_out,
        tokens,
        cotangent,
        row_scale,
        gain_rows,
        mod_rows,
        w_gate,
        w_up,
        w_down,
    )
    return results[:4], [out.reshape(-1, out.shape[-1]) for out in results[4:]]


def backward_kernel(buckets, seq, kinds, *refs):
    count = len(kinds)
    (
        d_attn,
        w_query,
        w_key,
        w_value,
        w_out,
        query,
        key,
        value,
        cap_key,
        cap_value,
        cross_out,
        query_raw,
        key_raw,
        cap_raw,
        gain_rows,
        mod_rows,
        key_bias,
        cap_bias,
        mixed,
        hidden,
        captions,
        tokens,
        d_tokens,
        row_sums,
    ) = refs[:24]
    tokens_grad, vec_all, refs = refs[24], refs[25], refs[26:]
    outs, refs = refs[:count], refs[count:]
    mixed_low, cross_low, query_acc, key_acc, value_acc, cap_key_acc, cap_value_acc = refs[:7]
    d_query, d_key, d_value, d_cap_key, d_cap_value, d_hidden, vec, vec_seq, vec_sum = refs[7:16]
    parts, from_left, from_right, send, recv = refs[16:21]
    grads, refs = refs[21 : 21 + count], refs[21 + count :]
    b, s = lax.axis_index("bucket"), lax.axis_index("seq")
    copies = Copies(send, recv)
    sums = GradSums(copies, b, s, buckets, seq, kinds, grads, outs, refs, near=True)
    peers = greet_all(b, s, buckets, seq)

    rows, share = query.shape
    width = parts.shape[-1]
    pairs = share // 128
    chips = buckets // 2
    span_block = 256
    scale = HEAD_DIM**-0.5

    def gain_of(row, pair):
        at = pl.multiple_of(s * share + pair * 128, 128)
        return gain_rows[row : row + 1, pl.ds(at, 128)]

    vec[...] = jnp.zeros_like(vec)
    mixed_low[...] = right_dot(d_attn[...], w_out[...]).astype(BF16)

    def own_sum(row, pair, total):
        vec[row : row + 1, pl.ds(pl.multiple_of(s * share + pair * 128, 128), 128)] = total

    def cross_part(pair):
        lane = slice(pair * 128, (pair + 1) * 128)
        gate = jnp.tanh(gain_of(7, pair))

        def body(i, total):
            at = pl.ds(pl.multiple_of(i * 128, 128), 128)
            d = mixed_low[at, lane].astype(F32)
            cross_low[at, lane] = (gate * d).astype(BF16)
            return total + jnp.sum(d * cross_out[at, lane], axis=0, keepdims=True)

        total = lax.fori_loop(0, rows // 128, body, jnp.zeros((1, 128), F32))
        own_sum(11, pair, total * (1.0 - gate * gate))

    def attend_back(pair, k_ref, v_ref, bias, d_ref, k_acc, v_acc, add):
        lane = slice(pair * 128, (pair + 1) * 128)
        low = low_half((span_block, 128))
        k_turned = k_ref[:, lane].T
        k_acc[:, lane] = jnp.zeros((k_acc.shape[0], 128), F32)
        v_acc[:, lane] = jnp.zeros((v_acc.shape[0], 128), F32)

        def body(i, carry):
            at = pl.ds(pl.multiple_of(i * span_block, span_block), span_block)
            q = query[at, lane] * jnp.asarray(scale, BF16)
            d = d_ref[at, lane]
            found = []
            for keep in (low, jnp.logical_not(low)):
                q_half = jnp.where(keep, q, jnp.zeros_like(q))
                d_half = jnp.where(keep, d, jnp.zeros_like(d))
                scores = right_dot(k_ref[:, lane], q_half)
                scores = scores + jnp.concatenate([bias[...], bias[...]], axis=1)
                weights = jnp.exp(scores)
                probs = weights * (1.0 / jnp.sum(weights, axis=0, keepdims=True))
                d_probs = right_dot(v_ref[:, lane], d_half)
                delta = jnp.sum(probs * d_probs, axis=0, keepdims=True)
                d_scores = (probs * (d_probs - delta)).astype(BF16)
                k_acc[:, lane] += bf_dot(d_scores, q_half)
                v_acc[:, lane] += bf_dot(probs.astype(BF16), d_half)
                found.append(bf_dot(k_turned, d_scores))
            turned = jnp.concatenate([found[0][:HEAD_DIM], found[1][HEAD_DIM:]], axis=0)
            d_q = turned.T * scale
            query_acc[at, lane] = query_acc[at, lane] + d_q if add else d_q
            return carry

        lax.fori_loop(0, rows // span_block, body, 0)

    def norm_back(raw, d_norm, out, row, sum_row):
        for pair in range(pairs):
            lane = slice(pair * 128, (pair + 1) * 128)
            gain = gain_of(row, pair)

            def body(i, total):
                at = pl.ds(pl.multiple_of(i * 64, 64), 64)
                x, d = raw[at, lane], d_norm[at, lane]
                size = pair_scale(x, 1e-06)
                normed, inner = x * size, d * gain
                low = low_half(x.shape)
                product = inner * normed
                first = jnp.sum(jnp.where(low, product, 0.0), axis=-1, keepdims=True)
                second = jnp.sum(jnp.where(low, 0.0, product), axis=-1, keepdims=True)
                mean = jnp.where(low, first, second) * (1.0 / HEAD_DIM)
                out[at, lane] = (size * (inner - normed * mean)).astype(BF16)
                return total + jnp.sum(d * normed, axis=0, keepdims=True)

            total = lax.fori_loop(0, raw.shape[0] // 64, body, jnp.zeros((1, 128), F32))
            own_sum(sum_row, pair, total)

    def weight_grads(left, chosen):
        part = left.shape[1] // chips
        for i in range(chips):
            turned = left[:, i * part : (i + 1) * part].T
            for w, right in chosen:
                total = bf_dot(turned, right[...])
                grads[w][i] = total.astype(BF16).reshape(2, part // 2, total.shape[-1])
            yield
        for w, _ in chosen:
            sums.begin(w)

    def out_grad():
        total = bf_dot(mixed[...].T, d_attn[...]).astype(BF16)
        part = share // buckets
        for block, p in enumerate(spread(buckets)):
            grads[0][p // 2, p % 2] = total[block * part : (block + 1) * part]
        sums.begin(0)

    pl.semaphore_wait(pltpu.get_barrier_semaphore(), peers)
    out_grad()
    for pair in range(pairs):
        cross_part(pair)
        attend_back(pair, cap_key, cap_value, cap_bias, cross_low, cap_key_acc, cap_value_acc, False)
    norm_back(cap_raw, cap_key_acc, d_cap_key, 6, 10)
    d_cap_value[...] = cap_value_acc[...].astype(BF16)
    for _ in weight_grads(captions, ((1, d_cap_key), (2, d_cap_value))):
        pass
    steps = {
        0: (lambda: sums.stage_a(0), lambda: sums.stage_a(1)),
        1: (lambda: sums.stage_b(0), lambda: sums.stage_b(1), lambda: sums.stage_a(2)),
        2: (lambda: sums.stage_c(0), lambda: sums.stage_b(2), lambda: sums.stage_c(1)),
    }
    for pair in range(pairs):
        attend_back(pair, key, value, key_bias, mixed_low, key_acc, value_acc, True)
        for step in steps.get(pair, ()):
            step()
    norm_back(query_raw, query_acc, d_query, 4, 8)
    norm_back(key_raw, key_acc, d_key, 5, 9)
    d_value[...] = value_acc[...].astype(BF16)
    pour = Pour(copies, parts, from_left, from_right, b, s, seq)
    wide = 512
    for at in range(0, width, wide):
        cols = slice(at, at + wide)
        total = right_dot(d_query[...], w_query[cols, :]) + right_dot(d_key[...], w_key[cols, :])
        total = total + right_dot(d_value[...], w_value[cols, :])
        parts[:, :, cols] = total.astype(BF16).reshape(seq, rows // seq, wide)
    pieces = weight_grads(hidden, ((3, d_query), (4, d_key), (5, d_value)))
    for q in range(pour.count):
        pour.step(q)
        next(pieces, None)
    for _ in pieces:
        pass
    sums.stage_c(2)
    sums.stage_a(3)
    sums.stage_a(4)
    sums.stage_b(3)
    sums.stage_a(5)
    pour.end(d_hidden)

    factor = gain_rows[0:1, :] * (1.0 + mod_rows[0:1, :])

    def body(i, total):
        at = pl.ds(pl.multiple_of(i * 16, 16), 16)
        x, d = tokens[at, :].astype(F32), d_hidden[at, :]
        size = lax.rsqrt(jnp.mean(x * x, axis=-1, keepdims=True) + 1e-05)
        normed, inner = x * size, d * factor
        mean = jnp.mean(inner * normed, axis=-1, keepdims=True)
        tokens_grad[at, :] = d_tokens[at, :] + size * (inner - normed * mean)
        return total + jnp.sum(d * normed, axis=0, keepdims=True)

    total = lax.fori_loop(0, tokens.shape[0] // 16, body, jnp.zeros((1, width), F32))
    post, last = jnp.tanh(mod_rows[1:2, :]), jnp.tanh(mod_rows[3:4, :])
    vec[0:1, :] = total * gain_rows[0:1, :]
    vec[1:2, :] = row_sums[0:1, :] * gain_rows[1:2, :] * (1.0 - post * post)
    vec[2:3, :] = row_sums[1:2, :] * gain_rows[2:3, :]
    vec[3:4, :] = row_sums[2:3, :] * gain_rows[3:4, :] * (1.0 - last * last)
    vec[4:5, :] = total * (1.0 + mod_rows[0:1, :])
    vec[5:6, :] = row_sums[0:1, :] * post
    vec[6:7, :] = row_sums[1:2, :] * (1.0 + mod_rows[2:3, :])
    vec[7:8, :] = row_sums[2:3, :] * last
    vec_moves = []
    for k in range(1, seq):
        vec_moves.append(sums.go(copies.remote(vec, vec_seq.at[k], b, lax.rem(s + k, seq))))
    sums.stage_b(4)
    sums.stage_b(5)
    for move in vec_moves:
        move.wait_recv()
    add_rows(vec_sum, [vec] + [vec_seq.at[k] for k in range(1, seq)])
    vec_next = []
    for k in range(1, buckets):
        peer = lax.rem(b + k, buckets)
        vec_next.append(sums.go(copies.remote(vec_sum, vec_all.at[b], peer, s)))
    vec_own = copies.local(vec_sum, vec_all.at[b])
    vec_own.start()
    for w in (3, 4, 5):
        sums.stage_c(w)
    sums.stage_d(0)
    for move in vec_next:
        move.wait_recv()
    vec_own.wait()
    sums.end()


def backward_all(buckets, seq, inputs, shapes, kinds):
    any_spec = pl.BlockSpec(memory_space=pl.ANY)
    vmem = pl.BlockSpec(memory_space=pltpu.VMEM)
    shapes, outs, scratch, n_sems = sums_shapes(buckets, seq, shapes, kinds, near=True)
    query, cap_key, tokens = inputs[5], inputs[8], inputs[21]
    rows, width = tokens.shape
    vec = (16, width)
    n_sems += 8 * seq + 2 * buckets
    results = pl.pallas_call(
        functools.partial(backward_kernel, buckets, seq, tuple(kinds)),
        out_shape=[
            jax.ShapeDtypeStruct((rows, width), F32),
            jax.ShapeDtypeStruct((buckets,) + vec, F32),
            *outs,
        ],
        in_specs=[vmem] * len(inputs),
        out_specs=[vmem, any_spec] + [vmem] * len(outs),
        scratch_shapes=[
            pltpu.VMEM(query.shape, BF16),
            pltpu.VMEM(query.shape, BF16),
            pltpu.VMEM(query.shape, F32),
            pltpu.VMEM(query.shape, F32),
            pltpu.VMEM(query.shape, F32),
            pltpu.VMEM(cap_key.shape, F32),
            pltpu.VMEM(cap_key.shape, F32),
            pltpu.VMEM(query.shape, BF16),
            pltpu.VMEM(query.shape, BF16),
            pltpu.VMEM(query.shape, BF16),
            pltpu.VMEM(cap_key.shape, BF16),
            pltpu.VMEM(cap_key.shape, BF16),
            pltpu.VMEM((rows, width), F32),
            pltpu.VMEM(vec, F32),
            pltpu.VMEM((seq,) + vec, F32),
            pltpu.VMEM(vec, F32),
            pltpu.VMEM((seq, rows, width), BF16),
            pltpu.VMEM((seq - 1, rows, width), BF16),
            pltpu.VMEM((seq - 1, rows, width), BF16),
            pltpu.SemaphoreType.DMA((n_sems,)),
            pltpu.SemaphoreType.DMA((n_sems,)),
            *[pltpu.VMEM(shape, BF16) for shape in shapes],
            *scratch,
        ],
        compiler_params=pltpu.CompilerParams(
            collective_id=10, has_side_effects=True, vmem_limit_bytes=62 * 2**20
        ),
    )(*inputs)
    return results[0], results[1], [out.reshape(-1, out.shape[-1]) for out in results[2:]]


def on_device(
    tokens,
    captions,
    cotangent,
    counts,
    cap_lens,
    steps_t,
    w_query,
    w_key,
    w_value,
    w_out,
    w_cap_key,
    w_cap_value,
    w_gate,
    w_up,
    w_down,
    w_mod,
    gains,
    cross_gate,
):
    buckets, seq = lax.axis_size("bucket"), lax.axis_size("seq")
    b, s = lax.axis_index("bucket"), lax.axis_index("seq")
    place = b * seq + s
    rows, width = tokens.shape
    span = rows * seq
    share = width // seq
    live_rows, cap_len = pick_entry(counts, b), pick_entry(cap_lens, b)
    token_total = jnp.sum(counts).astype(F32)

    cond_size = w_mod.shape[0] * buckets * seq
    cond = jax.nn.silu(time_embed(steps_t, cond_size)).astype(BF16)
    cond_part = lax.dynamic_slice_in_dim(cond, place * w_mod.shape[0], w_mod.shape[0], 1)
    slim = gains.shape[1]
    small = jnp.concatenate([gains, cross_gate[None]], axis=0).astype(F32)
    small = jnp.pad(small, ((0, 0), (0, 128 - slim)))
    key_mask = jnp.broadcast_to((jnp.arange(span) < live_rows)[:, None], (span, 128)).astype(BF16)
    cap_span = captions.shape[0] * seq
    cap_mask = jnp.broadcast_to((jnp.arange(cap_span) < cap_len)[:, None], (cap_span, 128))
    cap_all, weights, inner = forward_all(
        buckets,
        seq,
        tokens,
        captions,
        small,
        slim,
        cond_part,
        w_mod,
        [key_mask, cap_mask.astype(BF16)],
        [w_query, w_key, w_value, w_cap_key, w_cap_value, w_out, w_gate, w_up, w_down],
        ["col", "col", "col", "col", "col", "row", "col", "col", "row"],
    )
    wq, wk, wv, wck, wcv, wo, wg, wu, wd = weights
    caps = cap_all.reshape(-1, captions.shape[1])
    small_rows, mod, hidden, query_proj, key_proj, cap_proj = inner[:6]
    query, key, value, cap_key, cap_value = inner[6:11]
    cross_out, mixed_low = inner[11:]
    row_live = (s * rows + jnp.arange(rows) < live_rows).astype(F32)
    row_scale = row_live * (buckets * span / token_total)
    (block_out, d_tokens, d_attn_all, row_sums), (s_gate, s_up, s_down) = middle_all(
        buckets,
        seq,
        mixed_low,
        (wo, wg, wu, wd),
        tokens,
        cotangent,
        jnp.broadcast_to(row_scale[:, None], (rows, 128)),
        small_rows,
        mod,
    )
    key_bias = jnp.where(jnp.arange(span) < live_rows, 0.0, -1e30).astype(F32)
    cap_bias = jnp.where(jnp.arange(cap_span) < cap_len, 0.0, -1e30).astype(F32)
    tokens_grad, vec_all, sums = backward_all(
        buckets,
        seq,
        [
            d_attn_all.reshape(span, width),
            wq,
            wk,
            wv,
            wo,
            query,
            key,
            value,
            cap_key,
            cap_value,
            cross_out,
            query_proj,
            key_proj,
            cap_proj,
            small_rows,
            mod,
            jnp.broadcast_to(key_bias[:, None], (span, 128)),
            jnp.broadcast_to(cap_bias[:, None], (cap_span, 128)),
            mixed_low,
            hidden,
            caps,
            tokens,
            d_tokens,
            row_sums,
        ],
        [x.shape for x in (wo, wck, wcv, wq, wk, wv)],
        ["row", "col", "col", "col", "col", "col"],
    )
    s_out, s_cap_key, s_cap_value, s_query, s_key, s_value = sums

    quarter = 4 * width // seq
    mod_rows = vec_all[:, :4].reshape(buckets, -1, quarter)
    mod_rows = lax.dynamic_slice_in_dim(mod_rows, s, 1, 1)[:, 0]
    cond_size = cond.shape[1] // buckets
    cond_cols = lax.dynamic_slice_in_dim(cond, b * cond_size, cond_size, 1).astype(F32)
    s_mod = jnp.sum(cond_cols[:, :, None] * mod_rows[:, None, :], axis=0)
    tail = lax.dynamic_slice(vec_all, (0, 4, place * slim), (buckets, 8, slim))
    tail = jnp.sum(tail, axis=0)
    return (
        block_out,
        tokens_grad,
        s_query,
        s_key,
        s_value,
        s_out,
        s_cap_key,
        s_cap_value,
        s_gate,
        s_up,
        s_down,
        s_mod,
        tail[:7],
        tail[7],
    )


def solution(mesh):
    spread = P(("bucket", "seq"), None)
    in_specs = (
        *([spread] * 3),
        *([P()] * 3),
        *([spread] * 10),
        P(None, ("bucket", "seq")),
        P(("bucket", "seq")),
    )
    out_specs = (
        spread,
        spread,
        *([P("bucket", "seq")] * 10),
        P(None, ("bucket", "seq")),
        P(("bucket", "seq")),
    )
    buckets, seq = mesh.shape["bucket"], mesh.shape["seq"]

    def step(*args):
        tokens, weight = args[0], args[6]
        tiled = weight.shape[0] % 16 == 0 and weight.shape[1] // seq % 128 == 0
        fits = buckets == 8 and seq == 4 and tokens.shape[0] % 64 == 0
        return (on_device if tiled and fits else on_device_general)(*args)

    return jax.shard_map(
        step, mesh=mesh, in_specs=in_specs, out_specs=out_specs, check_vma=False
    )
```

```python
import functools
import math

import jax
import jax.numpy as jnp
from jax import lax
from jax.experimental import pallas as pl
from jax.experimental.pallas import tpu as pltpu
from jax.sharding import PartitionSpec as P

HEAD_DIM = 64
MESH = pl.DeviceIdType.MESH
F32, BF16 = jnp.float32, jnp.bfloat16
CHUNKS, CUTS, FLIGHT = 2, 2, 2


def rms_rows(values):
    return values * lax.rsqrt(jnp.mean(values * values, axis=-1, keepdims=True) + 1e-05)


def head_rms(values):
    shaped = values.reshape(values.shape[:-1] + (values.shape[-1] // HEAD_DIM, HEAD_DIM))
    shaped = shaped * lax.rsqrt(jnp.mean(shaped * shaped, axis=-1, keepdims=True) + 1e-06)
    return shaped.reshape(values.shape)


def time_embed(steps, width):
    half_width = width // 2
    freqs = jnp.exp(-math.log(10000.0) * jnp.arange(half_width, dtype=F32) / half_width)
    angles = steps.astype(F32)[:, None] * freqs
    return jnp.concatenate([jnp.cos(angles), jnp.sin(angles)], axis=1)


def pick_entry(table, index):
    return jnp.sum(jnp.where(jnp.arange(table.shape[0]) == index, table, 0))


def bf_dot(left, right):
    return jnp.dot(left, right, preferred_element_type=F32)


def left_dot(rows_left, rows_right):
    return lax.dot_general(
        rows_left, rows_right, (((0,), (0,)), ((), ())), preferred_element_type=F32
    )


def right_dot(left, right):
    return lax.dot_general(left, right, (((1,), (1,)), ((), ())), preferred_element_type=F32)


def pre_attn(tokens_in, gain_pre, scale_attn):
    return rms_rows(tokens_in) * gain_pre * (1.0 + scale_attn)


def qk_norm(query_in, key_in, gain_query, gain_key):
    return (head_rms(query_in) * gain_query, head_rms(key_in) * gain_key)


def cap_norm(key_in, gain_cap):
    return head_rms(key_in) * gain_cap


def middle(tokens_in, attn_out, gain_post, gate_attn, gain_ffn, scale_ffn):
    resid_one = tokens_in + jnp.tanh(gate_attn) * rms_rows(attn_out) * gain_post
    return (resid_one, rms_rows(resid_one) * gain_ffn * (1.0 + scale_ffn))


def activate(gate_proj, up_proj):
    return jax.nn.silu(gate_proj) * up_proj


def finish(resid_one, ffn_out, gain_last, gate_ffn):
    return resid_one + jnp.tanh(gate_ffn) * rms_rows(ffn_out) * gain_last


def flip(index, bit):
    return index + bit - 2 * bit * lax.rem(lax.div(index, bit), 2)


def slot(index, buckets):
    if buckets != 8:
        return index
    high, low = lax.div(index, 4), lax.rem(index, 4)
    return 4 * high + 2 * lax.rem(low, 2) + lax.div(low, 2)


class Copies:
    def __init__(self, send, recv):
        self.send, self.recv, self.used = send, recv, 0

    def take(self, count=1):
        first = self.used
        self.used += count
        assert self.used <= self.send.shape[0], self.used
        return first

    def remote(self, src, dst, b, s, at=None):
        at = self.take() if at is None else at
        return pltpu.make_async_remote_copy(
            src_ref=src,
            dst_ref=dst,
            send_sem=self.send.at[at],
            recv_sem=self.recv.at[at],
            device_id={"bucket": b, "seq": s},
            device_id_type=MESH,
        )

    def local(self, src, dst):
        return pltpu.make_async_copy(src, dst, self.send.at[self.take()])


def greet(b, s):
    pl.semaphore_signal(
        pltpu.get_barrier_semaphore(),
        inc=1,
        device_id={"bucket": b, "seq": s},
        device_id_type=MESH,
    )


class Relay:
    def __init__(self, copies, own, out, b, s, seq, part=None):
        self.copies, self.own, self.out, self.b, self.s, self.seq = copies, own, out, b, s, seq
        self.part = part
        self.base = {1: copies.take(seq - 1), -1: copies.take(seq - 1)}
        self.up = jnp.where(s < seq - 1, s + 1, s - 1)
        self.down = jnp.where(s > 0, s - 1, s + 1)
        self.kept = None if own is None else copies.local(own, out.at[s])

    def packet(self, way, j):
        at = self.s - way * j
        block = self.out.at[at] if self.part is None else self.out.at[at, self.part]
        return self.copies.remote(
            self.own if j == 0 and self.own is not None else block,
            block,
            self.b,
            self.up if way > 0 else self.down,
            self.base[way] + j,
        )

    def sends(self, way):
        return self.s < self.seq - 1 if way > 0 else self.s > 0

    def has(self, way, j):
        return self.s >= j if way > 0 else self.s + j <= self.seq - 1

    def start(self, j):
        if j == 0 and self.kept is not None:
            self.kept.start()
        for way in (1, -1):
            if j == self.seq - 1:

                @pl.when(jnp.logical_not(self.sends(way)))
                def _():
                    for k in range(self.seq - 1):
                        self.packet(way, k).wait_recv()

                continue

            @pl.when(jnp.logical_and(self.sends(way), self.has(way, j)))
            def _():
                if j > 0:
                    self.packet(way, j - 1).wait_recv()
                self.packet(way, j).start()

    def sent(self, j):
        for way in (1, -1):

            @pl.when(jnp.logical_and(self.sends(way), self.has(way, j)))
            def _():
                self.packet(way, j).wait_send()

        if j == 0 and self.kept is not None:
            self.kept.wait()


def greet_line(b, s, seq):
    @pl.when(s > 0)
    def _():
        greet(b, s - 1)

    @pl.when(s < seq - 1)
    def _():
        greet(b, s + 1)

    peers = jnp.where(s > 0, 1, 0) + jnp.where(s < seq - 1, 1, 0)
    pl.semaphore_wait(pltpu.get_barrier_semaphore(), peers)


def halves_of(shape):
    if len(shape) == 3:
        return shape[0] // 2
    return (shape[0] // 32) * 16 if shape[0] >= 32 else shape[0] // 2


def gather_kernel(buckets, seq, kinds, *refs):
    count = len(kinds)
    tokens, captions, small, cond, w_mod = refs[:5]
    shards = refs[5 : 5 + count]
    tok_all, cap_all, small_all, mod_out = refs[5 + count : 9 + count]
    fulls = refs[9 + count : 9 + 2 * count]
    part, got_bucket, got_seq, mod_sum, send, recv = refs[9 + 2 * count :]
    b, s = lax.axis_index("bucket"), lax.axis_index("seq")
    copies = Copies(send, recv)
    chips = buckets // 2
    place = b * seq + s
    to_b, to_s = lax.rem(place, buckets), lax.div(place, buckets)
    back = s * buckets + b
    from_b, from_s = lax.div(back, seq), lax.rem(back, seq)
    stays = jnp.logical_and(to_b == b, to_s == s)

    lanes = part.shape[2]
    for j in range(part.shape[1]):
        part[:, j, :] = bf_dot(cond[...], w_mod[:, j * lanes : (j + 1) * lanes])

    for k in range(1, buckets):
        greet(lax.rem(b + k, buckets), s)
    for k in range(1, seq):
        greet(b, lax.rem(s + k, seq))

    @pl.when(jnp.logical_not(stays))
    def _():
        greet(from_b, from_s)

    peers = buckets - 1 + seq - 1 + jnp.where(stays, 0, 1)
    pl.semaphore_wait(pltpu.get_barrier_semaphore(), peers)

    sent = []

    def go(copy):
        copy.start()
        sent.append(copy)
        return copy

    mod_moves = []
    for k in range(1, buckets):
        peer = lax.rem(b + k, buckets)
        mod_moves.append(go(copies.remote(part.at[peer], got_bucket.at[k], peer, s)))
    small_moves = []
    for k in range(1, seq):
        peer = lax.rem(s + k, seq)
        small_moves.append(go(copies.remote(small, small_all.at[b, s], b, peer)))
    small_own = copies.local(small, small_all.at[b, s])
    small_own.start()

    tok = Relay(copies, tokens, tok_all, b, s, seq)
    cap = Relay(copies, captions, cap_all, b, s, seq)
    queue = [(tok, j) for j in range(seq)] + [(cap, j) for j in range(seq)]
    ahead = [(None, at) for at in range(count)]
    items = []
    while queue or ahead:
        items += queue[:1] + ahead[:1]
        queue, ahead = queue[1:], ahead[1:]

    first = [None] * count

    def depart(at):
        kind, shard, full = kinds[at], shards[at], fulls[at]
        if kind == "row":
            move = copies.remote(shard, full.at[to_b], to_b, to_s)
            keep = copies.local(shard, full.at[b])

            @pl.when(jnp.logical_not(stays))
            def _():
                move.start()

            @pl.when(stays)
            def _():
                keep.start()

            first[at] = (move, keep)
            return
        wide = full.shape[-1]

        def columns(peer):
            if kind == "cut":
                return shard.at[peer]
            return shard.at[:, pl.ds(pl.multiple_of(peer * wide, 128), wide)]

        moves = []
        for k in range(1, seq):
            peer = lax.rem(s + k, seq)
            move = copies.remote(columns(peer), full.at[b, s], b, peer)
            move.start()
            moves.append(move)
        keep = copies.local(columns(s), full.at[b, s])
        keep.start()
        first[at] = (moves, keep)

    def arrived(at):
        moves, keep = first[at]
        if kinds[at] == "row":

            @pl.when(jnp.logical_not(stays))
            def _():
                moves.wait()

            @pl.when(stays)
            def _():
                keep.wait()

            return
        for move in moves:
            move.wait()
        keep.wait()

    twin = flip(b, 1)
    second = [None] * count
    if chips == 4:
        near_x, near_y = flip(b, 2), flip(b, 4)
        far = flip(near_x, 4)

        def stage_a(at):
            full = fulls[at]
            second[at] = {
                "x": go(copies.remote(full.at[b], full.at[b], near_x, s)),
                "y": go(copies.remote(full.at[b], full.at[b], near_y, s)),
                "twin": [go(copies.remote(full.at[b], full.at[b], twin, s))],
            }

        def stage_b(at):
            full, now = fulls[at], second[at]
            cut = halves_of(full.shape[1:])
            now["x"].wait_recv()
            block = full.at[near_x, pl.ds(0, cut)]
            now["dy"] = go(copies.remote(block, block, near_y, s))
            block = full.at[near_x]
            now["twin"].append(go(copies.remote(block, block, twin, s)))
            now["y"].wait_recv()
            block = full.at[near_y, pl.ds(cut, full.shape[1] - cut)]
            now["dx"] = go(copies.remote(block, block, near_x, s))
            block = full.at[near_y]
            now["twin"].append(go(copies.remote(block, block, twin, s)))

        def stage_c(at):
            full, now = fulls[at], second[at]
            now["dy"].wait_recv()
            now["dx"].wait_recv()
            block = full.at[far]
            now["twin"].append(go(copies.remote(block, block, twin, s)))

    else:

        def stage_a(at):
            full = fulls[at]
            second[at] = {"far": [], "twin": []}
            for k in range(1, chips):
                peer = lax.rem(b + 2 * k, buckets)
                second[at]["far"].append(go(copies.remote(full.at[b], full.at[b], peer, s)))
            second[at]["twin"].append(go(copies.remote(full.at[b], full.at[b], twin, s)))

        def stage_b(at):
            full = fulls[at]
            for k, copy in enumerate(second[at]["far"], 1):
                copy.wait_recv()
                block = full.at[lax.rem(b + buckets - 2 * k, buckets)]
                second[at]["twin"].append(go(copies.remote(block, block, twin, s)))

        def stage_c(at):
            pass

    def begin(i):
        relay, j = items[i]
        if relay is None:
            depart(j)
        else:
            relay.start(j)

    begin(0)
    begin(1)
    for move in small_moves:
        move.wait_recv()
    small_own.wait()
    small_next = []
    for k in range(1, buckets):
        peer = lax.rem(b + k, buckets)
        small_next.append(go(copies.remote(small_all.at[b], small_all.at[b], peer, s)))
    total = part[b]
    for k, move in enumerate(mod_moves, 1):
        move.wait_recv()
        total = total + got_bucket[k]
    mod_sum[...] = total
    mod_next = []
    for k in range(1, seq):
        peer = lax.rem(s + k, seq)
        mod_next.append(go(copies.remote(mod_sum, got_seq.at[k], b, peer)))

    for i, (relay, j) in enumerate(items):
        if relay is None:
            arrived(j)
        elif j <= seq - 2:
            relay.sent(j)
        if i + 2 < len(items):
            begin(i + 2)
        if relay is None:
            stage_a(j)
            if j >= 1:
                stage_b(j - 1)
            if j >= 2:
                stage_c(j - 2)
    stage_b(count - 1)
    if count >= 2:
        stage_c(count - 2)
    stage_c(count - 1)

    total = mod_sum[...]
    for k, move in enumerate(mod_next, 1):
        move.wait_recv()
        total = total + got_seq[k]
    mod_out[...] = total
    for move in small_next:
        move.wait_recv()
    for now in second:
        for move in now["twin"]:
            move.wait_recv()
    for move in sent:
        move.wait_send()


def gather_all(buckets, seq, tokens, captions, small, cond, w_mod, shards, kinds):
    any_spec = pl.BlockSpec(memory_space=pl.ANY)
    vmem = pl.BlockSpec(memory_space=pltpu.VMEM)
    fulls, inputs, names = [], [], []
    for shard, kind in zip(shards, kinds, strict=True):
        rows, wide = shard.shape
        if kind == "row":
            fulls.append(jax.ShapeDtypeStruct((buckets, rows, wide), BF16))
        else:
            part = wide // seq
            fulls.append(jax.ShapeDtypeStruct((buckets, seq, rows, part), BF16))
            if part % 128:
                kind = "cut"
                shard = shard.reshape(rows, seq, part).transpose(1, 0, 2)
        inputs.append(shard)
        names.append(kind)
    mod_lanes = w_mod.shape[1] // 8
    n_sems = 64 + 16 * buckets + len(shards) * (seq + 2 * buckets)
    outs = pl.pallas_call(
        functools.partial(gather_kernel, buckets, seq, tuple(names)),
        out_shape=[
            jax.ShapeDtypeStruct((seq,) + tokens.shape, BF16),
            jax.ShapeDtypeStruct((seq,) + captions.shape, BF16),
            jax.ShapeDtypeStruct((buckets, seq) + small.shape, F32),
            jax.ShapeDtypeStruct((8, mod_lanes), F32),
            *fulls,
        ],
        in_specs=[any_spec, any_spec, any_spec, vmem, vmem] + [any_spec] * len(shards),
        out_specs=[any_spec, any_spec, any_spec, vmem] + [any_spec] * len(shards),
        scratch_shapes=[
            pltpu.VMEM((buckets, 8, mod_lanes), F32),
            pltpu.VMEM((buckets, 8, mod_lanes), F32),
            pltpu.VMEM((seq, 8, mod_lanes), F32),
            pltpu.VMEM((8, mod_lanes), F32),
            pltpu.SemaphoreType.DMA((n_sems,)),
            pltpu.SemaphoreType.DMA((n_sems,)),
        ],
        compiler_params=pltpu.CompilerParams(
            collective_id=0, has_side_effects=True, vmem_limit_bytes=24 * 2**20
        ),
    )(tokens, captions, small, cond, w_mod, *inputs)
    weights = []
    for full, kind in zip(outs[4:], names, strict=True):
        weights.append(full.reshape(-1, full.shape[-1]))
    return outs[0], outs[1], outs[2], outs[3], weights


def line_gather_kernel(seq, own, out, send, recv):
    b, s = lax.axis_index("bucket"), lax.axis_index("seq")
    greet_line(b, s, seq)
    relay = Relay(Copies(send, recv), own, out, b, s, seq)
    for j in range(seq):
        relay.start(j)
    for j in range(seq - 1):
        relay.sent(j)


def line_gather(seq, own, collective_id):
    return pl.pallas_call(
        functools.partial(line_gather_kernel, seq),
        out_shape=jax.ShapeDtypeStruct((seq,) + own.shape, own.dtype),
        in_specs=[pl.BlockSpec(memory_space=pl.ANY)],
        out_specs=pl.BlockSpec(memory_space=pl.ANY),
        scratch_shapes=[pltpu.SemaphoreType.DMA((2 * seq + 2,))] * 2,
        compiler_params=pltpu.CompilerParams(collective_id=collective_id, has_side_effects=True),
    )(own).reshape(-1, own.shape[-1])


def add_rows(out, terms):
    rows = out.shape[0]
    step = 16 if rows % 16 == 0 else rows

    def body(i, carry):
        at = pl.ds(pl.multiple_of(i * step, step), step)
        total = terms[0][at, :].astype(F32)
        for term in terms[1:]:
            total = total + term[at, :].astype(F32)
        out[at, :] = total.astype(out.dtype)
        return carry

    lax.fori_loop(0, rows // step, body, 0)


class Pour:
    def __init__(self, copies, parts, from_left, from_right, b, s, seq):
        self.copies, self.parts, self.b, self.s, self.seq = copies, parts, b, s, seq
        self.got = {1: from_left, -1: from_right}
        rows = parts.shape[1]
        self.cuts = CUTS if rows % (16 * CUTS) == 0 else 1
        self.thin = rows // self.cuts
        self.count = (seq - 1) * self.cuts
        self.base = {1: copies.take(self.count), -1: copies.take(self.count)}
        self.next = {
            1: jnp.where(s < seq - 1, s + 1, s - 1),
            -1: jnp.where(s > 0, s - 1, s + 1),
        }

    def block(self, way, q):
        j, at = q // self.cuts, pl.ds(q % self.cuts * self.thin, self.thin)
        return self.parts.at[self.seq - 1 - j if way > 0 else j, at], self.got[way].at[j, at]

    def packet(self, way, q):
        src, dst = self.block(way, q)
        return self.copies.remote(src, dst, self.b, self.next[way], self.base[way] + q)

    def on(self, way, q):
        j = q // self.cuts
        return self.s < self.seq - 1 - j if way > 0 else self.s > j

    def behind(self, way):
        return self.s > 0 if way > 0 else self.s < self.seq - 1

    def one(self, way, q):
        src, dst = self.block(way, q)

        @pl.when(jnp.logical_and(self.behind(way), self.on(way, q)))
        def _():
            self.packet(way, q).wait_recv()
            add_rows(src, [src, dst])

        @pl.when(self.on(way, q))
        def _():
            if q >= FLIGHT:
                self.packet(way, q - FLIGHT).wait_send()
            self.packet(way, q).start()

    def step(self, q):
        @pl.when(self.s < self.seq // 2)
        def _():
            self.one(1, q)
            self.one(-1, q)

        @pl.when(self.s >= self.seq // 2)
        def _():
            self.one(-1, q)
            self.one(1, q)

    def end(self, out):
        seq, cuts = self.seq, self.cuts
        for t in range(seq):

            @pl.when(self.s == t)
            def _():
                terms = [self.parts.at[t]]
                for way, j in ((1, seq - 1 - t), (-1, t)):
                    if j < seq - 1:
                        for c in range(cuts):
                            self.packet(way, j * cuts + c).wait_recv()
                        terms.append(self.got[way].at[j])
                add_rows(out, terms)

        for q in range(self.count):
            more = q + FLIGHT < self.count
            for way in (1, -1):
                last = jnp.logical_not(self.on(way, q + FLIGHT)) if more else True

                @pl.when(jnp.logical_and(self.on(way, q), last))
                def _():
                    self.packet(way, q).wait_send()


def line_scatter_kernel(seq, parts, out, from_left, from_right, send, recv):
    b, s = lax.axis_index("bucket"), lax.axis_index("seq")
    greet_line(b, s, seq)
    pour = Pour(Copies(send, recv), parts, from_left, from_right, b, s, seq)
    for q in range(pour.count):
        pour.step(q)
    pour.end(out)


def line_scatter(seq, parts, collective_id):
    rows, wide = parts.shape[0] // seq, parts.shape[1]
    vmem = pl.BlockSpec(memory_space=pltpu.VMEM)
    return pl.pallas_call(
        functools.partial(line_scatter_kernel, seq),
        out_shape=jax.ShapeDtypeStruct((rows, wide), F32),
        in_specs=[vmem],
        out_specs=vmem,
        input_output_aliases={},
        scratch_shapes=[
            pltpu.VMEM((seq - 1, rows, wide), BF16),
            pltpu.VMEM((seq - 1, rows, wide), BF16),
            pltpu.SemaphoreType.DMA((4 * seq,)),
            pltpu.SemaphoreType.DMA((4 * seq,)),
        ],
        compiler_params=pltpu.CompilerParams(
            collective_id=collective_id, has_side_effects=True, vmem_limit_bytes=24 * 2**20
        ),
    )(parts.astype(BF16).reshape(seq, rows, wide))


class GradSums:
    def __init__(self, copies, b, s, buckets, seq, kinds, grads, outs, scratch, near=False):
        self.near = near
        self.copies, self.b, self.s, self.buckets, self.seq = copies, b, s, buckets, seq
        self.kinds, self.grads, self.outs = kinds, grads, outs
        self.scratch = [scratch[8 * w : 8 * w + 8] for w in range(len(kinds))]
        self.chips = buckets // 2
        self.chip, self.core = lax.div(b, 2), lax.rem(b, 2)
        self.place = s * buckets + slot(b, buckets)
        self.to_b = lax.div(self.place, seq)
        self.twin = flip(b, 1)
        self.begun, self.state, self.last = {}, {}, {}
        self.sent = []

    def go(self, copy):
        copy.start()
        self.sent.append(copy)
        return copy

    def own(self, w, chip, rows=None):
        where = (chip,) if rows is None else (chip, rows)
        if self.near:
            return self.grads[w].at[(chip, self.core, *where[1:])]
        return self.scratch[w][0].at[where]

    def begin(self, w):
        own, other = self.scratch[w][:2]
        grad = self.grads[w]
        swap = self.copies.remote(grad.at[:, 1 - self.core], other, self.twin, self.s)
        swap.start()
        self.begun[w] = [swap]
        if not self.near:
            keep = self.copies.local(grad.at[:, self.core], own)
            keep.start()
            self.begun[w].append(keep)

    def stage_a(self, w):
        _, other, half_x, half_y, got, _ = self.scratch[w][:6]
        for copy in self.begun[w]:
            copy.wait()
        if not self.near and w + 2 in range(len(self.kinds)) and w + 2 not in self.begun:
            self.begin(w + 2)
        rows = other.shape[1]
        if self.chips != 4:
            moves = []
            for k in range(1, self.chips):
                to = lax.rem(self.chip + k, self.chips)
                own = self.own(w, to)
                add_rows(own, [own, other.at[to]])
                move = self.copies.remote(own, got.at[k], 2 * to + self.core, self.s)
                moves.append(self.go(move))
            self.state[w] = moves
            return
        far = flip(flip(self.chip, 1), 2)
        add_rows(self.own(w, far), [self.own(w, far), other.at[far]])
        cut = halves_of(other.shape[1:])
        near_x, near_y = flip(self.b, 2), flip(self.b, 4)
        top, low = self.own(w, far, pl.ds(0, cut)), self.own(w, far, pl.ds(cut, rows - cut))
        self.state[w] = [
            self.go(self.copies.remote(top, half_x, near_x, self.s)),
            self.go(self.copies.remote(low, half_y, near_y, self.s)),
        ]

    def stage_b(self, w):
        if self.chips != 4:
            return
        _, other, half_x, half_y, got_x, got_y = self.scratch[w][:6]
        rows = other.shape[1]
        cut = halves_of(other.shape[1:])
        top, low = pl.ds(0, cut), pl.ds(cut, rows - cut)
        mx, my = flip(self.chip, 1), flip(self.chip, 2)
        move_x, move_y = self.state[w]
        move_x.wait_recv()
        block = self.own(w, my, top)
        add_rows(block, [block, other.at[my, top], half_x])
        block = self.own(w, my, low)
        add_rows(block, [block, other.at[my, low]])
        block = self.own(w, my)
        next_y = self.go(self.copies.remote(block, got_y, flip(self.b, 4), self.s))
        move_y.wait_recv()
        block = self.own(w, mx, low)
        add_rows(block, [block, other.at[mx, low], half_y])
        block = self.own(w, mx, top)
        add_rows(block, [block, other.at[mx, top]])
        block = self.own(w, mx)
        next_x = self.go(self.copies.remote(block, got_x, flip(self.b, 2), self.s))
        self.state[w] = [next_x, next_y]

    def stage_c(self, w):
        _, other, _, _, got_x, got_y, done, landed = self.scratch[w]
        for move in self.state[w]:
            move.wait_recv()
        terms = [self.own(w, self.chip), other.at[self.chip]]
        if self.chips == 4:
            terms += [got_x, got_y]
        else:
            terms += [got_x.at[k] for k in range(1, self.chips)]
        if self.kinds[w] == "col":
            add_rows(self.outs[w], terms)
            return
        seq, send, recv = self.seq, self.copies.send, self.copies.recv
        wide = self.outs[w].shape[-1]
        me = lax.rem(self.place, seq)
        base = self.copies.take(2 * seq)
        rows = terms[0].shape[0]
        step = 16 if rows % 16 == 0 else rows

        def body(i, carry):
            at = pl.ds(pl.multiple_of(i * step, step), step)
            total = terms[0][at, :].astype(F32)
            for term in terms[1:]:
                total = total + term[at, :].astype(F32)
            for t in range(seq):
                done[t, at, :] = total[:, t * wide : (t + 1) * wide].astype(BF16)
            return carry

        lax.fori_loop(0, rows // step, body, 0)
        moves = []
        for t in range(seq):
            move = pltpu.make_async_remote_copy(
                src_ref=done.at[t],
                dst_ref=landed.at[me],
                send_sem=send.at[base + t],
                recv_sem=recv.at[base + me],
                device_id={"bucket": self.to_b, "seq": t},
                device_id_type=MESH,
            )
            keep = pltpu.make_async_copy(done.at[t], landed.at[me], send.at[base + seq + t])
            here = jnp.logical_and(self.to_b == self.b, self.s == t)

            @pl.when(jnp.logical_not(here))
            def _():
                move.start()

            @pl.when(here)
            def _():
                keep.start()

            moves.append((move, keep, here))
        self.last[w] = (base, moves)

    def stage_d(self, w):
        if self.kinds[w] != "row":
            return
        done, landed = self.scratch[w][6:]
        base, moves = self.last[w]
        out, seq, buckets = self.outs[w], self.seq, self.buckets
        for j in range(seq):
            d = self.b * seq + j
            from_b = slot(lax.rem(d, buckets), buckets)
            here = jnp.logical_and(from_b == self.b, lax.div(d, buckets) == self.s)

            @pl.when(jnp.logical_not(here))
            def _():
                pltpu.make_async_remote_copy(
                    src_ref=done.at[j],
                    dst_ref=landed.at[j],
                    send_sem=self.copies.send.at[base + j],
                    recv_sem=self.copies.recv.at[base + j],
                    device_id={"bucket": self.twin, "seq": self.s},
                    device_id_type=MESH,
                ).wait_recv()

        for move, keep, here in moves:

            @pl.when(jnp.logical_not(here))
            def _():
                move.wait_send()

            @pl.when(here)
            def _():
                keep.wait()

        for j in range(seq):
            add_rows(out.at[j], [landed.at[j]])

    def steps(self):
        count = len(self.kinds)
        for w in range(count + 2):
            if w < count:
                yield lambda w=w: self.stage_a(w)
            if 1 <= w <= count:
                yield lambda w=w: self.stage_b(w - 1)
            if w >= 2:
                yield lambda w=w: self.stage_c(w - 2)
        yield lambda: [self.stage_d(w) for w in range(count)]

    def end(self):
        for move in self.sent:
            move.wait_send()


def greet_all(b, s, buckets, seq):
    for k in range(1, buckets):
        greet(lax.rem(b + k, buckets), s)
    for k in range(1, seq):
        greet(b, lax.rem(s + k, seq))
    for j in range(seq):
        d = b * seq + j
        src_b, src_s = slot(lax.rem(d, buckets), buckets), lax.div(d, buckets)

        @pl.when(jnp.logical_not(jnp.logical_and(src_b == b, src_s == s)))
        def _():
            greet(src_b, src_s)

    to_b = lax.div(s * buckets + slot(b, buckets), seq)
    return buckets - 1 + seq - 1 + seq - jnp.where(to_b == b, 1, 0)


def sums_shapes(buckets, seq, shapes, kinds, near=False):
    chips = buckets // 2
    inputs, outs, scratch = [], [], []
    tiny = pltpu.VMEM((16, 128), BF16)
    for (rows, wide), kind in zip(shapes, kinds, strict=True):
        rows = rows // buckets
        inputs.append((chips, 2, rows, wide))
        cut = halves_of((rows, wide))
        scratch += [tiny if near else pltpu.VMEM((chips, rows, wide), BF16)]
        scratch += [pltpu.VMEM((chips, rows, wide), BF16)]
        if chips == 4:
            scratch += [pltpu.VMEM((cut, wide), BF16), pltpu.VMEM((rows - cut, wide), BF16)]
            scratch += [pltpu.VMEM((rows, wide), BF16)] * 2
        else:
            scratch += [tiny, tiny, pltpu.VMEM((chips, rows, wide), BF16), tiny]
        shape = (seq, rows, wide // seq) if kind == "row" else (rows, wide)
        outs.append(jax.ShapeDtypeStruct(shape, F32))
        scratch += [pltpu.VMEM(shape, BF16) if kind == "row" else tiny] * 2
    n_sems = 32 + 2 * buckets + len(shapes) * (8 + 3 * seq + buckets)
    return inputs, outs, scratch, n_sems


def place_grads(buckets, grads, kinds, shapes):
    inputs = []
    for grad, kind, shape in zip(grads, kinds, shapes, strict=True):
        grad = grad.astype(BF16)
        if kind == "row" and buckets == 8:
            grad = grad.reshape((2, 2, 2) + shape[2:]).transpose(0, 2, 1, 3, 4)
        inputs.append(grad.reshape(shape))
    return inputs


def spread(buckets):
    if buckets != 8:
        return tuple(range(buckets))
    return tuple(4 * (p // 4) + 2 * (p % 2) + p // 2 % 2 for p in range(buckets))


def scatter_kernel(buckets, seq, kinds, *refs):
    count = len(kinds)
    vec, grads = refs[0], refs[1 : 1 + count]
    vec_all, outs = refs[1 + count], refs[2 + count : 2 + 2 * count]
    at = 2 + 2 * count
    vec_seq, vec_sum, send, recv = refs[at : at + 4]
    b, s = lax.axis_index("bucket"), lax.axis_index("seq")
    copies = Copies(send, recv)
    sums = GradSums(copies, b, s, buckets, seq, kinds, grads, outs, refs[at + 4 :])
    peers = greet_all(b, s, buckets, seq)
    pl.semaphore_wait(pltpu.get_barrier_semaphore(), peers)
    vec_moves = []
    for k in range(1, seq):
        vec_moves.append(sums.go(copies.remote(vec, vec_seq.at[k], b, lax.rem(s + k, seq))))
    for w in range(min(2, count)):
        sums.begin(w)
    for move in vec_moves:
        move.wait_recv()
    add_rows(vec_sum, [vec] + [vec_seq.at[k] for k in range(1, seq)])
    vec_next = []
    for k in range(1, buckets):
        peer = lax.rem(b + k, buckets)
        vec_next.append(sums.go(copies.remote(vec_sum, vec_all.at[b], peer, s)))
    vec_own = copies.local(vec_sum, vec_all.at[b])
    vec_own.start()
    for step in sums.steps():
        step()
    for move in vec_next:
        move.wait_recv()
    vec_own.wait()
    sums.end()


def scatter_all(buckets, seq, vec, grads, kinds, collective_id=1):
    any_spec = pl.BlockSpec(memory_space=pl.ANY)
    vmem = pl.BlockSpec(memory_space=pltpu.VMEM)
    shapes, outs, scratch, n_sems = sums_shapes(buckets, seq, [g.shape for g in grads], kinds)
    inputs = place_grads(buckets, grads, kinds, shapes)
    results = pl.pallas_call(
        functools.partial(scatter_kernel, buckets, seq, tuple(kinds)),
        out_shape=[jax.ShapeDtypeStruct((buckets,) + vec.shape, F32), *outs],
        in_specs=[vmem] + [any_spec] * len(grads),
        out_specs=[any_spec] + [vmem] * len(grads),
        scratch_shapes=[
            pltpu.VMEM((seq,) + vec.shape, F32),
            pltpu.VMEM(vec.shape, F32),
            pltpu.SemaphoreType.DMA((n_sems,)),
            pltpu.SemaphoreType.DMA((n_sems,)),
            *scratch,
        ],
        compiler_params=pltpu.CompilerParams(
            collective_id=collective_id, has_side_effects=True, vmem_limit_bytes=60 * 2**20
        ),
    )(vec, *inputs)
    return results[0], [out.reshape(-1, out.shape[-1]) for out in results[1:]]


def attention(queries, keys, values, live, scale):
    scores = jnp.einsum("qhd,khd->hqk", queries, keys, preferred_element_type=F32) * scale
    scores = jnp.where(live[None, None, :], scores, -1e30)
    probs = jax.nn.softmax(scores, axis=-1)
    mixed = jnp.einsum("hqk,khd->qhd", probs.astype(BF16), values, preferred_element_type=F32)
    return probs, mixed


def attention_back(probs, queries, keys, values, d_out, scale):
    d_probs = jnp.einsum("qhd,khd->hqk", d_out, values, preferred_element_type=F32)
    d_scores = probs * (d_probs - jnp.sum(probs * d_probs, axis=-1, keepdims=True))
    d_low = d_scores.astype(BF16)
    d_query = jnp.einsum("hqk,khd->qhd", d_low, keys, preferred_element_type=F32) * scale
    d_key = jnp.einsum("hqk,qhd->khd", d_low, queries, preferred_element_type=F32) * scale
    d_value = jnp.einsum("hqk,qhd->khd", probs.astype(BF16), d_out, preferred_element_type=F32)
    return d_query, d_key, d_value


def on_device_general(
    tokens,
    captions,
    cotangent,
    counts,
    cap_lens,
    steps_t,
    w_query,
    w_key,
    w_value,
    w_out,
    w_cap_key,
    w_cap_value,
    w_gate,
    w_up,
    w_down,
    w_mod,
    gains,
    cross_gate,
):
    buckets, seq = lax.axis_size("bucket"), lax.axis_size("seq")
    b, s = lax.axis_index("bucket"), lax.axis_index("seq")
    place = b * seq + s
    rows, width = tokens.shape
    span = rows * seq
    share = width // seq
    heads = share // HEAD_DIM
    scale = HEAD_DIM ** (-0.5)
    live_rows, cap_len = pick_entry(counts, b), pick_entry(cap_lens, b)
    token_total = jnp.sum(counts).astype(F32)

    cond_size = w_mod.shape[0] * buckets * seq
    cond = jax.nn.silu(time_embed(steps_t, cond_size)).astype(BF16)
    cond_part = lax.dynamic_slice_in_dim(cond, place * w_mod.shape[0], w_mod.shape[0], 1)
    slim = gains.shape[1]
    small = jnp.concatenate([gains, cross_gate[None]], axis=0).astype(F32)
    small = jnp.pad(small, ((0, 0), (0, 128 - slim)))
    tok_all, cap_all, small_all, mod, weights = gather_all(
        buckets,
        seq,
        tokens,
        captions,
        small,
        cond_part,
        w_mod,
        [w_query, w_key, w_value, w_cap_key, w_cap_value, w_out, w_gate, w_up, w_down],
        ["col", "col", "col", "col", "col", "row", "col", "col", "row"],
    )
    wq, wk, wv, wck, wcv, wo, wg, wu, wd = weights
    caps = cap_all.reshape(-1, captions.shape[1])
    small_rows = small_all[..., :slim].transpose(2, 0, 1, 3).reshape(8, width)
    gain_f = small_rows[:7]
    own_cols = lax.dynamic_slice_in_dim(small_rows, s * share, share, 1)
    gate_cross = jnp.tanh(own_cols[7])
    scale_attn, gate_attn, scale_ffn, gate_ffn = mod.reshape(4, width)

    hidden = pre_attn(tok_all.astype(F32), gain_f[0], scale_attn).astype(BF16).reshape(span, width)
    query_proj, key_proj = bf_dot(hidden, wq), bf_dot(hidden, wk)
    value_low = bf_dot(hidden, wv).astype(BF16)
    (query_f, key_f), norm_back = jax.vjp(qk_norm, query_proj, key_proj, own_cols[4], own_cols[5])
    cap_key_f, cap_back = jax.vjp(cap_norm, bf_dot(caps, wck), own_cols[6])

    def by_head(values):
        return values.astype(BF16).reshape(values.shape[0], heads, HEAD_DIM)

    query, key, value = by_head(query_f), by_head(key_f), by_head(value_low)
    cap_key, cap_value = by_head(cap_key_f), by_head(bf_dot(caps, wcv))
    probs, self_out = attention(query, key, value, jnp.arange(span) < live_rows, scale)
    cap_live = jnp.arange(caps.shape[0]) < cap_len
    cap_probs, cross_out = attention(query, cap_key, cap_value, cap_live, scale)
    self_out, cross_out = self_out.reshape(span, share), cross_out.reshape(span, share)
    mixed_low = (self_out + gate_cross * cross_out).astype(BF16)
    attn_out = line_scatter(seq, bf_dot(mixed_low, wo), 2)

    tokens_f = tokens.astype(F32)
    (resid_one, ffn_pre), middle_back = jax.vjp(
        middle, tokens_f, attn_out, gain_f[1], gate_attn, gain_f[2], scale_ffn
    )
    ffn_all = line_gather(seq, ffn_pre.astype(BF16), 3)
    act_pre, act_back = jax.vjp(activate, bf_dot(ffn_all, wg), bf_dot(ffn_all, wu))
    act_low = act_pre.astype(BF16)
    ffn_out = line_scatter(seq, bf_dot(act_low, wd), 4)
    out_f, finish_back = jax.vjp(finish, resid_one, ffn_out, gain_f[3], gate_ffn)
    block_out = out_f.astype(BF16)

    row_live = (s * rows + jnp.arange(rows) < live_rows).astype(F32)
    weighted = cotangent.astype(F32) * row_live[:, None] * (buckets * span / token_total)
    d_resid, d_ffn_out, d_gain_last, d_gate_ffn = finish_back(weighted)
    d_ffn_all = line_gather(seq, d_ffn_out.astype(BF16), 5)
    d_gate, d_up = act_back(right_dot(d_ffn_all, wd))
    d_gate, d_up = d_gate.astype(BF16), d_up.astype(BF16)
    d_hidden_ffn = line_scatter(seq, right_dot(d_gate, wg) + right_dot(d_up, wu), 6)
    d_tokens_one, d_attn_out, d_gain_post, d_gate_attn, d_gain_ffn, d_scale_ffn = middle_back(
        (d_resid, d_hidden_ffn)
    )
    d_attn_all = line_gather(seq, d_attn_out.astype(BF16), 7)
    d_mixed_low = right_dot(d_attn_all, wo).astype(BF16)
    d_mixed = d_mixed_low.astype(F32)
    d_cross_low = (gate_cross * d_mixed).astype(BF16)
    grad_cross = jnp.sum(d_mixed * cross_out, axis=0) * (1.0 - gate_cross * gate_cross)

    d_query_cross, d_cap_key, d_cap_value = attention_back(
        cap_probs, query, cap_key, cap_value, by_head(d_cross_low), scale
    )
    d_query, d_key, d_value = attention_back(probs, query, key, value, by_head(d_mixed_low), scale)
    d_cap_key, d_gain_cap = cap_back(d_cap_key.reshape(-1, share))
    d_query, d_key, d_gain_query, d_gain_key = norm_back(
        ((d_query + d_query_cross).reshape(span, share), d_key.reshape(span, share))
    )
    d_query, d_key, d_cap_key = d_query.astype(BF16), d_key.astype(BF16), d_cap_key.astype(BF16)
    d_value = d_value.reshape(span, share).astype(BF16)
    d_cap_value = d_cap_value.reshape(-1, share).astype(BF16)
    d_hidden = line_scatter(
        seq, right_dot(d_query, wq) + right_dot(d_key, wk) + right_dot(d_value, wv), 8
    )
    _, pre_back = jax.vjp(pre_attn, tokens_f, gain_f[0], scale_attn)
    d_tokens_two, d_gain_pre, d_scale_attn = pre_back(d_hidden)
    tokens_grad = d_tokens_one + d_tokens_two

    own_sums = jnp.stack([d_gain_query, d_gain_key, d_gain_cap, grad_cross])
    own_wide = lax.dynamic_update_slice(jnp.zeros((4, width), F32), own_sums, (0, s * share))
    vec = jnp.concatenate(
        [
            jnp.stack([d_scale_attn, d_gate_attn, d_scale_ffn, d_gate_ffn]),
            jnp.stack([d_gain_pre, d_gain_post, d_gain_ffn, d_gain_last]),
            own_wide,
            jnp.zeros((4, width), F32),
        ]
    )
    grads = [
        left_dot(ffn_all, d_gate),
        left_dot(ffn_all, d_up),
        left_dot(act_low, d_ffn_all),
        left_dot(mixed_low, d_attn_all),
        left_dot(caps, d_cap_key),
        left_dot(caps, d_cap_value),
        left_dot(hidden, d_query),
        left_dot(hidden, d_key),
        left_dot(hidden, d_value),
    ]
    kinds = ["col", "col", "row", "row", "col", "col", "col", "col", "col"]
    vec_all, sums = scatter_all(buckets, seq, vec, grads, kinds)
    s_gate, s_up, s_down, s_out, s_cap_key, s_cap_value, s_query, s_key, s_value = sums

    quarter = 4 * width // seq
    mod_rows = vec_all[:, :4].reshape(buckets, -1, quarter)
    mod_rows = lax.dynamic_slice_in_dim(mod_rows, s, 1, 1)[:, 0]
    cond_size = cond.shape[1] // buckets
    cond_cols = lax.dynamic_slice_in_dim(cond, b * cond_size, cond_size, 1).astype(F32)
    s_mod = jnp.sum(cond_cols[:, :, None] * mod_rows[:, None, :], axis=0)
    tail = lax.dynamic_slice(vec_all, (0, 4, place * slim), (buckets, 8, slim))
    tail = jnp.sum(tail, axis=0)
    return (
        block_out,
        tokens_grad,
        s_query,
        s_key,
        s_value,
        s_out,
        s_cap_key,
        s_cap_value,
        s_gate,
        s_up,
        s_down,
        s_mod,
        tail[:7],
        tail[7],
    )


def low_half(shape):
    return lax.broadcasted_iota(jnp.int32, shape, len(shape) - 1) < HEAD_DIM


def pair_sums(values):
    row = lax.broadcasted_iota(jnp.int32, (128, 128), 0) < HEAD_DIM
    same = (row == low_half((128, 128))).astype(BF16)
    high = values.astype(BF16)
    rest = (values - high.astype(F32)).astype(BF16)
    return bf_dot(high, same) + bf_dot(rest, same)


def pair_scale(values, eps):
    return lax.rsqrt(pair_sums(values * values) * (1.0 / HEAD_DIM) + eps)


def fill_rows(out, live, first, yes, no):
    row = lax.broadcasted_iota(jnp.int32, out.shape, 0) + first
    out[...] = jnp.where(row < live, yes, no).astype(out.dtype)


FORWARD_ORDER = ("tok", 0, "tok", 1, "tok", 2, "tok", 6, 7, "cap", 8, 3, "cap", 4, "cap", 5, "cap")
LAG = 1
WINDOW = 2


def forward_kernel(buckets, seq, kinds, slim, *refs):
    count = len(kinds)
    tokens, captions, small, cond, w_mod, counts, cap_lens = refs[:7]
    shards = refs[7 : 7 + count]
    refs = refs[7 + count :]
    cap_all = refs[0]
    far_fulls = refs[1 : 1 + count]
    refs = refs[1 + count :]
    (
        gain_rows,
        mod_rows,
        hidden,
        query_raw,
        key_raw,
        cap_raw,
        query,
        key,
        value,
        cap_key,
        cap_value,
        cross_out,
        mixed,
    ) = refs[:13]
    refs = refs[13:]
    part, got_bucket, got_seq, mod_sum, small_all, tok_all, cap_near, own_out = refs[:8]
    fulls = refs[8 : 8 + count]
    key_mask, cap_mask, send, recv = refs[8 + count :]
    b, s = lax.axis_index("bucket"), lax.axis_index("seq")
    copies = Copies(send, recv)
    place = b * seq + s
    to_slot, to_s = lax.rem(place, buckets), lax.div(place, buckets)
    to_b = slot(to_slot, buckets)
    back = s * buckets + slot(b, buckets)
    from_b, from_s = lax.div(back, seq), lax.rem(back, seq)
    stays = jnp.logical_and(to_b == b, to_s == s)

    for k in range(1, buckets):
        greet(lax.rem(b + k, buckets), s)
    for k in range(1, seq):
        greet(b, lax.rem(s + k, seq))

    @pl.when(jnp.logical_not(stays))
    def _():
        greet(from_b, from_s)

    fill_rows(key_mask, counts[b], 0, 1.0, 0.0)
    fill_rows(cap_mask, cap_lens[b], 0, 1.0, 0.0)
    lanes = part.shape[2]
    for j in range(part.shape[1]):
        part[:, j, :] = bf_dot(cond[...], w_mod[:, j * lanes : (j + 1) * lanes])

    peers = buckets - 1 + seq - 1 + jnp.where(stays, 0, 1)
    pl.semaphore_wait(pltpu.get_barrier_semaphore(), peers)

    sent = []

    def go(copy):
        copy.start()
        sent.append(copy)
        return copy

    mod_moves = []
    for k in range(1, buckets):
        peer = lax.rem(b + k, buckets)
        mod_moves.append(go(copies.remote(part.at[peer], got_bucket.at[k], peer, s)))
    small_moves = []
    for k in range(1, seq):
        peer = lax.rem(s + k, seq)
        small_moves.append(go(copies.remote(small, small_all.at[b, s], b, peer)))
    small_own = copies.local(small, small_all.at[b, s])
    small_own.start()

    tok = Relay(copies, tokens, tok_all, b, s, seq)
    cap = Relay(copies, captions, cap_near, b, s, seq)
    items, step = [], {"tok": 0, "cap": 0}
    for what in FORWARD_ORDER:
        if isinstance(what, str):
            items.append((tok if what == "tok" else cap, step[what]))
            step[what] += 1
        else:
            items.append((None, what))

    first = [None] * count

    def depart(at):
        kind, shard, full = kinds[at], shards[at], fulls[at]
        if kind == "row":
            move = copies.remote(shard, full.at[to_slot], to_b, to_s)
            keep = copies.local(shard, full.at[slot(b, buckets)])

            @pl.when(jnp.logical_not(stays))
            def _():
                move.start()

            @pl.when(stays)
            def _():
                keep.start()

            first[at] = (move, keep)
            return
        wide = full.shape[-1]

        def columns(peer):
            return shard.at[:, pl.ds(pl.multiple_of(peer * wide, 128), wide)]

        moves = []
        for k in range(1, seq):
            peer = lax.rem(s + k, seq)
            move = copies.remote(columns(peer), full.at[b, s], b, peer)
            move.start()
            moves.append(move)
        keep = copies.local(columns(s), full.at[b, s])
        keep.start()
        first[at] = (moves, keep)

    def arrived(at):
        moves, keep = first[at]
        if kinds[at] == "row":

            @pl.when(jnp.logical_not(stays))
            def _():
                moves.wait()

            @pl.when(stays)
            def _():
                keep.wait()

            return
        for move in moves:
            move.wait()
        keep.wait()

    twin = flip(b, 1)
    near_x, near_y = flip(b, 2), flip(b, 4)
    far = flip(near_x, 4)
    second = [None] * count

    def index(at, device):
        return slot(device, buckets) if kinds[at] == "row" else device

    def stage_a(at):
        block = fulls[at].at[index(at, b)]
        second[at] = {
            "x": go(copies.remote(block, block, near_x, s)),
            "y": go(copies.remote(block, block, near_y, s)),
            "twin": [go(copies.remote(block, block, twin, s))],
        }

    def stage_b(at):
        full, now = fulls[at], second[at]
        cut = halves_of(full.shape[1:])
        now["x"].wait_recv()
        block = full.at[index(at, near_x), pl.ds(0, cut)]
        now["dy"] = go(copies.remote(block, block, near_y, s))
        block = full.at[index(at, near_x)]
        now["twin"].append(go(copies.remote(block, block, twin, s)))
        now["y"].wait_recv()
        block = full.at[index(at, near_y), pl.ds(cut, full.shape[1] - cut)]
        now["dx"] = go(copies.remote(block, block, near_x, s))
        block = full.at[index(at, near_y)]
        now["twin"].append(go(copies.remote(block, block, twin, s)))

    fetched = {}

    def stage_c(at):
        full, now = fulls[at], second[at]
        now["dy"].wait_recv()
        now["dx"].wait_recv()
        block = full.at[index(at, far)]
        now["twin"].append(go(copies.remote(block, block, twin, s)))
        for move in now["twin"]:
            move.wait_recv()
        go_local = copies.local(full, far_fulls[at])
        go_local.start()
        fetched[at] = go_local
        done.add(at)

    def fetch(at):
        whole = fulls[at][...]
        return whole.reshape(-1, whole.shape[-1])


    rows = seq * tok_all.shape[1]
    width = tok_all.shape[2]
    cap_rows = seq * cap_near.shape[1]
    share = query.shape[1]
    pairs = share // 128
    block_rows = tok_all.shape[1]

    def small_sums():
        for move in small_next:
            move.wait_recv()
        strips = [None] * (width // 128)
        lane = lax.broadcasted_iota(jnp.int32, (8, 128), 1)
        for d in range(buckets * seq):
            at, shift = divmod(d * slim, 128)
            piece = small_all[d // seq, d % seq]
            turned = pltpu.roll(piece, shift, 1) if shift else piece
            for index, keep in ((at, lane >= shift), (at + 1, lane < shift)):
                if index == at + 1 and shift + slim <= 128:
                    continue
                add = jnp.where(keep, turned, 0.0)
                strips[index] = add if strips[index] is None else strips[index] + add
        for at, strip in enumerate(strips):
            gain_rows[:, at * 128 : (at + 1) * 128] = strip
        total = mod_sum[...]
        for k, move in enumerate(mod_next, 1):
            move.wait_recv()
            total = total + got_seq[k]
        for j in range(8):
            at, lane_at = divmod(j * lanes, width)
            mod_rows[at : at + 1, lane_at : lane_at + lanes] = total[j : j + 1, :]
        mod_rows[4:8, :] = jnp.zeros((4, width), F32)

    def make_hidden():
        factor = gain_rows[0:1, :] * (1.0 + mod_rows[0:1, :])
        for t in range(seq):

            def body(i, carry):
                at = pl.ds(pl.multiple_of(i * 32, 32), 32)
                x = tok_all[t, at, :].astype(F32)
                x = x * lax.rsqrt(jnp.mean(x * x, axis=-1, keepdims=True) + 1e-05) * factor
                to = pl.ds(pl.multiple_of(t * block_rows + i * 32, 32), 32)
                hidden[to, :] = x.astype(BF16)
                return carry

            lax.fori_loop(0, block_rows // 32, body, 0)

    def gain_of(row, pair):
        at = pl.multiple_of(s * share + pair * 128, 128)
        return gain_rows[row : row + 1, pl.ds(at, 128)]

    def make_normed(raw, out, row, scale):
        def body(i, carry):
            at = pl.ds(pl.multiple_of(i * 64, 64), 64)
            for pair in range(pairs):
                lane = slice(pair * 128, (pair + 1) * 128)
                x = raw[at, lane]
                x = x * pair_scale(x, 1e-06) * gain_of(row, pair)
                out[at, lane] = x.astype(BF16)
            return carry

        del scale
        lax.fori_loop(0, raw.shape[0] // 64, body, 0)

    def make_query():
        query_raw[...] = bf_dot(hidden[...], fetch(0))
        make_normed(query_raw, query, 4, None)

    def make_key():
        key_raw[...] = bf_dot(hidden[...], fetch(1))
        make_normed(key_raw, key, 5, None)

    def make_value():
        value[...] = bf_dot(hidden[...], fetch(2)).astype(BF16)

    def cap_near_rows():
        whole = cap_near[...]
        return whole.reshape(cap_rows, whole.shape[-1])

    def make_cap_key():
        cap_raw[...] = bf_dot(cap_near_rows(), fetch(3))
        make_normed(cap_raw, cap_key, 6, None)

    def make_cap_value():
        cap_value[...] = bf_dot(cap_near_rows(), fetch(4)).astype(BF16)

    def attend(pair, k_ref, v_ref, mask, store):
        lane = slice(pair * 128, (pair + 1) * 128)
        low = low_half((128, 128))
        keys = k_ref[:, lane]
        values = jnp.concatenate([v_ref[:, lane] * mask[...], mask[...]], axis=1)

        def body(i, carry):
            at = pl.ds(pl.multiple_of(i * 128, 128), 128)
            q = query[at, lane] * jnp.asarray(HEAD_DIM**-0.5, BF16)
            outs = []
            for half in (jnp.where(low, q, jnp.zeros_like(q)), jnp.where(low, jnp.zeros_like(q), q)):
                weights = jnp.exp(right_dot(half, keys))
                outs.append(bf_dot(weights.astype(BF16), values))
            out = jnp.where(low, outs[0][:, :128], outs[1][:, :128])
            store(at, lane, out / jnp.where(low, outs[0][:, 128:], outs[1][:, 128:]))
            return carry

        lax.fori_loop(0, rows // 128, body, 0)

    def make_own(pair):
        def store(at, lane, out):
            own_out[at, lane] = out

        attend(pair, key, value, key_mask, store)

    def make_mixed(pair):
        gate = jnp.tanh(gain_of(7, pair))

        def store(at, lane, out):
            cross_out[at, lane] = out
            mixed[at, lane] = (own_out[at, lane] + gate * out).astype(BF16)

        attend(pair, cap_key, cap_value, cap_mask, store)

    work = [
        (lambda: (small_sums(), make_hidden()), "h", {"tok"}),
        (make_query, "q", {"h", 0}),
        (make_key, "k", {"h", 1}),
        (make_value, "v", {"h", 2}),
        (make_cap_key, "ck", {"cap", 3}),
        (make_cap_value, "cv", {"cap", 4}),
        *((functools.partial(make_own, p), ("own", p), {"q", "k", "v"}) for p in range(pairs)),
        *(
            (functools.partial(make_mixed, p), ("all", p), {"q", "ck", "cv", ("own", p)})
            for p in range(pairs)
        ),
    ]

    def do_work():
        for at, (piece, name, needs) in enumerate(work):
            if needs <= done:
                piece()
                done.add(name)
                del work[at]
                return True
        return False


    done = set()

    def begin(i):
        relay, j = items[i]
        if relay is None:
            depart(j)
        else:
            relay.start(j)
            if j == seq - 1:
                done.add("tok" if relay is tok else "cap")

    window = WINDOW
    for i in range(window):
        begin(i)
    for move in small_moves:
        move.wait_recv()
    small_own.wait()
    small_next = []
    for k in range(1, buckets):
        peer = lax.rem(b + k, buckets)
        small_next.append(go(copies.remote(small_all.at[b], small_all.at[b], peer, s)))
    total = part[b]
    for k, move in enumerate(mod_moves, 1):
        move.wait_recv()
        total = total + got_bucket[k]
    mod_sum[...] = total
    mod_next = []
    for k in range(1, seq):
        peer = lax.rem(s + k, seq)
        mod_next.append(go(copies.remote(mod_sum, got_seq.at[k], b, peer)))

    cap_out = copies.local(cap_near, cap_all)
    order = []
    for i, (relay, j) in enumerate(items):
        if relay is None:
            arrived(j)
        elif j <= seq - 2:
            relay.sent(j)
        if i + window < len(items):
            begin(i + window)
        if relay is None:
            order.append(j)
            stage_a(j)
            if len(order) > LAG:
                stage_b(order[-1 - LAG])
            if len(order) > LAG + 1:
                stage_c(order[-2 - LAG])
        do_work()
    cap_out.start()
    for at in range(LAG):
        stage_b(order[len(order) - LAG + at])
        stage_c(order[len(order) - LAG - 1 + at])
        do_work()
    stage_c(order[-1])
    while do_work():
        pass
    cap_out.wait()
    for copy in fetched.values():
        copy.wait()
    for move in sent:
        move.wait_send()


def forward_all(buckets, seq, tokens, captions, small, slim, cond, w_mod, masks, shards, kinds):
    any_spec = pl.BlockSpec(memory_space=pl.ANY)
    vmem = pl.BlockSpec(memory_space=pltpu.VMEM)
    smem = pl.BlockSpec(memory_space=pltpu.SMEM)
    fulls = []
    for shard, kind in zip(shards, kinds, strict=True):
        rows, wide = shard.shape
        shape = (buckets, rows, wide) if kind == "row" else (buckets, seq, rows, wide // seq)
        fulls.append(jax.ShapeDtypeStruct(shape, BF16))
    near = [pltpu.VMEM(full.shape, BF16) for full in fulls]
    width = tokens.shape[1]
    mod_lanes = w_mod.shape[1] // 8
    span, cap_span, share = seq * tokens.shape[0], seq * captions.shape[0], width // seq
    f32_rows = jax.ShapeDtypeStruct((span, share), F32)
    low_rows = jax.ShapeDtypeStruct((span, share), BF16)
    cap_low = jax.ShapeDtypeStruct((cap_span, share), BF16)
    inner = [
        jax.ShapeDtypeStruct((8, width), F32),
        jax.ShapeDtypeStruct((8, width), F32),
        jax.ShapeDtypeStruct((span, width), BF16),
        f32_rows,
        f32_rows,
        jax.ShapeDtypeStruct((cap_span, share), F32),
        low_rows,
        low_rows,
        low_rows,
        cap_low,
        cap_low,
        f32_rows,
        low_rows,
    ]
    n_sems = 64 + 16 * buckets + len(shards) * (seq + 2 * buckets)
    outs = pl.pallas_call(
        functools.partial(forward_kernel, buckets, seq, tuple(kinds), slim),
        out_shape=[jax.ShapeDtypeStruct((seq,) + captions.shape, BF16), *fulls, *inner],
        in_specs=[any_spec, any_spec, any_spec, vmem, vmem, smem, smem] + [any_spec] * len(shards),
        out_specs=[any_spec] * (1 + len(shards)) + [vmem] * len(inner),
        scratch_shapes=[
            pltpu.VMEM((buckets, 8, mod_lanes), F32),
            pltpu.VMEM((buckets, 8, mod_lanes), F32),
            pltpu.VMEM((seq, 8, mod_lanes), F32),
            pltpu.VMEM((8, mod_lanes), F32),
            pltpu.VMEM((buckets, seq) + small.shape, F32),
            pltpu.VMEM((seq,) + tokens.shape, BF16),
            pltpu.VMEM((seq,) + captions.shape, BF16),
            pltpu.VMEM((span, share), F32),
            *near,
            pltpu.VMEM((span, 128), BF16),
            pltpu.VMEM((cap_span, 128), BF16),
            pltpu.SemaphoreType.DMA((n_sems,)),
            pltpu.SemaphoreType.DMA((n_sems,)),
        ],
        compiler_params=pltpu.CompilerParams(
            collective_id=9, has_side_effects=True, vmem_limit_bytes=62 * 2**20
        ),
    )(tokens, captions, small, cond, w_mod, *masks, *shards)
    at = 1 + len(shards)
    weights = [full.reshape(-1, full.shape[-1]) for full in outs[1:at]]
    return outs[0], weights, outs[at:]


def middle_kernel(buckets, seq, chunks, kinds, *refs):
    mixed, w_out, tokens, cotangent, counts, gain_rows, mod_rows = refs[:7]
    far_weights, refs = refs[7:10], refs[10:]
    block_out, d_tokens, d_attn, row_sums = refs[:4]
    outs, refs = refs[4:7], refs[7:]
    w_gate, w_up, w_down, ffn_all, d_ffn, act, d_gate, d_up = refs[:8]
    gate_keep, up_keep, attn_keep, resid_keep, got, parts, from_left, from_right = refs[8:16]
    row_scale, send, recv = refs[16:19]
    grads, refs = refs[19:22], refs[22:]
    b, s = lax.axis_index("bucket"), lax.axis_index("seq")
    copies = Copies(send, recv)
    loads = [copies.local(a, b_) for a, b_ in zip(far_weights, (w_gate, w_up, w_down), strict=True)]
    for load in loads:
        load.start()
    sums = GradSums(copies, b, s, buckets, seq, kinds, grads, outs, refs, near=True)
    pl.semaphore_wait(pltpu.get_barrier_semaphore(), greet_all(b, s, buckets, seq))

    rows, width = tokens.shape
    live = sum(counts[k] for k in range(buckets))
    factor = buckets * seq * rows / jnp.full((rows, 128), live, jnp.int32).astype(F32)
    row = lax.broadcasted_iota(jnp.int32, (rows, 128), 0) + s * rows
    row_scale[...] = jnp.where(row < counts[b], factor, 0.0)
    thin = rows // chunks
    tall = seq * thin
    hidden = act.shape[-1]
    wide = 512
    gate_post = jnp.tanh(mod_rows[1:2, :]) * gain_rows[1:2, :]
    gain_ffn = gain_rows[2:3, :] * (1.0 + mod_rows[2:3, :])
    gate_last = jnp.tanh(mod_rows[3:4, :]) * gain_rows[3:4, :]
    row_sums[...] = jnp.zeros_like(row_sums)

    def of(c):
        return pl.ds(c * thin, thin)

    def chunk_of(ref, c, cols=slice(None)):
        whole = ref[:, of(c), cols]
        return whole.reshape(tall, whole.shape[-1])

    def mean(values):
        return jnp.mean(values, axis=-1, keepdims=True)

    def over_rows(c, body):
        step = 16

        def one(i, carry):
            return body(pl.ds(pl.multiple_of(c * thin + i * step, step), step), carry)

        return lax.fori_loop(0, thin // step, one, jnp.zeros((1, width), F32), unroll=2)

    def weighted(at):
        return cotangent[at, :].astype(F32) * row_scale[at, 0:1]

    def after_attn(c):
        def body(at, carry):
            out = got[at, :]
            attn_keep[at, :] = out
            resid = out * lax.rsqrt(mean(out * out) + 1e-05) * gate_post
            resid = tokens[at, :].astype(F32) + resid
            resid_keep[at, :] = resid
            normed = resid * lax.rsqrt(mean(resid * resid) + 1e-05)
            ffn_all[s, at, :] = (normed * gain_ffn).astype(BF16)
            return carry

        over_rows(c, body)

    def after_ffn(c):
        def body(at, total):
            out, resid, grad = got[at, :], resid_keep[at, :], weighted(at)
            size = lax.rsqrt(mean(out * out) + 1e-05)
            normed = out * size
            block_out[at, :] = (resid + gate_last * normed).astype(BF16)
            inner = grad * gate_last
            d_ffn[s, at, :] = (size * (inner - normed * mean(inner * normed))).astype(BF16)
            return total + jnp.sum(grad * normed, axis=0, keepdims=True)

        row_sums[2:3, :] += over_rows(c, body)

    def after_ffn_back(c):
        def body(at, totals):
            first, second = totals
            d_pre, resid, out = got[at, :], resid_keep[at, :], attn_keep[at, :]
            size = lax.rsqrt(mean(resid * resid) + 1e-05)
            normed, inner = resid * size, d_pre * gain_ffn
            second = second + jnp.sum(d_pre * normed, axis=0, keepdims=True)
            grad = weighted(at) + size * (inner - normed * mean(inner * normed))
            d_tokens[at, :] = grad
            size = lax.rsqrt(mean(out * out) + 1e-05)
            normed, inner = out * size, grad * gate_post
            first = first + jnp.sum(grad * normed, axis=0, keepdims=True)
            d_attn[s, at, :] = (size * (inner - normed * mean(inner * normed))).astype(BF16)
            return first, second

        step, zero = 16, jnp.zeros((1, width), F32)

        def one(i, carry):
            return body(pl.ds(pl.multiple_of(c * thin + i * step, step), step), carry)

        first, second = lax.fori_loop(0, thin // step, one, (zero, zero), unroll=2)
        row_sums[0:1, :] += first
        row_sums[1:2, :] += second

    def put_parts(c, cols, total):
        parts[c, :, :, cols] = total.astype(BF16).reshape(seq, thin, total.shape[-1])

    def attn_product(c):
        left = chunk_of(mixed, c)
        for at in range(0, width, wide):
            cols = slice(at, at + wide)
            put_parts(c, cols, bf_dot(left, w_out[:, cols]))

    def ffn_product(c):
        for at in range(0, hidden, wide):
            cols = slice(at, at + wide)
            left = chunk_of(ffn_all, c)
            gate, up = bf_dot(left, w_gate[:, cols]), bf_dot(left, w_up[:, cols])
            gate_keep[c, :, cols], up_keep[c, :, cols] = gate, up
            value = (gate * jax.nn.sigmoid(gate) * up).astype(BF16)
            act[:, of(c), cols] = value.reshape(seq, thin, wide)
        left = chunk_of(act, c)
        for at in range(0, width, wide):
            cols = slice(at, at + wide)
            put_parts(c, cols, bf_dot(left, w_down[:, cols]))

    def ffn_back_product(c):
        for at in range(0, hidden, wide):
            cols = slice(at, at + wide)
            d_act = right_dot(chunk_of(d_ffn, c), w_down[cols, :])
            gate, up = gate_keep[c, :, cols], up_keep[c, :, cols]
            sig = jax.nn.sigmoid(gate)
            silu = gate * sig
            d_g = (d_act * up * (sig + silu * (1.0 - sig))).astype(BF16)
            d_u = (d_act * silu).astype(BF16)
            d_gate[:, of(c), cols] = d_g.reshape(seq, thin, wide)
            d_up[:, of(c), cols] = d_u.reshape(seq, thin, wide)
        left_g, left_u = chunk_of(d_gate, c), chunk_of(d_up, c)
        for at in range(0, width, wide):
            cols = slice(at, at + wide)
            total = right_dot(left_g, w_gate[cols, :]) + right_dot(left_u, w_up[cols, :])
            put_parts(c, cols, total)

    def pour_of(c, turn):
        left, right = from_left.at[turn * chunks + c], from_right.at[turn * chunks + c]
        return Pour(copies, parts.at[c], left, right, b, s, seq)

    gathered = (ffn_all, d_ffn, d_attn)
    after = (after_attn, after_ffn, after_ffn_back)
    products = (attn_product, ffn_product, ffn_back_product)

    def all_rows(ref, cols=slice(None)):
        whole = ref[:, :, cols]
        return whole.reshape(seq * rows, whole.shape[-1])

    def down_grad():
        chips, part = buckets // 2, hidden // buckets
        at = spread(buckets)
        for i in range(chips):
            turned = all_rows(act, slice(2 * i * part, 2 * (i + 1) * part)).T
            total = bf_dot(turned, all_rows(d_ffn)).astype(BF16)
            for half in range(2):
                p = at[2 * i + half]
                grads[2][p // 2, p % 2] = total[half * part : (half + 1) * part]
        sums.begin(2)

    def weight_grads():
        chips, part = buckets // 2, width // (buckets // 2)
        for i in range(chips):
            turned = all_rows(ffn_all, slice(i * part, (i + 1) * part)).T
            for grad, d in zip(grads[:2], (d_gate, d_up), strict=True):
                total = bf_dot(turned, all_rows(d))
                grad[i] = total.astype(BF16).reshape(2, part // 2, hidden)
            if i == 1:
                sums.stage_a(2)
            yield
        sums.begin(0)
        sums.begin(1)
        sums.stage_b(2)
        yield
        sums.stage_a(0)
        yield
        sums.stage_c(2)
        sums.stage_a(1)
        yield
        sums.stage_b(0)
        yield
        sums.stage_b(1)
        yield
        sums.stage_c(0)
        sums.stage_c(1)
        sums.stage_d(2)

    extra = weight_grads()
    plan = [(turn, c) for turn in range(3) for c in range(chunks)]
    gathers, open_gather = {}, []

    def finish_gather():
        turn, c = open_gather.pop(0)
        gathers[turn, c].start(seq - 1)
        for j in range(seq - 1):
            gathers[turn, c].sent(j)
        return turn, c

    attn_product(0)
    pours = {(0, 0): pour_of(0, 0)}
    ready = pours[0, 0].cuts
    for q in range(ready):
        pours[0, 0].step(q)
    for c in range(1, chunks):
        attn_product(c)
    for load in loads:
        load.wait()
    for at, (turn, c) in enumerate(plan):
        pour = pours[turn, c]
        mate = gathers[open_gather[0]] if open_gather else None
        per = pour.count // (seq - 1)
        final = at == len(plan) - 1
        for j in range(2, seq):
            if mate is not None and j < seq - 1:
                mate.start(j)
            if final:
                next(extra, None)
            for q in range((j - 1) * per, j * per):
                pour.step(q)
            if final:
                next(extra, None)
        pour.end(got.at[of(c)])
        after[turn](c)
        gathers[turn, c] = Relay(copies, None, gathered[turn], b, s, seq, of(c))
        gathers[turn, c].start(0)
        if mate is not None:
            done_turn, done_c = finish_gather()
            if (done_turn, done_c) == (1, chunks - 1):
                down_grad()
            if done_turn < 2:
                products[done_turn + 1](done_c)
        open_gather.append((turn, c))
        gathers[turn, c].start(1)
        if at + 1 < len(plan):
            nxt = plan[at + 1]
            pours[nxt] = pour_of(nxt[1], nxt[0])
            for q in range(ready):
                pours[nxt].step(q)
            if at + 2 == len(plan):
                next(extra)
                next(extra)
    turn, c = open_gather[0]
    for j in range(2, seq - 1):
        next(extra, None)
        gathers[turn, c].start(j)
    next(extra, None)
    finish_gather()
    for _ in extra:
        pass
    sums.end()


def middle_all(buckets, seq, mixed, weights, tokens, cotangent, counts, gain_rows, mod_rows):
    any_spec = pl.BlockSpec(memory_space=pl.ANY)
    vmem = pl.BlockSpec(memory_space=pltpu.VMEM)
    smem = pl.BlockSpec(memory_space=pltpu.SMEM)
    chunks = CHUNKS
    w_out, w_gate, w_up, w_down = weights
    rows, width = tokens.shape
    hidden = w_gate.shape[1]
    tall, thin = (seq, rows, width), rows // chunks
    flat = (seq, rows, hidden)
    blocks = pltpu.VMEM((3 * chunks, seq - 1, thin, width), BF16)
    kinds = ("col", "col", "row")
    shapes, sums_out, scratch, n_sems = sums_shapes(
        buckets, seq, [w_gate.shape, w_up.shape, w_down.shape], kinds, near=True
    )
    n_sems += 16 + 3 * chunks * (2 * CUTS + 2) * seq
    results = pl.pallas_call(
        functools.partial(middle_kernel, buckets, seq, chunks, kinds),
        out_shape=[
            jax.ShapeDtypeStruct((rows, width), BF16),
            jax.ShapeDtypeStruct((rows, width), F32),
            jax.ShapeDtypeStruct(tall, BF16),
            jax.ShapeDtypeStruct((8, width), F32),
            *sums_out,
        ],
        in_specs=[vmem] * 4 + [smem] + [vmem] * 2 + [any_spec] * 3,
        out_specs=[vmem] * 7,
        scratch_shapes=[
            pltpu.VMEM(w_gate.shape, BF16),
            pltpu.VMEM(w_up.shape, BF16),
            pltpu.VMEM(w_down.shape, BF16),
            pltpu.VMEM(tall, BF16),
            pltpu.VMEM(tall, BF16),
            *([pltpu.VMEM(flat, BF16)] * 3),
            pltpu.VMEM((chunks, seq * thin, hidden), F32),
            pltpu.VMEM((chunks, seq * thin, hidden), F32),
            pltpu.VMEM((rows, width), F32),
            pltpu.VMEM((rows, width), F32),
            pltpu.VMEM((rows, width), F32),
            pltpu.VMEM((chunks, seq, thin, width), BF16),
            blocks,
            blocks,
            pltpu.VMEM((rows, 128), F32),
            pltpu.SemaphoreType.DMA((n_sems,)),
            pltpu.SemaphoreType.DMA((n_sems,)),
            *[pltpu.VMEM(shape, BF16) for shape in shapes],
            *scratch,
        ],
        compiler_params=pltpu.CompilerParams(
            collective_id=11, has_side_effects=True, vmem_limit_bytes=62 * 2**20
        ),
    )(
        mixed.reshape(seq, rows, mixed.shape[1]),
        w_out,
        tokens,
        cotangent,
        counts,
        gain_rows,
        mod_rows,
        w_gate,
        w_up,
        w_down,
    )
    return results[:4], [out.reshape(-1, out.shape[-1]) for out in results[4:]]


def backward_kernel(buckets, seq, kinds, *refs):
    count = len(kinds)
    (
        d_attn,
        w_query,
        w_key,
        w_value,
        w_out,
        query,
        key,
        value,
        cap_key,
        cap_value,
        cross_out,
        query_raw,
        key_raw,
        cap_raw,
        gain_rows,
        mod_rows,
        counts,
        cap_lens,
        mixed,
        hidden,
        captions,
        tokens,
        d_tokens,
        row_sums,
    ) = refs[:24]
    tokens_grad, mod_all, small_out, refs = refs[24], refs[25], refs[26], refs[27:]
    outs, refs = refs[:count], refs[count:]
    mixed_low, cross_low, query_acc, key_acc, value_acc, cap_key_acc, cap_value_acc = refs[:7]
    d_query, d_key, d_value, d_cap_key, d_cap_value, d_hidden, vec = refs[7:14]
    mod_give, mod_got, mod_sum, wide_give, wide_got, slim_give, slim_got = refs[14:21]
    key_bias, cap_bias, parts, from_left, from_right, send, recv = refs[21:28]
    grads, refs = refs[28 : 28 + count], refs[28 + count :]
    b, s = lax.axis_index("bucket"), lax.axis_index("seq")
    copies = Copies(send, recv)
    sums = GradSums(copies, b, s, buckets, seq, kinds, grads, outs, refs, near=True)
    peers = greet_all(b, s, buckets, seq)

    rows, share = query.shape
    width = parts.shape[-1]
    pairs = share // 128
    chips = buckets // 2
    span_block = 256
    scale = HEAD_DIM**-0.5

    def gain_of(row, pair):
        at = pl.multiple_of(s * share + pair * 128, 128)
        return gain_rows[row : row + 1, pl.ds(at, 128)]

    vec[...] = jnp.zeros_like(vec)
    mod_give[...] = jnp.zeros_like(mod_give)
    wide_give[...] = jnp.zeros_like(wide_give)
    slim_give[...] = jnp.zeros_like(slim_give)
    fill_rows(key_bias, counts[b], 0, 0.0, -1e30)
    fill_rows(cap_bias, cap_lens[b], 0, 0.0, -1e30)
    mixed_low[...] = right_dot(d_attn[...], w_out[...]).astype(BF16)

    def own_sum(row, pair, total):
        vec[row : row + 1, pl.ds(pl.multiple_of(s * share + pair * 128, 128), 128)] = total

    def cross_part(pair):
        lane = slice(pair * 128, (pair + 1) * 128)
        gate = jnp.tanh(gain_of(7, pair))

        def body(i, total):
            at = pl.ds(pl.multiple_of(i * 128, 128), 128)
            d = mixed_low[at, lane].astype(F32)
            cross_low[at, lane] = (gate * d).astype(BF16)
            return total + jnp.sum(d * cross_out[at, lane], axis=0, keepdims=True)

        total = lax.fori_loop(0, rows // 128, body, jnp.zeros((1, 128), F32))
        own_sum(7, pair, total * (1.0 - gate * gate))

    def attend_back(pair, k_ref, v_ref, bias, d_ref, k_acc, v_acc, add):
        lane = slice(pair * 128, (pair + 1) * 128)
        low = low_half((span_block, 128))
        k_turned = k_ref[:, lane].T
        k_acc[:, lane] = jnp.zeros((k_acc.shape[0], 128), F32)
        v_acc[:, lane] = jnp.zeros((v_acc.shape[0], 128), F32)

        def body(i, carry):
            at = pl.ds(pl.multiple_of(i * span_block, span_block), span_block)
            q = query[at, lane] * jnp.asarray(scale, BF16)
            d = d_ref[at, lane]
            found = []
            for keep in (low, jnp.logical_not(low)):
                q_half = jnp.where(keep, q, jnp.zeros_like(q))
                d_half = jnp.where(keep, d, jnp.zeros_like(d))
                scores = right_dot(k_ref[:, lane], q_half)
                scores = scores + jnp.concatenate([bias[...], bias[...]], axis=1)
                weights = jnp.exp(scores)
                probs = weights * (1.0 / jnp.sum(weights, axis=0, keepdims=True))
                d_probs = right_dot(v_ref[:, lane], d_half)
                delta = jnp.sum(probs * d_probs, axis=0, keepdims=True)
                d_scores = (probs * (d_probs - delta)).astype(BF16)
                k_acc[:, lane] += bf_dot(d_scores, q_half)
                v_acc[:, lane] += bf_dot(probs.astype(BF16), d_half)
                found.append(bf_dot(k_turned, d_scores))
            turned = jnp.concatenate([found[0][:HEAD_DIM], found[1][HEAD_DIM:]], axis=0)
            d_q = turned.T * scale
            query_acc[at, lane] = query_acc[at, lane] + d_q if add else d_q
            return carry

        lax.fori_loop(0, rows // span_block, body, 0)

    def norm_back(raw, d_norm, out, row, sum_row):
        for pair in range(pairs):
            lane = slice(pair * 128, (pair + 1) * 128)
            gain = gain_of(row, pair)

            def body(i, total):
                at = pl.ds(pl.multiple_of(i * 128, 128), 128)
                x, d = raw[at, lane], d_norm[at, lane]
                size = pair_scale(x, 1e-06)
                normed, inner = x * size, d * gain
                mean = pair_sums(inner * normed) * (1.0 / HEAD_DIM)
                out[at, lane] = (size * (inner - normed * mean)).astype(BF16)
                return total + jnp.sum(d * normed, axis=0, keepdims=True)

            total = lax.fori_loop(0, raw.shape[0] // 128, body, jnp.zeros((1, 128), F32))
            own_sum(sum_row, pair, total)

    def weight_grads(left, chosen):
        part = left.shape[1] // chips
        for i in range(chips):
            turned = left[:, i * part : (i + 1) * part].T
            for w, right in chosen:
                total = bf_dot(turned, right[...])
                grads[w][i] = total.astype(BF16).reshape(2, part // 2, total.shape[-1])
            yield
        for w, _ in chosen:
            sums.begin(w)

    def out_grad():
        total = bf_dot(mixed[...].T, d_attn[...]).astype(BF16)
        part = share // buckets
        for block, p in enumerate(spread(buckets)):
            grads[0][p // 2, p % 2] = total[block * part : (block + 1) * part]
        sums.begin(0)

    pl.semaphore_wait(pltpu.get_barrier_semaphore(), peers)
    for pair in range(pairs):
        cross_part(pair)
        attend_back(pair, cap_key, cap_value, cap_bias, cross_low, cap_key_acc, cap_value_acc, False)
    norm_back(cap_raw, cap_key_acc, d_cap_key, 6, 6)
    d_cap_value[...] = cap_value_acc[...].astype(BF16)
    for _ in weight_grads(captions, ((1, d_cap_key), (2, d_cap_value))):
        pass
    steps = (lambda: sums.stage_a(1), lambda: sums.stage_a(2), lambda: sums.stage_b(1))
    for pair in range(pairs):
        attend_back(pair, key, value, key_bias, mixed_low, key_acc, value_acc, True)
        steps[pair]()
    norm_back(query_raw, query_acc, d_query, 4, 4)
    norm_back(key_raw, key_acc, d_key, 5, 5)
    d_value[...] = value_acc[...].astype(BF16)
    pour = Pour(copies, parts, from_left, from_right, b, s, seq)
    wide = 512
    for at in range(0, width, wide):
        cols = slice(at, at + wide)
        total = right_dot(d_query[...], w_query[cols, :]) + right_dot(d_key[...], w_key[cols, :])
        total = total + right_dot(d_value[...], w_value[cols, :])
        parts[:, :, cols] = total.astype(BF16).reshape(seq, rows // seq, wide)
    pieces = weight_grads(hidden, ((3, d_query), (4, d_key), (5, d_value)))
    between = {1: out_grad, 2: lambda: sums.stage_b(2)}
    for q in range(pour.count):
        pour.step(q)
        if q in between:
            between[q]()
        elif q > 2:
            next(pieces, None)
    for _ in pieces:
        pass
    sums.stage_a(0)
    sums.stage_c(1)
    sums.stage_c(2)
    pour.end(d_hidden)

    factor = gain_rows[0:1, :] * (1.0 + mod_rows[0:1, :])

    def body(i, total):
        at = pl.ds(pl.multiple_of(i * 16, 16), 16)
        x, d = tokens[at, :].astype(F32), d_hidden[at, :]
        size = lax.rsqrt(jnp.mean(x * x, axis=-1, keepdims=True) + 1e-05)
        normed, inner = x * size, d * factor
        mean = jnp.mean(inner * normed, axis=-1, keepdims=True)
        tokens_grad[at, :] = d_tokens[at, :] + size * (inner - normed * mean)
        return total + jnp.sum(d * normed, axis=0, keepdims=True)

    total = lax.fori_loop(0, tokens.shape[0] // 16, body, jnp.zeros((1, width), F32))
    post, last = jnp.tanh(mod_rows[1:2, :]), jnp.tanh(mod_rows[3:4, :])
    vec[8:9, :] = total * gain_rows[0:1, :]
    vec[9:10, :] = row_sums[0:1, :] * gain_rows[1:2, :] * (1.0 - post * post)
    vec[10:11, :] = row_sums[1:2, :] * gain_rows[2:3, :]
    vec[11:12, :] = row_sums[2:3, :] * gain_rows[3:4, :] * (1.0 - last * last)
    vec[0:1, :] = total * (1.0 + mod_rows[0:1, :])
    vec[1:2, :] = row_sums[0:1, :] * post
    vec[2:3, :] = row_sums[1:2, :] * (1.0 + mod_rows[2:3, :])
    vec[3:4, :] = row_sums[2:3, :] * last
    piece, wide = width // 4, width // buckets
    slim = wide // seq
    for t in range(seq):
        for j in range(4):
            mod_give[t, j : j + 1, :] = vec[8 + t : 9 + t, j * piece : (j + 1) * piece]
    for t in range(buckets):
        wide_give[t, :, :wide] = vec[0:8, t * wide : (t + 1) * wide]
    mod_moves, wide_moves = [], []
    for j in range(1, seq):
        peer = lax.rem(s + j, seq)
        mod_moves.append(sums.go(copies.remote(mod_give.at[peer], mod_got.at[j], b, peer)))
    for j in range(1, buckets):
        peer = lax.rem(b + j, buckets)
        wide_moves.append(sums.go(copies.remote(wide_give.at[peer], wide_got.at[j], peer, s)))
    sums.stage_a(3)
    sums.stage_a(4)
    sums.stage_a(5)
    total = mod_give[s]
    for j, move in enumerate(mod_moves, 1):
        move.wait_recv()
        total = total + mod_got[j]
    mod_sum[...] = total
    mod_next, slim_next = [], []
    for j in range(1, buckets):
        peer = lax.rem(b + j, buckets)
        mod_next.append(sums.go(copies.remote(mod_sum, mod_all.at[b], peer, s)))
    mod_own = copies.local(mod_sum, mod_all.at[b])
    mod_own.start()
    total = wide_give[b]
    for j, move in enumerate(wide_moves, 1):
        move.wait_recv()
        total = total + wide_got[j]
    for t in range(seq):
        slim_give[t, :, :slim] = total[:, t * slim : (t + 1) * slim]
    for j in range(1, seq):
        peer = lax.rem(s + j, seq)
        slim_next.append(sums.go(copies.remote(slim_give.at[peer], slim_got.at[j], b, peer)))
    for w in (0, 3, 4, 5):
        sums.stage_b(w)
    sums.stage_c(0)
    for w in (3, 4, 5):
        sums.stage_c(w)
    sums.stage_d(0)
    total = slim_give[s]
    for j, move in enumerate(slim_next, 1):
        move.wait_recv()
        total = total + slim_got[j]
    small_out[...] = total
    for move in mod_next:
        move.wait_recv()
    mod_own.wait()
    sums.end()


def backward_all(buckets, seq, inputs, shapes, kinds):
    any_spec = pl.BlockSpec(memory_space=pl.ANY)
    vmem = pl.BlockSpec(memory_space=pltpu.VMEM)
    smem = pl.BlockSpec(memory_space=pltpu.SMEM)
    shapes, outs, scratch, n_sems = sums_shapes(buckets, seq, shapes, kinds, near=True)
    query, cap_key, tokens = inputs[5], inputs[8], inputs[21]
    rows, width = tokens.shape
    vec = (16, width)
    n_sems += 12 * seq + 4 * buckets
    results = pl.pallas_call(
        functools.partial(backward_kernel, buckets, seq, tuple(kinds)),
        out_shape=[
            jax.ShapeDtypeStruct((rows, width), F32),
            jax.ShapeDtypeStruct((buckets, 8, width // 4), F32),
            jax.ShapeDtypeStruct((8, 128), F32),
            *outs,
        ],
        in_specs=[vmem] * 16 + [smem] * 2 + [vmem] * (len(inputs) - 18),
        out_specs=[vmem, any_spec, vmem] + [vmem] * len(outs),
        scratch_shapes=[
            pltpu.VMEM(query.shape, BF16),
            pltpu.VMEM(query.shape, BF16),
            pltpu.VMEM(query.shape, F32),
            pltpu.VMEM(query.shape, F32),
            pltpu.VMEM(query.shape, F32),
            pltpu.VMEM(cap_key.shape, F32),
            pltpu.VMEM(cap_key.shape, F32),
            pltpu.VMEM(query.shape, BF16),
            pltpu.VMEM(query.shape, BF16),
            pltpu.VMEM(query.shape, BF16),
            pltpu.VMEM(cap_key.shape, BF16),
            pltpu.VMEM(cap_key.shape, BF16),
            pltpu.VMEM((rows, width), F32),
            pltpu.VMEM(vec, F32),
            pltpu.VMEM((seq, 8, width // 4), F32),
            pltpu.VMEM((seq, 8, width // 4), F32),
            pltpu.VMEM((8, width // 4), F32),
            pltpu.VMEM((buckets, 8, 256), F32),
            pltpu.VMEM((buckets, 8, 256), F32),
            pltpu.VMEM((seq, 8, 128), F32),
            pltpu.VMEM((seq, 8, 128), F32),
            pltpu.VMEM((query.shape[0], 128), F32),
            pltpu.VMEM((cap_key.shape[0], 128), F32),
            pltpu.VMEM((seq, rows, width), BF16),
            pltpu.VMEM((seq - 1, rows, width), BF16),
            pltpu.VMEM((seq - 1, rows, width), BF16),
            pltpu.SemaphoreType.DMA((n_sems,)),
            pltpu.SemaphoreType.DMA((n_sems,)),
            *[pltpu.VMEM(shape, BF16) for shape in shapes],
            *scratch,
        ],
        compiler_params=pltpu.CompilerParams(
            collective_id=10, has_side_effects=True, vmem_limit_bytes=62 * 2**20
        ),
    )(*inputs)
    sums = [out.reshape(-1, out.shape[-1]) for out in results[3:]]
    return results[0], results[1], results[2], sums


def last_kernel(buckets, seq, slim, *refs):
    cond, mod_all, small = refs[:3]
    count = (len(refs) - 7) // 2
    sources, refs = refs[3 : 3 + count], refs[3 + count :]
    mod_grad, gains, cross = refs[:3]
    targets, sems = refs[3 : 3 + count], refs[3 + count]
    copies = [
        pltpu.make_async_copy(a, b, sems.at[i])
        for i, (a, b) in enumerate(zip(sources, targets, strict=True))
    ]
    for copy in copies:
        copy.start()
    piece = mod_all.shape[2]
    for j in range(4):
        total = None
        for k in range(buckets):
            term = cond[:, k : k + 1] * mod_all[k, j : j + 1, :]
            total = term if total is None else total + term
        mod_grad[:, j * piece : (j + 1) * piece] = total
    gains[...] = small[0:7, :slim]
    cross[...] = small[7:8, :slim]
    for copy in copies:
        copy.wait()


def last_all(buckets, seq, slim, cond, mod_all, small, results):
    any_spec = pl.BlockSpec(memory_space=pl.ANY)
    vmem = pl.BlockSpec(memory_space=pltpu.VMEM)
    outs = pl.pallas_call(
        functools.partial(last_kernel, buckets, seq, slim),
        out_shape=[
            jax.ShapeDtypeStruct((cond.shape[0], 4 * mod_all.shape[2]), F32),
            jax.ShapeDtypeStruct((7, slim), F32),
            jax.ShapeDtypeStruct((1, slim), F32),
            *[jax.ShapeDtypeStruct(x.shape, x.dtype) for x in results],
        ],
        in_specs=[vmem] * 3 + [any_spec] * len(results),
        out_specs=[vmem] * (3 + len(results)),
        scratch_shapes=[pltpu.SemaphoreType.DMA((len(results),))],
        compiler_params=pltpu.CompilerParams(vmem_limit_bytes=62 * 2**20),
    )(cond, mod_all, small, *results)
    return outs[0], outs[1], outs[2].reshape(slim), outs[3:]


def on_device(
    tokens,
    captions,
    cotangent,
    counts,
    cap_lens,
    steps_t,
    w_query,
    w_key,
    w_value,
    w_out,
    w_cap_key,
    w_cap_value,
    w_gate,
    w_up,
    w_down,
    w_mod,
    gains,
    cross_gate,
):
    buckets, seq = lax.axis_size("bucket"), lax.axis_size("seq")
    b, s = lax.axis_index("bucket"), lax.axis_index("seq")
    place = b * seq + s
    rows, width = tokens.shape
    span = rows * seq
    share = width // seq

    cond_size = w_mod.shape[0] * buckets * seq
    cond = jax.nn.silu(time_embed(steps_t, cond_size)).astype(BF16)
    cond_part = lax.dynamic_slice_in_dim(cond, place * w_mod.shape[0], w_mod.shape[0], 1)
    slim = gains.shape[1]
    small = jnp.concatenate([gains, cross_gate[None]], axis=0).astype(F32)
    small = jnp.pad(small, ((0, 0), (0, 128 - slim)))
    cap_all, weights, inner = forward_all(
        buckets,
        seq,
        tokens,
        captions,
        small,
        slim,
        cond_part,
        w_mod,
        [counts, cap_lens],
        [w_query, w_key, w_value, w_cap_key, w_cap_value, w_out, w_gate, w_up, w_down],
        ["col", "col", "col", "col", "col", "row", "col", "col", "row"],
    )
    wq, wk, wv, wck, wcv, wo, wg, wu, wd = weights
    caps = cap_all.reshape(-1, captions.shape[1])
    small_rows, mod, hidden, query_proj, key_proj, cap_proj = inner[:6]
    query, key, value, cap_key, cap_value = inner[6:11]
    cross_out, mixed_low = inner[11:]
    (block_out, d_tokens, d_attn_all, row_sums), (s_gate, s_up, s_down) = middle_all(
        buckets,
        seq,
        mixed_low,
        (wo, wg, wu, wd),
        tokens,
        cotangent,
        counts,
        small_rows,
        mod,
    )
    tokens_grad, mod_all, small_sums, sums = backward_all(
        buckets,
        seq,
        [
            d_attn_all.reshape(span, width),
            wq,
            wk,
            wv,
            wo,
            query,
            key,
            value,
            cap_key,
            cap_value,
            cross_out,
            query_proj,
            key_proj,
            cap_proj,
            small_rows,
            mod,
            counts,
            cap_lens,
            mixed_low,
            hidden,
            caps,
            tokens,
            d_tokens,
            row_sums,
        ],
        [x.shape for x in (wo, wck, wcv, wq, wk, wv)],
        ["row", "col", "col", "col", "col", "col"],
    )
    s_out, s_cap_key, s_cap_value, s_query, s_key, s_value = sums

    cond_size = cond.shape[1] // buckets
    cond_cols = lax.dynamic_slice_in_dim(cond, b * cond_size, cond_size, 1).astype(F32).T
    results = [block_out, tokens_grad, s_query, s_key, s_value, s_out]
    results += [s_cap_key, s_cap_value, s_gate, s_up, s_down]
    s_mod, s_gains, s_cross, results = last_all(
        buckets, seq, slim, cond_cols, mod_all, small_sums, results
    )
    return (*results, s_mod, s_gains, s_cross)


def solution(mesh):
    spread = P(("bucket", "seq"), None)
    in_specs = (
        *([spread] * 3),
        *([P()] * 3),
        *([spread] * 10),
        P(None, ("bucket", "seq")),
        P(("bucket", "seq")),
    )
    out_specs = (
        spread,
        spread,
        *([P("bucket", "seq")] * 10),
        P(None, ("bucket", "seq")),
        P(("bucket", "seq")),
    )
    buckets, seq = mesh.shape["bucket"], mesh.shape["seq"]

    def step(*args):
        tokens, weight = args[0], args[6]
        tiled = weight.shape[0] % 16 == 0 and weight.shape[1] // seq % 128 == 0
        fits = buckets == 8 and seq == 4 and tokens.shape[0] % 64 == 0
        return (on_device if tiled and fits else on_device_general)(*args)

    return jax.shard_map(
        step, mesh=mesh, in_specs=in_specs, out_specs=out_specs, check_vma=False
    )
```

```python
import functools
import math

import jax
import jax.numpy as jnp
from jax import lax
from jax.experimental import pallas as pl
from jax.experimental.pallas import tpu as pltpu
from jax.sharding import PartitionSpec as P

HEAD_DIM = 64
MESH = pl.DeviceIdType.MESH
F32, BF16 = jnp.float32, jnp.bfloat16
CHUNKS, CUTS, FLIGHT = 2, 2, 2


def rms_rows(values):
    return values * lax.rsqrt(jnp.mean(values * values, axis=-1, keepdims=True) + 1e-05)


def head_rms(values):
    shaped = values.reshape(values.shape[:-1] + (values.shape[-1] // HEAD_DIM, HEAD_DIM))
    shaped = shaped * lax.rsqrt(jnp.mean(shaped * shaped, axis=-1, keepdims=True) + 1e-06)
    return shaped.reshape(values.shape)


def time_embed(steps, width):
    half_width = width // 2
    freqs = jnp.exp(-math.log(10000.0) * jnp.arange(half_width, dtype=F32) / half_width)
    angles = steps.astype(F32)[:, None] * freqs
    return jnp.concatenate([jnp.cos(angles), jnp.sin(angles)], axis=1)


def pick_entry(table, index):
    return jnp.sum(jnp.where(jnp.arange(table.shape[0]) == index, table, 0))


def bf_dot(left, right):
    return jnp.dot(left, right, preferred_element_type=F32)


def left_dot(rows_left, rows_right):
    return lax.dot_general(
        rows_left, rows_right, (((0,), (0,)), ((), ())), preferred_element_type=F32
    )


def right_dot(left, right):
    return lax.dot_general(left, right, (((1,), (1,)), ((), ())), preferred_element_type=F32)


def pre_attn(tokens_in, gain_pre, scale_attn):
    return rms_rows(tokens_in) * gain_pre * (1.0 + scale_attn)


def qk_norm(query_in, key_in, gain_query, gain_key):
    return (head_rms(query_in) * gain_query, head_rms(key_in) * gain_key)


def cap_norm(key_in, gain_cap):
    return head_rms(key_in) * gain_cap


def middle(tokens_in, attn_out, gain_post, gate_attn, gain_ffn, scale_ffn):
    resid_one = tokens_in + jnp.tanh(gate_attn) * rms_rows(attn_out) * gain_post
    return (resid_one, rms_rows(resid_one) * gain_ffn * (1.0 + scale_ffn))


def activate(gate_proj, up_proj):
    return jax.nn.silu(gate_proj) * up_proj


def finish(resid_one, ffn_out, gain_last, gate_ffn):
    return resid_one + jnp.tanh(gate_ffn) * rms_rows(ffn_out) * gain_last


def flip(index, bit):
    return index + bit - 2 * bit * lax.rem(lax.div(index, bit), 2)


def slot(index, buckets):
    if buckets != 8:
        return index
    high, low = lax.div(index, 4), lax.rem(index, 4)
    return 4 * high + 2 * lax.rem(low, 2) + lax.div(low, 2)


class Copies:
    def __init__(self, send, recv):
        self.send, self.recv, self.used = send, recv, 0

    def take(self, count=1):
        first = self.used
        self.used += count
        assert self.used <= self.send.shape[0], self.used
        return first

    def remote(self, src, dst, b, s, at=None):
        at = self.take() if at is None else at
        return pltpu.make_async_remote_copy(
            src_ref=src,
            dst_ref=dst,
            send_sem=self.send.at[at],
            recv_sem=self.recv.at[at],
            device_id={"bucket": b, "seq": s},
            device_id_type=MESH,
        )

    def local(self, src, dst):
        return pltpu.make_async_copy(src, dst, self.send.at[self.take()])


def greet(b, s):
    pl.semaphore_signal(
        pltpu.get_barrier_semaphore(),
        inc=1,
        device_id={"bucket": b, "seq": s},
        device_id_type=MESH,
    )


class Relay:
    def __init__(self, copies, own, out, b, s, seq, part=None):
        self.copies, self.own, self.out, self.b, self.s, self.seq = copies, own, out, b, s, seq
        self.part = part
        self.base = {1: copies.take(seq - 1), -1: copies.take(seq - 1)}
        self.up = jnp.where(s < seq - 1, s + 1, s - 1)
        self.down = jnp.where(s > 0, s - 1, s + 1)
        self.kept = None if own is None else copies.local(own, out.at[s])

    def packet(self, way, j):
        at = self.s - way * j
        block = self.out.at[at] if self.part is None else self.out.at[at, self.part]
        return self.copies.remote(
            self.own if j == 0 and self.own is not None else block,
            block,
            self.b,
            self.up if way > 0 else self.down,
            self.base[way] + j,
        )

    def sends(self, way):
        return self.s < self.seq - 1 if way > 0 else self.s > 0

    def has(self, way, j):
        return self.s >= j if way > 0 else self.s + j <= self.seq - 1

    def start(self, j):
        if j == 0 and self.kept is not None:
            self.kept.start()
        for way in (1, -1):
            if j == self.seq - 1:

                @pl.when(jnp.logical_not(self.sends(way)))
                def _():
                    for k in range(self.seq - 1):
                        self.packet(way, k).wait_recv()

                continue

            @pl.when(jnp.logical_and(self.sends(way), self.has(way, j)))
            def _():
                if j > 0:
                    self.packet(way, j - 1).wait_recv()
                self.packet(way, j).start()

    def sent(self, j):
        for way in (1, -1):

            @pl.when(jnp.logical_and(self.sends(way), self.has(way, j)))
            def _():
                self.packet(way, j).wait_send()

        if j == 0 and self.kept is not None:
            self.kept.wait()


def greet_line(b, s, seq):
    @pl.when(s > 0)
    def _():
        greet(b, s - 1)

    @pl.when(s < seq - 1)
    def _():
        greet(b, s + 1)

    peers = jnp.where(s > 0, 1, 0) + jnp.where(s < seq - 1, 1, 0)
    pl.semaphore_wait(pltpu.get_barrier_semaphore(), peers)


def halves_of(shape):
    if len(shape) == 3:
        return shape[0] // 2
    return (shape[0] // 32) * 16 if shape[0] >= 32 else shape[0] // 2


def gather_kernel(buckets, seq, kinds, *refs):
    count = len(kinds)
    tokens, captions, small, cond, w_mod = refs[:5]
    shards = refs[5 : 5 + count]
    tok_all, cap_all, small_all, mod_out = refs[5 + count : 9 + count]
    fulls = refs[9 + count : 9 + 2 * count]
    part, got_bucket, got_seq, mod_sum, send, recv = refs[9 + 2 * count :]
    b, s = lax.axis_index("bucket"), lax.axis_index("seq")
    copies = Copies(send, recv)
    chips = buckets // 2
    place = b * seq + s
    to_b, to_s = lax.rem(place, buckets), lax.div(place, buckets)
    back = s * buckets + b
    from_b, from_s = lax.div(back, seq), lax.rem(back, seq)
    stays = jnp.logical_and(to_b == b, to_s == s)

    lanes = part.shape[2]
    for j in range(part.shape[1]):
        part[:, j, :] = bf_dot(cond[...], w_mod[:, j * lanes : (j + 1) * lanes])

    for k in range(1, buckets):
        greet(lax.rem(b + k, buckets), s)
    for k in range(1, seq):
        greet(b, lax.rem(s + k, seq))

    @pl.when(jnp.logical_not(stays))
    def _():
        greet(from_b, from_s)

    peers = buckets - 1 + seq - 1 + jnp.where(stays, 0, 1)
    pl.semaphore_wait(pltpu.get_barrier_semaphore(), peers)

    sent = []

    def go(copy):
        copy.start()
        sent.append(copy)
        return copy

    mod_moves = []
    for k in range(1, buckets):
        peer = lax.rem(b + k, buckets)
        mod_moves.append(go(copies.remote(part.at[peer], got_bucket.at[k], peer, s)))
    small_moves = []
    for k in range(1, seq):
        peer = lax.rem(s + k, seq)
        small_moves.append(go(copies.remote(small, small_all.at[b, s], b, peer)))
    small_own = copies.local(small, small_all.at[b, s])
    small_own.start()

    tok = Relay(copies, tokens, tok_all, b, s, seq)
    cap = Relay(copies, captions, cap_all, b, s, seq)
    queue = [(tok, j) for j in range(seq)] + [(cap, j) for j in range(seq)]
    ahead = [(None, at) for at in range(count)]
    items = []
    while queue or ahead:
        items += queue[:1] + ahead[:1]
        queue, ahead = queue[1:], ahead[1:]

    first = [None] * count

    def depart(at):
        kind, shard, full = kinds[at], shards[at], fulls[at]
        if kind == "row":
            move = copies.remote(shard, full.at[to_b], to_b, to_s)
            keep = copies.local(shard, full.at[b])

            @pl.when(jnp.logical_not(stays))
            def _():
                move.start()

            @pl.when(stays)
            def _():
                keep.start()

            first[at] = (move, keep)
            return
        wide = full.shape[-1]

        def columns(peer):
            if kind == "cut":
                return shard.at[peer]
            return shard.at[:, pl.ds(pl.multiple_of(peer * wide, 128), wide)]

        moves = []
        for k in range(1, seq):
            peer = lax.rem(s + k, seq)
            move = copies.remote(columns(peer), full.at[b, s], b, peer)
            move.start()
            moves.append(move)
        keep = copies.local(columns(s), full.at[b, s])
        keep.start()
        first[at] = (moves, keep)

    def arrived(at):
        moves, keep = first[at]
        if kinds[at] == "row":

            @pl.when(jnp.logical_not(stays))
            def _():
                moves.wait()

            @pl.when(stays)
            def _():
                keep.wait()

            return
        for move in moves:
            move.wait()
        keep.wait()

    twin = flip(b, 1)
    second = [None] * count
    if chips == 4:
        near_x, near_y = flip(b, 2), flip(b, 4)
        far = flip(near_x, 4)

        def stage_a(at):
            full = fulls[at]
            second[at] = {
                "x": go(copies.remote(full.at[b], full.at[b], near_x, s)),
                "y": go(copies.remote(full.at[b], full.at[b], near_y, s)),
                "twin": [go(copies.remote(full.at[b], full.at[b], twin, s))],
            }

        def stage_b(at):
            full, now = fulls[at], second[at]
            cut = halves_of(full.shape[1:])
            now["x"].wait_recv()
            block = full.at[near_x, pl.ds(0, cut)]
            now["dy"] = go(copies.remote(block, block, near_y, s))
            block = full.at[near_x]
            now["twin"].append(go(copies.remote(block, block, twin, s)))
            now["y"].wait_recv()
            block = full.at[near_y, pl.ds(cut, full.shape[1] - cut)]
            now["dx"] = go(copies.remote(block, block, near_x, s))
            block = full.at[near_y]
            now["twin"].append(go(copies.remote(block, block, twin, s)))

        def stage_c(at):
            full, now = fulls[at], second[at]
            now["dy"].wait_recv()
            now["dx"].wait_recv()
            block = full.at[far]
            now["twin"].append(go(copies.remote(block, block, twin, s)))

    else:

        def stage_a(at):
            full = fulls[at]
            second[at] = {"far": [], "twin": []}
            for k in range(1, chips):
                peer = lax.rem(b + 2 * k, buckets)
                second[at]["far"].append(go(copies.remote(full.at[b], full.at[b], peer, s)))
            second[at]["twin"].append(go(copies.remote(full.at[b], full.at[b], twin, s)))

        def stage_b(at):
            full = fulls[at]
            for k, copy in enumerate(second[at]["far"], 1):
                copy.wait_recv()
                block = full.at[lax.rem(b + buckets - 2 * k, buckets)]
                second[at]["twin"].append(go(copies.remote(block, block, twin, s)))

        def stage_c(at):
            pass

    def begin(i):
        relay, j = items[i]
        if relay is None:
            depart(j)
        else:
            relay.start(j)

    begin(0)
    begin(1)
    for move in small_moves:
        move.wait_recv()
    small_own.wait()
    small_next = []
    for k in range(1, buckets):
        peer = lax.rem(b + k, buckets)
        small_next.append(go(copies.remote(small_all.at[b], small_all.at[b], peer, s)))
    total = part[b]
    for k, move in enumerate(mod_moves, 1):
        move.wait_recv()
        total = total + got_bucket[k]
    mod_sum[...] = total
    mod_next = []
    for k in range(1, seq):
        peer = lax.rem(s + k, seq)
        mod_next.append(go(copies.remote(mod_sum, got_seq.at[k], b, peer)))

    for i, (relay, j) in enumerate(items):
        if relay is None:
            arrived(j)
        elif j <= seq - 2:
            relay.sent(j)
        if i + 2 < len(items):
            begin(i + 2)
        if relay is None:
            stage_a(j)
            if j >= 1:
                stage_b(j - 1)
            if j >= 2:
                stage_c(j - 2)
    stage_b(count - 1)
    if count >= 2:
        stage_c(count - 2)
    stage_c(count - 1)

    total = mod_sum[...]
    for k, move in enumerate(mod_next, 1):
        move.wait_recv()
        total = total + got_seq[k]
    mod_out[...] = total
    for move in small_next:
        move.wait_recv()
    for now in second:
        for move in now["twin"]:
            move.wait_recv()
    for move in sent:
        move.wait_send()


def gather_all(buckets, seq, tokens, captions, small, cond, w_mod, shards, kinds):
    any_spec = pl.BlockSpec(memory_space=pl.ANY)
    vmem = pl.BlockSpec(memory_space=pltpu.VMEM)
    fulls, inputs, names = [], [], []
    for shard, kind in zip(shards, kinds, strict=True):
        rows, wide = shard.shape
        if kind == "row":
            fulls.append(jax.ShapeDtypeStruct((buckets, rows, wide), BF16))
        else:
            part = wide // seq
            fulls.append(jax.ShapeDtypeStruct((buckets, seq, rows, part), BF16))
            if part % 128:
                kind = "cut"
                shard = shard.reshape(rows, seq, part).transpose(1, 0, 2)
        inputs.append(shard)
        names.append(kind)
    mod_lanes = w_mod.shape[1] // 8
    n_sems = 64 + 16 * buckets + len(shards) * (seq + 2 * buckets)
    outs = pl.pallas_call(
        functools.partial(gather_kernel, buckets, seq, tuple(names)),
        out_shape=[
            jax.ShapeDtypeStruct((seq,) + tokens.shape, BF16),
            jax.ShapeDtypeStruct((seq,) + captions.shape, BF16),
            jax.ShapeDtypeStruct((buckets, seq) + small.shape, F32),
            jax.ShapeDtypeStruct((8, mod_lanes), F32),
            *fulls,
        ],
        in_specs=[any_spec, any_spec, any_spec, vmem, vmem] + [any_spec] * len(shards),
        out_specs=[any_spec, any_spec, any_spec, vmem] + [any_spec] * len(shards),
        scratch_shapes=[
            pltpu.VMEM((buckets, 8, mod_lanes), F32),
            pltpu.VMEM((buckets, 8, mod_lanes), F32),
            pltpu.VMEM((seq, 8, mod_lanes), F32),
            pltpu.VMEM((8, mod_lanes), F32),
            pltpu.SemaphoreType.DMA((n_sems,)),
            pltpu.SemaphoreType.DMA((n_sems,)),
        ],
        compiler_params=pltpu.CompilerParams(
            collective_id=0, has_side_effects=True, vmem_limit_bytes=24 * 2**20
        ),
    )(tokens, captions, small, cond, w_mod, *inputs)
    weights = []
    for full, kind in zip(outs[4:], names, strict=True):
        weights.append(full.reshape(-1, full.shape[-1]))
    return outs[0], outs[1], outs[2], outs[3], weights


def line_gather_kernel(seq, own, out, send, recv):
    b, s = lax.axis_index("bucket"), lax.axis_index("seq")
    greet_line(b, s, seq)
    relay = Relay(Copies(send, recv), own, out, b, s, seq)
    for j in range(seq):
        relay.start(j)
    for j in range(seq - 1):
        relay.sent(j)


def line_gather(seq, own, collective_id):
    return pl.pallas_call(
        functools.partial(line_gather_kernel, seq),
        out_shape=jax.ShapeDtypeStruct((seq,) + own.shape, own.dtype),
        in_specs=[pl.BlockSpec(memory_space=pl.ANY)],
        out_specs=pl.BlockSpec(memory_space=pl.ANY),
        scratch_shapes=[pltpu.SemaphoreType.DMA((2 * seq + 2,))] * 2,
        compiler_params=pltpu.CompilerParams(collective_id=collective_id, has_side_effects=True),
    )(own).reshape(-1, own.shape[-1])


def add_rows(out, terms):
    rows = out.shape[0]
    step = 16 if rows % 16 == 0 else rows

    def body(i, carry):
        at = pl.ds(pl.multiple_of(i * step, step), step)
        total = terms[0][at, :].astype(F32)
        for term in terms[1:]:
            total = total + term[at, :].astype(F32)
        out[at, :] = total.astype(out.dtype)
        return carry

    lax.fori_loop(0, rows // step, body, 0)


class Pour:
    def __init__(self, copies, parts, from_left, from_right, b, s, seq):
        self.copies, self.parts, self.b, self.s, self.seq = copies, parts, b, s, seq
        self.got = {1: from_left, -1: from_right}
        rows = parts.shape[1]
        self.cuts = CUTS if rows % (16 * CUTS) == 0 else 1
        self.thin = rows // self.cuts
        self.count = (seq - 1) * self.cuts
        self.base = {1: copies.take(self.count), -1: copies.take(self.count)}
        self.next = {
            1: jnp.where(s < seq - 1, s + 1, s - 1),
            -1: jnp.where(s > 0, s - 1, s + 1),
        }

    def block(self, way, q):
        j, at = q // self.cuts, pl.ds(q % self.cuts * self.thin, self.thin)
        return self.parts.at[self.seq - 1 - j if way > 0 else j, at], self.got[way].at[j, at]

    def packet(self, way, q):
        src, dst = self.block(way, q)
        return self.copies.remote(src, dst, self.b, self.next[way], self.base[way] + q)

    def on(self, way, q):
        j = q // self.cuts
        return self.s < self.seq - 1 - j if way > 0 else self.s > j

    def behind(self, way):
        return self.s > 0 if way > 0 else self.s < self.seq - 1

    def one(self, way, q):
        src, dst = self.block(way, q)

        @pl.when(jnp.logical_and(self.behind(way), self.on(way, q)))
        def _():
            self.packet(way, q).wait_recv()
            add_rows(src, [src, dst])

        @pl.when(self.on(way, q))
        def _():
            if q >= FLIGHT:
                self.packet(way, q - FLIGHT).wait_send()
            self.packet(way, q).start()

    def step(self, q):
        @pl.when(self.s < self.seq // 2)
        def _():
            self.one(1, q)
            self.one(-1, q)

        @pl.when(self.s >= self.seq // 2)
        def _():
            self.one(-1, q)
            self.one(1, q)

    def end(self, out):
        seq, cuts = self.seq, self.cuts
        for t in range(seq):

            @pl.when(self.s == t)
            def _():
                terms = [self.parts.at[t]]
                for way, j in ((1, seq - 1 - t), (-1, t)):
                    if j < seq - 1:
                        for c in range(cuts):
                            self.packet(way, j * cuts + c).wait_recv()
                        terms.append(self.got[way].at[j])
                add_rows(out, terms)

        for q in range(self.count):
            more = q + FLIGHT < self.count
            for way in (1, -1):
                last = jnp.logical_not(self.on(way, q + FLIGHT)) if more else True

                @pl.when(jnp.logical_and(self.on(way, q), last))
                def _():
                    self.packet(way, q).wait_send()


def line_scatter_kernel(seq, parts, out, from_left, from_right, send, recv):
    b, s = lax.axis_index("bucket"), lax.axis_index("seq")
    greet_line(b, s, seq)
    pour = Pour(Copies(send, recv), parts, from_left, from_right, b, s, seq)
    for q in range(pour.count):
        pour.step(q)
    pour.end(out)


def line_scatter(seq, parts, collective_id):
    rows, wide = parts.shape[0] // seq, parts.shape[1]
    vmem = pl.BlockSpec(memory_space=pltpu.VMEM)
    return pl.pallas_call(
        functools.partial(line_scatter_kernel, seq),
        out_shape=jax.ShapeDtypeStruct((rows, wide), F32),
        in_specs=[vmem],
        out_specs=vmem,
        input_output_aliases={},
        scratch_shapes=[
            pltpu.VMEM((seq - 1, rows, wide), BF16),
            pltpu.VMEM((seq - 1, rows, wide), BF16),
            pltpu.SemaphoreType.DMA((4 * seq,)),
            pltpu.SemaphoreType.DMA((4 * seq,)),
        ],
        compiler_params=pltpu.CompilerParams(
            collective_id=collective_id, has_side_effects=True, vmem_limit_bytes=24 * 2**20
        ),
    )(parts.astype(BF16).reshape(seq, rows, wide))


class GradSums:
    def __init__(self, copies, b, s, buckets, seq, kinds, grads, outs, scratch, near=False):
        self.near = near
        self.copies, self.b, self.s, self.buckets, self.seq = copies, b, s, buckets, seq
        self.kinds, self.grads, self.outs = kinds, grads, outs
        self.scratch = [scratch[8 * w : 8 * w + 8] for w in range(len(kinds))]
        self.chips = buckets // 2
        self.chip, self.core = lax.div(b, 2), lax.rem(b, 2)
        self.place = s * buckets + slot(b, buckets)
        self.to_b = lax.div(self.place, seq)
        self.twin = flip(b, 1)
        self.begun, self.state, self.last = {}, {}, {}
        self.sent = []

    def go(self, copy):
        copy.start()
        self.sent.append(copy)
        return copy

    def own(self, w, chip, rows=None):
        where = (chip,) if rows is None else (chip, rows)
        if self.near:
            return self.grads[w].at[(chip, self.core, *where[1:])]
        return self.scratch[w][0].at[where]

    def begin(self, w):
        own, other = self.scratch[w][:2]
        grad = self.grads[w]
        swap = self.copies.remote(grad.at[:, 1 - self.core], other, self.twin, self.s)
        swap.start()
        self.begun[w] = [swap]
        if not self.near:
            keep = self.copies.local(grad.at[:, self.core], own)
            keep.start()
            self.begun[w].append(keep)

    def stage_a(self, w):
        _, other, half_x, half_y, got, _ = self.scratch[w][:6]
        for copy in self.begun[w]:
            copy.wait()
        if not self.near and w + 2 in range(len(self.kinds)) and w + 2 not in self.begun:
            self.begin(w + 2)
        rows = other.shape[1]
        if self.chips != 4:
            moves = []
            for k in range(1, self.chips):
                to = lax.rem(self.chip + k, self.chips)
                own = self.own(w, to)
                add_rows(own, [own, other.at[to]])
                move = self.copies.remote(own, got.at[k], 2 * to + self.core, self.s)
                moves.append(self.go(move))
            self.state[w] = moves
            return
        far = flip(flip(self.chip, 1), 2)
        add_rows(self.own(w, far), [self.own(w, far), other.at[far]])
        cut = halves_of(other.shape[1:])
        near_x, near_y = flip(self.b, 2), flip(self.b, 4)
        top, low = self.own(w, far, pl.ds(0, cut)), self.own(w, far, pl.ds(cut, rows - cut))
        self.state[w] = [
            self.go(self.copies.remote(top, half_x, near_x, self.s)),
            self.go(self.copies.remote(low, half_y, near_y, self.s)),
        ]

    def stage_b(self, w):
        if self.chips != 4:
            return
        _, other, half_x, half_y, got_x, got_y = self.scratch[w][:6]
        rows = other.shape[1]
        cut = halves_of(other.shape[1:])
        top, low = pl.ds(0, cut), pl.ds(cut, rows - cut)
        mx, my = flip(self.chip, 1), flip(self.chip, 2)
        move_x, move_y = self.state[w]
        move_x.wait_recv()
        block = self.own(w, my, top)
        add_rows(block, [block, other.at[my, top], half_x])
        block = self.own(w, my, low)
        add_rows(block, [block, other.at[my, low]])
        block = self.own(w, my)
        next_y = self.go(self.copies.remote(block, got_y, flip(self.b, 4), self.s))
        move_y.wait_recv()
        block = self.own(w, mx, low)
        add_rows(block, [block, other.at[mx, low], half_y])
        block = self.own(w, mx, top)
        add_rows(block, [block, other.at[mx, top]])
        block = self.own(w, mx)
        next_x = self.go(self.copies.remote(block, got_x, flip(self.b, 2), self.s))
        self.state[w] = [next_x, next_y]

    def stage_c(self, w):
        _, other, _, _, got_x, got_y, done, landed = self.scratch[w]
        for move in self.state[w]:
            move.wait_recv()
        terms = [self.own(w, self.chip), other.at[self.chip]]
        if self.chips == 4:
            terms += [got_x, got_y]
        else:
            terms += [got_x.at[k] for k in range(1, self.chips)]
        if self.kinds[w] == "col":
            add_rows(self.outs[w], terms)
            return
        seq, send, recv = self.seq, self.copies.send, self.copies.recv
        wide = done.shape[-1]
        far = self.kinds[w] == "row"
        to_b, me = (self.to_b, lax.rem(self.place, seq)) if far else (self.b, self.s)
        base = self.copies.take(2 * seq)
        rows = terms[0].shape[0]
        step = 16 if rows % 16 == 0 else rows

        def body(i, carry):
            at = pl.ds(pl.multiple_of(i * step, step), step)
            total = terms[0][at, :].astype(F32)
            for term in terms[1:]:
                total = total + term[at, :].astype(F32)
            for t in range(seq):
                done[t, at, :] = total[:, t * wide : (t + 1) * wide].astype(BF16)
            return carry

        lax.fori_loop(0, rows // step, body, 0)
        moves = []
        for t in range(seq):
            move = pltpu.make_async_remote_copy(
                src_ref=done.at[t],
                dst_ref=landed.at[me],
                send_sem=send.at[base + t],
                recv_sem=recv.at[base + me],
                device_id={"bucket": to_b, "seq": t},
                device_id_type=MESH,
            )
            keep = pltpu.make_async_copy(done.at[t], landed.at[me], send.at[base + seq + t])
            here = jnp.logical_and(to_b == self.b, self.s == t) if far else self.s == t

            @pl.when(jnp.logical_not(here))
            def _():
                move.start()

            @pl.when(here)
            def _():
                keep.start()

            moves.append((move, keep, here))
        self.last[w] = (base, moves)

    def stage_d(self, w):
        if self.kinds[w] == "col":
            return
        done, landed = self.scratch[w][6:]
        base, moves = self.last[w]
        out, seq, buckets = self.outs[w], self.seq, self.buckets
        for j in range(seq):
            d = self.b * seq + j
            from_b = slot(lax.rem(d, buckets), buckets)
            here = jnp.logical_and(from_b == self.b, lax.div(d, buckets) == self.s)
            if self.kinds[w] != "row":
                here = self.s == j

            @pl.when(jnp.logical_not(here))
            def _():
                pltpu.make_async_remote_copy(
                    src_ref=done.at[j],
                    dst_ref=landed.at[j],
                    send_sem=self.copies.send.at[base + j],
                    recv_sem=self.copies.recv.at[base + j],
                    device_id={"bucket": self.twin, "seq": self.s},
                    device_id_type=MESH,
                ).wait_recv()

        for move, keep, here in moves:

            @pl.when(jnp.logical_not(here))
            def _():
                move.wait_send()

            @pl.when(here)
            def _():
                keep.wait()

        for j in range(seq):
            if self.kinds[w] != "strip":
                add_rows(out.at[j], [landed.at[j]])
                continue
            for part in range(landed.shape[-1] // 128):
                cols = slice((part * seq + j) * 128, (part * seq + j + 1) * 128)
                out[:, cols] = landed[j, :, part * 128 : (part + 1) * 128].astype(F32)

    def steps(self):
        count = len(self.kinds)
        for w in range(count + 2):
            if w < count:
                yield lambda w=w: self.stage_a(w)
            if 1 <= w <= count:
                yield lambda w=w: self.stage_b(w - 1)
            if w >= 2:
                yield lambda w=w: self.stage_c(w - 2)
        yield lambda: [self.stage_d(w) for w in range(count)]

    def end(self):
        for move in self.sent:
            move.wait_send()


def greet_all(b, s, buckets, seq):
    for k in range(1, buckets):
        greet(lax.rem(b + k, buckets), s)
    for k in range(1, seq):
        greet(b, lax.rem(s + k, seq))
    for j in range(seq):
        d = b * seq + j
        src_b, src_s = slot(lax.rem(d, buckets), buckets), lax.div(d, buckets)

        @pl.when(jnp.logical_not(jnp.logical_and(src_b == b, src_s == s)))
        def _():
            greet(src_b, src_s)

    to_b = lax.div(s * buckets + slot(b, buckets), seq)
    return buckets - 1 + seq - 1 + seq - jnp.where(to_b == b, 1, 0)


def sums_shapes(buckets, seq, shapes, kinds, near=False):
    chips = buckets // 2
    inputs, outs, scratch = [], [], []
    tiny = pltpu.VMEM((16, 128), BF16)
    for (rows, wide), kind in zip(shapes, kinds, strict=True):
        rows = rows // buckets
        inputs.append((chips, 2, rows, wide))
        cut = halves_of((rows, wide))
        scratch += [tiny if near else pltpu.VMEM((chips, rows, wide), BF16)]
        scratch += [pltpu.VMEM((chips, rows, wide), BF16)]
        if chips == 4:
            scratch += [pltpu.VMEM((cut, wide), BF16), pltpu.VMEM((rows - cut, wide), BF16)]
            scratch += [pltpu.VMEM((rows, wide), BF16)] * 2
        else:
            scratch += [tiny, tiny, pltpu.VMEM((chips, rows, wide), BF16), tiny]
        split = (seq, rows, wide // seq)
        outs.append(jax.ShapeDtypeStruct(split if kind in ("row", "stay") else (rows, wide), F32))
        scratch += [tiny if kind == "col" else pltpu.VMEM(split, BF16)] * 2
    n_sems = 32 + 2 * buckets + len(shapes) * (8 + 3 * seq + buckets)
    return inputs, outs, scratch, n_sems


def place_grads(buckets, grads, kinds, shapes):
    inputs = []
    for grad, kind, shape in zip(grads, kinds, shapes, strict=True):
        grad = grad.astype(BF16)
        if kind == "row" and buckets == 8:
            grad = grad.reshape((2, 2, 2) + shape[2:]).transpose(0, 2, 1, 3, 4)
        inputs.append(grad.reshape(shape))
    return inputs


def spread(buckets):
    if buckets != 8:
        return tuple(range(buckets))
    return tuple(4 * (p // 4) + 2 * (p % 2) + p // 2 % 2 for p in range(buckets))


def scatter_kernel(buckets, seq, kinds, *refs):
    count = len(kinds)
    vec, grads = refs[0], refs[1 : 1 + count]
    vec_all, outs = refs[1 + count], refs[2 + count : 2 + 2 * count]
    at = 2 + 2 * count
    vec_seq, vec_sum, send, recv = refs[at : at + 4]
    b, s = lax.axis_index("bucket"), lax.axis_index("seq")
    copies = Copies(send, recv)
    sums = GradSums(copies, b, s, buckets, seq, kinds, grads, outs, refs[at + 4 :])
    peers = greet_all(b, s, buckets, seq)
    pl.semaphore_wait(pltpu.get_barrier_semaphore(), peers)
    vec_moves = []
    for k in range(1, seq):
        vec_moves.append(sums.go(copies.remote(vec, vec_seq.at[k], b, lax.rem(s + k, seq))))
    for w in range(min(2, count)):
        sums.begin(w)
    for move in vec_moves:
        move.wait_recv()
    add_rows(vec_sum, [vec] + [vec_seq.at[k] for k in range(1, seq)])
    vec_next = []
    for k in range(1, buckets):
        peer = lax.rem(b + k, buckets)
        vec_next.append(sums.go(copies.remote(vec_sum, vec_all.at[b], peer, s)))
    vec_own = copies.local(vec_sum, vec_all.at[b])
    vec_own.start()
    for step in sums.steps():
        step()
    for move in vec_next:
        move.wait_recv()
    vec_own.wait()
    sums.end()


def scatter_all(buckets, seq, vec, grads, kinds, collective_id=1):
    any_spec = pl.BlockSpec(memory_space=pl.ANY)
    vmem = pl.BlockSpec(memory_space=pltpu.VMEM)
    shapes, outs, scratch, n_sems = sums_shapes(buckets, seq, [g.shape for g in grads], kinds)
    inputs = place_grads(buckets, grads, kinds, shapes)
    results = pl.pallas_call(
        functools.partial(scatter_kernel, buckets, seq, tuple(kinds)),
        out_shape=[jax.ShapeDtypeStruct((buckets,) + vec.shape, F32), *outs],
        in_specs=[vmem] + [any_spec] * len(grads),
        out_specs=[any_spec] + [vmem] * len(grads),
        scratch_shapes=[
            pltpu.VMEM((seq,) + vec.shape, F32),
            pltpu.VMEM(vec.shape, F32),
            pltpu.SemaphoreType.DMA((n_sems,)),
            pltpu.SemaphoreType.DMA((n_sems,)),
            *scratch,
        ],
        compiler_params=pltpu.CompilerParams(
            collective_id=collective_id, has_side_effects=True, vmem_limit_bytes=60 * 2**20
        ),
    )(vec, *inputs)
    return results[0], [out.reshape(-1, out.shape[-1]) for out in results[1:]]


def attention(queries, keys, values, live, scale):
    scores = jnp.einsum("qhd,khd->hqk", queries, keys, preferred_element_type=F32) * scale
    scores = jnp.where(live[None, None, :], scores, -1e30)
    probs = jax.nn.softmax(scores, axis=-1)
    mixed = jnp.einsum("hqk,khd->qhd", probs.astype(BF16), values, preferred_element_type=F32)
    return probs, mixed


def attention_back(probs, queries, keys, values, d_out, scale):
    d_probs = jnp.einsum("qhd,khd->hqk", d_out, values, preferred_element_type=F32)
    d_scores = probs * (d_probs - jnp.sum(probs * d_probs, axis=-1, keepdims=True))
    d_low = d_scores.astype(BF16)
    d_query = jnp.einsum("hqk,khd->qhd", d_low, keys, preferred_element_type=F32) * scale
    d_key = jnp.einsum("hqk,qhd->khd", d_low, queries, preferred_element_type=F32) * scale
    d_value = jnp.einsum("hqk,qhd->khd", probs.astype(BF16), d_out, preferred_element_type=F32)
    return d_query, d_key, d_value


def on_device_general(
    tokens,
    captions,
    cotangent,
    counts,
    cap_lens,
    steps_t,
    w_query,
    w_key,
    w_value,
    w_out,
    w_cap_key,
    w_cap_value,
    w_gate,
    w_up,
    w_down,
    w_mod,
    gains,
    cross_gate,
):
    buckets, seq = lax.axis_size("bucket"), lax.axis_size("seq")
    b, s = lax.axis_index("bucket"), lax.axis_index("seq")
    place = b * seq + s
    rows, width = tokens.shape
    span = rows * seq
    share = width // seq
    heads = share // HEAD_DIM
    scale = HEAD_DIM ** (-0.5)
    live_rows, cap_len = pick_entry(counts, b), pick_entry(cap_lens, b)
    token_total = jnp.sum(counts).astype(F32)

    cond_size = w_mod.shape[0] * buckets * seq
    cond = jax.nn.silu(time_embed(steps_t, cond_size)).astype(BF16)
    cond_part = lax.dynamic_slice_in_dim(cond, place * w_mod.shape[0], w_mod.shape[0], 1)
    slim = gains.shape[1]
    small = jnp.concatenate([gains, cross_gate[None]], axis=0).astype(F32)
    small = jnp.pad(small, ((0, 0), (0, 128 - slim)))
    tok_all, cap_all, small_all, mod, weights = gather_all(
        buckets,
        seq,
        tokens,
        captions,
        small,
        cond_part,
        w_mod,
        [w_query, w_key, w_value, w_cap_key, w_cap_value, w_out, w_gate, w_up, w_down],
        ["col", "col", "col", "col", "col", "row", "col", "col", "row"],
    )
    wq, wk, wv, wck, wcv, wo, wg, wu, wd = weights
    caps = cap_all.reshape(-1, captions.shape[1])
    small_rows = small_all[..., :slim].transpose(2, 0, 1, 3).reshape(8, width)
    gain_f = small_rows[:7]
    own_cols = lax.dynamic_slice_in_dim(small_rows, s * share, share, 1)
    gate_cross = jnp.tanh(own_cols[7])
    scale_attn, gate_attn, scale_ffn, gate_ffn = mod.reshape(4, width)

    hidden = pre_attn(tok_all.astype(F32), gain_f[0], scale_attn).astype(BF16).reshape(span, width)
    query_proj, key_proj = bf_dot(hidden, wq), bf_dot(hidden, wk)
    value_low = bf_dot(hidden, wv).astype(BF16)
    (query_f, key_f), norm_back = jax.vjp(qk_norm, query_proj, key_proj, own_cols[4], own_cols[5])
    cap_key_f, cap_back = jax.vjp(cap_norm, bf_dot(caps, wck), own_cols[6])

    def by_head(values):
        return values.astype(BF16).reshape(values.shape[0], heads, HEAD_DIM)

    query, key, value = by_head(query_f), by_head(key_f), by_head(value_low)
    cap_key, cap_value = by_head(cap_key_f), by_head(bf_dot(caps, wcv))
    probs, self_out = attention(query, key, value, jnp.arange(span) < live_rows, scale)
    cap_live = jnp.arange(caps.shape[0]) < cap_len
    cap_probs, cross_out = attention(query, cap_key, cap_value, cap_live, scale)
    self_out, cross_out = self_out.reshape(span, share), cross_out.reshape(span, share)
    mixed_low = (self_out + gate_cross * cross_out).astype(BF16)
    attn_out = line_scatter(seq, bf_dot(mixed_low, wo), 2)

    tokens_f = tokens.astype(F32)
    (resid_one, ffn_pre), middle_back = jax.vjp(
        middle, tokens_f, attn_out, gain_f[1], gate_attn, gain_f[2], scale_ffn
    )
    ffn_all = line_gather(seq, ffn_pre.astype(BF16), 3)
    act_pre, act_back = jax.vjp(activate, bf_dot(ffn_all, wg), bf_dot(ffn_all, wu))
    act_low = act_pre.astype(BF16)
    ffn_out = line_scatter(seq, bf_dot(act_low, wd), 4)
    out_f, finish_back = jax.vjp(finish, resid_one, ffn_out, gain_f[3], gate_ffn)
    block_out = out_f.astype(BF16)

    row_live = (s * rows + jnp.arange(rows) < live_rows).astype(F32)
    weighted = cotangent.astype(F32) * row_live[:, None] * (buckets * span / token_total)
    d_resid, d_ffn_out, d_gain_last, d_gate_ffn = finish_back(weighted)
    d_ffn_all = line_gather(seq, d_ffn_out.astype(BF16), 5)
    d_gate, d_up = act_back(right_dot(d_ffn_all, wd))
    d_gate, d_up = d_gate.astype(BF16), d_up.astype(BF16)
    d_hidden_ffn = line_scatter(seq, right_dot(d_gate, wg) + right_dot(d_up, wu), 6)
    d_tokens_one, d_attn_out, d_gain_post, d_gate_attn, d_gain_ffn, d_scale_ffn = middle_back(
        (d_resid, d_hidden_ffn)
    )
    d_attn_all = line_gather(seq, d_attn_out.astype(BF16), 7)
    d_mixed_low = right_dot(d_attn_all, wo).astype(BF16)
    d_mixed = d_mixed_low.astype(F32)
    d_cross_low = (gate_cross * d_mixed).astype(BF16)
    grad_cross = jnp.sum(d_mixed * cross_out, axis=0) * (1.0 - gate_cross * gate_cross)

    d_query_cross, d_cap_key, d_cap_value = attention_back(
        cap_probs, query, cap_key, cap_value, by_head(d_cross_low), scale
    )
    d_query, d_key, d_value = attention_back(probs, query, key, value, by_head(d_mixed_low), scale)
    d_cap_key, d_gain_cap = cap_back(d_cap_key.reshape(-1, share))
    d_query, d_key, d_gain_query, d_gain_key = norm_back(
        ((d_query + d_query_cross).reshape(span, share), d_key.reshape(span, share))
    )
    d_query, d_key, d_cap_key = d_query.astype(BF16), d_key.astype(BF16), d_cap_key.astype(BF16)
    d_value = d_value.reshape(span, share).astype(BF16)
    d_cap_value = d_cap_value.reshape(-1, share).astype(BF16)
    d_hidden = line_scatter(
        seq, right_dot(d_query, wq) + right_dot(d_key, wk) + right_dot(d_value, wv), 8
    )
    _, pre_back = jax.vjp(pre_attn, tokens_f, gain_f[0], scale_attn)
    d_tokens_two, d_gain_pre, d_scale_attn = pre_back(d_hidden)
    tokens_grad = d_tokens_one + d_tokens_two

    own_sums = jnp.stack([d_gain_query, d_gain_key, d_gain_cap, grad_cross])
    own_wide = lax.dynamic_update_slice(jnp.zeros((4, width), F32), own_sums, (0, s * share))
    vec = jnp.concatenate(
        [
            jnp.stack([d_scale_attn, d_gate_attn, d_scale_ffn, d_gate_ffn]),
            jnp.stack([d_gain_pre, d_gain_post, d_gain_ffn, d_gain_last]),
            own_wide,
            jnp.zeros((4, width), F32),
        ]
    )
    grads = [
        left_dot(ffn_all, d_gate),
        left_dot(ffn_all, d_up),
        left_dot(act_low, d_ffn_all),
        left_dot(mixed_low, d_attn_all),
        left_dot(caps, d_cap_key),
        left_dot(caps, d_cap_value),
        left_dot(hidden, d_query),
        left_dot(hidden, d_key),
        left_dot(hidden, d_value),
    ]
    kinds = ["col", "col", "row", "row", "col", "col", "col", "col", "col"]
    vec_all, sums = scatter_all(buckets, seq, vec, grads, kinds)
    s_gate, s_up, s_down, s_out, s_cap_key, s_cap_value, s_query, s_key, s_value = sums

    quarter = 4 * width // seq
    mod_rows = vec_all[:, :4].reshape(buckets, -1, quarter)
    mod_rows = lax.dynamic_slice_in_dim(mod_rows, s, 1, 1)[:, 0]
    cond_size = cond.shape[1] // buckets
    cond_cols = lax.dynamic_slice_in_dim(cond, b * cond_size, cond_size, 1).astype(F32)
    s_mod = jnp.sum(cond_cols[:, :, None] * mod_rows[:, None, :], axis=0)
    tail = lax.dynamic_slice(vec_all, (0, 4, place * slim), (buckets, 8, slim))
    tail = jnp.sum(tail, axis=0)
    return (
        block_out,
        tokens_grad,
        s_query,
        s_key,
        s_value,
        s_out,
        s_cap_key,
        s_cap_value,
        s_gate,
        s_up,
        s_down,
        s_mod,
        tail[:7],
        tail[7],
    )


def low_half(shape):
    return lax.broadcasted_iota(jnp.int32, shape, len(shape) - 1) < HEAD_DIM


def pair_sums(values):
    row = lax.broadcasted_iota(jnp.int32, (128, 128), 0) < HEAD_DIM
    same = (row == low_half((128, 128))).astype(BF16)
    high = values.astype(BF16)
    rest = (values - high.astype(F32)).astype(BF16)
    return bf_dot(high, same) + bf_dot(rest, same)


def pair_scale(values, eps):
    return lax.rsqrt(pair_sums(values * values) * (1.0 / HEAD_DIM) + eps)


def fill_rows(out, live, first, yes, no):
    row = lax.broadcasted_iota(jnp.int32, out.shape, 0) + first
    out[...] = jnp.where(row < live, yes, no).astype(out.dtype)


FORWARD_ORDER = (8, "tok", 0, "tok", 1, "tok", 2, "tok", 6, 7, "cap", 3, "cap", 4, "cap", 5, "cap")
MOVED = ()
LAG = 1
WINDOW = 2


class Gather:
    def __init__(self, copies, b, s, buckets, seq, kinds, shards, fulls, keep_at=None):
        self.copies, self.b, self.s, self.buckets, self.seq = copies, b, s, buckets, seq
        self.kinds, self.shards, self.fulls, self.keep_at = kinds, shards, fulls, keep_at
        place = b * seq + s
        self.to_slot, self.to_s = lax.rem(place, buckets), lax.div(place, buckets)
        self.to_b = slot(self.to_slot, buckets)
        back = s * buckets + slot(b, buckets)
        self.from_b, self.from_s = lax.div(back, seq), lax.rem(back, seq)
        self.stays = jnp.logical_and(self.to_b == b, self.to_s == s)
        self.twin, self.near_x, self.near_y = flip(b, 1), flip(b, 2), flip(b, 4)
        self.far = flip(self.near_x, 4)
        self.first, self.second, self.kept, self.sent = {}, {}, [], []

    def greet_source(self):
        @pl.when(jnp.logical_not(self.stays))
        def _():
            greet(self.from_b, self.from_s)

        return jnp.where(self.stays, 0, 1)

    def go(self, src, dst, b):
        copy = self.copies.remote(src, dst, b, self.s)
        copy.start()
        self.sent.append(copy)
        return copy

    def depart(self, at):
        copies, b, s, seq = self.copies, self.b, self.s, self.seq
        shard, full = self.shards[at], self.fulls[at]
        if self.kinds[at] == "stay":
            keep = copies.local(shard, full.at[b])
            keep.start()
            self.first[at] = ((), keep)
            return
        if self.kinds[at] == "row":
            move = copies.remote(shard, full.at[self.to_slot], self.to_b, self.to_s)
            keep = copies.local(shard, full.at[slot(b, self.buckets)])

            @pl.when(jnp.logical_not(self.stays))
            def _():
                move.start()

            @pl.when(self.stays)
            def _():
                keep.start()

            self.first[at] = (move, keep)
            return
        wide = full.shape[-1]

        def columns(peer):
            if self.kinds[at] == "cut":
                return shard.at[peer]
            return shard.at[:, pl.ds(pl.multiple_of(peer * wide, 128), wide)]

        moves = []
        for k in range(1, seq):
            peer = lax.rem(s + k, seq)
            move = copies.remote(columns(peer), full.at[b, s], b, peer)
            move.start()
            moves.append(move)
        keep = copies.local(columns(s), full.at[b, s])
        keep.start()
        self.first[at] = (moves, keep)

    def arrived(self, at):
        moves, keep = self.first[at]
        if self.kinds[at] == "row":

            @pl.when(jnp.logical_not(self.stays))
            def _():
                moves.wait()

            @pl.when(self.stays)
            def _():
                keep.wait()

            return
        for move in moves:
            move.wait()
        keep.wait()

    def index(self, at, device):
        return slot(device, self.buckets) if self.kinds[at] == "row" else device

    def stage_a(self, at):
        block = self.fulls[at].at[self.index(at, self.b)]
        self.second[at] = {
            "x": self.go(block, block, self.near_x),
            "y": self.go(block, block, self.near_y),
            "twin": [self.go(block, block, self.twin)],
        }

    def stage_b(self, at):
        full, now = self.fulls[at], self.second[at]
        cut = halves_of(full.shape[1:])
        now["x"].wait_recv()
        block = full.at[self.index(at, self.near_x), pl.ds(0, cut)]
        now["dy"] = self.go(block, block, self.near_y)
        block = full.at[self.index(at, self.near_x)]
        now["twin"].append(self.go(block, block, self.twin))
        now["y"].wait_recv()
        block = full.at[self.index(at, self.near_y), pl.ds(cut, full.shape[1] - cut)]
        now["dx"] = self.go(block, block, self.near_x)
        block = full.at[self.index(at, self.near_y)]
        now["twin"].append(self.go(block, block, self.twin))

    def stage_c(self, at):
        full, now = self.fulls[at], self.second[at]
        now["dy"].wait_recv()
        now["dx"].wait_recv()
        block = full.at[self.index(at, self.far)]
        now["twin"].append(self.go(block, block, self.twin))

    def stage_d(self, at):
        for move in self.second[at]["twin"]:
            move.wait_recv()
        if self.keep_at is not None:
            copy = self.copies.local(self.fulls[at], self.keep_at[at])
            copy.start()
            self.kept.append(copy)

    def end(self):
        for copy in self.kept:
            copy.wait()
        for move in self.sent:
            move.wait_send()


def forward_kernel(buckets, seq, kinds, slim, *refs):
    count = len(kinds)
    tokens, captions, small, cond, w_mod, counts, cap_lens = refs[:7]
    shards = refs[7 : 7 + count]
    refs = refs[7 + count :]
    cap_all = refs[0]
    far_fulls = refs[1 : 1 + count]
    refs = refs[1 + count :]
    (
        gain_rows,
        mod_rows,
        hidden,
        query_raw,
        key_raw,
        cap_raw,
        query,
        key,
        value,
        cap_key,
        cap_value,
        cross_out,
        mixed,
    ) = refs[:13]
    refs = refs[13:]
    part, got_bucket, got_seq, mod_sum, small_all, tok_all, cap_near, own_out = refs[:8]
    fulls = refs[8 : 8 + count]
    key_mask, cap_mask, send, recv = refs[8 + count : 12 + count]
    strips = refs[12 + count :]
    b, s = lax.axis_index("bucket"), lax.axis_index("seq")
    copies = Copies(send, recv)
    shards = list(shards)
    cuts = [at for at in range(count) if kinds[at] == "cut"]
    for at, strip in zip(cuts, strips, strict=True):
        for t in range(seq):
            for j in range(strip.shape[2] // 128):
                cols = slice((j * seq + t) * 128, (j * seq + t + 1) * 128)
                strip[t, :, j * 128 : (j + 1) * 128] = shards[at][:, cols]
        shards[at] = strip
    weights = Gather(copies, b, s, buckets, seq, kinds, shards, fulls, far_fulls)
    for k in range(1, buckets):
        greet(lax.rem(b + k, buckets), s)
    for k in range(1, seq):
        greet(b, lax.rem(s + k, seq))
    peers = buckets - 1 + seq - 1 + weights.greet_source()

    fill_rows(key_mask, counts[b], 0, 1.0, 0.0)
    fill_rows(cap_mask, cap_lens[b], 0, 1.0, 0.0)
    lanes = part.shape[2]
    for j in range(part.shape[1]):
        part[:, j, :] = bf_dot(cond[...], w_mod[:, j * lanes : (j + 1) * lanes])

    pl.semaphore_wait(pltpu.get_barrier_semaphore(), peers)

    sent = []

    def go(copy):
        copy.start()
        sent.append(copy)
        return copy

    mod_moves = []
    for k in range(1, buckets):
        peer = lax.rem(b + k, buckets)
        mod_moves.append(go(copies.remote(part.at[peer], got_bucket.at[k], peer, s)))
    small_moves = []
    for k in range(1, seq):
        peer = lax.rem(s + k, seq)
        small_moves.append(go(copies.remote(small, small_all.at[b, s], b, peer)))
    small_own = copies.local(small, small_all.at[b, s])
    small_own.start()

    tok = Relay(copies, tokens, tok_all, b, s, seq)
    cap = Relay(copies, captions, cap_near, b, s, seq)
    items, step = [], {"tok": 0, "cap": 0}
    for what in FORWARD_ORDER:
        if isinstance(what, str):
            items.append((tok if what == "tok" else cap, step[what]))
            step[what] += 1
        else:
            items.append((None, what))

    def fetch(at):
        whole = fulls[at][...]
        return whole.reshape(-1, whole.shape[-1])


    rows = seq * tok_all.shape[1]
    width = tok_all.shape[2]
    cap_rows = seq * cap_near.shape[1]
    share = query.shape[1]
    pairs = share // 128
    block_rows = tok_all.shape[1]

    def small_sums():
        for move in small_next:
            move.wait_recv()
        strips = [None] * (width // 128)
        lane = lax.broadcasted_iota(jnp.int32, (8, 128), 1)
        for d in range(buckets * seq):
            at, shift = divmod(d * slim, 128)
            piece = small_all[d // seq, d % seq]
            turned = pltpu.roll(piece, shift, 1) if shift else piece
            for index, keep in ((at, lane >= shift), (at + 1, lane < shift)):
                if index == at + 1 and shift + slim <= 128:
                    continue
                add = jnp.where(keep, turned, 0.0)
                strips[index] = add if strips[index] is None else strips[index] + add
        for at, strip in enumerate(strips):
            gain_rows[:, at * 128 : (at + 1) * 128] = strip
        total = mod_sum[...]
        for k, move in enumerate(mod_next, 1):
            move.wait_recv()
            total = total + got_seq[k]
        for j in range(8):
            at, lane_at = divmod(j * lanes, width)
            mod_rows[at : at + 1, lane_at : lane_at + lanes] = total[j : j + 1, :]
        mod_rows[4:8, :] = jnp.zeros((4, width), F32)

    def make_hidden():
        factor = gain_rows[0:1, :] * (1.0 + mod_rows[0:1, :])
        for t in range(seq):

            def body(i, carry):
                at = pl.ds(pl.multiple_of(i * 32, 32), 32)
                x = tok_all[t, at, :].astype(F32)
                x = x * lax.rsqrt(jnp.mean(x * x, axis=-1, keepdims=True) + 1e-05) * factor
                to = pl.ds(pl.multiple_of(t * block_rows + i * 32, 32), 32)
                hidden[to, :] = x.astype(BF16)
                return carry

            lax.fori_loop(0, block_rows // 32, body, 0)

    def gain_of(row, pair):
        at = pl.multiple_of(s * share + pair * 128, 128)
        return gain_rows[row : row + 1, pl.ds(at, 128)]

    def make_normed(raw, out, row, scale):
        def body(i, carry):
            at = pl.ds(pl.multiple_of(i * 64, 64), 64)
            for pair in range(pairs):
                lane = slice(pair * 128, (pair + 1) * 128)
                x = raw[at, lane]
                x = x * pair_scale(x, 1e-06) * gain_of(row, pair)
                out[at, lane] = x.astype(BF16)
            return carry

        del scale
        lax.fori_loop(0, raw.shape[0] // 64, body, 0)

    def make_query():
        query_raw[...] = bf_dot(hidden[...], fetch(0))
        make_normed(query_raw, query, 4, None)

    def make_key():
        key_raw[...] = bf_dot(hidden[...], fetch(1))
        make_normed(key_raw, key, 5, None)

    def make_value():
        value[...] = bf_dot(hidden[...], fetch(2)).astype(BF16)

    def cap_near_rows():
        whole = cap_near[...]
        return whole.reshape(cap_rows, whole.shape[-1])

    def make_cap_key():
        cap_raw[...] = bf_dot(cap_near_rows(), fetch(3))
        make_normed(cap_raw, cap_key, 6, None)

    def make_cap_value():
        cap_value[...] = bf_dot(cap_near_rows(), fetch(4)).astype(BF16)

    def attend(pair, k_ref, v_ref, mask, store):
        lane = slice(pair * 128, (pair + 1) * 128)
        low = low_half((128, 128))
        keys = k_ref[:, lane]
        values = jnp.concatenate([v_ref[:, lane] * mask[...], mask[...]], axis=1)

        def body(i, carry):
            at = pl.ds(pl.multiple_of(i * 128, 128), 128)
            q = query[at, lane] * jnp.asarray(HEAD_DIM**-0.5, BF16)
            outs = []
            for half in (jnp.where(low, q, jnp.zeros_like(q)), jnp.where(low, jnp.zeros_like(q), q)):
                weights = jnp.exp(right_dot(half, keys))
                outs.append(bf_dot(weights.astype(BF16), values))
            out = jnp.where(low, outs[0][:, :128], outs[1][:, :128])
            store(at, lane, out / jnp.where(low, outs[0][:, 128:], outs[1][:, 128:]))
            return carry

        lax.fori_loop(0, rows // 128, body, 0)

    def make_own(pair):
        def store(at, lane, out):
            own_out[at, lane] = out

        attend(pair, key, value, key_mask, store)

    def make_mixed(pair):
        gate = jnp.tanh(gain_of(7, pair))

        def store(at, lane, out):
            cross_out[at, lane] = out
            mixed[at, lane] = (own_out[at, lane] + gate * out).astype(BF16)

        attend(pair, cap_key, cap_value, cap_mask, store)

    work = [
        (lambda: (small_sums(), make_hidden()), "h", {"tok"}),
        (make_query, "q", {"h", 0}),
        (make_key, "k", {"h", 1}),
        (make_value, "v", {"h", 2}),
        (make_cap_key, "ck", {"cap", 3}),
        (make_cap_value, "cv", {"cap", 4}),
        *((functools.partial(make_own, p), ("own", p), {"q", "k", "v"}) for p in range(pairs)),
        *(
            (functools.partial(make_mixed, p), ("all", p), {"q", "ck", "cv", ("own", p)})
            for p in range(pairs)
        ),
    ]

    def do_work():
        for at, (piece, name, needs) in enumerate(work):
            if needs <= done:
                piece()
                done.add(name)
                del work[at]
                return True
        return False


    done = set()

    def begin(i):
        relay, j = items[i]
        if relay is None:
            weights.depart(j)
        else:
            relay.start(j)
            if j == seq - 1:
                done.add("tok" if relay is tok else "cap")

    def complete(at):
        weights.stage_c(at)
        weights.stage_d(at)
        done.add(at)

    window = WINDOW
    for i in range(window):
        begin(i)
    for move in small_moves:
        move.wait_recv()
    small_own.wait()
    small_next = []
    for k in range(1, buckets):
        peer = lax.rem(b + k, buckets)
        small_next.append(go(copies.remote(small_all.at[b], small_all.at[b], peer, s)))
    total = part[b]
    for k, move in enumerate(mod_moves, 1):
        move.wait_recv()
        total = total + got_bucket[k]
    mod_sum[...] = total
    mod_next = []
    for k in range(1, seq):
        peer = lax.rem(s + k, seq)
        mod_next.append(go(copies.remote(mod_sum, got_seq.at[k], b, peer)))

    cap_out = copies.local(cap_near, cap_all)
    order = []
    for i, (relay, j) in enumerate(items):
        if relay is None:
            weights.arrived(j)
        elif j <= seq - 2:
            relay.sent(j)
        if i + window < len(items):
            begin(i + window)
        if relay is None:
            order.append(j)
            weights.stage_a(j)
            if len(order) > LAG:
                weights.stage_b(order[-1 - LAG])
            if len(order) > LAG + 1:
                complete(order[-2 - LAG])
        do_work()
    cap_out.start()
    for at in range(LAG):
        weights.stage_b(order[len(order) - LAG + at])
        complete(order[len(order) - LAG - 1 + at])
        do_work()
    complete(order[-1])
    while do_work():
        pass
    cap_out.wait()
    weights.end()
    for move in sent:
        move.wait_send()


def forward_all(buckets, seq, tokens, captions, small, slim, cond, w_mod, masks, shards, kinds):
    any_spec = pl.BlockSpec(memory_space=pl.ANY)
    vmem = pl.BlockSpec(memory_space=pltpu.VMEM)
    smem = pl.BlockSpec(memory_space=pltpu.SMEM)
    fulls = []
    for shard, kind in zip(shards, kinds, strict=True):
        rows, wide = shard.shape
        shape = (buckets, rows, wide) if kind in ("row", "stay") else (buckets, seq, rows, wide // seq)
        fulls.append(jax.ShapeDtypeStruct(shape, BF16))
    near = [pltpu.VMEM(full.shape, BF16) for full in fulls]
    width = tokens.shape[1]
    mod_lanes = w_mod.shape[1] // 8
    span, cap_span, share = seq * tokens.shape[0], seq * captions.shape[0], width // seq
    f32_rows = jax.ShapeDtypeStruct((span, share), F32)
    low_rows = jax.ShapeDtypeStruct((span, share), BF16)
    cap_low = jax.ShapeDtypeStruct((cap_span, share), BF16)
    inner = [
        jax.ShapeDtypeStruct((8, width), F32),
        jax.ShapeDtypeStruct((8, width), F32),
        jax.ShapeDtypeStruct((span, width), BF16),
        f32_rows,
        f32_rows,
        jax.ShapeDtypeStruct((cap_span, share), F32),
        low_rows,
        low_rows,
        low_rows,
        cap_low,
        cap_low,
        f32_rows,
        low_rows,
    ]
    n_sems = 64 + 16 * buckets + len(shards) * (seq + 2 * buckets)
    outs = pl.pallas_call(
        functools.partial(forward_kernel, buckets, seq, tuple(kinds), slim),
        out_shape=[jax.ShapeDtypeStruct((seq,) + captions.shape, BF16), *fulls, *inner],
        in_specs=[any_spec, any_spec, any_spec, vmem, vmem, smem, smem]
        + [vmem if kind == "cut" else any_spec for kind in kinds],
        out_specs=[any_spec] * (1 + len(shards)) + [vmem] * len(inner),
        scratch_shapes=[
            pltpu.VMEM((buckets, 8, mod_lanes), F32),
            pltpu.VMEM((buckets, 8, mod_lanes), F32),
            pltpu.VMEM((seq, 8, mod_lanes), F32),
            pltpu.VMEM((8, mod_lanes), F32),
            pltpu.VMEM((buckets, seq) + small.shape, F32),
            pltpu.VMEM((seq,) + tokens.shape, BF16),
            pltpu.VMEM((seq,) + captions.shape, BF16),
            pltpu.VMEM((span, share), F32),
            *near,
            pltpu.VMEM((span, 128), BF16),
            pltpu.VMEM((cap_span, 128), BF16),
            pltpu.SemaphoreType.DMA((n_sems,)),
            pltpu.SemaphoreType.DMA((n_sems,)),
            *(
                pltpu.VMEM((seq,) + full.shape[2:], BF16)
                for full, kind in zip(fulls, kinds, strict=True)
                if kind == "cut"
            ),
        ],
        compiler_params=pltpu.CompilerParams(
            collective_id=9, has_side_effects=True, vmem_limit_bytes=62 * 2**20
        ),
    )(tokens, captions, small, cond, w_mod, *masks, *shards)
    at = 1 + len(shards)
    return outs[0], outs[1:at], outs[at:]


def middle_kernel(buckets, seq, chunks, kinds, *refs):
    mixed, w_out, tokens, cotangent, counts, gain_rows, mod_rows = refs[:7]
    far_weights, refs = refs[7:10], refs[10:]
    block_out, d_tokens, d_attn, row_sums = refs[:4]
    outs, refs = refs[4:7], refs[7:]
    w_gate, w_up, w_down, ffn_all, d_ffn, act, d_gate, d_up = refs[:8]
    gate_keep, up_keep, attn_keep, resid_keep, got, parts, from_left, from_right = refs[8:16]
    row_scale, send, recv = refs[16:19]
    grads, refs = refs[19:22], refs[22:]
    b, s = lax.axis_index("bucket"), lax.axis_index("seq")
    copies = Copies(send, recv)
    sums = GradSums(copies, b, s, buckets, seq, kinds, grads, outs, refs, near=True)
    shards = (w_gate, w_up, w_down)
    weights = Gather(copies, b, s, buckets, seq, ("cut", "cut", "stay"), far_weights, shards)
    peers = greet_all(b, s, buckets, seq) + weights.greet_source()
    pl.semaphore_wait(pltpu.get_barrier_semaphore(), peers)
    loads = [copies.local(far_weights[w], shards[w]) for w in range(3) if w not in MOVED]
    for load in loads:
        load.start()
    if MOVED:
        weights.depart(MOVED[0])

    rows, width = tokens.shape
    live = sum(counts[k] for k in range(buckets))
    factor = buckets * seq * rows / jnp.full((rows, 128), live, jnp.int32).astype(F32)
    row = lax.broadcasted_iota(jnp.int32, (rows, 128), 0) + s * rows
    row_scale[...] = jnp.where(row < counts[b], factor, 0.0)
    thin = rows // chunks
    tall = seq * thin
    hidden = act.shape[-1]
    wide = 512
    gate_post = jnp.tanh(mod_rows[1:2, :]) * gain_rows[1:2, :]
    gain_ffn = gain_rows[2:3, :] * (1.0 + mod_rows[2:3, :])
    gate_last = jnp.tanh(mod_rows[3:4, :]) * gain_rows[3:4, :]
    row_sums[...] = jnp.zeros_like(row_sums)

    def of(c):
        return pl.ds(c * thin, thin)

    def chunk_of(ref, c, cols=slice(None)):
        whole = ref[:, of(c), cols]
        return whole.reshape(tall, whole.shape[-1])

    def mean(values):
        return jnp.mean(values, axis=-1, keepdims=True)

    def over_rows(c, body):
        step = 16

        def one(i, carry):
            return body(pl.ds(pl.multiple_of(c * thin + i * step, step), step), carry)

        return lax.fori_loop(0, thin // step, one, jnp.zeros((1, width), F32), unroll=2)

    def weighted(at):
        return cotangent[at, :].astype(F32) * row_scale[at, 0:1]

    def after_attn(c):
        def body(at, carry):
            out = got[at, :]
            attn_keep[at, :] = out
            resid = out * lax.rsqrt(mean(out * out) + 1e-05) * gate_post
            resid = tokens[at, :].astype(F32) + resid
            resid_keep[at, :] = resid
            normed = resid * lax.rsqrt(mean(resid * resid) + 1e-05)
            ffn_all[s, at, :] = (normed * gain_ffn).astype(BF16)
            return carry

        over_rows(c, body)

    def after_ffn(c):
        def body(at, total):
            out, resid, grad = got[at, :], resid_keep[at, :], weighted(at)
            size = lax.rsqrt(mean(out * out) + 1e-05)
            normed = out * size
            block_out[at, :] = (resid + gate_last * normed).astype(BF16)
            inner = grad * gate_last
            d_ffn[s, at, :] = (size * (inner - normed * mean(inner * normed))).astype(BF16)
            return total + jnp.sum(grad * normed, axis=0, keepdims=True)

        row_sums[2:3, :] += over_rows(c, body)

    def after_ffn_back(c):
        def body(at, totals):
            first, second = totals
            d_pre, resid, out = got[at, :], resid_keep[at, :], attn_keep[at, :]
            size = lax.rsqrt(mean(resid * resid) + 1e-05)
            normed, inner = resid * size, d_pre * gain_ffn
            second = second + jnp.sum(d_pre * normed, axis=0, keepdims=True)
            grad = weighted(at) + size * (inner - normed * mean(inner * normed))
            d_tokens[at, :] = grad
            size = lax.rsqrt(mean(out * out) + 1e-05)
            normed, inner = out * size, grad * gate_post
            first = first + jnp.sum(grad * normed, axis=0, keepdims=True)
            d_attn[s, at, :] = (size * (inner - normed * mean(inner * normed))).astype(BF16)
            return first, second

        step, zero = 16, jnp.zeros((1, width), F32)

        def one(i, carry):
            return body(pl.ds(pl.multiple_of(c * thin + i * step, step), step), carry)

        first, second = lax.fori_loop(0, thin // step, one, (zero, zero), unroll=2)
        row_sums[0:1, :] += first
        row_sums[1:2, :] += second

    def flat(values):
        return values.reshape(-1, values.shape[-1])

    def put_parts(c, cols, total):
        parts[c, :, :, cols] = total.astype(BF16).reshape(seq, thin, total.shape[-1])

    def attn_product(c):
        left = chunk_of(mixed, c)
        for at in range(0, width, wide):
            cols = slice(at, at + wide)
            put_parts(c, cols, bf_dot(left, w_out[:, cols]))

    def ffn_product(c):
        for at in range(0, hidden, wide):
            cols = slice(at, at + wide)
            left = chunk_of(ffn_all, c)
            gate = bf_dot(left, flat(w_gate[:, :, :, cols]))
            up = bf_dot(left, flat(w_up[:, :, :, cols]))
            gate_keep[c, :, cols], up_keep[c, :, cols] = gate, up
            value = (gate * jax.nn.sigmoid(gate) * up).astype(BF16)
            act[:, of(c), cols] = value.reshape(seq, thin, wide)
        left = chunk_of(act, c)
        for at in range(0, width, wide):
            cols = slice(at, at + wide)
            put_parts(c, cols, bf_dot(left, flat(w_down[:, :, cols])))

    def ffn_back_product(c):
        block = w_down.shape[1]
        for at in range(0, hidden, wide):
            cols = slice(at, at + wide)
            d_act = right_dot(chunk_of(d_ffn, c), flat(w_down[at // block : (at + wide) // block]))
            gate, up = gate_keep[c, :, cols], up_keep[c, :, cols]
            sig = jax.nn.sigmoid(gate)
            silu = gate * sig
            d_g = (d_act * up * (sig + silu * (1.0 - sig))).astype(BF16)
            d_u = (d_act * silu).astype(BF16)
            d_gate[:, of(c), cols] = d_g.reshape(seq, thin, wide)
            d_up[:, of(c), cols] = d_u.reshape(seq, thin, wide)
        left_g, left_u = chunk_of(d_gate, c), chunk_of(d_up, c)
        half = buckets // 2
        for at in range(0, buckets, half):
            cols = slice(at * width // buckets, (at + half) * width // buckets)
            total = right_dot(left_g, flat(w_gate[at : at + half]))
            total = total + right_dot(left_u, flat(w_up[at : at + half]))
            put_parts(c, cols, total)

    def pour_of(c, turn):
        left, right = from_left.at[turn * chunks + c], from_right.at[turn * chunks + c]
        return Pour(copies, parts.at[c], left, right, b, s, seq)

    gathered = (ffn_all, d_ffn, d_attn)
    after = (after_attn, after_ffn, after_ffn_back)
    products = (attn_product, ffn_product, ffn_back_product)

    def all_rows(ref, cols=slice(None)):
        whole = ref[:, :, cols]
        return whole.reshape(seq * rows, whole.shape[-1])

    def down_grad():
        chips, part = buckets // 2, hidden // buckets
        for i in range(chips):
            turned = all_rows(act, slice(2 * i * part, 2 * (i + 1) * part)).T
            total = bf_dot(turned, all_rows(d_ffn)).astype(BF16)
            for half in range(2):
                grads[2][i, half] = total[half * part : (half + 1) * part]
        sums.begin(2)

    def weight_grads():
        chips, part = buckets // 2, width // (buckets // 2)
        for i in range(chips):
            turned = all_rows(ffn_all, slice(i * part, (i + 1) * part)).T
            for grad, d in zip(grads[:2], (d_gate, d_up), strict=True):
                total = bf_dot(turned, all_rows(d))
                grad[i] = total.astype(BF16).reshape(2, part // 2, hidden)
            if i == 1:
                sums.stage_a(2)
            yield
        sums.begin(0)
        sums.begin(1)
        sums.stage_b(2)
        yield
        sums.stage_a(0)
        yield
        sums.stage_c(2)
        sums.stage_a(1)
        yield
        sums.stage_b(0)
        yield
        sums.stage_b(1)
        yield
        sums.stage_c(0)
        sums.stage_d(2)
        sums.stage_c(1)
        sums.stage_d(0)
        sums.stage_d(1)

    extra = weight_grads()
    plan = [(turn, c) for turn in range(3) for c in range(chunks)]
    gathers, open_gather = {}, []

    def finish_gather():
        turn, c = open_gather.pop(0)
        gathers[turn, c].start(seq - 1)
        for j in range(seq - 1):
            gathers[turn, c].sent(j)
        return turn, c

    def weights_come():
        count = len(MOVED)
        for n in range(count + 3):
            if n < count:
                weights.arrived(MOVED[n])
                if n + 1 < count:
                    weights.depart(MOVED[n + 1])
                weights.stage_a(MOVED[n])
                yield
            if 1 <= n <= count:
                weights.stage_b(MOVED[n - 1])
                yield
            if 2 <= n <= count + 1:
                weights.stage_c(MOVED[n - 2])
            if 3 <= n:
                weights.stage_d(MOVED[n - 3])
            yield

    coming = weights_come()
    attn_product(0)
    pours = {(0, 0): pour_of(0, 0)}
    ready = pours[0, 0].cuts
    for q in range(ready):
        pours[0, 0].step(q)
    for c in range(1, chunks):
        attn_product(c)
    for load in loads:
        load.wait()
    for at, (turn, c) in enumerate(plan):
        pour = pours[turn, c]
        mate = gathers[open_gather[0]] if open_gather else None
        per = pour.count // (seq - 1)
        final = at == len(plan) - 1
        for j in range(2, seq):
            if mate is not None and j < seq - 1:
                mate.start(j)
            if final:
                next(extra, None)
            for q in range((j - 1) * per, j * per):
                pour.step(q)
                next(coming, None)
            if final:
                next(extra, None)
        pour.end(got.at[of(c)])
        after[turn](c)
        gathers[turn, c] = Relay(copies, None, gathered[turn], b, s, seq, of(c))
        gathers[turn, c].start(0)
        if mate is not None:
            done_turn, done_c = finish_gather()
            if (done_turn, done_c) == (1, chunks - 1):
                down_grad()
            for _ in coming:
                pass
            if done_turn < 2:
                products[done_turn + 1](done_c)
        open_gather.append((turn, c))
        gathers[turn, c].start(1)
        if at + 1 < len(plan):
            nxt = plan[at + 1]
            pours[nxt] = pour_of(nxt[1], nxt[0])
            for q in range(ready):
                pours[nxt].step(q)
            if at + 2 == len(plan):
                next(extra)
                next(extra)
    turn, c = open_gather[0]
    for j in range(2, seq - 1):
        next(extra, None)
        gathers[turn, c].start(j)
    next(extra, None)
    finish_gather()
    for _ in extra:
        pass
    sums.end()
    weights.end()


def middle_all(buckets, seq, mixed, weights, tokens, cotangent, counts, gain_rows, mod_rows):
    any_spec = pl.BlockSpec(memory_space=pl.ANY)
    vmem = pl.BlockSpec(memory_space=pltpu.VMEM)
    smem = pl.BlockSpec(memory_space=pltpu.SMEM)
    chunks = CHUNKS
    w_out, w_gate, w_up, w_down = weights
    rows, width = tokens.shape
    hidden = w_down.shape[-2] * buckets if 2 in MOVED else w_down.shape[0] * w_down.shape[1]
    part = width // (buckets * seq)
    tall, thin = (seq, rows, width), rows // chunks
    flat = (seq, rows, hidden)
    blocks = pltpu.VMEM((3 * chunks, seq - 1, thin, width), BF16)
    kinds = ("strip", "strip", "stay")
    shapes, sums_out, scratch, n_sems = sums_shapes(
        buckets, seq, [(width, hidden), (width, hidden), (hidden, width)], kinds, near=True
    )
    n_sems += 64 + 3 * chunks * (2 * CUTS + 2) * seq
    results = pl.pallas_call(
        functools.partial(middle_kernel, buckets, seq, chunks, kinds),
        out_shape=[
            jax.ShapeDtypeStruct((rows, width), BF16),
            jax.ShapeDtypeStruct((rows, width), F32),
            jax.ShapeDtypeStruct(tall, BF16),
            jax.ShapeDtypeStruct((8, width), F32),
            *sums_out,
        ],
        in_specs=[vmem] * 4 + [smem] + [vmem] * 2 + [any_spec] * 3,
        out_specs=[vmem] * 7,
        scratch_shapes=[
            pltpu.VMEM((buckets, seq, part, hidden), BF16),
            pltpu.VMEM((buckets, seq, part, hidden), BF16),
            pltpu.VMEM((buckets, hidden // buckets, width), BF16),
            pltpu.VMEM(tall, BF16),
            pltpu.VMEM(tall, BF16),
            *([pltpu.VMEM(flat, BF16)] * 3),
            pltpu.VMEM((chunks, seq * thin, hidden), F32),
            pltpu.VMEM((chunks, seq * thin, hidden), F32),
            pltpu.VMEM((rows, width), F32),
            pltpu.VMEM((rows, width), F32),
            pltpu.VMEM((rows, width), F32),
            pltpu.VMEM((chunks, seq, thin, width), BF16),
            blocks,
            blocks,
            pltpu.VMEM((rows, 128), F32),
            pltpu.SemaphoreType.DMA((n_sems,)),
            pltpu.SemaphoreType.DMA((n_sems,)),
            *[pltpu.VMEM(shape, BF16) for shape in shapes],
            *scratch,
        ],
        compiler_params=pltpu.CompilerParams(
            collective_id=11, has_side_effects=True, vmem_limit_bytes=62 * 2**20
        ),
    )(
        mixed.reshape(seq, rows, mixed.shape[1]),
        w_out,
        tokens,
        cotangent,
        counts,
        gain_rows,
        mod_rows,
        w_gate,
        w_up,
        w_down,
    )
    return results[:4], [out.reshape(-1, out.shape[-1]) for out in results[4:]]


def backward_kernel(buckets, seq, kinds, *refs):
    count = len(kinds)
    (
        d_attn,
        w_query,
        w_key,
        w_value,
        w_out,
        query,
        key,
        value,
        cap_key,
        cap_value,
        cross_out,
        query_raw,
        key_raw,
        cap_raw,
        gain_rows,
        mod_rows,
        counts,
        cap_lens,
        mixed,
        hidden,
        captions,
        tokens,
        d_tokens,
        row_sums,
    ) = refs[:24]
    tokens_grad, mod_all, small_out, refs = refs[24], refs[25], refs[26], refs[27:]
    outs, refs = refs[:count], refs[count:]
    mixed_low, cross_low, query_acc, key_acc, value_acc, cap_key_acc, cap_value_acc = refs[:7]
    d_query, d_key, d_value, d_cap_key, d_cap_value, d_hidden, vec = refs[7:14]
    mod_give, mod_got, mod_sum, wide_give, wide_got, slim_give, slim_got = refs[14:21]
    key_bias, cap_bias, parts, from_left, from_right, send, recv = refs[21:28]
    grads, refs = refs[28 : 28 + count], refs[28 + count :]
    b, s = lax.axis_index("bucket"), lax.axis_index("seq")
    copies = Copies(send, recv)
    sums = GradSums(copies, b, s, buckets, seq, kinds, grads, outs, refs, near=True)
    peers = greet_all(b, s, buckets, seq)

    rows, share = query.shape
    width = parts.shape[-1]
    pairs = share // 128
    chips = buckets // 2
    span_block = 256
    scale = HEAD_DIM**-0.5

    def gain_of(row, pair):
        at = pl.multiple_of(s * share + pair * 128, 128)
        return gain_rows[row : row + 1, pl.ds(at, 128)]

    vec[...] = jnp.zeros_like(vec)
    mod_give[...] = jnp.zeros_like(mod_give)
    wide_give[...] = jnp.zeros_like(wide_give)
    slim_give[...] = jnp.zeros_like(slim_give)
    fill_rows(key_bias, counts[b], 0, 0.0, -1e30)
    fill_rows(cap_bias, cap_lens[b], 0, 0.0, -1e30)
    mixed_low[...] = right_dot(d_attn[...], w_out[...]).astype(BF16)

    def own_sum(row, pair, total):
        vec[row : row + 1, pl.ds(pl.multiple_of(s * share + pair * 128, 128), 128)] = total

    def cross_part(pair):
        lane = slice(pair * 128, (pair + 1) * 128)
        gate = jnp.tanh(gain_of(7, pair))

        def body(i, total):
            at = pl.ds(pl.multiple_of(i * 128, 128), 128)
            d = mixed_low[at, lane].astype(F32)
            cross_low[at, lane] = (gate * d).astype(BF16)
            return total + jnp.sum(d * cross_out[at, lane], axis=0, keepdims=True)

        total = lax.fori_loop(0, rows // 128, body, jnp.zeros((1, 128), F32))
        own_sum(7, pair, total * (1.0 - gate * gate))

    def attend_back(pair, k_ref, v_ref, bias, d_ref, k_acc, v_acc, add):
        lane = slice(pair * 128, (pair + 1) * 128)
        low = low_half((span_block, 128))
        k_turned = k_ref[:, lane].T
        k_acc[:, lane] = jnp.zeros((k_acc.shape[0], 128), F32)
        v_acc[:, lane] = jnp.zeros((v_acc.shape[0], 128), F32)

        def body(i, carry):
            at = pl.ds(pl.multiple_of(i * span_block, span_block), span_block)
            q = query[at, lane] * jnp.asarray(scale, BF16)
            d = d_ref[at, lane]
            found = []
            for keep in (low, jnp.logical_not(low)):
                q_half = jnp.where(keep, q, jnp.zeros_like(q))
                d_half = jnp.where(keep, d, jnp.zeros_like(d))
                scores = right_dot(k_ref[:, lane], q_half)
                scores = scores + jnp.concatenate([bias[...], bias[...]], axis=1)
                weights = jnp.exp(scores)
                probs = weights * (1.0 / jnp.sum(weights, axis=0, keepdims=True))
                d_probs = right_dot(v_ref[:, lane], d_half)
                delta = jnp.sum(probs * d_probs, axis=0, keepdims=True)
                d_scores = (probs * (d_probs - delta)).astype(BF16)
                k_acc[:, lane] += bf_dot(d_scores, q_half)
                v_acc[:, lane] += bf_dot(probs.astype(BF16), d_half)
                found.append(bf_dot(k_turned, d_scores))
            turned = jnp.concatenate([found[0][:HEAD_DIM], found[1][HEAD_DIM:]], axis=0)
            d_q = turned.T * scale
            query_acc[at, lane] = query_acc[at, lane] + d_q if add else d_q
            return carry

        lax.fori_loop(0, rows // span_block, body, 0)

    def norm_back(raw, d_norm, out, row, sum_row):
        for pair in range(pairs):
            lane = slice(pair * 128, (pair + 1) * 128)
            gain = gain_of(row, pair)

            def body(i, total):
                at = pl.ds(pl.multiple_of(i * 128, 128), 128)
                x, d = raw[at, lane], d_norm[at, lane]
                size = pair_scale(x, 1e-06)
                normed, inner = x * size, d * gain
                mean = pair_sums(inner * normed) * (1.0 / HEAD_DIM)
                out[at, lane] = (size * (inner - normed * mean)).astype(BF16)
                return total + jnp.sum(d * normed, axis=0, keepdims=True)

            total = lax.fori_loop(0, raw.shape[0] // 128, body, jnp.zeros((1, 128), F32))
            own_sum(sum_row, pair, total)

    def weight_grads(left, chosen):
        part = left.shape[1] // chips
        for i in range(chips):
            turned = left[:, i * part : (i + 1) * part].T
            for w, right in chosen:
                total = bf_dot(turned, right[...])
                grads[w][i] = total.astype(BF16).reshape(2, part // 2, total.shape[-1])
            yield
        for w, _ in chosen:
            sums.begin(w)

    def out_grad():
        total = bf_dot(mixed[...].T, d_attn[...]).astype(BF16)
        part = share // buckets
        for block, p in enumerate(spread(buckets)):
            grads[0][p // 2, p % 2] = total[block * part : (block + 1) * part]
        sums.begin(0)

    pl.semaphore_wait(pltpu.get_barrier_semaphore(), peers)
    for pair in range(pairs):
        cross_part(pair)
        attend_back(pair, cap_key, cap_value, cap_bias, cross_low, cap_key_acc, cap_value_acc, False)
    norm_back(cap_raw, cap_key_acc, d_cap_key, 6, 6)
    d_cap_value[...] = cap_value_acc[...].astype(BF16)
    for _ in weight_grads(captions, ((1, d_cap_key), (2, d_cap_value))):
        pass
    steps = (lambda: sums.stage_a(1), lambda: sums.stage_a(2), lambda: sums.stage_b(1))
    for pair in range(pairs):
        attend_back(pair, key, value, key_bias, mixed_low, key_acc, value_acc, True)
        steps[pair]()
    norm_back(query_raw, query_acc, d_query, 4, 4)
    norm_back(key_raw, key_acc, d_key, 5, 5)
    d_value[...] = value_acc[...].astype(BF16)
    pour = Pour(copies, parts, from_left, from_right, b, s, seq)
    wide = 512
    for at in range(0, width, wide):
        cols = slice(at, at + wide)
        total = right_dot(d_query[...], w_query[cols, :]) + right_dot(d_key[...], w_key[cols, :])
        total = total + right_dot(d_value[...], w_value[cols, :])
        parts[:, :, cols] = total.astype(BF16).reshape(seq, rows // seq, wide)
    pieces = weight_grads(hidden, ((3, d_query), (4, d_key), (5, d_value)))
    between = {1: out_grad, 2: lambda: sums.stage_b(2)}
    for q in range(pour.count):
        pour.step(q)
        if q in between:
            between[q]()
        elif q > 2:
            next(pieces, None)
    for _ in pieces:
        pass
    sums.stage_a(0)
    sums.stage_c(1)
    sums.stage_c(2)
    pour.end(d_hidden)

    factor = gain_rows[0:1, :] * (1.0 + mod_rows[0:1, :])

    def body(i, total):
        at = pl.ds(pl.multiple_of(i * 16, 16), 16)
        x, d = tokens[at, :].astype(F32), d_hidden[at, :]
        size = lax.rsqrt(jnp.mean(x * x, axis=-1, keepdims=True) + 1e-05)
        normed, inner = x * size, d * factor
        mean = jnp.mean(inner * normed, axis=-1, keepdims=True)
        tokens_grad[at, :] = d_tokens[at, :] + size * (inner - normed * mean)
        return total + jnp.sum(d * normed, axis=0, keepdims=True)

    total = lax.fori_loop(0, tokens.shape[0] // 16, body, jnp.zeros((1, width), F32))
    post, last = jnp.tanh(mod_rows[1:2, :]), jnp.tanh(mod_rows[3:4, :])
    vec[8:9, :] = total * gain_rows[0:1, :]
    vec[9:10, :] = row_sums[0:1, :] * gain_rows[1:2, :] * (1.0 - post * post)
    vec[10:11, :] = row_sums[1:2, :] * gain_rows[2:3, :]
    vec[11:12, :] = row_sums[2:3, :] * gain_rows[3:4, :] * (1.0 - last * last)
    vec[0:1, :] = total * (1.0 + mod_rows[0:1, :])
    vec[1:2, :] = row_sums[0:1, :] * post
    vec[2:3, :] = row_sums[1:2, :] * (1.0 + mod_rows[2:3, :])
    vec[3:4, :] = row_sums[2:3, :] * last
    piece, wide = width // 4, width // buckets
    slim = wide // seq
    for t in range(seq):
        for j in range(4):
            mod_give[t, j : j + 1, :] = vec[8 + t : 9 + t, j * piece : (j + 1) * piece]
    for t in range(buckets):
        wide_give[t, :, :wide] = vec[0:8, t * wide : (t + 1) * wide]
    mod_moves, wide_moves = [], []
    for j in range(1, seq):
        peer = lax.rem(s + j, seq)
        mod_moves.append(sums.go(copies.remote(mod_give.at[peer], mod_got.at[j], b, peer)))
    for j in range(1, buckets):
        peer = lax.rem(b + j, buckets)
        wide_moves.append(sums.go(copies.remote(wide_give.at[peer], wide_got.at[j], peer, s)))
    sums.stage_a(3)
    sums.stage_a(4)
    sums.stage_a(5)
    total = mod_give[s]
    for j, move in enumerate(mod_moves, 1):
        move.wait_recv()
        total = total + mod_got[j]
    mod_sum[...] = total
    mod_next, slim_next = [], []
    for j in range(1, buckets):
        peer = lax.rem(b + j, buckets)
        mod_next.append(sums.go(copies.remote(mod_sum, mod_all.at[b], peer, s)))
    mod_own = copies.local(mod_sum, mod_all.at[b])
    mod_own.start()
    total = wide_give[b]
    for j, move in enumerate(wide_moves, 1):
        move.wait_recv()
        total = total + wide_got[j]
    for t in range(seq):
        slim_give[t, :, :slim] = total[:, t * slim : (t + 1) * slim]
    for j in range(1, seq):
        peer = lax.rem(s + j, seq)
        slim_next.append(sums.go(copies.remote(slim_give.at[peer], slim_got.at[j], b, peer)))
    for w in (0, 3, 4, 5):
        sums.stage_b(w)
    sums.stage_c(0)
    for w in (3, 4, 5):
        sums.stage_c(w)
    sums.stage_d(0)
    total = slim_give[s]
    for j, move in enumerate(slim_next, 1):
        move.wait_recv()
        total = total + slim_got[j]
    small_out[...] = total
    for move in mod_next:
        move.wait_recv()
    mod_own.wait()
    sums.end()


def backward_all(buckets, seq, inputs, shapes, kinds):
    any_spec = pl.BlockSpec(memory_space=pl.ANY)
    vmem = pl.BlockSpec(memory_space=pltpu.VMEM)
    smem = pl.BlockSpec(memory_space=pltpu.SMEM)
    shapes, outs, scratch, n_sems = sums_shapes(buckets, seq, shapes, kinds, near=True)
    query, cap_key, tokens = inputs[5], inputs[8], inputs[21]
    rows, width = tokens.shape
    vec = (16, width)
    n_sems += 12 * seq + 4 * buckets
    results = pl.pallas_call(
        functools.partial(backward_kernel, buckets, seq, tuple(kinds)),
        out_shape=[
            jax.ShapeDtypeStruct((rows, width), F32),
            jax.ShapeDtypeStruct((buckets, 8, width // 4), F32),
            jax.ShapeDtypeStruct((8, 128), F32),
            *outs,
        ],
        in_specs=[vmem] * 16 + [smem] * 2 + [vmem] * (len(inputs) - 18),
        out_specs=[vmem, any_spec, vmem] + [vmem] * len(outs),
        scratch_shapes=[
            pltpu.VMEM(query.shape, BF16),
            pltpu.VMEM(query.shape, BF16),
            pltpu.VMEM(query.shape, F32),
            pltpu.VMEM(query.shape, F32),
            pltpu.VMEM(query.shape, F32),
            pltpu.VMEM(cap_key.shape, F32),
            pltpu.VMEM(cap_key.shape, F32),
            pltpu.VMEM(query.shape, BF16),
            pltpu.VMEM(query.shape, BF16),
            pltpu.VMEM(query.shape, BF16),
            pltpu.VMEM(cap_key.shape, BF16),
            pltpu.VMEM(cap_key.shape, BF16),
            pltpu.VMEM((rows, width), F32),
            pltpu.VMEM(vec, F32),
            pltpu.VMEM((seq, 8, width // 4), F32),
            pltpu.VMEM((seq, 8, width // 4), F32),
            pltpu.VMEM((8, width // 4), F32),
            pltpu.VMEM((buckets, 8, 256), F32),
            pltpu.VMEM((buckets, 8, 256), F32),
            pltpu.VMEM((seq, 8, 128), F32),
            pltpu.VMEM((seq, 8, 128), F32),
            pltpu.VMEM((query.shape[0], 128), F32),
            pltpu.VMEM((cap_key.shape[0], 128), F32),
            pltpu.VMEM((seq, rows, width), BF16),
            pltpu.VMEM((seq - 1, rows, width), BF16),
            pltpu.VMEM((seq - 1, rows, width), BF16),
            pltpu.SemaphoreType.DMA((n_sems,)),
            pltpu.SemaphoreType.DMA((n_sems,)),
            *[pltpu.VMEM(shape, BF16) for shape in shapes],
            *scratch,
        ],
        compiler_params=pltpu.CompilerParams(
            collective_id=10, has_side_effects=True, vmem_limit_bytes=62 * 2**20
        ),
    )(*inputs)
    sums = [out.reshape(-1, out.shape[-1]) for out in results[3:]]
    return results[0], results[1], results[2], sums


def last_kernel(buckets, seq, slim, *refs):
    cond, mod_all, small = refs[:3]
    count = (len(refs) - 7) // 2
    sources, refs = refs[3 : 3 + count], refs[3 + count :]
    mod_grad, gains, cross = refs[:3]
    targets, sems = refs[3 : 3 + count], refs[3 + count]
    copies = [
        pltpu.make_async_copy(a, b, sems.at[i])
        for i, (a, b) in enumerate(zip(sources, targets, strict=True))
    ]
    for copy in copies:
        copy.start()
    piece = mod_all.shape[2]
    for j in range(4):
        total = None
        for k in range(buckets):
            term = cond[:, k : k + 1] * mod_all[k, j : j + 1, :]
            total = term if total is None else total + term
        mod_grad[:, j * piece : (j + 1) * piece] = total
    gains[...] = small[0:7, :slim]
    cross[...] = small[7:8, :slim]
    for copy in copies:
        copy.wait()


def last_all(buckets, seq, slim, cond, mod_all, small, results):
    any_spec = pl.BlockSpec(memory_space=pl.ANY)
    vmem = pl.BlockSpec(memory_space=pltpu.VMEM)
    outs = pl.pallas_call(
        functools.partial(last_kernel, buckets, seq, slim),
        out_shape=[
            jax.ShapeDtypeStruct((cond.shape[0], 4 * mod_all.shape[2]), F32),
            jax.ShapeDtypeStruct((7, slim), F32),
            jax.ShapeDtypeStruct((1, slim), F32),
            *[jax.ShapeDtypeStruct(x.shape, x.dtype) for x in results],
        ],
        in_specs=[vmem] * 3 + [any_spec] * len(results),
        out_specs=[vmem] * (3 + len(results)),
        scratch_shapes=[pltpu.SemaphoreType.DMA((len(results),))],
        compiler_params=pltpu.CompilerParams(vmem_limit_bytes=62 * 2**20),
    )(cond, mod_all, small, *results)
    return outs[0], outs[1], outs[2].reshape(slim), outs[3:]


def on_device(
    tokens,
    captions,
    cotangent,
    counts,
    cap_lens,
    steps_t,
    w_query,
    w_key,
    w_value,
    w_out,
    w_cap_key,
    w_cap_value,
    w_gate,
    w_up,
    w_down,
    w_mod,
    gains,
    cross_gate,
):
    buckets, seq = lax.axis_size("bucket"), lax.axis_size("seq")
    b, s = lax.axis_index("bucket"), lax.axis_index("seq")
    place = b * seq + s
    rows, width = tokens.shape
    span = rows * seq
    share = width // seq

    cond_size = w_mod.shape[0] * buckets * seq
    cond = jax.nn.silu(time_embed(steps_t, cond_size)).astype(BF16)
    cond_part = lax.dynamic_slice_in_dim(cond, place * w_mod.shape[0], w_mod.shape[0], 1)
    slim = gains.shape[1]
    small = jnp.concatenate([gains, cross_gate[None]], axis=0).astype(F32)
    small = jnp.pad(small, ((0, 0), (0, 128 - slim)))
    feed = [w_gate, w_up, w_down]
    early = [w for w in range(3) if w not in MOVED]
    cap_all, weights, inner = forward_all(
        buckets,
        seq,
        tokens,
        captions,
        small,
        slim,
        cond_part,
        w_mod,
        [counts, cap_lens],
        [w_query, w_key, w_value, w_cap_key, w_cap_value, w_out, *(feed[w] for w in early)],
        ["col", "col", "col", "col", "col", "row", *(("cut", "cut", "stay")[w] for w in early)],
    )
    wq, wk, wv, wck, wcv, wo = (x.reshape(-1, x.shape[-1]) for x in weights[:6])
    for w, full in zip(early, weights[6:], strict=True):
        feed[w] = full
    caps = cap_all.reshape(-1, captions.shape[1])
    small_rows, mod, hidden, query_proj, key_proj, cap_proj = inner[:6]
    query, key, value, cap_key, cap_value = inner[6:11]
    cross_out, mixed_low = inner[11:]
    (block_out, d_tokens, d_attn_all, row_sums), (s_gate, s_up, s_down) = middle_all(
        buckets,
        seq,
        mixed_low,
        (wo, *feed),
        tokens,
        cotangent,
        counts,
        small_rows,
        mod,
    )
    tokens_grad, mod_all, small_sums, sums = backward_all(
        buckets,
        seq,
        [
            d_attn_all.reshape(span, width),
            wq,
            wk,
            wv,
            wo,
            query,
            key,
            value,
            cap_key,
            cap_value,
            cross_out,
            query_proj,
            key_proj,
            cap_proj,
            small_rows,
            mod,
            counts,
            cap_lens,
            mixed_low,
            hidden,
            caps,
            tokens,
            d_tokens,
            row_sums,
        ],
        [x.shape for x in (wo, wck, wcv, wq, wk, wv)],
        ["row", "col", "col", "col", "col", "col"],
    )
    s_out, s_cap_key, s_cap_value, s_query, s_key, s_value = sums

    cond_size = cond.shape[1] // buckets
    cond_cols = lax.dynamic_slice_in_dim(cond, b * cond_size, cond_size, 1).astype(F32).T
    results = [block_out, tokens_grad, s_query, s_key, s_value, s_out]
    results += [s_cap_key, s_cap_value, s_gate, s_up, s_down]
    s_mod, s_gains, s_cross, results = last_all(
        buckets, seq, slim, cond_cols, mod_all, small_sums, results
    )
    return (*results, s_mod, s_gains, s_cross)


def solution(mesh):
    spread = P(("bucket", "seq"), None)
    in_specs = (
        *([spread] * 3),
        *([P()] * 3),
        *([spread] * 10),
        P(None, ("bucket", "seq")),
        P(("bucket", "seq")),
    )
    out_specs = (
        spread,
        spread,
        *([P("bucket", "seq")] * 10),
        P(None, ("bucket", "seq")),
        P(("bucket", "seq")),
    )
    buckets, seq = mesh.shape["bucket"], mesh.shape["seq"]

    def step(*args):
        tokens, weight = args[0], args[6]
        tiled = weight.shape[0] % 16 == 0 and weight.shape[1] // seq % 128 == 0
        fits = buckets == 8 and seq == 4 and tokens.shape[0] % 64 == 0
        return (on_device if tiled and fits else on_device_general)(*args)

    return jax.shard_map(
        step, mesh=mesh, in_specs=in_specs, out_specs=out_specs, check_vma=False
    )
```

```python
import functools
import math

import jax
import jax.numpy as jnp
from jax import lax
from jax.experimental import pallas as pl
from jax.experimental.pallas import tpu as pltpu
from jax.sharding import PartitionSpec as P

HEAD_DIM = 64
MESH = pl.DeviceIdType.MESH
F32, BF16 = jnp.float32, jnp.bfloat16
CHUNKS, CUTS, FLIGHT = 2, 2, 2


def rms_rows(values):
    return values * lax.rsqrt(jnp.mean(values * values, axis=-1, keepdims=True) + 1e-05)


def head_rms(values):
    shaped = values.reshape(values.shape[:-1] + (values.shape[-1] // HEAD_DIM, HEAD_DIM))
    shaped = shaped * lax.rsqrt(jnp.mean(shaped * shaped, axis=-1, keepdims=True) + 1e-06)
    return shaped.reshape(values.shape)


def time_embed(steps, width):
    half_width = width // 2
    freqs = jnp.exp(-math.log(10000.0) * jnp.arange(half_width, dtype=F32) / half_width)
    angles = steps.astype(F32)[:, None] * freqs
    return jnp.concatenate([jnp.cos(angles), jnp.sin(angles)], axis=1)


def pick_entry(table, index):
    return jnp.sum(jnp.where(jnp.arange(table.shape[0]) == index, table, 0))


def bf_dot(left, right):
    return jnp.dot(left, right, preferred_element_type=F32)


def left_dot(rows_left, rows_right):
    return lax.dot_general(
        rows_left, rows_right, (((0,), (0,)), ((), ())), preferred_element_type=F32
    )


def right_dot(left, right):
    return lax.dot_general(left, right, (((1,), (1,)), ((), ())), preferred_element_type=F32)


def pre_attn(tokens_in, gain_pre, scale_attn):
    return rms_rows(tokens_in) * gain_pre * (1.0 + scale_attn)


def qk_norm(query_in, key_in, gain_query, gain_key):
    return (head_rms(query_in) * gain_query, head_rms(key_in) * gain_key)


def cap_norm(key_in, gain_cap):
    return head_rms(key_in) * gain_cap


def middle(tokens_in, attn_out, gain_post, gate_attn, gain_ffn, scale_ffn):
    resid_one = tokens_in + jnp.tanh(gate_attn) * rms_rows(attn_out) * gain_post
    return (resid_one, rms_rows(resid_one) * gain_ffn * (1.0 + scale_ffn))


def activate(gate_proj, up_proj):
    return jax.nn.silu(gate_proj) * up_proj


def finish(resid_one, ffn_out, gain_last, gate_ffn):
    return resid_one + jnp.tanh(gate_ffn) * rms_rows(ffn_out) * gain_last


def flip(index, bit):
    return index + bit - 2 * bit * lax.rem(lax.div(index, bit), 2)


def slot(index, buckets):
    if buckets != 8:
        return index
    high, low = lax.div(index, 4), lax.rem(index, 4)
    return 4 * high + 2 * lax.rem(low, 2) + lax.div(low, 2)


class Copies:
    def __init__(self, send, recv):
        self.send, self.recv, self.used = send, recv, 0

    def take(self, count=1):
        first = self.used
        self.used += count
        assert self.used <= self.send.shape[0], self.used
        return first

    def remote(self, src, dst, b, s, at=None):
        at = self.take() if at is None else at
        return pltpu.make_async_remote_copy(
            src_ref=src,
            dst_ref=dst,
            send_sem=self.send.at[at],
            recv_sem=self.recv.at[at],
            device_id={"bucket": b, "seq": s},
            device_id_type=MESH,
        )

    def local(self, src, dst):
        return pltpu.make_async_copy(src, dst, self.send.at[self.take()])


def greet(b, s):
    pl.semaphore_signal(
        pltpu.get_barrier_semaphore(),
        inc=1,
        device_id={"bucket": b, "seq": s},
        device_id_type=MESH,
    )


class Relay:
    def __init__(self, copies, own, out, b, s, seq, part=None):
        self.copies, self.own, self.out, self.b, self.s, self.seq = copies, own, out, b, s, seq
        self.part = part
        self.base = {1: copies.take(seq - 1), -1: copies.take(seq - 1)}
        self.up = jnp.where(s < seq - 1, s + 1, s - 1)
        self.down = jnp.where(s > 0, s - 1, s + 1)
        self.kept = None if own is None else copies.local(own, out.at[s])

    def packet(self, way, j):
        at = self.s - way * j
        block = self.out.at[at] if self.part is None else self.out.at[at, self.part]
        return self.copies.remote(
            self.own if j == 0 and self.own is not None else block,
            block,
            self.b,
            self.up if way > 0 else self.down,
            self.base[way] + j,
        )

    def sends(self, way):
        return self.s < self.seq - 1 if way > 0 else self.s > 0

    def has(self, way, j):
        return self.s >= j if way > 0 else self.s + j <= self.seq - 1

    def start(self, j):
        if j == 0 and self.kept is not None:
            self.kept.start()
        for way in (1, -1):
            if j == self.seq - 1:

                @pl.when(jnp.logical_not(self.sends(way)))
                def _():
                    for k in range(self.seq - 1):
                        self.packet(way, k).wait_recv()

                continue

            @pl.when(jnp.logical_and(self.sends(way), self.has(way, j)))
            def _():
                if j > 0:
                    self.packet(way, j - 1).wait_recv()
                self.packet(way, j).start()

    def sent(self, j):
        for way in (1, -1):

            @pl.when(jnp.logical_and(self.sends(way), self.has(way, j)))
            def _():
                self.packet(way, j).wait_send()

        if j == 0 and self.kept is not None:
            self.kept.wait()


def greet_line(b, s, seq):
    @pl.when(s > 0)
    def _():
        greet(b, s - 1)

    @pl.when(s < seq - 1)
    def _():
        greet(b, s + 1)

    peers = jnp.where(s > 0, 1, 0) + jnp.where(s < seq - 1, 1, 0)
    pl.semaphore_wait(pltpu.get_barrier_semaphore(), peers)


def halves_of(shape):
    if len(shape) == 3:
        return shape[0] // 2
    return (shape[0] // 32) * 16 if shape[0] >= 32 else shape[0] // 2


def gather_kernel(buckets, seq, kinds, *refs):
    count = len(kinds)
    tokens, captions, small, cond, w_mod = refs[:5]
    shards = refs[5 : 5 + count]
    tok_all, cap_all, small_all, mod_out = refs[5 + count : 9 + count]
    fulls = refs[9 + count : 9 + 2 * count]
    part, got_bucket, got_seq, mod_sum, send, recv = refs[9 + 2 * count :]
    b, s = lax.axis_index("bucket"), lax.axis_index("seq")
    copies = Copies(send, recv)
    chips = buckets // 2
    place = b * seq + s
    to_b, to_s = lax.rem(place, buckets), lax.div(place, buckets)
    back = s * buckets + b
    from_b, from_s = lax.div(back, seq), lax.rem(back, seq)
    stays = jnp.logical_and(to_b == b, to_s == s)

    lanes = part.shape[2]
    for j in range(part.shape[1]):
        part[:, j, :] = bf_dot(cond[...], w_mod[:, j * lanes : (j + 1) * lanes])

    for k in range(1, buckets):
        greet(lax.rem(b + k, buckets), s)
    for k in range(1, seq):
        greet(b, lax.rem(s + k, seq))

    @pl.when(jnp.logical_not(stays))
    def _():
        greet(from_b, from_s)

    peers = buckets - 1 + seq - 1 + jnp.where(stays, 0, 1)
    pl.semaphore_wait(pltpu.get_barrier_semaphore(), peers)

    sent = []

    def go(copy):
        copy.start()
        sent.append(copy)
        return copy

    mod_moves = []
    for k in range(1, buckets):
        peer = lax.rem(b + k, buckets)
        mod_moves.append(go(copies.remote(part.at[peer], got_bucket.at[k], peer, s)))
    small_moves = []
    for k in range(1, seq):
        peer = lax.rem(s + k, seq)
        small_moves.append(go(copies.remote(small, small_all.at[b, s], b, peer)))
    small_own = copies.local(small, small_all.at[b, s])
    small_own.start()

    tok = Relay(copies, tokens, tok_all, b, s, seq)
    cap = Relay(copies, captions, cap_all, b, s, seq)
    queue = [(tok, j) for j in range(seq)] + [(cap, j) for j in range(seq)]
    ahead = [(None, at) for at in range(count)]
    items = []
    while queue or ahead:
        items += queue[:1] + ahead[:1]
        queue, ahead = queue[1:], ahead[1:]

    first = [None] * count

    def depart(at):
        kind, shard, full = kinds[at], shards[at], fulls[at]
        if kind == "row":
            move = copies.remote(shard, full.at[to_b], to_b, to_s)
            keep = copies.local(shard, full.at[b])

            @pl.when(jnp.logical_not(stays))
            def _():
                move.start()

            @pl.when(stays)
            def _():
                keep.start()

            first[at] = (move, keep)
            return
        wide = full.shape[-1]

        def columns(peer):
            if kind == "cut":
                return shard.at[peer]
            return shard.at[:, pl.ds(pl.multiple_of(peer * wide, 128), wide)]

        moves = []
        for k in range(1, seq):
            peer = lax.rem(s + k, seq)
            move = copies.remote(columns(peer), full.at[b, s], b, peer)
            move.start()
            moves.append(move)
        keep = copies.local(columns(s), full.at[b, s])
        keep.start()
        first[at] = (moves, keep)

    def arrived(at):
        moves, keep = first[at]
        if kinds[at] == "row":

            @pl.when(jnp.logical_not(stays))
            def _():
                moves.wait()

            @pl.when(stays)
            def _():
                keep.wait()

            return
        for move in moves:
            move.wait()
        keep.wait()

    twin = flip(b, 1)
    second = [None] * count
    if chips == 4:
        near_x, near_y = flip(b, 2), flip(b, 4)
        far = flip(near_x, 4)

        def stage_a(at):
            full = fulls[at]
            second[at] = {
                "x": go(copies.remote(full.at[b], full.at[b], near_x, s)),
                "y": go(copies.remote(full.at[b], full.at[b], near_y, s)),
                "twin": [go(copies.remote(full.at[b], full.at[b], twin, s))],
            }

        def stage_b(at):
            full, now = fulls[at], second[at]
            cut = halves_of(full.shape[1:])
            now["x"].wait_recv()
            block = full.at[near_x, pl.ds(0, cut)]
            now["dy"] = go(copies.remote(block, block, near_y, s))
            block = full.at[near_x]
            now["twin"].append(go(copies.remote(block, block, twin, s)))
            now["y"].wait_recv()
            block = full.at[near_y, pl.ds(cut, full.shape[1] - cut)]
            now["dx"] = go(copies.remote(block, block, near_x, s))
            block = full.at[near_y]
            now["twin"].append(go(copies.remote(block, block, twin, s)))

        def stage_c(at):
            full, now = fulls[at], second[at]
            now["dy"].wait_recv()
            now["dx"].wait_recv()
            block = full.at[far]
            now["twin"].append(go(copies.remote(block, block, twin, s)))

    else:

        def stage_a(at):
            full = fulls[at]
            second[at] = {"far": [], "twin": []}
            for k in range(1, chips):
                peer = lax.rem(b + 2 * k, buckets)
                second[at]["far"].append(go(copies.remote(full.at[b], full.at[b], peer, s)))
            second[at]["twin"].append(go(copies.remote(full.at[b], full.at[b], twin, s)))

        def stage_b(at):
            full = fulls[at]
            for k, copy in enumerate(second[at]["far"], 1):
                copy.wait_recv()
                block = full.at[lax.rem(b + buckets - 2 * k, buckets)]
                second[at]["twin"].append(go(copies.remote(block, block, twin, s)))

        def stage_c(at):
            pass

    def begin(i):
        relay, j = items[i]
        if relay is None:
            depart(j)
        else:
            relay.start(j)

    begin(0)
    begin(1)
    for move in small_moves:
        move.wait_recv()
    small_own.wait()
    small_next = []
    for k in range(1, buckets):
        peer = lax.rem(b + k, buckets)
        small_next.append(go(copies.remote(small_all.at[b], small_all.at[b], peer, s)))
    total = part[b]
    for k, move in enumerate(mod_moves, 1):
        move.wait_recv()
        total = total + got_bucket[k]
    mod_sum[...] = total
    mod_next = []
    for k in range(1, seq):
        peer = lax.rem(s + k, seq)
        mod_next.append(go(copies.remote(mod_sum, got_seq.at[k], b, peer)))

    for i, (relay, j) in enumerate(items):
        if relay is None:
            arrived(j)
        elif j <= seq - 2:
            relay.sent(j)
        if i + 2 < len(items):
            begin(i + 2)
        if relay is None:
            stage_a(j)
            if j >= 1:
                stage_b(j - 1)
            if j >= 2:
                stage_c(j - 2)
    stage_b(count - 1)
    if count >= 2:
        stage_c(count - 2)
    stage_c(count - 1)

    total = mod_sum[...]
    for k, move in enumerate(mod_next, 1):
        move.wait_recv()
        total = total + got_seq[k]
    mod_out[...] = total
    for move in small_next:
        move.wait_recv()
    for now in second:
        for move in now["twin"]:
            move.wait_recv()
    for move in sent:
        move.wait_send()


def gather_all(buckets, seq, tokens, captions, small, cond, w_mod, shards, kinds):
    any_spec = pl.BlockSpec(memory_space=pl.ANY)
    vmem = pl.BlockSpec(memory_space=pltpu.VMEM)
    fulls, inputs, names = [], [], []
    for shard, kind in zip(shards, kinds, strict=True):
        rows, wide = shard.shape
        if kind == "row":
            fulls.append(jax.ShapeDtypeStruct((buckets, rows, wide), BF16))
        else:
            part = wide // seq
            fulls.append(jax.ShapeDtypeStruct((buckets, seq, rows, part), BF16))
            if part % 128:
                kind = "cut"
                shard = shard.reshape(rows, seq, part).transpose(1, 0, 2)
        inputs.append(shard)
        names.append(kind)
    mod_lanes = w_mod.shape[1] // 8
    n_sems = 64 + 16 * buckets + len(shards) * (seq + 2 * buckets)
    outs = pl.pallas_call(
        functools.partial(gather_kernel, buckets, seq, tuple(names)),
        out_shape=[
            jax.ShapeDtypeStruct((seq,) + tokens.shape, BF16),
            jax.ShapeDtypeStruct((seq,) + captions.shape, BF16),
            jax.ShapeDtypeStruct((buckets, seq) + small.shape, F32),
            jax.ShapeDtypeStruct((8, mod_lanes), F32),
            *fulls,
        ],
        in_specs=[any_spec, any_spec, any_spec, vmem, vmem] + [any_spec] * len(shards),
        out_specs=[any_spec, any_spec, any_spec, vmem] + [any_spec] * len(shards),
        scratch_shapes=[
            pltpu.VMEM((buckets, 8, mod_lanes), F32),
            pltpu.VMEM((buckets, 8, mod_lanes), F32),
            pltpu.VMEM((seq, 8, mod_lanes), F32),
            pltpu.VMEM((8, mod_lanes), F32),
            pltpu.SemaphoreType.DMA((n_sems,)),
            pltpu.SemaphoreType.DMA((n_sems,)),
        ],
        compiler_params=pltpu.CompilerParams(
            collective_id=0, has_side_effects=True, vmem_limit_bytes=24 * 2**20
        ),
    )(tokens, captions, small, cond, w_mod, *inputs)
    weights = []
    for full, kind in zip(outs[4:], names, strict=True):
        weights.append(full.reshape(-1, full.shape[-1]))
    return outs[0], outs[1], outs[2], outs[3], weights


def line_gather_kernel(seq, own, out, send, recv):
    b, s = lax.axis_index("bucket"), lax.axis_index("seq")
    greet_line(b, s, seq)
    relay = Relay(Copies(send, recv), own, out, b, s, seq)
    for j in range(seq):
        relay.start(j)
    for j in range(seq - 1):
        relay.sent(j)


def line_gather(seq, own, collective_id):
    return pl.pallas_call(
        functools.partial(line_gather_kernel, seq),
        out_shape=jax.ShapeDtypeStruct((seq,) + own.shape, own.dtype),
        in_specs=[pl.BlockSpec(memory_space=pl.ANY)],
        out_specs=pl.BlockSpec(memory_space=pl.ANY),
        scratch_shapes=[pltpu.SemaphoreType.DMA((2 * seq + 2,))] * 2,
        compiler_params=pltpu.CompilerParams(collective_id=collective_id, has_side_effects=True),
    )(own).reshape(-1, own.shape[-1])


def add_rows(out, terms):
    rows = out.shape[0]
    step = 16 if rows % 16 == 0 else rows

    def body(i, carry):
        at = pl.ds(pl.multiple_of(i * step, step), step)
        total = terms[0][at, :].astype(F32)
        for term in terms[1:]:
            total = total + term[at, :].astype(F32)
        out[at, :] = total.astype(out.dtype)
        return carry

    lax.fori_loop(0, rows // step, body, 0)


class Pour:
    def __init__(self, copies, parts, from_left, from_right, b, s, seq):
        self.copies, self.parts, self.b, self.s, self.seq = copies, parts, b, s, seq
        self.got = {1: from_left, -1: from_right}
        rows = parts.shape[1]
        self.cuts = CUTS if rows % (16 * CUTS) == 0 else 1
        self.thin = rows // self.cuts
        self.count = (seq - 1) * self.cuts
        self.base = {1: copies.take(self.count), -1: copies.take(self.count)}
        self.next = {
            1: jnp.where(s < seq - 1, s + 1, s - 1),
            -1: jnp.where(s > 0, s - 1, s + 1),
        }

    def block(self, way, q):
        j, at = q // self.cuts, pl.ds(q % self.cuts * self.thin, self.thin)
        return self.parts.at[self.seq - 1 - j if way > 0 else j, at], self.got[way].at[j, at]

    def packet(self, way, q):
        src, dst = self.block(way, q)
        return self.copies.remote(src, dst, self.b, self.next[way], self.base[way] + q)

    def on(self, way, q):
        j = q // self.cuts
        return self.s < self.seq - 1 - j if way > 0 else self.s > j

    def behind(self, way):
        return self.s > 0 if way > 0 else self.s < self.seq - 1

    def one(self, way, q):
        src, dst = self.block(way, q)

        @pl.when(jnp.logical_and(self.behind(way), self.on(way, q)))
        def _():
            self.packet(way, q).wait_recv()
            add_rows(src, [src, dst])

        @pl.when(self.on(way, q))
        def _():
            if q >= FLIGHT:
                self.packet(way, q - FLIGHT).wait_send()
            self.packet(way, q).start()

    def step(self, q):
        @pl.when(self.s < self.seq // 2)
        def _():
            self.one(1, q)
            self.one(-1, q)

        @pl.when(self.s >= self.seq // 2)
        def _():
            self.one(-1, q)
            self.one(1, q)

    def end(self, out):
        seq, cuts = self.seq, self.cuts
        for t in range(seq):

            @pl.when(self.s == t)
            def _():
                terms = [self.parts.at[t]]
                for way, j in ((1, seq - 1 - t), (-1, t)):
                    if j < seq - 1:
                        for c in range(cuts):
                            self.packet(way, j * cuts + c).wait_recv()
                        terms.append(self.got[way].at[j])
                add_rows(out, terms)

        for q in range(self.count):
            more = q + FLIGHT < self.count
            for way in (1, -1):
                last = jnp.logical_not(self.on(way, q + FLIGHT)) if more else True

                @pl.when(jnp.logical_and(self.on(way, q), last))
                def _():
                    self.packet(way, q).wait_send()


def line_scatter_kernel(seq, parts, out, from_left, from_right, send, recv):
    b, s = lax.axis_index("bucket"), lax.axis_index("seq")
    greet_line(b, s, seq)
    pour = Pour(Copies(send, recv), parts, from_left, from_right, b, s, seq)
    for q in range(pour.count):
        pour.step(q)
    pour.end(out)


def line_scatter(seq, parts, collective_id):
    rows, wide = parts.shape[0] // seq, parts.shape[1]
    vmem = pl.BlockSpec(memory_space=pltpu.VMEM)
    return pl.pallas_call(
        functools.partial(line_scatter_kernel, seq),
        out_shape=jax.ShapeDtypeStruct((rows, wide), F32),
        in_specs=[vmem],
        out_specs=vmem,
        input_output_aliases={},
        scratch_shapes=[
            pltpu.VMEM((seq - 1, rows, wide), BF16),
            pltpu.VMEM((seq - 1, rows, wide), BF16),
            pltpu.SemaphoreType.DMA((4 * seq,)),
            pltpu.SemaphoreType.DMA((4 * seq,)),
        ],
        compiler_params=pltpu.CompilerParams(
            collective_id=collective_id, has_side_effects=True, vmem_limit_bytes=24 * 2**20
        ),
    )(parts.astype(BF16).reshape(seq, rows, wide))


class GradSums:
    def __init__(self, copies, b, s, buckets, seq, kinds, grads, outs, scratch, near=False):
        self.near = near
        self.copies, self.b, self.s, self.buckets, self.seq = copies, b, s, buckets, seq
        self.kinds, self.grads, self.outs = kinds, grads, outs
        self.scratch = [scratch[8 * w : 8 * w + 8] for w in range(len(kinds))]
        self.chips = buckets // 2
        self.chip, self.core = lax.div(b, 2), lax.rem(b, 2)
        self.place = s * buckets + slot(b, buckets)
        self.to_b = lax.div(self.place, seq)
        self.twin = flip(b, 1)
        self.begun, self.state, self.last = {}, {}, {}
        self.sent = []

    def go(self, copy):
        copy.start()
        self.sent.append(copy)
        return copy

    def own(self, w, chip, rows=None):
        where = (chip,) if rows is None else (chip, rows)
        if self.near:
            return self.grads[w].at[(chip, self.core, *where[1:])]
        return self.scratch[w][0].at[where]

    def begin(self, w):
        own, other = self.scratch[w][:2]
        grad = self.grads[w]
        swap = self.copies.remote(grad.at[:, 1 - self.core], other, self.twin, self.s)
        swap.start()
        self.begun[w] = [swap]
        if not self.near:
            keep = self.copies.local(grad.at[:, self.core], own)
            keep.start()
            self.begun[w].append(keep)

    def stage_a(self, w):
        _, other, half_x, half_y, got, _ = self.scratch[w][:6]
        for copy in self.begun[w]:
            copy.wait()
        if not self.near and w + 2 in range(len(self.kinds)) and w + 2 not in self.begun:
            self.begin(w + 2)
        rows = other.shape[1]
        if self.chips != 4:
            moves = []
            for k in range(1, self.chips):
                to = lax.rem(self.chip + k, self.chips)
                own = self.own(w, to)
                add_rows(own, [own, other.at[to]])
                move = self.copies.remote(own, got.at[k], 2 * to + self.core, self.s)
                moves.append(self.go(move))
            self.state[w] = moves
            return
        far = flip(flip(self.chip, 1), 2)
        add_rows(self.own(w, far), [self.own(w, far), other.at[far]])
        cut = halves_of(other.shape[1:])
        near_x, near_y = flip(self.b, 2), flip(self.b, 4)
        top, low = self.own(w, far, pl.ds(0, cut)), self.own(w, far, pl.ds(cut, rows - cut))
        self.state[w] = [
            self.go(self.copies.remote(top, half_x, near_x, self.s)),
            self.go(self.copies.remote(low, half_y, near_y, self.s)),
        ]

    def stage_b(self, w):
        if self.chips != 4:
            return
        _, other, half_x, half_y, got_x, got_y = self.scratch[w][:6]
        rows = other.shape[1]
        cut = halves_of(other.shape[1:])
        top, low = pl.ds(0, cut), pl.ds(cut, rows - cut)
        mx, my = flip(self.chip, 1), flip(self.chip, 2)
        move_x, move_y = self.state[w]
        move_x.wait_recv()
        block = self.own(w, my, top)
        add_rows(block, [block, other.at[my, top], half_x])
        block = self.own(w, my, low)
        add_rows(block, [block, other.at[my, low]])
        block = self.own(w, my)
        next_y = self.go(self.copies.remote(block, got_y, flip(self.b, 4), self.s))
        move_y.wait_recv()
        block = self.own(w, mx, low)
        add_rows(block, [block, other.at[mx, low], half_y])
        block = self.own(w, mx, top)
        add_rows(block, [block, other.at[mx, top]])
        block = self.own(w, mx)
        next_x = self.go(self.copies.remote(block, got_x, flip(self.b, 2), self.s))
        self.state[w] = [next_x, next_y]

    def stage_c(self, w):
        _, other, _, _, got_x, got_y, done, landed = self.scratch[w]
        for move in self.state[w]:
            move.wait_recv()
        terms = [self.own(w, self.chip), other.at[self.chip]]
        if self.chips == 4:
            terms += [got_x, got_y]
        else:
            terms += [got_x.at[k] for k in range(1, self.chips)]
        if self.kinds[w] == "col":
            add_rows(self.outs[w], terms)
            return
        seq, send, recv = self.seq, self.copies.send, self.copies.recv
        hold = self.kinds[w] == "hold"
        if hold:
            done = self.outs[w]
        wide = done.shape[-1]
        far = self.kinds[w] == "row"
        to_b, me = (self.to_b, lax.rem(self.place, seq)) if far else (self.b, self.s)
        base = 0 if hold else self.copies.take(2 * seq)
        rows = terms[0].shape[0]
        step = 16 if rows % 16 == 0 else rows

        def body(i, carry):
            at = pl.ds(pl.multiple_of(i * step, step), step)
            total = terms[0][at, :].astype(F32)
            for term in terms[1:]:
                total = total + term[at, :].astype(F32)
            for t in range(seq):
                done[t, at, :] = total[:, t * wide : (t + 1) * wide].astype(BF16)
            return carry

        lax.fori_loop(0, rows // step, body, 0)
        if hold:
            return
        moves = []
        for t in range(seq):
            move = pltpu.make_async_remote_copy(
                src_ref=done.at[t],
                dst_ref=landed.at[me],
                send_sem=send.at[base + t],
                recv_sem=recv.at[base + me],
                device_id={"bucket": to_b, "seq": t},
                device_id_type=MESH,
            )
            keep = pltpu.make_async_copy(done.at[t], landed.at[me], send.at[base + seq + t])
            here = jnp.logical_and(to_b == self.b, self.s == t) if far else self.s == t

            @pl.when(jnp.logical_not(here))
            def _():
                move.start()

            @pl.when(here)
            def _():
                keep.start()

            moves.append((move, keep, here))
        self.last[w] = (base, moves)

    def stage_d(self, w):
        if self.kinds[w] in ("col", "hold"):
            return
        done, landed = self.scratch[w][6:]
        base, moves = self.last[w]
        out, seq, buckets = self.outs[w], self.seq, self.buckets
        for j in range(seq):
            d = self.b * seq + j
            from_b = slot(lax.rem(d, buckets), buckets)
            here = jnp.logical_and(from_b == self.b, lax.div(d, buckets) == self.s)
            if self.kinds[w] != "row":
                here = self.s == j

            @pl.when(jnp.logical_not(here))
            def _():
                pltpu.make_async_remote_copy(
                    src_ref=done.at[j],
                    dst_ref=landed.at[j],
                    send_sem=self.copies.send.at[base + j],
                    recv_sem=self.copies.recv.at[base + j],
                    device_id={"bucket": self.twin, "seq": self.s},
                    device_id_type=MESH,
                ).wait_recv()

        for move, keep, here in moves:

            @pl.when(jnp.logical_not(here))
            def _():
                move.wait_send()

            @pl.when(here)
            def _():
                keep.wait()

        for j in range(seq):
            add_rows(out.at[j], [landed.at[j]])

    def steps(self):
        count = len(self.kinds)
        for w in range(count + 2):
            if w < count:
                yield lambda w=w: self.stage_a(w)
            if 1 <= w <= count:
                yield lambda w=w: self.stage_b(w - 1)
            if w >= 2:
                yield lambda w=w: self.stage_c(w - 2)
        yield lambda: [self.stage_d(w) for w in range(count)]

    def end(self):
        for move in self.sent:
            move.wait_send()


def greet_all(b, s, buckets, seq):
    for k in range(1, buckets):
        greet(lax.rem(b + k, buckets), s)
    for k in range(1, seq):
        greet(b, lax.rem(s + k, seq))
    for j in range(seq):
        d = b * seq + j
        src_b, src_s = slot(lax.rem(d, buckets), buckets), lax.div(d, buckets)

        @pl.when(jnp.logical_not(jnp.logical_and(src_b == b, src_s == s)))
        def _():
            greet(src_b, src_s)

    to_b = lax.div(s * buckets + slot(b, buckets), seq)
    return buckets - 1 + seq - 1 + seq - jnp.where(to_b == b, 1, 0)


def sums_shapes(buckets, seq, shapes, kinds, near=False):
    chips = buckets // 2
    inputs, outs, scratch = [], [], []
    tiny = pltpu.VMEM((16, 128), BF16)
    for (rows, wide), kind in zip(shapes, kinds, strict=True):
        rows = rows // buckets
        inputs.append((chips, 2, rows, wide))
        cut = halves_of((rows, wide))
        scratch += [tiny if near else pltpu.VMEM((chips, rows, wide), BF16)]
        scratch += [pltpu.VMEM((chips, rows, wide), BF16)]
        if chips == 4:
            scratch += [pltpu.VMEM((cut, wide), BF16), pltpu.VMEM((rows - cut, wide), BF16)]
            scratch += [pltpu.VMEM((rows, wide), BF16)] * 2
        else:
            scratch += [tiny, tiny, pltpu.VMEM((chips, rows, wide), BF16), tiny]
        split = (seq, rows, wide // seq)
        kept = BF16 if kind == "hold" else F32
        outs.append(jax.ShapeDtypeStruct((rows, wide) if kind == "col" else split, kept))
        scratch += [tiny if kind in ("col", "hold") else pltpu.VMEM(split, BF16)] * 2
    n_sems = 32 + 2 * buckets + len(shapes) * (8 + 3 * seq + buckets)
    return inputs, outs, scratch, n_sems


def place_grads(buckets, grads, kinds, shapes):
    inputs = []
    for grad, kind, shape in zip(grads, kinds, shapes, strict=True):
        grad = grad.astype(BF16)
        if kind == "row" and buckets == 8:
            grad = grad.reshape((2, 2, 2) + shape[2:]).transpose(0, 2, 1, 3, 4)
        inputs.append(grad.reshape(shape))
    return inputs


def spread(buckets):
    if buckets != 8:
        return tuple(range(buckets))
    return tuple(4 * (p // 4) + 2 * (p % 2) + p // 2 % 2 for p in range(buckets))


def scatter_kernel(buckets, seq, kinds, *refs):
    count = len(kinds)
    vec, grads = refs[0], refs[1 : 1 + count]
    vec_all, outs = refs[1 + count], refs[2 + count : 2 + 2 * count]
    at = 2 + 2 * count
    vec_seq, vec_sum, send, recv = refs[at : at + 4]
    b, s = lax.axis_index("bucket"), lax.axis_index("seq")
    copies = Copies(send, recv)
    sums = GradSums(copies, b, s, buckets, seq, kinds, grads, outs, refs[at + 4 :])
    peers = greet_all(b, s, buckets, seq)
    pl.semaphore_wait(pltpu.get_barrier_semaphore(), peers)
    vec_moves = []
    for k in range(1, seq):
        vec_moves.append(sums.go(copies.remote(vec, vec_seq.at[k], b, lax.rem(s + k, seq))))
    for w in range(min(2, count)):
        sums.begin(w)
    for move in vec_moves:
        move.wait_recv()
    add_rows(vec_sum, [vec] + [vec_seq.at[k] for k in range(1, seq)])
    vec_next = []
    for k in range(1, buckets):
        peer = lax.rem(b + k, buckets)
        vec_next.append(sums.go(copies.remote(vec_sum, vec_all.at[b], peer, s)))
    vec_own = copies.local(vec_sum, vec_all.at[b])
    vec_own.start()
    for step in sums.steps():
        step()
    for move in vec_next:
        move.wait_recv()
    vec_own.wait()
    sums.end()


def scatter_all(buckets, seq, vec, grads, kinds, collective_id=1):
    any_spec = pl.BlockSpec(memory_space=pl.ANY)
    vmem = pl.BlockSpec(memory_space=pltpu.VMEM)
    shapes, outs, scratch, n_sems = sums_shapes(buckets, seq, [g.shape for g in grads], kinds)
    inputs = place_grads(buckets, grads, kinds, shapes)
    results = pl.pallas_call(
        functools.partial(scatter_kernel, buckets, seq, tuple(kinds)),
        out_shape=[jax.ShapeDtypeStruct((buckets,) + vec.shape, F32), *outs],
        in_specs=[vmem] + [any_spec] * len(grads),
        out_specs=[any_spec] + [vmem] * len(grads),
        scratch_shapes=[
            pltpu.VMEM((seq,) + vec.shape, F32),
            pltpu.VMEM(vec.shape, F32),
            pltpu.SemaphoreType.DMA((n_sems,)),
            pltpu.SemaphoreType.DMA((n_sems,)),
            *scratch,
        ],
        compiler_params=pltpu.CompilerParams(
            collective_id=collective_id, has_side_effects=True, vmem_limit_bytes=60 * 2**20
        ),
    )(vec, *inputs)
    return results[0], [out.reshape(-1, out.shape[-1]) for out in results[1:]]


def attention(queries, keys, values, live, scale):
    scores = jnp.einsum("qhd,khd->hqk", queries, keys, preferred_element_type=F32) * scale
    scores = jnp.where(live[None, None, :], scores, -1e30)
    probs = jax.nn.softmax(scores, axis=-1)
    mixed = jnp.einsum("hqk,khd->qhd", probs.astype(BF16), values, preferred_element_type=F32)
    return probs, mixed


def attention_back(probs, queries, keys, values, d_out, scale):
    d_probs = jnp.einsum("qhd,khd->hqk", d_out, values, preferred_element_type=F32)
    d_scores = probs * (d_probs - jnp.sum(probs * d_probs, axis=-1, keepdims=True))
    d_low = d_scores.astype(BF16)
    d_query = jnp.einsum("hqk,khd->qhd", d_low, keys, preferred_element_type=F32) * scale
    d_key = jnp.einsum("hqk,qhd->khd", d_low, queries, preferred_element_type=F32) * scale
    d_value = jnp.einsum("hqk,qhd->khd", probs.astype(BF16), d_out, preferred_element_type=F32)
    return d_query, d_key, d_value


def on_device_general(
    tokens,
    captions,
    cotangent,
    counts,
    cap_lens,
    steps_t,
    w_query,
    w_key,
    w_value,
    w_out,
    w_cap_key,
    w_cap_value,
    w_gate,
    w_up,
    w_down,
    w_mod,
    gains,
    cross_gate,
):
    buckets, seq = lax.axis_size("bucket"), lax.axis_size("seq")
    b, s = lax.axis_index("bucket"), lax.axis_index("seq")
    place = b * seq + s
    rows, width = tokens.shape
    span = rows * seq
    share = width // seq
    heads = share // HEAD_DIM
    scale = HEAD_DIM ** (-0.5)
    live_rows, cap_len = pick_entry(counts, b), pick_entry(cap_lens, b)
    token_total = jnp.sum(counts).astype(F32)

    cond_size = w_mod.shape[0] * buckets * seq
    cond = jax.nn.silu(time_embed(steps_t, cond_size)).astype(BF16)
    cond_part = lax.dynamic_slice_in_dim(cond, place * w_mod.shape[0], w_mod.shape[0], 1)
    slim = gains.shape[1]
    small = jnp.concatenate([gains, cross_gate[None]], axis=0).astype(F32)
    small = jnp.pad(small, ((0, 0), (0, 128 - slim)))
    tok_all, cap_all, small_all, mod, weights = gather_all(
        buckets,
        seq,
        tokens,
        captions,
        small,
        cond_part,
        w_mod,
        [w_query, w_key, w_value, w_cap_key, w_cap_value, w_out, w_gate, w_up, w_down],
        ["col", "col", "col", "col", "col", "row", "col", "col", "row"],
    )
    wq, wk, wv, wck, wcv, wo, wg, wu, wd = weights
    caps = cap_all.reshape(-1, captions.shape[1])
    small_rows = small_all[..., :slim].transpose(2, 0, 1, 3).reshape(8, width)
    gain_f = small_rows[:7]
    own_cols = lax.dynamic_slice_in_dim(small_rows, s * share, share, 1)
    gate_cross = jnp.tanh(own_cols[7])
    scale_attn, gate_attn, scale_ffn, gate_ffn = mod.reshape(4, width)

    hidden = pre_attn(tok_all.astype(F32), gain_f[0], scale_attn).astype(BF16).reshape(span, width)
    query_proj, key_proj = bf_dot(hidden, wq), bf_dot(hidden, wk)
    value_low = bf_dot(hidden, wv).astype(BF16)
    (query_f, key_f), norm_back = jax.vjp(qk_norm, query_proj, key_proj, own_cols[4], own_cols[5])
    cap_key_f, cap_back = jax.vjp(cap_norm, bf_dot(caps, wck), own_cols[6])

    def by_head(values):
        return values.astype(BF16).reshape(values.shape[0], heads, HEAD_DIM)

    query, key, value = by_head(query_f), by_head(key_f), by_head(value_low)
    cap_key, cap_value = by_head(cap_key_f), by_head(bf_dot(caps, wcv))
    probs, self_out = attention(query, key, value, jnp.arange(span) < live_rows, scale)
    cap_live = jnp.arange(caps.shape[0]) < cap_len
    cap_probs, cross_out = attention(query, cap_key, cap_value, cap_live, scale)
    self_out, cross_out = self_out.reshape(span, share), cross_out.reshape(span, share)
    mixed_low = (self_out + gate_cross * cross_out).astype(BF16)
    attn_out = line_scatter(seq, bf_dot(mixed_low, wo), 2)

    tokens_f = tokens.astype(F32)
    (resid_one, ffn_pre), middle_back = jax.vjp(
        middle, tokens_f, attn_out, gain_f[1], gate_attn, gain_f[2], scale_ffn
    )
    ffn_all = line_gather(seq, ffn_pre.astype(BF16), 3)
    act_pre, act_back = jax.vjp(activate, bf_dot(ffn_all, wg), bf_dot(ffn_all, wu))
    act_low = act_pre.astype(BF16)
    ffn_out = line_scatter(seq, bf_dot(act_low, wd), 4)
    out_f, finish_back = jax.vjp(finish, resid_one, ffn_out, gain_f[3], gate_ffn)
    block_out = out_f.astype(BF16)

    row_live = (s * rows + jnp.arange(rows) < live_rows).astype(F32)
    weighted = cotangent.astype(F32) * row_live[:, None] * (buckets * span / token_total)
    d_resid, d_ffn_out, d_gain_last, d_gate_ffn = finish_back(weighted)
    d_ffn_all = line_gather(seq, d_ffn_out.astype(BF16), 5)
    d_gate, d_up = act_back(right_dot(d_ffn_all, wd))
    d_gate, d_up = d_gate.astype(BF16), d_up.astype(BF16)
    d_hidden_ffn = line_scatter(seq, right_dot(d_gate, wg) + right_dot(d_up, wu), 6)
    d_tokens_one, d_attn_out, d_gain_post, d_gate_attn, d_gain_ffn, d_scale_ffn = middle_back(
        (d_resid, d_hidden_ffn)
    )
    d_attn_all = line_gather(seq, d_attn_out.astype(BF16), 7)
    d_mixed_low = right_dot(d_attn_all, wo).astype(BF16)
    d_mixed = d_mixed_low.astype(F32)
    d_cross_low = (gate_cross * d_mixed).astype(BF16)
    grad_cross = jnp.sum(d_mixed * cross_out, axis=0) * (1.0 - gate_cross * gate_cross)

    d_query_cross, d_cap_key, d_cap_value = attention_back(
        cap_probs, query, cap_key, cap_value, by_head(d_cross_low), scale
    )
    d_query, d_key, d_value = attention_back(probs, query, key, value, by_head(d_mixed_low), scale)
    d_cap_key, d_gain_cap = cap_back(d_cap_key.reshape(-1, share))
    d_query, d_key, d_gain_query, d_gain_key = norm_back(
        ((d_query + d_query_cross).reshape(span, share), d_key.reshape(span, share))
    )
    d_query, d_key, d_cap_key = d_query.astype(BF16), d_key.astype(BF16), d_cap_key.astype(BF16)
    d_value = d_value.reshape(span, share).astype(BF16)
    d_cap_value = d_cap_value.reshape(-1, share).astype(BF16)
    d_hidden = line_scatter(
        seq, right_dot(d_query, wq) + right_dot(d_key, wk) + right_dot(d_value, wv), 8
    )
    _, pre_back = jax.vjp(pre_attn, tokens_f, gain_f[0], scale_attn)
    d_tokens_two, d_gain_pre, d_scale_attn = pre_back(d_hidden)
    tokens_grad = d_tokens_one + d_tokens_two

    own_sums = jnp.stack([d_gain_query, d_gain_key, d_gain_cap, grad_cross])
    own_wide = lax.dynamic_update_slice(jnp.zeros((4, width), F32), own_sums, (0, s * share))
    vec = jnp.concatenate(
        [
            jnp.stack([d_scale_attn, d_gate_attn, d_scale_ffn, d_gate_ffn]),
            jnp.stack([d_gain_pre, d_gain_post, d_gain_ffn, d_gain_last]),
            own_wide,
            jnp.zeros((4, width), F32),
        ]
    )
    grads = [
        left_dot(ffn_all, d_gate),
        left_dot(ffn_all, d_up),
        left_dot(act_low, d_ffn_all),
        left_dot(mixed_low, d_attn_all),
        left_dot(caps, d_cap_key),
        left_dot(caps, d_cap_value),
        left_dot(hidden, d_query),
        left_dot(hidden, d_key),
        left_dot(hidden, d_value),
    ]
    kinds = ["col", "col", "row", "row", "col", "col", "col", "col", "col"]
    vec_all, sums = scatter_all(buckets, seq, vec, grads, kinds)
    s_gate, s_up, s_down, s_out, s_cap_key, s_cap_value, s_query, s_key, s_value = sums

    quarter = 4 * width // seq
    mod_rows = vec_all[:, :4].reshape(buckets, -1, quarter)
    mod_rows = lax.dynamic_slice_in_dim(mod_rows, s, 1, 1)[:, 0]
    cond_size = cond.shape[1] // buckets
    cond_cols = lax.dynamic_slice_in_dim(cond, b * cond_size, cond_size, 1).astype(F32)
    s_mod = jnp.sum(cond_cols[:, :, None] * mod_rows[:, None, :], axis=0)
    tail = lax.dynamic_slice(vec_all, (0, 4, place * slim), (buckets, 8, slim))
    tail = jnp.sum(tail, axis=0)
    return (
        block_out,
        tokens_grad,
        s_query,
        s_key,
        s_value,
        s_out,
        s_cap_key,
        s_cap_value,
        s_gate,
        s_up,
        s_down,
        s_mod,
        tail[:7],
        tail[7],
    )


def low_half(shape):
    return lax.broadcasted_iota(jnp.int32, shape, len(shape) - 1) < HEAD_DIM


def pair_sums(values):
    row = lax.broadcasted_iota(jnp.int32, (128, 128), 0) < HEAD_DIM
    same = (row == low_half((128, 128))).astype(BF16)
    high = values.astype(BF16)
    rest = (values - high.astype(F32)).astype(BF16)
    return bf_dot(high, same) + bf_dot(rest, same)


def pair_scale(values, eps):
    return lax.rsqrt(pair_sums(values * values) * (1.0 / HEAD_DIM) + eps)


def fill_rows(out, live, first, yes, no):
    row = lax.broadcasted_iota(jnp.int32, out.shape, 0) + first
    out[...] = jnp.where(row < live, yes, no).astype(out.dtype)


FORWARD_ORDER = (8, "tok", 0, "tok", 1, "tok", 2, "tok", 6, 7, "cap", 3, "cap", 4, "cap", 5, "cap")
MOVED = ()
LAG = 1
WINDOW = 2


class Gather:
    def __init__(self, copies, b, s, buckets, seq, kinds, shards, fulls, keep_at=None):
        self.copies, self.b, self.s, self.buckets, self.seq = copies, b, s, buckets, seq
        self.kinds, self.shards, self.fulls, self.keep_at = kinds, shards, fulls, keep_at
        place = b * seq + s
        self.to_slot, self.to_s = lax.rem(place, buckets), lax.div(place, buckets)
        self.to_b = slot(self.to_slot, buckets)
        back = s * buckets + slot(b, buckets)
        self.from_b, self.from_s = lax.div(back, seq), lax.rem(back, seq)
        self.stays = jnp.logical_and(self.to_b == b, self.to_s == s)
        self.twin, self.near_x, self.near_y = flip(b, 1), flip(b, 2), flip(b, 4)
        self.far = flip(self.near_x, 4)
        self.first, self.second, self.kept, self.sent = {}, {}, [], []

    def greet_source(self):
        @pl.when(jnp.logical_not(self.stays))
        def _():
            greet(self.from_b, self.from_s)

        return jnp.where(self.stays, 0, 1)

    def go(self, src, dst, b):
        copy = self.copies.remote(src, dst, b, self.s)
        copy.start()
        self.sent.append(copy)
        return copy

    def depart(self, at):
        copies, b, s, seq = self.copies, self.b, self.s, self.seq
        shard, full = self.shards[at], self.fulls[at]
        if self.kinds[at] == "stay":
            keep = copies.local(shard, full.at[b])
            keep.start()
            self.first[at] = ((), keep)
            return
        if self.kinds[at] == "row":
            move = copies.remote(shard, full.at[self.to_slot], self.to_b, self.to_s)
            keep = copies.local(shard, full.at[slot(b, self.buckets)])

            @pl.when(jnp.logical_not(self.stays))
            def _():
                move.start()

            @pl.when(self.stays)
            def _():
                keep.start()

            self.first[at] = (move, keep)
            return
        wide = full.shape[-1]

        def columns(peer):
            if self.kinds[at] == "cut":
                return shard.at[peer]
            return shard.at[:, pl.ds(pl.multiple_of(peer * wide, 128), wide)]

        moves = []
        for k in range(1, seq):
            peer = lax.rem(s + k, seq)
            move = copies.remote(columns(peer), full.at[b, s], b, peer)
            move.start()
            moves.append(move)
        keep = copies.local(columns(s), full.at[b, s])
        keep.start()
        self.first[at] = (moves, keep)

    def arrived(self, at):
        moves, keep = self.first[at]
        if self.kinds[at] == "row":

            @pl.when(jnp.logical_not(self.stays))
            def _():
                moves.wait()

            @pl.when(self.stays)
            def _():
                keep.wait()

            return
        for move in moves:
            move.wait()
        keep.wait()

    def index(self, at, device):
        return slot(device, self.buckets) if self.kinds[at] == "row" else device

    def stage_a(self, at):
        block = self.fulls[at].at[self.index(at, self.b)]
        self.second[at] = {
            "x": self.go(block, block, self.near_x),
            "y": self.go(block, block, self.near_y),
            "twin": [self.go(block, block, self.twin)],
        }

    def stage_b(self, at):
        full, now = self.fulls[at], self.second[at]
        cut = halves_of(full.shape[1:])
        now["x"].wait_recv()
        block = full.at[self.index(at, self.near_x), pl.ds(0, cut)]
        now["dy"] = self.go(block, block, self.near_y)
        block = full.at[self.index(at, self.near_x)]
        now["twin"].append(self.go(block, block, self.twin))
        now["y"].wait_recv()
        block = full.at[self.index(at, self.near_y), pl.ds(cut, full.shape[1] - cut)]
        now["dx"] = self.go(block, block, self.near_x)
        block = full.at[self.index(at, self.near_y)]
        now["twin"].append(self.go(block, block, self.twin))

    def stage_c(self, at):
        full, now = self.fulls[at], self.second[at]
        now["dy"].wait_recv()
        now["dx"].wait_recv()
        block = full.at[self.index(at, self.far)]
        now["twin"].append(self.go(block, block, self.twin))

    def stage_d(self, at):
        for move in self.second[at]["twin"]:
            move.wait_recv()
        if self.keep_at is not None:
            copy = self.copies.local(self.fulls[at], self.keep_at[at])
            copy.start()
            self.kept.append(copy)

    def end(self):
        for copy in self.kept:
            copy.wait()
        for move in self.sent:
            move.wait_send()


def forward_kernel(buckets, seq, kinds, slim, *refs):
    count = len(kinds)
    tokens, captions, small, cond, w_mod, counts, cap_lens = refs[:7]
    shards = refs[7 : 7 + count]
    refs = refs[7 + count :]
    cap_all = refs[0]
    far_fulls = refs[1 : 1 + count]
    refs = refs[1 + count :]
    (
        gain_rows,
        mod_rows,
        hidden,
        query_raw,
        key_raw,
        cap_raw,
        query,
        key,
        value,
        cap_key,
        cap_value,
        cross_out,
        mixed,
    ) = refs[:13]
    refs = refs[13:]
    part, got_bucket, got_seq, mod_sum, small_all, tok_all, cap_near, own_out = refs[:8]
    fulls = refs[8 : 8 + count]
    key_mask, cap_mask, send, recv = refs[8 + count : 12 + count]
    strips = refs[12 + count :]
    b, s = lax.axis_index("bucket"), lax.axis_index("seq")
    copies = Copies(send, recv)
    shards = list(shards)
    cuts = [at for at in range(count) if kinds[at] == "cut"]
    for at, strip in zip(cuts, strips, strict=True):
        for t in range(seq):
            for j in range(strip.shape[2] // 128):
                cols = slice((j * seq + t) * 128, (j * seq + t + 1) * 128)
                strip[t, :, j * 128 : (j + 1) * 128] = shards[at][:, cols]
        shards[at] = strip
    weights = Gather(copies, b, s, buckets, seq, kinds, shards, fulls, far_fulls)
    for k in range(1, buckets):
        greet(lax.rem(b + k, buckets), s)
    for k in range(1, seq):
        greet(b, lax.rem(s + k, seq))
    peers = buckets - 1 + seq - 1 + weights.greet_source()

    fill_rows(key_mask, counts[b], 0, 1.0, 0.0)
    fill_rows(cap_mask, cap_lens[b], 0, 1.0, 0.0)
    lanes = part.shape[2]
    for j in range(part.shape[1]):
        part[:, j, :] = bf_dot(cond[...], w_mod[:, j * lanes : (j + 1) * lanes])

    pl.semaphore_wait(pltpu.get_barrier_semaphore(), peers)

    sent = []

    def go(copy):
        copy.start()
        sent.append(copy)
        return copy

    mod_moves = []
    for k in range(1, buckets):
        peer = lax.rem(b + k, buckets)
        mod_moves.append(go(copies.remote(part.at[peer], got_bucket.at[k], peer, s)))
    small_moves = []
    for k in range(1, seq):
        peer = lax.rem(s + k, seq)
        small_moves.append(go(copies.remote(small, small_all.at[b, s], b, peer)))
    small_own = copies.local(small, small_all.at[b, s])
    small_own.start()

    tok = Relay(copies, tokens, tok_all, b, s, seq)
    cap = Relay(copies, captions, cap_near, b, s, seq)
    items, step = [], {"tok": 0, "cap": 0}
    for what in FORWARD_ORDER:
        if isinstance(what, str):
            items.append((tok if what == "tok" else cap, step[what]))
            step[what] += 1
        else:
            items.append((None, what))

    def fetch(at):
        whole = fulls[at][...]
        return whole.reshape(-1, whole.shape[-1])


    rows = seq * tok_all.shape[1]
    width = tok_all.shape[2]
    cap_rows = seq * cap_near.shape[1]
    share = query.shape[1]
    pairs = share // 128
    block_rows = tok_all.shape[1]

    def small_sums():
        for move in small_next:
            move.wait_recv()
        strips = [None] * (width // 128)
        lane = lax.broadcasted_iota(jnp.int32, (8, 128), 1)
        for d in range(buckets * seq):
            at, shift = divmod(d * slim, 128)
            piece = small_all[d // seq, d % seq]
            turned = pltpu.roll(piece, shift, 1) if shift else piece
            for index, keep in ((at, lane >= shift), (at + 1, lane < shift)):
                if index == at + 1 and shift + slim <= 128:
                    continue
                add = jnp.where(keep, turned, 0.0)
                strips[index] = add if strips[index] is None else strips[index] + add
        for at, strip in enumerate(strips):
            gain_rows[:, at * 128 : (at + 1) * 128] = strip
        total = mod_sum[...]
        for k, move in enumerate(mod_next, 1):
            move.wait_recv()
            total = total + got_seq[k]
        for j in range(8):
            at, lane_at = divmod(j * lanes, width)
            mod_rows[at : at + 1, lane_at : lane_at + lanes] = total[j : j + 1, :]
        mod_rows[4:8, :] = jnp.zeros((4, width), F32)

    def make_hidden():
        factor = gain_rows[0:1, :] * (1.0 + mod_rows[0:1, :])
        for t in range(seq):

            def body(i, carry):
                at = pl.ds(pl.multiple_of(i * 32, 32), 32)
                x = tok_all[t, at, :].astype(F32)
                x = x * lax.rsqrt(jnp.mean(x * x, axis=-1, keepdims=True) + 1e-05) * factor
                to = pl.ds(pl.multiple_of(t * block_rows + i * 32, 32), 32)
                hidden[to, :] = x.astype(BF16)
                return carry

            lax.fori_loop(0, block_rows // 32, body, 0)

    def gain_of(row, pair):
        at = pl.multiple_of(s * share + pair * 128, 128)
        return gain_rows[row : row + 1, pl.ds(at, 128)]

    def make_normed(raw, out, row, scale):
        def body(i, carry):
            at = pl.ds(pl.multiple_of(i * 64, 64), 64)
            for pair in range(pairs):
                lane = slice(pair * 128, (pair + 1) * 128)
                x = raw[at, lane]
                x = x * pair_scale(x, 1e-06) * gain_of(row, pair)
                out[at, lane] = x.astype(BF16)
            return carry

        del scale
        lax.fori_loop(0, raw.shape[0] // 64, body, 0)

    def make_query():
        query_raw[...] = bf_dot(hidden[...], fetch(0))
        make_normed(query_raw, query, 4, None)

    def make_key():
        key_raw[...] = bf_dot(hidden[...], fetch(1))
        make_normed(key_raw, key, 5, None)

    def make_value():
        value[...] = bf_dot(hidden[...], fetch(2)).astype(BF16)

    def cap_near_rows():
        whole = cap_near[...]
        return whole.reshape(cap_rows, whole.shape[-1])

    def make_cap_key():
        cap_raw[...] = bf_dot(cap_near_rows(), fetch(3))
        make_normed(cap_raw, cap_key, 6, None)

    def make_cap_value():
        cap_value[...] = bf_dot(cap_near_rows(), fetch(4)).astype(BF16)

    def attend(pair, k_ref, v_ref, mask, store):
        lane = slice(pair * 128, (pair + 1) * 128)
        low = low_half((128, 128))
        keys = k_ref[:, lane]
        values = jnp.concatenate([v_ref[:, lane] * mask[...], mask[...]], axis=1)

        def body(i, carry):
            at = pl.ds(pl.multiple_of(i * 128, 128), 128)
            q = query[at, lane] * jnp.asarray(HEAD_DIM**-0.5, BF16)
            outs = []
            for half in (jnp.where(low, q, jnp.zeros_like(q)), jnp.where(low, jnp.zeros_like(q), q)):
                weights = jnp.exp(right_dot(half, keys))
                outs.append(bf_dot(weights.astype(BF16), values))
            out = jnp.where(low, outs[0][:, :128], outs[1][:, :128])
            store(at, lane, out / jnp.where(low, outs[0][:, 128:], outs[1][:, 128:]))
            return carry

        lax.fori_loop(0, rows // 128, body, 0)

    def make_own(pair):
        def store(at, lane, out):
            own_out[at, lane] = out

        attend(pair, key, value, key_mask, store)

    def make_mixed(pair):
        gate = jnp.tanh(gain_of(7, pair))

        def store(at, lane, out):
            cross_out[at, lane] = out
            mixed[at, lane] = (own_out[at, lane] + gate * out).astype(BF16)

        attend(pair, cap_key, cap_value, cap_mask, store)

    work = [
        (lambda: (small_sums(), make_hidden()), "h", {"tok"}),
        (make_query, "q", {"h", 0}),
        (make_key, "k", {"h", 1}),
        (make_value, "v", {"h", 2}),
        (make_cap_key, "ck", {"cap", 3}),
        (make_cap_value, "cv", {"cap", 4}),
        *((functools.partial(make_own, p), ("own", p), {"q", "k", "v"}) for p in range(pairs)),
        *(
            (functools.partial(make_mixed, p), ("all", p), {"q", "ck", "cv", ("own", p)})
            for p in range(pairs)
        ),
    ]

    def do_work():
        for at, (piece, name, needs) in enumerate(work):
            if needs <= done:
                piece()
                done.add(name)
                del work[at]
                return True
        return False


    done = set()

    def begin(i):
        relay, j = items[i]
        if relay is None:
            weights.depart(j)
        else:
            relay.start(j)
            if j == seq - 1:
                done.add("tok" if relay is tok else "cap")

    def complete(at):
        weights.stage_c(at)
        weights.stage_d(at)
        done.add(at)

    window = WINDOW
    for i in range(window):
        begin(i)
    for move in small_moves:
        move.wait_recv()
    small_own.wait()
    small_next = []
    for k in range(1, buckets):
        peer = lax.rem(b + k, buckets)
        small_next.append(go(copies.remote(small_all.at[b], small_all.at[b], peer, s)))
    total = part[b]
    for k, move in enumerate(mod_moves, 1):
        move.wait_recv()
        total = total + got_bucket[k]
    mod_sum[...] = total
    mod_next = []
    for k in range(1, seq):
        peer = lax.rem(s + k, seq)
        mod_next.append(go(copies.remote(mod_sum, got_seq.at[k], b, peer)))

    cap_out = copies.local(cap_near, cap_all)
    order = []
    for i, (relay, j) in enumerate(items):
        if relay is None:
            weights.arrived(j)
        elif j <= seq - 2:
            relay.sent(j)
        if i + window < len(items):
            begin(i + window)
        if relay is None:
            order.append(j)
            weights.stage_a(j)
            if len(order) > LAG:
                weights.stage_b(order[-1 - LAG])
            if len(order) > LAG + 1:
                complete(order[-2 - LAG])
        do_work()
    cap_out.start()
    for at in range(LAG):
        weights.stage_b(order[len(order) - LAG + at])
        complete(order[len(order) - LAG - 1 + at])
        do_work()
    complete(order[-1])
    while do_work():
        pass
    cap_out.wait()
    weights.end()
    for move in sent:
        move.wait_send()


def forward_all(buckets, seq, tokens, captions, small, slim, cond, w_mod, masks, shards, kinds):
    any_spec = pl.BlockSpec(memory_space=pl.ANY)
    vmem = pl.BlockSpec(memory_space=pltpu.VMEM)
    smem = pl.BlockSpec(memory_space=pltpu.SMEM)
    fulls = []
    for shard, kind in zip(shards, kinds, strict=True):
        rows, wide = shard.shape
        shape = (buckets, rows, wide) if kind in ("row", "stay") else (buckets, seq, rows, wide // seq)
        fulls.append(jax.ShapeDtypeStruct(shape, BF16))
    near = [pltpu.VMEM(full.shape, BF16) for full in fulls]
    width = tokens.shape[1]
    mod_lanes = w_mod.shape[1] // 8
    span, cap_span, share = seq * tokens.shape[0], seq * captions.shape[0], width // seq
    f32_rows = jax.ShapeDtypeStruct((span, share), F32)
    low_rows = jax.ShapeDtypeStruct((span, share), BF16)
    cap_low = jax.ShapeDtypeStruct((cap_span, share), BF16)
    inner = [
        jax.ShapeDtypeStruct((8, width), F32),
        jax.ShapeDtypeStruct((8, width), F32),
        jax.ShapeDtypeStruct((span, width), BF16),
        f32_rows,
        f32_rows,
        jax.ShapeDtypeStruct((cap_span, share), F32),
        low_rows,
        low_rows,
        low_rows,
        cap_low,
        cap_low,
        f32_rows,
        low_rows,
    ]
    n_sems = 64 + 16 * buckets + len(shards) * (seq + 2 * buckets)
    outs = pl.pallas_call(
        functools.partial(forward_kernel, buckets, seq, tuple(kinds), slim),
        out_shape=[jax.ShapeDtypeStruct((seq,) + captions.shape, BF16), *fulls, *inner],
        in_specs=[any_spec, any_spec, any_spec, vmem, vmem, smem, smem]
        + [vmem if kind == "cut" else any_spec for kind in kinds],
        out_specs=[any_spec] * (1 + len(shards)) + [vmem] * len(inner),
        scratch_shapes=[
            pltpu.VMEM((buckets, 8, mod_lanes), F32),
            pltpu.VMEM((buckets, 8, mod_lanes), F32),
            pltpu.VMEM((seq, 8, mod_lanes), F32),
            pltpu.VMEM((8, mod_lanes), F32),
            pltpu.VMEM((buckets, seq) + small.shape, F32),
            pltpu.VMEM((seq,) + tokens.shape, BF16),
            pltpu.VMEM((seq,) + captions.shape, BF16),
            pltpu.VMEM((span, share), F32),
            *near,
            pltpu.VMEM((span, 128), BF16),
            pltpu.VMEM((cap_span, 128), BF16),
            pltpu.SemaphoreType.DMA((n_sems,)),
            pltpu.SemaphoreType.DMA((n_sems,)),
            *(
                pltpu.VMEM((seq,) + full.shape[2:], BF16)
                for full, kind in zip(fulls, kinds, strict=True)
                if kind == "cut"
            ),
        ],
        compiler_params=pltpu.CompilerParams(
            collective_id=9, has_side_effects=True, vmem_limit_bytes=62 * 2**20
        ),
    )(tokens, captions, small, cond, w_mod, *masks, *shards)
    at = 1 + len(shards)
    return outs[0], outs[1:at], outs[at:]


def middle_kernel(buckets, seq, chunks, kinds, *refs):
    mixed, w_out, tokens, cotangent, counts, gain_rows, mod_rows = refs[:7]
    far_weights, refs = refs[7:10], refs[10:]
    block_out, d_tokens, d_attn, row_sums = refs[:4]
    outs, refs = refs[4:7], refs[7:]
    w_gate, w_up, w_down, ffn_all, d_ffn, act, d_gate, d_up = refs[:8]
    gate_keep, up_keep, attn_keep, resid_keep, got, parts, from_left, from_right = refs[8:16]
    row_scale, send, recv = refs[16:19]
    grads, refs = refs[19:22], refs[22:]
    b, s = lax.axis_index("bucket"), lax.axis_index("seq")
    copies = Copies(send, recv)
    sums = GradSums(copies, b, s, buckets, seq, kinds, grads, outs, refs, near=True)
    shards = (w_gate, w_up, w_down)
    weights = Gather(copies, b, s, buckets, seq, ("cut", "cut", "stay"), far_weights, shards)
    peers = greet_all(b, s, buckets, seq) + weights.greet_source()
    pl.semaphore_wait(pltpu.get_barrier_semaphore(), peers)
    loads = [copies.local(far_weights[w], shards[w]) for w in range(3) if w not in MOVED]
    for load in loads:
        load.start()
    if MOVED:
        weights.depart(MOVED[0])

    rows, width = tokens.shape
    live = sum(counts[k] for k in range(buckets))
    factor = buckets * seq * rows / jnp.full((rows, 128), live, jnp.int32).astype(F32)
    row = lax.broadcasted_iota(jnp.int32, (rows, 128), 0) + s * rows
    row_scale[...] = jnp.where(row < counts[b], factor, 0.0)
    thin = rows // chunks
    tall = seq * thin
    hidden = act.shape[-1]
    wide = 512
    gate_post = jnp.tanh(mod_rows[1:2, :]) * gain_rows[1:2, :]
    gain_ffn = gain_rows[2:3, :] * (1.0 + mod_rows[2:3, :])
    gate_last = jnp.tanh(mod_rows[3:4, :]) * gain_rows[3:4, :]
    row_sums[...] = jnp.zeros_like(row_sums)

    def of(c):
        return pl.ds(c * thin, thin)

    def chunk_of(ref, c, cols=slice(None)):
        whole = ref[:, of(c), cols]
        return whole.reshape(tall, whole.shape[-1])

    def mean(values):
        return jnp.mean(values, axis=-1, keepdims=True)

    def over_rows(c, body):
        step = 16

        def one(i, carry):
            return body(pl.ds(pl.multiple_of(c * thin + i * step, step), step), carry)

        return lax.fori_loop(0, thin // step, one, jnp.zeros((1, width), F32), unroll=2)

    def weighted(at):
        return cotangent[at, :].astype(F32) * row_scale[at, 0:1]

    def after_attn(c):
        def body(at, carry):
            out = got[at, :]
            attn_keep[at, :] = out
            resid = out * lax.rsqrt(mean(out * out) + 1e-05) * gate_post
            resid = tokens[at, :].astype(F32) + resid
            resid_keep[at, :] = resid
            normed = resid * lax.rsqrt(mean(resid * resid) + 1e-05)
            ffn_all[s, at, :] = (normed * gain_ffn).astype(BF16)
            return carry

        over_rows(c, body)

    def after_ffn(c):
        def body(at, total):
            out, resid, grad = got[at, :], resid_keep[at, :], weighted(at)
            size = lax.rsqrt(mean(out * out) + 1e-05)
            normed = out * size
            block_out[at, :] = (resid + gate_last * normed).astype(BF16)
            inner = grad * gate_last
            d_ffn[s, at, :] = (size * (inner - normed * mean(inner * normed))).astype(BF16)
            return total + jnp.sum(grad * normed, axis=0, keepdims=True)

        row_sums[2:3, :] += over_rows(c, body)

    def after_ffn_back(c):
        def body(at, totals):
            first, second = totals
            d_pre, resid, out = got[at, :], resid_keep[at, :], attn_keep[at, :]
            size = lax.rsqrt(mean(resid * resid) + 1e-05)
            normed, inner = resid * size, d_pre * gain_ffn
            second = second + jnp.sum(d_pre * normed, axis=0, keepdims=True)
            grad = weighted(at) + size * (inner - normed * mean(inner * normed))
            d_tokens[at, :] = grad
            size = lax.rsqrt(mean(out * out) + 1e-05)
            normed, inner = out * size, grad * gate_post
            first = first + jnp.sum(grad * normed, axis=0, keepdims=True)
            d_attn[s, at, :] = (size * (inner - normed * mean(inner * normed))).astype(BF16)
            return first, second

        step, zero = 16, jnp.zeros((1, width), F32)

        def one(i, carry):
            return body(pl.ds(pl.multiple_of(c * thin + i * step, step), step), carry)

        first, second = lax.fori_loop(0, thin // step, one, (zero, zero), unroll=2)
        row_sums[0:1, :] += first
        row_sums[1:2, :] += second

    def flat(values):
        return values.reshape(-1, values.shape[-1])

    def put_parts(c, cols, total):
        parts[c, :, :, cols] = total.astype(BF16).reshape(seq, thin, total.shape[-1])

    def attn_product(c):
        left = chunk_of(mixed, c)
        for at in range(0, width, wide):
            cols = slice(at, at + wide)
            put_parts(c, cols, bf_dot(left, w_out[:, cols]))

    def ffn_product(c):
        for at in range(0, hidden, wide):
            cols = slice(at, at + wide)
            left = chunk_of(ffn_all, c)
            gate = bf_dot(left, flat(w_gate[:, :, :, cols]))
            up = bf_dot(left, flat(w_up[:, :, :, cols]))
            gate_keep[c, :, cols], up_keep[c, :, cols] = gate, up
            value = (gate * jax.nn.sigmoid(gate) * up).astype(BF16)
            act[:, of(c), cols] = value.reshape(seq, thin, wide)
        left = chunk_of(act, c)
        for at in range(0, width, wide):
            cols = slice(at, at + wide)
            put_parts(c, cols, bf_dot(left, flat(w_down[:, :, cols])))

    def ffn_back_product(c):
        block = w_down.shape[1]
        for at in range(0, hidden, wide):
            cols = slice(at, at + wide)
            d_act = right_dot(chunk_of(d_ffn, c), flat(w_down[at // block : (at + wide) // block]))
            gate, up = gate_keep[c, :, cols], up_keep[c, :, cols]
            sig = jax.nn.sigmoid(gate)
            silu = gate * sig
            d_g = (d_act * up * (sig + silu * (1.0 - sig))).astype(BF16)
            d_u = (d_act * silu).astype(BF16)
            d_gate[:, of(c), cols] = d_g.reshape(seq, thin, wide)
            d_up[:, of(c), cols] = d_u.reshape(seq, thin, wide)
        left_g, left_u = chunk_of(d_gate, c), chunk_of(d_up, c)
        half = buckets // 2
        for at in range(0, buckets, half):
            cols = slice(at * width // buckets, (at + half) * width // buckets)
            total = right_dot(left_g, flat(w_gate[at : at + half]))
            total = total + right_dot(left_u, flat(w_up[at : at + half]))
            put_parts(c, cols, total)

    def pour_of(c, turn):
        left, right = from_left.at[turn * chunks + c], from_right.at[turn * chunks + c]
        return Pour(copies, parts.at[c], left, right, b, s, seq)

    gathered = (ffn_all, d_ffn, d_attn)
    after = (after_attn, after_ffn, after_ffn_back)
    products = (attn_product, ffn_product, ffn_back_product)

    def all_rows(ref, cols=slice(None)):
        whole = ref[:, :, cols]
        return whole.reshape(seq * rows, whole.shape[-1])

    def down_grad():
        chips, part = buckets // 2, hidden // buckets
        for i in range(chips):
            turned = all_rows(act, slice(2 * i * part, 2 * (i + 1) * part)).T
            total = bf_dot(turned, all_rows(d_ffn)).astype(BF16)
            for half in range(2):
                grads[2][i, half] = total[half * part : (half + 1) * part]
        sums.begin(2)

    def weight_grads():
        chips, part = buckets // 2, width // (buckets // 2)
        for i in range(chips):
            turned = all_rows(ffn_all, slice(i * part, (i + 1) * part)).T
            for grad, d in zip(grads[:2], (d_gate, d_up), strict=True):
                total = bf_dot(turned, all_rows(d))
                grad[i] = total.astype(BF16).reshape(2, part // 2, hidden)
            if i == 1:
                sums.stage_a(2)
            yield
        sums.begin(0)
        sums.begin(1)
        sums.stage_b(2)
        yield
        sums.stage_a(0)
        yield
        sums.stage_c(2)
        sums.stage_a(1)
        yield
        sums.stage_b(0)
        yield
        sums.stage_b(1)
        yield
        sums.stage_c(0)
        sums.stage_d(2)
        sums.stage_c(1)
        sums.stage_d(0)
        sums.stage_d(1)

    extra = weight_grads()
    plan = [(turn, c) for turn in range(3) for c in range(chunks)]
    gathers, open_gather = {}, []

    def finish_gather():
        turn, c = open_gather.pop(0)
        gathers[turn, c].start(seq - 1)
        for j in range(seq - 1):
            gathers[turn, c].sent(j)
        return turn, c

    def weights_come():
        count = len(MOVED)
        for n in range(count + 3):
            if n < count:
                weights.arrived(MOVED[n])
                if n + 1 < count:
                    weights.depart(MOVED[n + 1])
                weights.stage_a(MOVED[n])
                yield
            if 1 <= n <= count:
                weights.stage_b(MOVED[n - 1])
                yield
            if 2 <= n <= count + 1:
                weights.stage_c(MOVED[n - 2])
            if 3 <= n:
                weights.stage_d(MOVED[n - 3])
            yield

    coming = weights_come()
    attn_product(0)
    pours = {(0, 0): pour_of(0, 0)}
    ready = pours[0, 0].cuts
    for q in range(ready):
        pours[0, 0].step(q)
    for c in range(1, chunks):
        attn_product(c)
    for load in loads:
        load.wait()
    for at, (turn, c) in enumerate(plan):
        pour = pours[turn, c]
        mate = gathers[open_gather[0]] if open_gather else None
        per = pour.count // (seq - 1)
        final = at == len(plan) - 1
        for j in range(2, seq):
            if mate is not None and j < seq - 1:
                mate.start(j)
            if final:
                next(extra, None)
            for q in range((j - 1) * per, j * per):
                pour.step(q)
                next(coming, None)
            if final:
                next(extra, None)
        pour.end(got.at[of(c)])
        after[turn](c)
        gathers[turn, c] = Relay(copies, None, gathered[turn], b, s, seq, of(c))
        gathers[turn, c].start(0)
        if mate is not None:
            done_turn, done_c = finish_gather()
            if (done_turn, done_c) == (1, chunks - 1):
                down_grad()
            for _ in coming:
                pass
            if done_turn < 2:
                products[done_turn + 1](done_c)
        open_gather.append((turn, c))
        gathers[turn, c].start(1)
        if at + 1 < len(plan):
            nxt = plan[at + 1]
            pours[nxt] = pour_of(nxt[1], nxt[0])
            for q in range(ready):
                pours[nxt].step(q)
            if at + 2 == len(plan):
                next(extra)
                next(extra)
    turn, c = open_gather[0]
    for j in range(2, seq - 1):
        next(extra, None)
        gathers[turn, c].start(j)
    next(extra, None)
    finish_gather()
    for _ in extra:
        pass
    sums.end()
    weights.end()


def middle_all(buckets, seq, mixed, weights, tokens, cotangent, counts, gain_rows, mod_rows):
    any_spec = pl.BlockSpec(memory_space=pl.ANY)
    vmem = pl.BlockSpec(memory_space=pltpu.VMEM)
    smem = pl.BlockSpec(memory_space=pltpu.SMEM)
    chunks = CHUNKS
    w_out, w_gate, w_up, w_down = weights
    rows, width = tokens.shape
    hidden = w_down.shape[-2] * buckets if 2 in MOVED else w_down.shape[0] * w_down.shape[1]
    part = width // (buckets * seq)
    tall, thin = (seq, rows, width), rows // chunks
    flat = (seq, rows, hidden)
    blocks = pltpu.VMEM((3 * chunks, seq - 1, thin, width), BF16)
    kinds = ("hold", "hold", "stay")
    shapes, sums_out, scratch, n_sems = sums_shapes(
        buckets, seq, [(width, hidden), (width, hidden), (hidden, width)], kinds, near=True
    )
    n_sems += 64 + 3 * chunks * (2 * CUTS + 2) * seq
    results = pl.pallas_call(
        functools.partial(middle_kernel, buckets, seq, chunks, kinds),
        out_shape=[
            jax.ShapeDtypeStruct((rows, width), BF16),
            jax.ShapeDtypeStruct((rows, width), F32),
            jax.ShapeDtypeStruct(tall, BF16),
            jax.ShapeDtypeStruct((8, width), F32),
            *sums_out,
        ],
        in_specs=[vmem] * 4 + [smem] + [vmem] * 2 + [any_spec] * 3,
        out_specs=[vmem] * 7,
        scratch_shapes=[
            pltpu.VMEM((buckets, seq, part, hidden), BF16),
            pltpu.VMEM((buckets, seq, part, hidden), BF16),
            pltpu.VMEM((buckets, hidden // buckets, width), BF16),
            pltpu.VMEM(tall, BF16),
            pltpu.VMEM(tall, BF16),
            *([pltpu.VMEM(flat, BF16)] * 3),
            pltpu.VMEM((chunks, seq * thin, hidden), F32),
            pltpu.VMEM((chunks, seq * thin, hidden), F32),
            pltpu.VMEM((rows, width), F32),
            pltpu.VMEM((rows, width), F32),
            pltpu.VMEM((rows, width), F32),
            pltpu.VMEM((chunks, seq, thin, width), BF16),
            blocks,
            blocks,
            pltpu.VMEM((rows, 128), F32),
            pltpu.SemaphoreType.DMA((n_sems,)),
            pltpu.SemaphoreType.DMA((n_sems,)),
            *[pltpu.VMEM(shape, BF16) for shape in shapes],
            *scratch,
        ],
        compiler_params=pltpu.CompilerParams(
            collective_id=11, has_side_effects=True, vmem_limit_bytes=62 * 2**20
        ),
    )(
        mixed.reshape(seq, rows, mixed.shape[1]),
        w_out,
        tokens,
        cotangent,
        counts,
        gain_rows,
        mod_rows,
        w_gate,
        w_up,
        w_down,
    )
    return results[:4], (results[4], results[5], results[6].reshape(-1, results[6].shape[-1]))


LATE = (1, 2, 3, 11, 12, 19, 20, 21, 22)


def backward_kernel(buckets, seq, kinds, *refs):
    count = len(kinds)
    (
        d_attn,
        w_query,
        w_key,
        w_value,
        w_out,
        query,
        key,
        value,
        cap_key,
        cap_value,
        cross_out,
        query_raw,
        key_raw,
        cap_raw,
        gain_rows,
        mod_rows,
        counts,
        cap_lens,
        mixed,
        hidden,
        captions,
        tokens,
        d_tokens,
        row_sums,
    ) = refs[:24]
    holds, strip_outs = refs[24:26], refs[29:31]
    tokens_grad, mod_all, small_out, refs = refs[26], refs[27], refs[28], refs[31:]
    outs, refs = refs[:count], refs[count:]
    mixed_low, cross_low, query_acc, key_acc, value_acc, cap_key_acc, cap_value_acc = refs[:7]
    d_query, d_key, d_value, d_cap_key, d_cap_value, d_hidden, vec = refs[7:14]
    mod_give, mod_got, mod_sum, wide_give, wide_got, slim_give, slim_got = refs[14:21]
    key_bias, cap_bias, parts, from_left, from_right, send, recv = refs[21:28]
    late, refs = refs[28 : 28 + len(LATE)], refs[28 + len(LATE) :]
    strips, refs = refs[:2], refs[2:]
    grads, refs = refs[:count], refs[count:]
    b, s = lax.axis_index("bucket"), lax.axis_index("seq")
    copies = Copies(send, recv)
    far = (w_query, w_key, w_value, query_raw, key_raw, hidden, captions, tokens, d_tokens)
    loads = [copies.local(src, dst) for src, dst in zip(far, late, strict=True)]
    for at in (6, 3, 4, 0, 1, 2, 5, 7, 8):
        loads[at].start()
    w_query, w_key, w_value, query_raw, key_raw, hidden, captions, tokens, d_tokens = late
    sums = GradSums(copies, b, s, buckets, seq, kinds, grads, outs, refs, near=True)
    peers = greet_all(b, s, buckets, seq)

    rows, share = query.shape
    width = parts.shape[-1]
    pairs = share // 128
    chips = buckets // 2
    span_block = 256
    scale = HEAD_DIM**-0.5

    def gain_of(row, pair):
        at = pl.multiple_of(s * share + pair * 128, 128)
        return gain_rows[row : row + 1, pl.ds(at, 128)]

    vec[...] = jnp.zeros_like(vec)
    mod_give[...] = jnp.zeros_like(mod_give)
    wide_give[...] = jnp.zeros_like(wide_give)
    slim_give[...] = jnp.zeros_like(slim_give)
    fill_rows(key_bias, counts[b], 0, 0.0, -1e30)
    fill_rows(cap_bias, cap_lens[b], 0, 0.0, -1e30)
    mixed_low[...] = right_dot(d_attn[...], w_out[...]).astype(BF16)

    def own_sum(row, pair, total):
        vec[row : row + 1, pl.ds(pl.multiple_of(s * share + pair * 128, 128), 128)] = total

    def cross_part(pair):
        lane = slice(pair * 128, (pair + 1) * 128)
        gate = jnp.tanh(gain_of(7, pair))

        def body(i, total):
            at = pl.ds(pl.multiple_of(i * 128, 128), 128)
            d = mixed_low[at, lane].astype(F32)
            cross_low[at, lane] = (gate * d).astype(BF16)
            return total + jnp.sum(d * cross_out[at, lane], axis=0, keepdims=True)

        total = lax.fori_loop(0, rows // 128, body, jnp.zeros((1, 128), F32))
        own_sum(7, pair, total * (1.0 - gate * gate))

    def attend_back(pair, k_ref, v_ref, bias, d_ref, k_acc, v_acc, add):
        lane = slice(pair * 128, (pair + 1) * 128)
        low = low_half((span_block, 128))
        k_turned = k_ref[:, lane].T
        k_acc[:, lane] = jnp.zeros((k_acc.shape[0], 128), F32)
        v_acc[:, lane] = jnp.zeros((v_acc.shape[0], 128), F32)

        def body(i, carry):
            at = pl.ds(pl.multiple_of(i * span_block, span_block), span_block)
            q = query[at, lane] * jnp.asarray(scale, BF16)
            d = d_ref[at, lane]
            found = []
            for keep in (low, jnp.logical_not(low)):
                q_half = jnp.where(keep, q, jnp.zeros_like(q))
                d_half = jnp.where(keep, d, jnp.zeros_like(d))
                scores = right_dot(k_ref[:, lane], q_half)
                scores = scores + jnp.concatenate([bias[...], bias[...]], axis=1)
                weights = jnp.exp(scores)
                probs = weights * (1.0 / jnp.sum(weights, axis=0, keepdims=True))
                d_probs = right_dot(v_ref[:, lane], d_half)
                delta = jnp.sum(probs * d_probs, axis=0, keepdims=True)
                d_scores = (probs * (d_probs - delta)).astype(BF16)
                k_acc[:, lane] += bf_dot(d_scores, q_half)
                v_acc[:, lane] += bf_dot(probs.astype(BF16), d_half)
                found.append(bf_dot(k_turned, d_scores))
            turned = jnp.concatenate([found[0][:HEAD_DIM], found[1][HEAD_DIM:]], axis=0)
            d_q = turned.T * scale
            query_acc[at, lane] = query_acc[at, lane] + d_q if add else d_q
            return carry

        lax.fori_loop(0, rows // span_block, body, 0)

    def norm_back(raw, d_norm, out, row, sum_row):
        for pair in range(pairs):
            lane = slice(pair * 128, (pair + 1) * 128)
            gain = gain_of(row, pair)

            def body(i, total):
                at = pl.ds(pl.multiple_of(i * 128, 128), 128)
                x, d = raw[at, lane], d_norm[at, lane]
                size = pair_scale(x, 1e-06)
                normed, inner = x * size, d * gain
                mean = pair_sums(inner * normed) * (1.0 / HEAD_DIM)
                out[at, lane] = (size * (inner - normed * mean)).astype(BF16)
                return total + jnp.sum(d * normed, axis=0, keepdims=True)

            total = lax.fori_loop(0, raw.shape[0] // 128, body, jnp.zeros((1, 128), F32))
            own_sum(sum_row, pair, total)

    def weight_grads(left, chosen):
        part = left.shape[1] // chips
        for i in range(chips):
            turned = left[:, i * part : (i + 1) * part].T
            for w, right in chosen:
                total = bf_dot(turned, right[...])
                grads[w][i] = total.astype(BF16).reshape(2, part // 2, total.shape[-1])
            yield
        for w, _ in chosen:
            sums.begin(w)

    def out_grad():
        total = bf_dot(mixed[...].T, d_attn[...]).astype(BF16)
        part = share // buckets
        for block, p in enumerate(spread(buckets)):
            grads[0][p // 2, p % 2] = total[block * part : (block + 1) * part]
        sums.begin(0)

    pl.semaphore_wait(pltpu.get_barrier_semaphore(), peers)
    strip_moves = []
    for hold, strip in zip(holds, strips, strict=True):
        strip[s] = hold[s]
        for j in range(1, seq):
            peer = lax.rem(s + j, seq)
            strip_moves.append(sums.go(copies.remote(hold.at[peer], strip.at[s], b, peer)))
    for pair in range(pairs):
        cross_part(pair)
        attend_back(pair, cap_key, cap_value, cap_bias, cross_low, cap_key_acc, cap_value_acc, False)
    norm_back(cap_raw, cap_key_acc, d_cap_key, 6, 6)
    d_cap_value[...] = cap_value_acc[...].astype(BF16)
    loads[6].wait()
    for _ in weight_grads(captions, ((1, d_cap_key), (2, d_cap_value))):
        pass
    def deal_back():
        for move in strip_moves:
            move.wait_recv()
        for strip, out in zip(strips, strip_outs, strict=True):
            for j in range(seq):
                for part in range(strip.shape[2] // 128):
                    cols = slice((part * seq + j) * 128, (part * seq + j + 1) * 128)
                    out[:, cols] = strip[j, :, part * 128 : (part + 1) * 128].astype(F32)

    steps = (lambda: sums.stage_a(1), lambda: sums.stage_a(2), lambda: sums.stage_b(1))
    for pair in range(pairs):
        attend_back(pair, key, value, key_bias, mixed_low, key_acc, value_acc, True)
        steps[pair]()
    for at in (3, 4, 0, 1, 2, 5, 7, 8):
        loads[at].wait()
    norm_back(query_raw, query_acc, d_query, 4, 4)
    norm_back(key_raw, key_acc, d_key, 5, 5)
    d_value[...] = value_acc[...].astype(BF16)
    pour = Pour(copies, parts, from_left, from_right, b, s, seq)
    wide = 512
    for at in range(0, width, wide):
        cols = slice(at, at + wide)
        total = right_dot(d_query[...], w_query[cols, :]) + right_dot(d_key[...], w_key[cols, :])
        total = total + right_dot(d_value[...], w_value[cols, :])
        parts[:, :, cols] = total.astype(BF16).reshape(seq, rows // seq, wide)
    pieces = weight_grads(hidden, ((3, d_query), (4, d_key), (5, d_value)))
    between = {1: out_grad, 2: lambda: sums.stage_b(2)}
    for q in range(pour.count):
        pour.step(q)
        if q in between:
            between[q]()
        elif q > 2:
            next(pieces, None)
    for _ in pieces:
        pass
    deal_back()
    sums.stage_a(0)
    sums.stage_c(1)
    sums.stage_c(2)
    pour.end(d_hidden)

    factor = gain_rows[0:1, :] * (1.0 + mod_rows[0:1, :])

    def body(i, total):
        at = pl.ds(pl.multiple_of(i * 16, 16), 16)
        x, d = tokens[at, :].astype(F32), d_hidden[at, :]
        size = lax.rsqrt(jnp.mean(x * x, axis=-1, keepdims=True) + 1e-05)
        normed, inner = x * size, d * factor
        mean = jnp.mean(inner * normed, axis=-1, keepdims=True)
        tokens_grad[at, :] = d_tokens[at, :] + size * (inner - normed * mean)
        return total + jnp.sum(d * normed, axis=0, keepdims=True)

    total = lax.fori_loop(0, tokens.shape[0] // 16, body, jnp.zeros((1, width), F32))
    post, last = jnp.tanh(mod_rows[1:2, :]), jnp.tanh(mod_rows[3:4, :])
    vec[8:9, :] = total * gain_rows[0:1, :]
    vec[9:10, :] = row_sums[0:1, :] * gain_rows[1:2, :] * (1.0 - post * post)
    vec[10:11, :] = row_sums[1:2, :] * gain_rows[2:3, :]
    vec[11:12, :] = row_sums[2:3, :] * gain_rows[3:4, :] * (1.0 - last * last)
    vec[0:1, :] = total * (1.0 + mod_rows[0:1, :])
    vec[1:2, :] = row_sums[0:1, :] * post
    vec[2:3, :] = row_sums[1:2, :] * (1.0 + mod_rows[2:3, :])
    vec[3:4, :] = row_sums[2:3, :] * last
    piece, wide = width // 4, width // buckets
    slim = wide // seq
    for t in range(seq):
        for j in range(4):
            mod_give[t, j : j + 1, :] = vec[8 + t : 9 + t, j * piece : (j + 1) * piece]
    for t in range(buckets):
        wide_give[t, :, :wide] = vec[0:8, t * wide : (t + 1) * wide]
    mod_moves, wide_moves = [], []
    for j in range(1, seq):
        peer = lax.rem(s + j, seq)
        mod_moves.append(sums.go(copies.remote(mod_give.at[peer], mod_got.at[j], b, peer)))
    for j in range(1, buckets):
        peer = lax.rem(b + j, buckets)
        wide_moves.append(sums.go(copies.remote(wide_give.at[peer], wide_got.at[j], peer, s)))
    sums.stage_a(3)
    sums.stage_a(4)
    sums.stage_a(5)
    total = mod_give[s]
    for j, move in enumerate(mod_moves, 1):
        move.wait_recv()
        total = total + mod_got[j]
    mod_sum[...] = total
    mod_next, slim_next = [], []
    for j in range(1, buckets):
        peer = lax.rem(b + j, buckets)
        mod_next.append(sums.go(copies.remote(mod_sum, mod_all.at[b], peer, s)))
    mod_own = copies.local(mod_sum, mod_all.at[b])
    mod_own.start()
    total = wide_give[b]
    for j, move in enumerate(wide_moves, 1):
        move.wait_recv()
        total = total + wide_got[j]
    for t in range(seq):
        slim_give[t, :, :slim] = total[:, t * slim : (t + 1) * slim]
    for j in range(1, seq):
        peer = lax.rem(s + j, seq)
        slim_next.append(sums.go(copies.remote(slim_give.at[peer], slim_got.at[j], b, peer)))
    for w in (0, 3, 4, 5):
        sums.stage_b(w)
    sums.stage_c(0)
    for w in (3, 4, 5):
        sums.stage_c(w)
    sums.stage_d(0)
    total = slim_give[s]
    for j, move in enumerate(slim_next, 1):
        move.wait_recv()
        total = total + slim_got[j]
    small_out[...] = total
    for move in mod_next:
        move.wait_recv()
    mod_own.wait()
    sums.end()


def backward_all(buckets, seq, inputs, shapes, kinds):
    any_spec = pl.BlockSpec(memory_space=pl.ANY)
    vmem = pl.BlockSpec(memory_space=pltpu.VMEM)
    smem = pl.BlockSpec(memory_space=pltpu.SMEM)
    shapes, outs, scratch, n_sems = sums_shapes(buckets, seq, shapes, kinds, near=True)
    query, cap_key, tokens = inputs[5], inputs[8], inputs[21]
    rows, width = tokens.shape
    vec = (16, width)
    n_sems += 12 * seq + 4 * buckets + len(LATE) + 2 * seq
    results = pl.pallas_call(
        functools.partial(backward_kernel, buckets, seq, tuple(kinds)),
        out_shape=[
            jax.ShapeDtypeStruct((rows, width), F32),
            jax.ShapeDtypeStruct((buckets, 8, width // 4), F32),
            jax.ShapeDtypeStruct((8, 128), F32),
            *[jax.ShapeDtypeStruct((x.shape[1], x.shape[2] * seq), F32) for x in inputs[24:26]],
            *outs,
        ],
        in_specs=[
            smem if at in (16, 17) else any_spec if at in LATE else vmem for at in range(len(inputs))
        ],
        out_specs=[vmem, any_spec] + [vmem] * (3 + len(outs)),
        scratch_shapes=[
            pltpu.VMEM(query.shape, BF16),
            pltpu.VMEM(query.shape, BF16),
            pltpu.VMEM(query.shape, F32),
            pltpu.VMEM(query.shape, F32),
            pltpu.VMEM(query.shape, F32),
            pltpu.VMEM(cap_key.shape, F32),
            pltpu.VMEM(cap_key.shape, F32),
            pltpu.VMEM(query.shape, BF16),
            pltpu.VMEM(query.shape, BF16),
            pltpu.VMEM(query.shape, BF16),
            pltpu.VMEM(cap_key.shape, BF16),
            pltpu.VMEM(cap_key.shape, BF16),
            pltpu.VMEM((rows, width), F32),
            pltpu.VMEM(vec, F32),
            pltpu.VMEM((seq, 8, width // 4), F32),
            pltpu.VMEM((seq, 8, width // 4), F32),
            pltpu.VMEM((8, width // 4), F32),
            pltpu.VMEM((buckets, 8, 256), F32),
            pltpu.VMEM((buckets, 8, 256), F32),
            pltpu.VMEM((seq, 8, 128), F32),
            pltpu.VMEM((seq, 8, 128), F32),
            pltpu.VMEM((query.shape[0], 128), F32),
            pltpu.VMEM((cap_key.shape[0], 128), F32),
            pltpu.VMEM((seq, rows, width), BF16),
            pltpu.VMEM((seq - 1, rows, width), BF16),
            pltpu.VMEM((seq - 1, rows, width), BF16),
            pltpu.SemaphoreType.DMA((n_sems,)),
            pltpu.SemaphoreType.DMA((n_sems,)),
            *[pltpu.VMEM(inputs[at].shape, inputs[at].dtype) for at in LATE],
            *[pltpu.VMEM(x.shape, BF16) for x in inputs[24:26]],
            *[pltpu.VMEM(shape, BF16) for shape in shapes],
            *scratch,
        ],
        compiler_params=pltpu.CompilerParams(
            collective_id=10, has_side_effects=True, vmem_limit_bytes=62 * 2**20
        ),
    )(*inputs)
    sums = [*results[3:5], *(out.reshape(-1, out.shape[-1]) for out in results[5:])]
    return results[0], results[1], results[2], sums


def last_kernel(buckets, seq, slim, *refs):
    cond, mod_all, small = refs[:3]
    count = (len(refs) - 7) // 2
    sources, refs = refs[3 : 3 + count], refs[3 + count :]
    mod_grad, gains, cross = refs[:3]
    targets, sems = refs[3 : 3 + count], refs[3 + count]
    copies = [
        pltpu.make_async_copy(a, b, sems.at[i])
        for i, (a, b) in enumerate(zip(sources, targets, strict=True))
    ]
    for copy in copies:
        copy.start()
    piece = mod_all.shape[2]
    for j in range(4):
        total = None
        for k in range(buckets):
            term = cond[:, k : k + 1] * mod_all[k, j : j + 1, :]
            total = term if total is None else total + term
        mod_grad[:, j * piece : (j + 1) * piece] = total
    gains[...] = small[0:7, :slim]
    cross[...] = small[7:8, :slim]
    for copy in copies:
        copy.wait()


def last_all(buckets, seq, slim, cond, mod_all, small, results):
    any_spec = pl.BlockSpec(memory_space=pl.ANY)
    vmem = pl.BlockSpec(memory_space=pltpu.VMEM)
    outs = pl.pallas_call(
        functools.partial(last_kernel, buckets, seq, slim),
        out_shape=[
            jax.ShapeDtypeStruct((cond.shape[0], 4 * mod_all.shape[2]), F32),
            jax.ShapeDtypeStruct((7, slim), F32),
            jax.ShapeDtypeStruct((1, slim), F32),
            *[jax.ShapeDtypeStruct(x.shape, x.dtype) for x in results],
        ],
        in_specs=[vmem] * 3 + [any_spec] * len(results),
        out_specs=[vmem] * (3 + len(results)),
        scratch_shapes=[pltpu.SemaphoreType.DMA((len(results),))],
        compiler_params=pltpu.CompilerParams(vmem_limit_bytes=62 * 2**20),
    )(cond, mod_all, small, *results)
    return outs[0], outs[1], outs[2].reshape(slim), outs[3:]


def on_device(
    tokens,
    captions,
    cotangent,
    counts,
    cap_lens,
    steps_t,
    w_query,
    w_key,
    w_value,
    w_out,
    w_cap_key,
    w_cap_value,
    w_gate,
    w_up,
    w_down,
    w_mod,
    gains,
    cross_gate,
):
    buckets, seq = lax.axis_size("bucket"), lax.axis_size("seq")
    b, s = lax.axis_index("bucket"), lax.axis_index("seq")
    place = b * seq + s
    rows, width = tokens.shape
    span = rows * seq
    share = width // seq

    cond_size = w_mod.shape[0] * buckets * seq
    cond = jax.nn.silu(time_embed(steps_t, cond_size)).astype(BF16)
    cond_part = lax.dynamic_slice_in_dim(cond, place * w_mod.shape[0], w_mod.shape[0], 1)
    slim = gains.shape[1]
    small = jnp.concatenate([gains, cross_gate[None]], axis=0).astype(F32)
    small = jnp.pad(small, ((0, 0), (0, 128 - slim)))
    feed = [w_gate, w_up, w_down]
    early = [w for w in range(3) if w not in MOVED]
    cap_all, weights, inner = forward_all(
        buckets,
        seq,
        tokens,
        captions,
        small,
        slim,
        cond_part,
        w_mod,
        [counts, cap_lens],
        [w_query, w_key, w_value, w_cap_key, w_cap_value, w_out, *(feed[w] for w in early)],
        ["col", "col", "col", "col", "col", "row", *(("cut", "cut", "stay")[w] for w in early)],
    )
    wq, wk, wv, wck, wcv, wo = (x.reshape(-1, x.shape[-1]) for x in weights[:6])
    for w, full in zip(early, weights[6:], strict=True):
        feed[w] = full
    caps = cap_all.reshape(-1, captions.shape[1])
    small_rows, mod, hidden, query_proj, key_proj, cap_proj = inner[:6]
    query, key, value, cap_key, cap_value = inner[6:11]
    cross_out, mixed_low = inner[11:]
    (block_out, d_tokens, d_attn_all, row_sums), (h_gate, h_up, s_down) = middle_all(
        buckets,
        seq,
        mixed_low,
        (wo, *feed),
        tokens,
        cotangent,
        counts,
        small_rows,
        mod,
    )
    tokens_grad, mod_all, small_sums, sums = backward_all(
        buckets,
        seq,
        [
            d_attn_all.reshape(span, width),
            wq,
            wk,
            wv,
            wo,
            query,
            key,
            value,
            cap_key,
            cap_value,
            cross_out,
            query_proj,
            key_proj,
            cap_proj,
            small_rows,
            mod,
            counts,
            cap_lens,
            mixed_low,
            hidden,
            caps,
            tokens,
            d_tokens,
            row_sums,
            h_gate,
            h_up,
        ],
        [x.shape for x in (wo, wck, wcv, wq, wk, wv)],
        ["row", "col", "col", "col", "col", "col"],
    )
    s_gate, s_up, s_out, s_cap_key, s_cap_value, s_query, s_key, s_value = sums

    cond_size = cond.shape[1] // buckets
    cond_cols = lax.dynamic_slice_in_dim(cond, b * cond_size, cond_size, 1).astype(F32).T
    results = [block_out, tokens_grad, s_query, s_key, s_value, s_out]
    results += [s_cap_key, s_cap_value, s_gate, s_up, s_down]
    s_mod, s_gains, s_cross, results = last_all(
        buckets, seq, slim, cond_cols, mod_all, small_sums, results
    )
    return (*results, s_mod, s_gains, s_cross)


def solution(mesh):
    spread = P(("bucket", "seq"), None)
    in_specs = (
        *([spread] * 3),
        *([P()] * 3),
        *([spread] * 10),
        P(None, ("bucket", "seq")),
        P(("bucket", "seq")),
    )
    out_specs = (
        spread,
        spread,
        *([P("bucket", "seq")] * 10),
        P(None, ("bucket", "seq")),
        P(("bucket", "seq")),
    )
    buckets, seq = mesh.shape["bucket"], mesh.shape["seq"]

    def step(*args):
        tokens, weight = args[0], args[6]
        tiled = weight.shape[0] % 16 == 0 and weight.shape[1] // seq % 128 == 0
        fits = buckets == 8 and seq == 4 and tokens.shape[0] % 64 == 0
        return (on_device if tiled and fits else on_device_general)(*args)

    return jax.shard_map(
        step, mesh=mesh, in_specs=in_specs, out_specs=out_specs, check_vma=False
    )
```

```python
import functools
import math

import jax
import jax.numpy as jnp
from jax import lax
from jax.experimental import pallas as pl
from jax.experimental.pallas import tpu as pltpu
from jax.sharding import PartitionSpec as P

HEAD_DIM = 64
MESH = pl.DeviceIdType.MESH
F32, BF16 = jnp.float32, jnp.bfloat16
CHUNKS, CUTS, FLIGHT = 2, 2, 2


def rms_rows(values):
    return values * lax.rsqrt(jnp.mean(values * values, axis=-1, keepdims=True) + 1e-05)


def head_rms(values):
    shaped = values.reshape(values.shape[:-1] + (values.shape[-1] // HEAD_DIM, HEAD_DIM))
    shaped = shaped * lax.rsqrt(jnp.mean(shaped * shaped, axis=-1, keepdims=True) + 1e-06)
    return shaped.reshape(values.shape)


def time_embed(steps, width):
    half_width = width // 2
    freqs = jnp.exp(-math.log(10000.0) * jnp.arange(half_width, dtype=F32) / half_width)
    angles = steps.astype(F32)[:, None] * freqs
    return jnp.concatenate([jnp.cos(angles), jnp.sin(angles)], axis=1)


def pick_entry(table, index):
    return jnp.sum(jnp.where(jnp.arange(table.shape[0]) == index, table, 0))


def bf_dot(left, right):
    return jnp.dot(left, right, preferred_element_type=F32)


def left_dot(rows_left, rows_right):
    return lax.dot_general(
        rows_left, rows_right, (((0,), (0,)), ((), ())), preferred_element_type=F32
    )


def right_dot(left, right):
    return lax.dot_general(left, right, (((1,), (1,)), ((), ())), preferred_element_type=F32)


def pre_attn(tokens_in, gain_pre, scale_attn):
    return rms_rows(tokens_in) * gain_pre * (1.0 + scale_attn)


def qk_norm(query_in, key_in, gain_query, gain_key):
    return (head_rms(query_in) * gain_query, head_rms(key_in) * gain_key)


def cap_norm(key_in, gain_cap):
    return head_rms(key_in) * gain_cap


def middle(tokens_in, attn_out, gain_post, gate_attn, gain_ffn, scale_ffn):
    resid_one = tokens_in + jnp.tanh(gate_attn) * rms_rows(attn_out) * gain_post
    return (resid_one, rms_rows(resid_one) * gain_ffn * (1.0 + scale_ffn))


def activate(gate_proj, up_proj):
    return jax.nn.silu(gate_proj) * up_proj


def finish(resid_one, ffn_out, gain_last, gate_ffn):
    return resid_one + jnp.tanh(gate_ffn) * rms_rows(ffn_out) * gain_last


def flip(index, bit):
    return index + bit - 2 * bit * lax.rem(lax.div(index, bit), 2)


def slot(index, buckets):
    if buckets != 8:
        return index
    high, low = lax.div(index, 4), lax.rem(index, 4)
    return 4 * high + 2 * lax.rem(low, 2) + lax.div(low, 2)


class Copies:
    def __init__(self, send, recv):
        self.send, self.recv, self.used = send, recv, 0

    def take(self, count=1):
        first = self.used
        self.used += count
        assert self.used <= self.send.shape[0], self.used
        return first

    def remote(self, src, dst, b, s, at=None):
        at = self.take() if at is None else at
        return pltpu.make_async_remote_copy(
            src_ref=src,
            dst_ref=dst,
            send_sem=self.send.at[at],
            recv_sem=self.recv.at[at],
            device_id={"bucket": b, "seq": s},
            device_id_type=MESH,
        )

    def local(self, src, dst):
        return pltpu.make_async_copy(src, dst, self.send.at[self.take()])


def greet(b, s):
    pl.semaphore_signal(
        pltpu.get_barrier_semaphore(),
        inc=1,
        device_id={"bucket": b, "seq": s},
        device_id_type=MESH,
    )


class Relay:
    def __init__(self, copies, own, out, b, s, seq, part=None):
        self.copies, self.own, self.out, self.b, self.s, self.seq = copies, own, out, b, s, seq
        self.part = part
        self.base = {1: copies.take(seq - 1), -1: copies.take(seq - 1)}
        self.up = jnp.where(s < seq - 1, s + 1, s - 1)
        self.down = jnp.where(s > 0, s - 1, s + 1)
        self.kept = None if own is None else copies.local(own, out.at[s])

    def packet(self, way, j):
        at = self.s - way * j
        block = self.out.at[at] if self.part is None else self.out.at[at, self.part]
        return self.copies.remote(
            self.own if j == 0 and self.own is not None else block,
            block,
            self.b,
            self.up if way > 0 else self.down,
            self.base[way] + j,
        )

    def sends(self, way):
        return self.s < self.seq - 1 if way > 0 else self.s > 0

    def has(self, way, j):
        return self.s >= j if way > 0 else self.s + j <= self.seq - 1

    def start(self, j):
        if j == 0 and self.kept is not None:
            self.kept.start()
        for way in (1, -1):
            if j == self.seq - 1:

                @pl.when(jnp.logical_not(self.sends(way)))
                def _():
                    for k in range(self.seq - 1):
                        self.packet(way, k).wait_recv()

                continue

            @pl.when(jnp.logical_and(self.sends(way), self.has(way, j)))
            def _():
                if j > 0:
                    self.packet(way, j - 1).wait_recv()
                self.packet(way, j).start()

    def sent(self, j):
        for way in (1, -1):

            @pl.when(jnp.logical_and(self.sends(way), self.has(way, j)))
            def _():
                self.packet(way, j).wait_send()

        if j == 0 and self.kept is not None:
            self.kept.wait()


def greet_line(b, s, seq):
    @pl.when(s > 0)
    def _():
        greet(b, s - 1)

    @pl.when(s < seq - 1)
    def _():
        greet(b, s + 1)

    peers = jnp.where(s > 0, 1, 0) + jnp.where(s < seq - 1, 1, 0)
    pl.semaphore_wait(pltpu.get_barrier_semaphore(), peers)


def halves_of(shape):
    if len(shape) == 3:
        return shape[0] // 2
    return (shape[0] // 32) * 16 if shape[0] >= 32 else shape[0] // 2


def gather_kernel(buckets, seq, kinds, *refs):
    count = len(kinds)
    tokens, captions, small, cond, w_mod = refs[:5]
    shards = refs[5 : 5 + count]
    tok_all, cap_all, small_all, mod_out = refs[5 + count : 9 + count]
    fulls = refs[9 + count : 9 + 2 * count]
    part, got_bucket, got_seq, mod_sum, send, recv = refs[9 + 2 * count :]
    b, s = lax.axis_index("bucket"), lax.axis_index("seq")
    copies = Copies(send, recv)
    chips = buckets // 2
    place = b * seq + s
    to_b, to_s = lax.rem(place, buckets), lax.div(place, buckets)
    back = s * buckets + b
    from_b, from_s = lax.div(back, seq), lax.rem(back, seq)
    stays = jnp.logical_and(to_b == b, to_s == s)

    lanes = part.shape[2]
    for j in range(part.shape[1]):
        part[:, j, :] = bf_dot(cond[...], w_mod[:, j * lanes : (j + 1) * lanes])

    for k in range(1, buckets):
        greet(lax.rem(b + k, buckets), s)
    for k in range(1, seq):
        greet(b, lax.rem(s + k, seq))

    @pl.when(jnp.logical_not(stays))
    def _():
        greet(from_b, from_s)

    peers = buckets - 1 + seq - 1 + jnp.where(stays, 0, 1)
    pl.semaphore_wait(pltpu.get_barrier_semaphore(), peers)

    sent = []

    def go(copy):
        copy.start()
        sent.append(copy)
        return copy

    mod_moves = []
    for k in range(1, buckets):
        peer = lax.rem(b + k, buckets)
        mod_moves.append(go(copies.remote(part.at[peer], got_bucket.at[k], peer, s)))
    small_moves = []
    for k in range(1, seq):
        peer = lax.rem(s + k, seq)
        small_moves.append(go(copies.remote(small, small_all.at[b, s], b, peer)))
    small_own = copies.local(small, small_all.at[b, s])
    small_own.start()

    tok = Relay(copies, tokens, tok_all, b, s, seq)
    cap = Relay(copies, captions, cap_all, b, s, seq)
    queue = [(tok, j) for j in range(seq)] + [(cap, j) for j in range(seq)]
    ahead = [(None, at) for at in range(count)]
    items = []
    while queue or ahead:
        items += queue[:1] + ahead[:1]
        queue, ahead = queue[1:], ahead[1:]

    first = [None] * count

    def depart(at):
        kind, shard, full = kinds[at], shards[at], fulls[at]
        if kind == "row":
            move = copies.remote(shard, full.at[to_b], to_b, to_s)
            keep = copies.local(shard, full.at[b])

            @pl.when(jnp.logical_not(stays))
            def _():
                move.start()

            @pl.when(stays)
            def _():
                keep.start()

            first[at] = (move, keep)
            return
        wide = full.shape[-1]

        def columns(peer):
            if kind == "cut":
                return shard.at[peer]
            return shard.at[:, pl.ds(pl.multiple_of(peer * wide, 128), wide)]

        moves = []
        for k in range(1, seq):
            peer = lax.rem(s + k, seq)
            move = copies.remote(columns(peer), full.at[b, s], b, peer)
            move.start()
            moves.append(move)
        keep = copies.local(columns(s), full.at[b, s])
        keep.start()
        first[at] = (moves, keep)

    def arrived(at):
        moves, keep = first[at]
        if kinds[at] == "row":

            @pl.when(jnp.logical_not(stays))
            def _():
                moves.wait()

            @pl.when(stays)
            def _():
                keep.wait()

            return
        for move in moves:
            move.wait()
        keep.wait()

    twin = flip(b, 1)
    second = [None] * count
    if chips == 4:
        near_x, near_y = flip(b, 2), flip(b, 4)
        far = flip(near_x, 4)

        def stage_a(at):
            full = fulls[at]
            second[at] = {
                "x": go(copies.remote(full.at[b], full.at[b], near_x, s)),
                "y": go(copies.remote(full.at[b], full.at[b], near_y, s)),
                "twin": [go(copies.remote(full.at[b], full.at[b], twin, s))],
            }

        def stage_b(at):
            full, now = fulls[at], second[at]
            cut = halves_of(full.shape[1:])
            now["x"].wait_recv()
            block = full.at[near_x, pl.ds(0, cut)]
            now["dy"] = go(copies.remote(block, block, near_y, s))
            block = full.at[near_x]
            now["twin"].append(go(copies.remote(block, block, twin, s)))
            now["y"].wait_recv()
            block = full.at[near_y, pl.ds(cut, full.shape[1] - cut)]
            now["dx"] = go(copies.remote(block, block, near_x, s))
            block = full.at[near_y]
            now["twin"].append(go(copies.remote(block, block, twin, s)))

        def stage_c(at):
            full, now = fulls[at], second[at]
            now["dy"].wait_recv()
            now["dx"].wait_recv()
            block = full.at[far]
            now["twin"].append(go(copies.remote(block, block, twin, s)))

    else:

        def stage_a(at):
            full = fulls[at]
            second[at] = {"far": [], "twin": []}
            for k in range(1, chips):
                peer = lax.rem(b + 2 * k, buckets)
                second[at]["far"].append(go(copies.remote(full.at[b], full.at[b], peer, s)))
            second[at]["twin"].append(go(copies.remote(full.at[b], full.at[b], twin, s)))

        def stage_b(at):
            full = fulls[at]
            for k, copy in enumerate(second[at]["far"], 1):
                copy.wait_recv()
                block = full.at[lax.rem(b + buckets - 2 * k, buckets)]
                second[at]["twin"].append(go(copies.remote(block, block, twin, s)))

        def stage_c(at):
            pass

    def begin(i):
        relay, j = items[i]
        if relay is None:
            depart(j)
        else:
            relay.start(j)

    begin(0)
    begin(1)
    for move in small_moves:
        move.wait_recv()
    small_own.wait()
    small_next = []
    for k in range(1, buckets):
        peer = lax.rem(b + k, buckets)
        small_next.append(go(copies.remote(small_all.at[b], small_all.at[b], peer, s)))
    total = part[b]
    for k, move in enumerate(mod_moves, 1):
        move.wait_recv()
        total = total + got_bucket[k]
    mod_sum[...] = total
    mod_next = []
    for k in range(1, seq):
        peer = lax.rem(s + k, seq)
        mod_next.append(go(copies.remote(mod_sum, got_seq.at[k], b, peer)))

    for i, (relay, j) in enumerate(items):
        if relay is None:
            arrived(j)
        elif j <= seq - 2:
            relay.sent(j)
        if i + 2 < len(items):
            begin(i + 2)
        if relay is None:
            stage_a(j)
            if j >= 1:
                stage_b(j - 1)
            if j >= 2:
                stage_c(j - 2)
    stage_b(count - 1)
    if count >= 2:
        stage_c(count - 2)
    stage_c(count - 1)

    total = mod_sum[...]
    for k, move in enumerate(mod_next, 1):
        move.wait_recv()
        total = total + got_seq[k]
    mod_out[...] = total
    for move in small_next:
        move.wait_recv()
    for now in second:
        for move in now["twin"]:
            move.wait_recv()
    for move in sent:
        move.wait_send()


def gather_all(buckets, seq, tokens, captions, small, cond, w_mod, shards, kinds):
    any_spec = pl.BlockSpec(memory_space=pl.ANY)
    vmem = pl.BlockSpec(memory_space=pltpu.VMEM)
    fulls, inputs, names = [], [], []
    for shard, kind in zip(shards, kinds, strict=True):
        rows, wide = shard.shape
        if kind == "row":
            fulls.append(jax.ShapeDtypeStruct((buckets, rows, wide), BF16))
        else:
            part = wide // seq
            fulls.append(jax.ShapeDtypeStruct((buckets, seq, rows, part), BF16))
            if part % 128:
                kind = "cut"
                shard = shard.reshape(rows, seq, part).transpose(1, 0, 2)
        inputs.append(shard)
        names.append(kind)
    mod_lanes = w_mod.shape[1] // 8
    n_sems = 64 + 16 * buckets + len(shards) * (seq + 2 * buckets)
    outs = pl.pallas_call(
        functools.partial(gather_kernel, buckets, seq, tuple(names)),
        out_shape=[
            jax.ShapeDtypeStruct((seq,) + tokens.shape, BF16),
            jax.ShapeDtypeStruct((seq,) + captions.shape, BF16),
            jax.ShapeDtypeStruct((buckets, seq) + small.shape, F32),
            jax.ShapeDtypeStruct((8, mod_lanes), F32),
            *fulls,
        ],
        in_specs=[any_spec, any_spec, any_spec, vmem, vmem] + [any_spec] * len(shards),
        out_specs=[any_spec, any_spec, any_spec, vmem] + [any_spec] * len(shards),
        scratch_shapes=[
            pltpu.VMEM((buckets, 8, mod_lanes), F32),
            pltpu.VMEM((buckets, 8, mod_lanes), F32),
            pltpu.VMEM((seq, 8, mod_lanes), F32),
            pltpu.VMEM((8, mod_lanes), F32),
            pltpu.SemaphoreType.DMA((n_sems,)),
            pltpu.SemaphoreType.DMA((n_sems,)),
        ],
        compiler_params=pltpu.CompilerParams(
            collective_id=0, has_side_effects=True, vmem_limit_bytes=24 * 2**20
        ),
    )(tokens, captions, small, cond, w_mod, *inputs)
    weights = []
    for full, kind in zip(outs[4:], names, strict=True):
        weights.append(full.reshape(-1, full.shape[-1]))
    return outs[0], outs[1], outs[2], outs[3], weights


def line_gather_kernel(seq, own, out, send, recv):
    b, s = lax.axis_index("bucket"), lax.axis_index("seq")
    greet_line(b, s, seq)
    relay = Relay(Copies(send, recv), own, out, b, s, seq)
    for j in range(seq):
        relay.start(j)
    for j in range(seq - 1):
        relay.sent(j)


def line_gather(seq, own, collective_id):
    return pl.pallas_call(
        functools.partial(line_gather_kernel, seq),
        out_shape=jax.ShapeDtypeStruct((seq,) + own.shape, own.dtype),
        in_specs=[pl.BlockSpec(memory_space=pl.ANY)],
        out_specs=pl.BlockSpec(memory_space=pl.ANY),
        scratch_shapes=[pltpu.SemaphoreType.DMA((2 * seq + 2,))] * 2,
        compiler_params=pltpu.CompilerParams(collective_id=collective_id, has_side_effects=True),
    )(own).reshape(-1, own.shape[-1])


def add_rows(out, terms):
    rows = out.shape[0]
    step = 16 if rows % 16 == 0 else rows

    def body(i, carry):
        at = pl.ds(pl.multiple_of(i * step, step), step)
        total = terms[0][at, :].astype(F32)
        for term in terms[1:]:
            total = total + term[at, :].astype(F32)
        out[at, :] = total.astype(out.dtype)
        return carry

    lax.fori_loop(0, rows // step, body, 0)


class Pour:
    def __init__(self, copies, parts, from_left, from_right, b, s, seq):
        self.copies, self.parts, self.b, self.s, self.seq = copies, parts, b, s, seq
        self.got = {1: from_left, -1: from_right}
        rows = parts.shape[1]
        self.cuts = CUTS if rows % (16 * CUTS) == 0 else 1
        self.thin = rows // self.cuts
        self.count = (seq - 1) * self.cuts
        self.base = {1: copies.take(self.count), -1: copies.take(self.count)}
        self.next = {
            1: jnp.where(s < seq - 1, s + 1, s - 1),
            -1: jnp.where(s > 0, s - 1, s + 1),
        }

    def block(self, way, q):
        j, at = q // self.cuts, pl.ds(q % self.cuts * self.thin, self.thin)
        return self.parts.at[self.seq - 1 - j if way > 0 else j, at], self.got[way].at[j, at]

    def packet(self, way, q):
        src, dst = self.block(way, q)
        return self.copies.remote(src, dst, self.b, self.next[way], self.base[way] + q)

    def on(self, way, q):
        j = q // self.cuts
        return self.s < self.seq - 1 - j if way > 0 else self.s > j

    def behind(self, way):
        return self.s > 0 if way > 0 else self.s < self.seq - 1

    def one(self, way, q):
        src, dst = self.block(way, q)

        @pl.when(jnp.logical_and(self.behind(way), self.on(way, q)))
        def _():
            self.packet(way, q).wait_recv()
            add_rows(src, [src, dst])

        @pl.when(self.on(way, q))
        def _():
            if q >= FLIGHT:
                self.packet(way, q - FLIGHT).wait_send()
            self.packet(way, q).start()

    def step(self, q):
        @pl.when(self.s < self.seq // 2)
        def _():
            self.one(1, q)
            self.one(-1, q)

        @pl.when(self.s >= self.seq // 2)
        def _():
            self.one(-1, q)
            self.one(1, q)

    def end(self, out):
        seq, cuts = self.seq, self.cuts
        for t in range(seq):

            @pl.when(self.s == t)
            def _():
                terms = [self.parts.at[t]]
                for way, j in ((1, seq - 1 - t), (-1, t)):
                    if j < seq - 1:
                        for c in range(cuts):
                            self.packet(way, j * cuts + c).wait_recv()
                        terms.append(self.got[way].at[j])
                add_rows(out, terms)

        for q in range(self.count):
            more = q + FLIGHT < self.count
            for way in (1, -1):
                last = jnp.logical_not(self.on(way, q + FLIGHT)) if more else True

                @pl.when(jnp.logical_and(self.on(way, q), last))
                def _():
                    self.packet(way, q).wait_send()


def line_scatter_kernel(seq, parts, out, from_left, from_right, send, recv):
    b, s = lax.axis_index("bucket"), lax.axis_index("seq")
    greet_line(b, s, seq)
    pour = Pour(Copies(send, recv), parts, from_left, from_right, b, s, seq)
    for q in range(pour.count):
        pour.step(q)
    pour.end(out)


def line_scatter(seq, parts, collective_id):
    rows, wide = parts.shape[0] // seq, parts.shape[1]
    vmem = pl.BlockSpec(memory_space=pltpu.VMEM)
    return pl.pallas_call(
        functools.partial(line_scatter_kernel, seq),
        out_shape=jax.ShapeDtypeStruct((rows, wide), F32),
        in_specs=[vmem],
        out_specs=vmem,
        input_output_aliases={},
        scratch_shapes=[
            pltpu.VMEM((seq - 1, rows, wide), BF16),
            pltpu.VMEM((seq - 1, rows, wide), BF16),
            pltpu.SemaphoreType.DMA((4 * seq,)),
            pltpu.SemaphoreType.DMA((4 * seq,)),
        ],
        compiler_params=pltpu.CompilerParams(
            collective_id=collective_id, has_side_effects=True, vmem_limit_bytes=24 * 2**20
        ),
    )(parts.astype(BF16).reshape(seq, rows, wide))


class GradSums:
    def __init__(self, copies, b, s, buckets, seq, kinds, grads, outs, scratch, near=False):
        self.near = near
        self.copies, self.b, self.s, self.buckets, self.seq = copies, b, s, buckets, seq
        self.kinds, self.grads, self.outs = kinds, grads, outs
        self.scratch = [scratch[8 * w : 8 * w + 8] for w in range(len(kinds))]
        self.chips = buckets // 2
        self.chip, self.core = lax.div(b, 2), lax.rem(b, 2)
        self.place = s * buckets + slot(b, buckets)
        self.to_b = lax.div(self.place, seq)
        self.twin = flip(b, 1)
        self.begun, self.state, self.last = {}, {}, {}
        self.sent = []

    def go(self, copy):
        copy.start()
        self.sent.append(copy)
        return copy

    def own(self, w, chip, rows=None):
        where = (chip,) if rows is None else (chip, rows)
        if self.near:
            return self.grads[w].at[(chip, self.core, *where[1:])]
        return self.scratch[w][0].at[where]

    def begin(self, w):
        own, other = self.scratch[w][:2]
        grad = self.grads[w]
        swap = self.copies.remote(grad.at[:, 1 - self.core], other, self.twin, self.s)
        swap.start()
        self.begun[w] = [swap]
        if not self.near:
            keep = self.copies.local(grad.at[:, self.core], own)
            keep.start()
            self.begun[w].append(keep)

    def stage_a(self, w):
        _, other, half_x, half_y, got, _ = self.scratch[w][:6]
        for copy in self.begun[w]:
            copy.wait()
        if not self.near and w + 2 in range(len(self.kinds)) and w + 2 not in self.begun:
            self.begin(w + 2)
        rows = other.shape[1]
        if self.chips != 4:
            moves = []
            for k in range(1, self.chips):
                to = lax.rem(self.chip + k, self.chips)
                own = self.own(w, to)
                add_rows(own, [own, other.at[to]])
                move = self.copies.remote(own, got.at[k], 2 * to + self.core, self.s)
                moves.append(self.go(move))
            self.state[w] = moves
            return
        far = flip(flip(self.chip, 1), 2)
        add_rows(self.own(w, far), [self.own(w, far), other.at[far]])
        cut = halves_of(other.shape[1:])
        near_x, near_y = flip(self.b, 2), flip(self.b, 4)
        top, low = self.own(w, far, pl.ds(0, cut)), self.own(w, far, pl.ds(cut, rows - cut))
        self.state[w] = [
            self.go(self.copies.remote(top, half_x, near_x, self.s)),
            self.go(self.copies.remote(low, half_y, near_y, self.s)),
        ]

    def stage_b(self, w):
        if self.chips != 4:
            return
        _, other, half_x, half_y, got_x, got_y = self.scratch[w][:6]
        rows = other.shape[1]
        cut = halves_of(other.shape[1:])
        top, low = pl.ds(0, cut), pl.ds(cut, rows - cut)
        mx, my = flip(self.chip, 1), flip(self.chip, 2)
        move_x, move_y = self.state[w]
        move_x.wait_recv()
        block = self.own(w, my, top)
        add_rows(block, [block, other.at[my, top], half_x])
        block = self.own(w, my, low)
        add_rows(block, [block, other.at[my, low]])
        block = self.own(w, my)
        next_y = self.go(self.copies.remote(block, got_y, flip(self.b, 4), self.s))
        move_y.wait_recv()
        block = self.own(w, mx, low)
        add_rows(block, [block, other.at[mx, low], half_y])
        block = self.own(w, mx, top)
        add_rows(block, [block, other.at[mx, top]])
        block = self.own(w, mx)
        next_x = self.go(self.copies.remote(block, got_x, flip(self.b, 2), self.s))
        self.state[w] = [next_x, next_y]

    def stage_c(self, w):
        _, other, _, _, got_x, got_y, done, landed = self.scratch[w]
        for move in self.state[w]:
            move.wait_recv()
        terms = [self.own(w, self.chip), other.at[self.chip]]
        if self.chips == 4:
            terms += [got_x, got_y]
        else:
            terms += [got_x.at[k] for k in range(1, self.chips)]
        if self.kinds[w] == "col":
            add_rows(self.outs[w], terms)
            return
        seq, send, recv = self.seq, self.copies.send, self.copies.recv
        hold = self.kinds[w] == "hold"
        if hold:
            done = self.outs[w]
        wide = done.shape[-1]
        far = self.kinds[w] == "row"
        to_b, me = (self.to_b, lax.rem(self.place, seq)) if far else (self.b, self.s)
        base = 0 if hold else self.copies.take(2 * seq)
        rows = terms[0].shape[0]
        step = 16 if rows % 16 == 0 else rows

        def body(i, carry):
            at = pl.ds(pl.multiple_of(i * step, step), step)
            total = terms[0][at, :].astype(F32)
            for term in terms[1:]:
                total = total + term[at, :].astype(F32)
            for t in range(seq):
                done[t, at, :] = total[:, t * wide : (t + 1) * wide].astype(BF16)
            return carry

        lax.fori_loop(0, rows // step, body, 0)
        if hold:
            return
        moves = []
        for t in range(seq):
            move = pltpu.make_async_remote_copy(
                src_ref=done.at[t],
                dst_ref=landed.at[me],
                send_sem=send.at[base + t],
                recv_sem=recv.at[base + me],
                device_id={"bucket": to_b, "seq": t},
                device_id_type=MESH,
            )
            keep = pltpu.make_async_copy(done.at[t], landed.at[me], send.at[base + seq + t])
            here = jnp.logical_and(to_b == self.b, self.s == t) if far else self.s == t

            @pl.when(jnp.logical_not(here))
            def _():
                move.start()

            @pl.when(here)
            def _():
                keep.start()

            moves.append((move, keep, here))
        self.last[w] = (base, moves)

    def stage_d(self, w):
        if self.kinds[w] in ("col", "hold"):
            return
        done, landed = self.scratch[w][6:]
        base, moves = self.last[w]
        out, seq, buckets = self.outs[w], self.seq, self.buckets
        for j in range(seq):
            d = self.b * seq + j
            from_b = slot(lax.rem(d, buckets), buckets)
            here = jnp.logical_and(from_b == self.b, lax.div(d, buckets) == self.s)
            if self.kinds[w] != "row":
                here = self.s == j

            @pl.when(jnp.logical_not(here))
            def _():
                pltpu.make_async_remote_copy(
                    src_ref=done.at[j],
                    dst_ref=landed.at[j],
                    send_sem=self.copies.send.at[base + j],
                    recv_sem=self.copies.recv.at[base + j],
                    device_id={"bucket": self.twin, "seq": self.s},
                    device_id_type=MESH,
                ).wait_recv()

        for move, keep, here in moves:

            @pl.when(jnp.logical_not(here))
            def _():
                move.wait_send()

            @pl.when(here)
            def _():
                keep.wait()

        for j in range(seq):
            add_rows(out.at[j], [landed.at[j]])

    def steps(self):
        count = len(self.kinds)
        for w in range(count + 2):
            if w < count:
                yield lambda w=w: self.stage_a(w)
            if 1 <= w <= count:
                yield lambda w=w: self.stage_b(w - 1)
            if w >= 2:
                yield lambda w=w: self.stage_c(w - 2)
        yield lambda: [self.stage_d(w) for w in range(count)]

    def end(self):
        for move in self.sent:
            move.wait_send()


def greet_all(b, s, buckets, seq):
    for k in range(1, buckets):
        greet(lax.rem(b + k, buckets), s)
    for k in range(1, seq):
        greet(b, lax.rem(s + k, seq))
    for j in range(seq):
        d = b * seq + j
        src_b, src_s = slot(lax.rem(d, buckets), buckets), lax.div(d, buckets)

        @pl.when(jnp.logical_not(jnp.logical_and(src_b == b, src_s == s)))
        def _():
            greet(src_b, src_s)

    to_b = lax.div(s * buckets + slot(b, buckets), seq)
    return buckets - 1 + seq - 1 + seq - jnp.where(to_b == b, 1, 0)


def sums_shapes(buckets, seq, shapes, kinds, near=False):
    chips = buckets // 2
    inputs, outs, scratch = [], [], []
    tiny = pltpu.VMEM((16, 128), BF16)
    for (rows, wide), kind in zip(shapes, kinds, strict=True):
        rows = rows // buckets
        inputs.append((chips, 2, rows, wide))
        cut = halves_of((rows, wide))
        scratch += [tiny if near else pltpu.VMEM((chips, rows, wide), BF16)]
        scratch += [pltpu.VMEM((chips, rows, wide), BF16)]
        if chips == 4:
            scratch += [pltpu.VMEM((cut, wide), BF16), pltpu.VMEM((rows - cut, wide), BF16)]
            scratch += [pltpu.VMEM((rows, wide), BF16)] * 2
        else:
            scratch += [tiny, tiny, pltpu.VMEM((chips, rows, wide), BF16), tiny]
        split = (seq, rows, wide // seq)
        kept = BF16 if kind == "hold" else F32
        outs.append(jax.ShapeDtypeStruct((rows, wide) if kind == "col" else split, kept))
        scratch += [tiny if kind in ("col", "hold") else pltpu.VMEM(split, BF16)] * 2
    n_sems = 32 + 2 * buckets + len(shapes) * (8 + 3 * seq + buckets)
    return inputs, outs, scratch, n_sems


def place_grads(buckets, grads, kinds, shapes):
    inputs = []
    for grad, kind, shape in zip(grads, kinds, shapes, strict=True):
        grad = grad.astype(BF16)
        if kind == "row" and buckets == 8:
            grad = grad.reshape((2, 2, 2) + shape[2:]).transpose(0, 2, 1, 3, 4)
        inputs.append(grad.reshape(shape))
    return inputs


def spread(buckets):
    if buckets != 8:
        return tuple(range(buckets))
    return tuple(4 * (p // 4) + 2 * (p % 2) + p // 2 % 2 for p in range(buckets))


def scatter_kernel(buckets, seq, kinds, *refs):
    count = len(kinds)
    vec, grads = refs[0], refs[1 : 1 + count]
    vec_all, outs = refs[1 + count], refs[2 + count : 2 + 2 * count]
    at = 2 + 2 * count
    vec_seq, vec_sum, send, recv = refs[at : at + 4]
    b, s = lax.axis_index("bucket"), lax.axis_index("seq")
    copies = Copies(send, recv)
    sums = GradSums(copies, b, s, buckets, seq, kinds, grads, outs, refs[at + 4 :])
    peers = greet_all(b, s, buckets, seq)
    pl.semaphore_wait(pltpu.get_barrier_semaphore(), peers)
    vec_moves = []
    for k in range(1, seq):
        vec_moves.append(sums.go(copies.remote(vec, vec_seq.at[k], b, lax.rem(s + k, seq))))
    for w in range(min(2, count)):
        sums.begin(w)
    for move in vec_moves:
        move.wait_recv()
    add_rows(vec_sum, [vec] + [vec_seq.at[k] for k in range(1, seq)])
    vec_next = []
    for k in range(1, buckets):
        peer = lax.rem(b + k, buckets)
        vec_next.append(sums.go(copies.remote(vec_sum, vec_all.at[b], peer, s)))
    vec_own = copies.local(vec_sum, vec_all.at[b])
    vec_own.start()
    for step in sums.steps():
        step()
    for move in vec_next:
        move.wait_recv()
    vec_own.wait()
    sums.end()


def scatter_all(buckets, seq, vec, grads, kinds, collective_id=1):
    any_spec = pl.BlockSpec(memory_space=pl.ANY)
    vmem = pl.BlockSpec(memory_space=pltpu.VMEM)
    shapes, outs, scratch, n_sems = sums_shapes(buckets, seq, [g.shape for g in grads], kinds)
    inputs = place_grads(buckets, grads, kinds, shapes)
    results = pl.pallas_call(
        functools.partial(scatter_kernel, buckets, seq, tuple(kinds)),
        out_shape=[jax.ShapeDtypeStruct((buckets,) + vec.shape, F32), *outs],
        in_specs=[vmem] + [any_spec] * len(grads),
        out_specs=[any_spec] + [vmem] * len(grads),
        scratch_shapes=[
            pltpu.VMEM((seq,) + vec.shape, F32),
            pltpu.VMEM(vec.shape, F32),
            pltpu.SemaphoreType.DMA((n_sems,)),
            pltpu.SemaphoreType.DMA((n_sems,)),
            *scratch,
        ],
        compiler_params=pltpu.CompilerParams(
            collective_id=collective_id, has_side_effects=True, vmem_limit_bytes=60 * 2**20
        ),
    )(vec, *inputs)
    return results[0], [out.reshape(-1, out.shape[-1]) for out in results[1:]]


def attention(queries, keys, values, live, scale):
    scores = jnp.einsum("qhd,khd->hqk", queries, keys, preferred_element_type=F32) * scale
    scores = jnp.where(live[None, None, :], scores, -1e30)
    probs = jax.nn.softmax(scores, axis=-1)
    mixed = jnp.einsum("hqk,khd->qhd", probs.astype(BF16), values, preferred_element_type=F32)
    return probs, mixed


def attention_back(probs, queries, keys, values, d_out, scale):
    d_probs = jnp.einsum("qhd,khd->hqk", d_out, values, preferred_element_type=F32)
    d_scores = probs * (d_probs - jnp.sum(probs * d_probs, axis=-1, keepdims=True))
    d_low = d_scores.astype(BF16)
    d_query = jnp.einsum("hqk,khd->qhd", d_low, keys, preferred_element_type=F32) * scale
    d_key = jnp.einsum("hqk,qhd->khd", d_low, queries, preferred_element_type=F32) * scale
    d_value = jnp.einsum("hqk,qhd->khd", probs.astype(BF16), d_out, preferred_element_type=F32)
    return d_query, d_key, d_value


def on_device_general(
    tokens,
    captions,
    cotangent,
    counts,
    cap_lens,
    steps_t,
    w_query,
    w_key,
    w_value,
    w_out,
    w_cap_key,
    w_cap_value,
    w_gate,
    w_up,
    w_down,
    w_mod,
    gains,
    cross_gate,
):
    buckets, seq = lax.axis_size("bucket"), lax.axis_size("seq")
    b, s = lax.axis_index("bucket"), lax.axis_index("seq")
    place = b * seq + s
    rows, width = tokens.shape
    span = rows * seq
    share = width // seq
    heads = share // HEAD_DIM
    scale = HEAD_DIM ** (-0.5)
    live_rows, cap_len = pick_entry(counts, b), pick_entry(cap_lens, b)
    token_total = jnp.sum(counts).astype(F32)

    cond_size = w_mod.shape[0] * buckets * seq
    cond = jax.nn.silu(time_embed(steps_t, cond_size)).astype(BF16)
    cond_part = lax.dynamic_slice_in_dim(cond, place * w_mod.shape[0], w_mod.shape[0], 1)
    slim = gains.shape[1]
    small = jnp.concatenate([gains, cross_gate[None]], axis=0).astype(F32)
    small = jnp.pad(small, ((0, 0), (0, 128 - slim)))
    tok_all, cap_all, small_all, mod, weights = gather_all(
        buckets,
        seq,
        tokens,
        captions,
        small,
        cond_part,
        w_mod,
        [w_query, w_key, w_value, w_cap_key, w_cap_value, w_out, w_gate, w_up, w_down],
        ["col", "col", "col", "col", "col", "row", "col", "col", "row"],
    )
    wq, wk, wv, wck, wcv, wo, wg, wu, wd = weights
    caps = cap_all.reshape(-1, captions.shape[1])
    small_rows = small_all[..., :slim].transpose(2, 0, 1, 3).reshape(8, width)
    gain_f = small_rows[:7]
    own_cols = lax.dynamic_slice_in_dim(small_rows, s * share, share, 1)
    gate_cross = jnp.tanh(own_cols[7])
    scale_attn, gate_attn, scale_ffn, gate_ffn = mod.reshape(4, width)

    hidden = pre_attn(tok_all.astype(F32), gain_f[0], scale_attn).astype(BF16).reshape(span, width)
    query_proj, key_proj = bf_dot(hidden, wq), bf_dot(hidden, wk)
    value_low = bf_dot(hidden, wv).astype(BF16)
    (query_f, key_f), norm_back = jax.vjp(qk_norm, query_proj, key_proj, own_cols[4], own_cols[5])
    cap_key_f, cap_back = jax.vjp(cap_norm, bf_dot(caps, wck), own_cols[6])

    def by_head(values):
        return values.astype(BF16).reshape(values.shape[0], heads, HEAD_DIM)

    query, key, value = by_head(query_f), by_head(key_f), by_head(value_low)
    cap_key, cap_value = by_head(cap_key_f), by_head(bf_dot(caps, wcv))
    probs, self_out = attention(query, key, value, jnp.arange(span) < live_rows, scale)
    cap_live = jnp.arange(caps.shape[0]) < cap_len
    cap_probs, cross_out = attention(query, cap_key, cap_value, cap_live, scale)
    self_out, cross_out = self_out.reshape(span, share), cross_out.reshape(span, share)
    mixed_low = (self_out + gate_cross * cross_out).astype(BF16)
    attn_out = line_scatter(seq, bf_dot(mixed_low, wo), 2)

    tokens_f = tokens.astype(F32)
    (resid_one, ffn_pre), middle_back = jax.vjp(
        middle, tokens_f, attn_out, gain_f[1], gate_attn, gain_f[2], scale_ffn
    )
    ffn_all = line_gather(seq, ffn_pre.astype(BF16), 3)
    act_pre, act_back = jax.vjp(activate, bf_dot(ffn_all, wg), bf_dot(ffn_all, wu))
    act_low = act_pre.astype(BF16)
    ffn_out = line_scatter(seq, bf_dot(act_low, wd), 4)
    out_f, finish_back = jax.vjp(finish, resid_one, ffn_out, gain_f[3], gate_ffn)
    block_out = out_f.astype(BF16)

    row_live = (s * rows + jnp.arange(rows) < live_rows).astype(F32)
    weighted = cotangent.astype(F32) * row_live[:, None] * (buckets * span / token_total)
    d_resid, d_ffn_out, d_gain_last, d_gate_ffn = finish_back(weighted)
    d_ffn_all = line_gather(seq, d_ffn_out.astype(BF16), 5)
    d_gate, d_up = act_back(right_dot(d_ffn_all, wd))
    d_gate, d_up = d_gate.astype(BF16), d_up.astype(BF16)
    d_hidden_ffn = line_scatter(seq, right_dot(d_gate, wg) + right_dot(d_up, wu), 6)
    d_tokens_one, d_attn_out, d_gain_post, d_gate_attn, d_gain_ffn, d_scale_ffn = middle_back(
        (d_resid, d_hidden_ffn)
    )
    d_attn_all = line_gather(seq, d_attn_out.astype(BF16), 7)
    d_mixed_low = right_dot(d_attn_all, wo).astype(BF16)
    d_mixed = d_mixed_low.astype(F32)
    d_cross_low = (gate_cross * d_mixed).astype(BF16)
    grad_cross = jnp.sum(d_mixed * cross_out, axis=0) * (1.0 - gate_cross * gate_cross)

    d_query_cross, d_cap_key, d_cap_value = attention_back(
        cap_probs, query, cap_key, cap_value, by_head(d_cross_low), scale
    )
    d_query, d_key, d_value = attention_back(probs, query, key, value, by_head(d_mixed_low), scale)
    d_cap_key, d_gain_cap = cap_back(d_cap_key.reshape(-1, share))
    d_query, d_key, d_gain_query, d_gain_key = norm_back(
        ((d_query + d_query_cross).reshape(span, share), d_key.reshape(span, share))
    )
    d_query, d_key, d_cap_key = d_query.astype(BF16), d_key.astype(BF16), d_cap_key.astype(BF16)
    d_value = d_value.reshape(span, share).astype(BF16)
    d_cap_value = d_cap_value.reshape(-1, share).astype(BF16)
    d_hidden = line_scatter(
        seq, right_dot(d_query, wq) + right_dot(d_key, wk) + right_dot(d_value, wv), 8
    )
    _, pre_back = jax.vjp(pre_attn, tokens_f, gain_f[0], scale_attn)
    d_tokens_two, d_gain_pre, d_scale_attn = pre_back(d_hidden)
    tokens_grad = d_tokens_one + d_tokens_two

    own_sums = jnp.stack([d_gain_query, d_gain_key, d_gain_cap, grad_cross])
    own_wide = lax.dynamic_update_slice(jnp.zeros((4, width), F32), own_sums, (0, s * share))
    vec = jnp.concatenate(
        [
            jnp.stack([d_scale_attn, d_gate_attn, d_scale_ffn, d_gate_ffn]),
            jnp.stack([d_gain_pre, d_gain_post, d_gain_ffn, d_gain_last]),
            own_wide,
            jnp.zeros((4, width), F32),
        ]
    )
    grads = [
        left_dot(ffn_all, d_gate),
        left_dot(ffn_all, d_up),
        left_dot(act_low, d_ffn_all),
        left_dot(mixed_low, d_attn_all),
        left_dot(caps, d_cap_key),
        left_dot(caps, d_cap_value),
        left_dot(hidden, d_query),
        left_dot(hidden, d_key),
        left_dot(hidden, d_value),
    ]
    kinds = ["col", "col", "row", "row", "col", "col", "col", "col", "col"]
    vec_all, sums = scatter_all(buckets, seq, vec, grads, kinds)
    s_gate, s_up, s_down, s_out, s_cap_key, s_cap_value, s_query, s_key, s_value = sums

    quarter = 4 * width // seq
    mod_rows = vec_all[:, :4].reshape(buckets, -1, quarter)
    mod_rows = lax.dynamic_slice_in_dim(mod_rows, s, 1, 1)[:, 0]
    cond_size = cond.shape[1] // buckets
    cond_cols = lax.dynamic_slice_in_dim(cond, b * cond_size, cond_size, 1).astype(F32)
    s_mod = jnp.sum(cond_cols[:, :, None] * mod_rows[:, None, :], axis=0)
    tail = lax.dynamic_slice(vec_all, (0, 4, place * slim), (buckets, 8, slim))
    tail = jnp.sum(tail, axis=0)
    return (
        block_out,
        tokens_grad,
        s_query,
        s_key,
        s_value,
        s_out,
        s_cap_key,
        s_cap_value,
        s_gate,
        s_up,
        s_down,
        s_mod,
        tail[:7],
        tail[7],
    )


def low_half(shape):
    return lax.broadcasted_iota(jnp.int32, shape, len(shape) - 1) < HEAD_DIM


def pair_sums(values):
    row = lax.broadcasted_iota(jnp.int32, (128, 128), 0) < HEAD_DIM
    same = (row == low_half((128, 128))).astype(BF16)
    high = values.astype(BF16)
    rest = (values - high.astype(F32)).astype(BF16)
    return bf_dot(high, same) + bf_dot(rest, same)


def pair_scale(values, eps):
    return lax.rsqrt(pair_sums(values * values) * (1.0 / HEAD_DIM) + eps)


def fill_rows(out, live, first, yes, no):
    row = lax.broadcasted_iota(jnp.int32, out.shape, 0) + first
    out[...] = jnp.where(row < live, yes, no).astype(out.dtype)


FORWARD_ORDER = (8, "tok", 0, "tok", 1, "tok", 2, "tok", 6, 7, "cap", 3, "cap", 4, "cap", 5, "cap")
MOVED = ()
AHEAD = 4
LAG = 1
WINDOW = 2


class Gather:
    def __init__(self, copies, b, s, buckets, seq, kinds, shards, fulls, keep_at=None):
        self.copies, self.b, self.s, self.buckets, self.seq = copies, b, s, buckets, seq
        self.kinds, self.shards, self.fulls, self.keep_at = kinds, shards, fulls, keep_at
        place = b * seq + s
        self.to_slot, self.to_s = lax.rem(place, buckets), lax.div(place, buckets)
        self.to_b = slot(self.to_slot, buckets)
        back = s * buckets + slot(b, buckets)
        self.from_b, self.from_s = lax.div(back, seq), lax.rem(back, seq)
        self.stays = jnp.logical_and(self.to_b == b, self.to_s == s)
        self.twin, self.near_x, self.near_y = flip(b, 1), flip(b, 2), flip(b, 4)
        self.far = flip(self.near_x, 4)
        self.first, self.second, self.kept, self.sent = {}, {}, [], []

    def greet_source(self):
        @pl.when(jnp.logical_not(self.stays))
        def _():
            greet(self.from_b, self.from_s)

        return jnp.where(self.stays, 0, 1)

    def go(self, src, dst, b):
        copy = self.copies.remote(src, dst, b, self.s)
        copy.start()
        self.sent.append(copy)
        return copy

    def depart(self, at):
        copies, b, s, seq = self.copies, self.b, self.s, self.seq
        shard, full = self.shards[at], self.fulls[at]
        if self.kinds[at] == "stay":
            keep = copies.local(shard, full.at[b])
            keep.start()
            self.first[at] = ((), keep)
            return
        if self.kinds[at] == "row":
            move = copies.remote(shard, full.at[self.to_slot], self.to_b, self.to_s)
            keep = copies.local(shard, full.at[slot(b, self.buckets)])

            @pl.when(jnp.logical_not(self.stays))
            def _():
                move.start()

            @pl.when(self.stays)
            def _():
                keep.start()

            self.first[at] = (move, keep)
            return
        wide = full.shape[-1]

        def columns(peer):
            if self.kinds[at] == "cut":
                return shard.at[peer]
            return shard.at[:, pl.ds(pl.multiple_of(peer * wide, 128), wide)]

        moves = []
        for k in range(1, seq):
            peer = lax.rem(s + k, seq)
            move = copies.remote(columns(peer), full.at[b, s], b, peer)
            move.start()
            moves.append(move)
        keep = copies.local(columns(s), full.at[b, s])
        keep.start()
        self.first[at] = (moves, keep)

    def arrived(self, at):
        moves, keep = self.first[at]
        if self.kinds[at] == "row":

            @pl.when(jnp.logical_not(self.stays))
            def _():
                moves.wait()

            @pl.when(self.stays)
            def _():
                keep.wait()

            return
        for move in moves:
            move.wait()
        keep.wait()

    def index(self, at, device):
        return slot(device, self.buckets) if self.kinds[at] == "row" else device

    def stage_a(self, at):
        block = self.fulls[at].at[self.index(at, self.b)]
        self.second[at] = {
            "x": self.go(block, block, self.near_x),
            "y": self.go(block, block, self.near_y),
            "twin": [self.go(block, block, self.twin)],
        }

    def stage_b(self, at):
        full, now = self.fulls[at], self.second[at]
        cut = halves_of(full.shape[1:])
        now["x"].wait_recv()
        block = full.at[self.index(at, self.near_x), pl.ds(0, cut)]
        now["dy"] = self.go(block, block, self.near_y)
        block = full.at[self.index(at, self.near_x)]
        now["twin"].append(self.go(block, block, self.twin))
        now["y"].wait_recv()
        block = full.at[self.index(at, self.near_y), pl.ds(cut, full.shape[1] - cut)]
        now["dx"] = self.go(block, block, self.near_x)
        block = full.at[self.index(at, self.near_y)]
        now["twin"].append(self.go(block, block, self.twin))

    def stage_c(self, at):
        full, now = self.fulls[at], self.second[at]
        now["dy"].wait_recv()
        now["dx"].wait_recv()
        block = full.at[self.index(at, self.far)]
        now["twin"].append(self.go(block, block, self.twin))

    def stage_d(self, at):
        for move in self.second[at]["twin"]:
            move.wait_recv()
        if self.keep_at is not None:
            copy = self.copies.local(self.fulls[at], self.keep_at[at])
            copy.start()
            self.kept.append(copy)

    def end(self):
        for copy in self.kept:
            copy.wait()
        for move in self.sent:
            move.wait_send()


def forward_kernel(buckets, seq, kinds, slim, *refs):
    count = len(kinds)
    tokens, captions, small, cond, w_mod, counts, cap_lens = refs[:7]
    shards = refs[7 : 7 + count]
    refs = refs[7 + count :]
    cap_all = refs[0]
    far_fulls = refs[1 : 1 + count]
    refs = refs[1 + count :]
    (
        gain_rows,
        mod_rows,
        hidden,
        query_raw,
        key_raw,
        cap_raw,
        query,
        key,
        value,
        cap_key,
        cap_value,
        cross_out,
        mixed,
    ) = refs[:13]
    refs = refs[13:]
    part, got_bucket, got_seq, mod_sum, small_all, tok_all, cap_near, own_out = refs[:8]
    fulls = refs[8 : 8 + count]
    key_mask, cap_mask, send, recv = refs[8 + count : 12 + count]
    strips = refs[12 + count :]
    b, s = lax.axis_index("bucket"), lax.axis_index("seq")
    copies = Copies(send, recv)
    shards = list(shards)
    cuts = [at for at in range(count) if kinds[at] == "cut"]
    for at, strip in zip(cuts, strips, strict=True):
        for t in range(seq):
            for j in range(strip.shape[2] // 128):
                cols = slice((j * seq + t) * 128, (j * seq + t + 1) * 128)
                strip[t, :, j * 128 : (j + 1) * 128] = shards[at][:, cols]
        shards[at] = strip
    weights = Gather(copies, b, s, buckets, seq, kinds, shards, fulls, far_fulls)
    for k in range(1, buckets):
        greet(lax.rem(b + k, buckets), s)
    for k in range(1, seq):
        greet(b, lax.rem(s + k, seq))
    peers = buckets - 1 + seq - 1 + weights.greet_source()

    fill_rows(key_mask, counts[b], 0, 1.0, 0.0)
    fill_rows(cap_mask, cap_lens[b], 0, 1.0, 0.0)
    lanes = part.shape[2]
    for j in range(part.shape[1]):
        part[:, j, :] = bf_dot(cond[...], w_mod[:, j * lanes : (j + 1) * lanes])

    pl.semaphore_wait(pltpu.get_barrier_semaphore(), peers)

    sent = []

    def go(copy):
        copy.start()
        sent.append(copy)
        return copy

    mod_moves = []
    for k in range(1, buckets):
        peer = lax.rem(b + k, buckets)
        mod_moves.append(go(copies.remote(part.at[peer], got_bucket.at[k], peer, s)))
    small_moves = []
    for k in range(1, seq):
        peer = lax.rem(s + k, seq)
        small_moves.append(go(copies.remote(small, small_all.at[b, s], b, peer)))
    small_own = copies.local(small, small_all.at[b, s])
    small_own.start()

    tok = Relay(copies, tokens, tok_all, b, s, seq)
    cap = Relay(copies, captions, cap_near, b, s, seq)
    items, step = [], {"tok": 0, "cap": 0}
    for what in FORWARD_ORDER:
        if isinstance(what, str):
            items.append((tok if what == "tok" else cap, step[what]))
            step[what] += 1
        else:
            items.append((None, what))

    def fetch(at):
        whole = fulls[at][...]
        return whole.reshape(-1, whole.shape[-1])


    rows = seq * tok_all.shape[1]
    width = tok_all.shape[2]
    cap_rows = seq * cap_near.shape[1]
    share = query.shape[1]
    pairs = share // 128
    block_rows = tok_all.shape[1]

    def small_sums():
        for move in small_next:
            move.wait_recv()
        strips = [None] * (width // 128)
        lane = lax.broadcasted_iota(jnp.int32, (8, 128), 1)
        for d in range(buckets * seq):
            at, shift = divmod(d * slim, 128)
            piece = small_all[d // seq, d % seq]
            turned = pltpu.roll(piece, shift, 1) if shift else piece
            for index, keep in ((at, lane >= shift), (at + 1, lane < shift)):
                if index == at + 1 and shift + slim <= 128:
                    continue
                add = jnp.where(keep, turned, 0.0)
                strips[index] = add if strips[index] is None else strips[index] + add
        for at, strip in enumerate(strips):
            gain_rows[:, at * 128 : (at + 1) * 128] = strip
        total = mod_sum[...]
        for k, move in enumerate(mod_next, 1):
            move.wait_recv()
            total = total + got_seq[k]
        for j in range(8):
            at, lane_at = divmod(j * lanes, width)
            mod_rows[at : at + 1, lane_at : lane_at + lanes] = total[j : j + 1, :]
        mod_rows[4:8, :] = jnp.zeros((4, width), F32)

    def make_hidden():
        factor = gain_rows[0:1, :] * (1.0 + mod_rows[0:1, :])
        for t in range(seq):

            def body(i, carry):
                at = pl.ds(pl.multiple_of(i * 32, 32), 32)
                x = tok_all[t, at, :].astype(F32)
                x = x * lax.rsqrt(jnp.mean(x * x, axis=-1, keepdims=True) + 1e-05) * factor
                to = pl.ds(pl.multiple_of(t * block_rows + i * 32, 32), 32)
                hidden[to, :] = x.astype(BF16)
                return carry

            lax.fori_loop(0, block_rows // 32, body, 0)

    def gain_of(row, pair):
        at = pl.multiple_of(s * share + pair * 128, 128)
        return gain_rows[row : row + 1, pl.ds(at, 128)]

    def make_normed(raw, out, row, scale):
        def body(i, carry):
            at = pl.ds(pl.multiple_of(i * 64, 64), 64)
            for pair in range(pairs):
                lane = slice(pair * 128, (pair + 1) * 128)
                x = raw[at, lane]
                x = x * pair_scale(x, 1e-06) * gain_of(row, pair)
                out[at, lane] = x.astype(BF16)
            return carry

        del scale
        lax.fori_loop(0, raw.shape[0] // 64, body, 0)

    def make_query():
        query_raw[...] = bf_dot(hidden[...], fetch(0))
        make_normed(query_raw, query, 4, None)

    def make_key():
        key_raw[...] = bf_dot(hidden[...], fetch(1))
        make_normed(key_raw, key, 5, None)

    def make_value():
        value[...] = bf_dot(hidden[...], fetch(2)).astype(BF16)

    def cap_near_rows():
        whole = cap_near[...]
        return whole.reshape(cap_rows, whole.shape[-1])

    def make_cap_key():
        cap_raw[...] = bf_dot(cap_near_rows(), fetch(3))
        make_normed(cap_raw, cap_key, 6, None)

    def make_cap_value():
        cap_value[...] = bf_dot(cap_near_rows(), fetch(4)).astype(BF16)

    def attend(pair, k_ref, v_ref, mask, store):
        lane = slice(pair * 128, (pair + 1) * 128)
        low = low_half((128, 128))
        keys = k_ref[:, lane]
        values = jnp.concatenate([v_ref[:, lane] * mask[...], mask[...]], axis=1)

        def body(i, carry):
            at = pl.ds(pl.multiple_of(i * 128, 128), 128)
            q = query[at, lane] * jnp.asarray(HEAD_DIM**-0.5, BF16)
            outs = []
            for half in (jnp.where(low, q, jnp.zeros_like(q)), jnp.where(low, jnp.zeros_like(q), q)):
                weights = jnp.exp(right_dot(half, keys))
                outs.append(bf_dot(weights.astype(BF16), values))
            out = jnp.where(low, outs[0][:, :128], outs[1][:, :128])
            store(at, lane, out / jnp.where(low, outs[0][:, 128:], outs[1][:, 128:]))
            return carry

        lax.fori_loop(0, rows // 128, body, 0)

    def make_own(pair):
        def store(at, lane, out):
            own_out[at, lane] = out

        attend(pair, key, value, key_mask, store)

    def make_mixed(pair):
        gate = jnp.tanh(gain_of(7, pair))

        def store(at, lane, out):
            cross_out[at, lane] = out
            mixed[at, lane] = (own_out[at, lane] + gate * out).astype(BF16)

        attend(pair, cap_key, cap_value, cap_mask, store)

    work = [
        (lambda: (small_sums(), make_hidden()), "h", {"tok"}),
        (make_query, "q", {"h", 0}),
        (make_key, "k", {"h", 1}),
        (make_value, "v", {"h", 2}),
        (make_cap_key, "ck", {"cap", 3}),
        (make_cap_value, "cv", {"cap", 4}),
        *((functools.partial(make_own, p), ("own", p), {"q", "k", "v"}) for p in range(pairs)),
        *(
            (functools.partial(make_mixed, p), ("all", p), {"q", "ck", "cv", ("own", p)})
            for p in range(pairs)
        ),
    ]

    def do_work():
        for at, (piece, name, needs) in enumerate(work):
            if needs <= done:
                piece()
                done.add(name)
                del work[at]
                return True
        return False


    done = set()

    def begin(i):
        relay, j = items[i]
        if relay is None:
            weights.depart(j)
        else:
            relay.start(j)
            if j == seq - 1:
                done.add("tok" if relay is tok else "cap")

    def complete(at):
        weights.stage_c(at)
        weights.stage_d(at)
        done.add(at)

    window = WINDOW
    for i in range(window):
        begin(i)
    for move in small_moves:
        move.wait_recv()
    small_own.wait()
    small_next = []
    for k in range(1, buckets):
        peer = lax.rem(b + k, buckets)
        small_next.append(go(copies.remote(small_all.at[b], small_all.at[b], peer, s)))
    total = part[b]
    for k, move in enumerate(mod_moves, 1):
        move.wait_recv()
        total = total + got_bucket[k]
    mod_sum[...] = total
    mod_next = []
    for k in range(1, seq):
        peer = lax.rem(s + k, seq)
        mod_next.append(go(copies.remote(mod_sum, got_seq.at[k], b, peer)))

    cap_out = copies.local(cap_near, cap_all)
    order = []
    for i, (relay, j) in enumerate(items):
        if relay is None:
            weights.arrived(j)
        elif j <= seq - 2:
            relay.sent(j)
        if i + window < len(items):
            begin(i + window)
        if relay is None:
            order.append(j)
            weights.stage_a(j)
            if len(order) > LAG:
                weights.stage_b(order[-1 - LAG])
            if len(order) > LAG + 1:
                complete(order[-2 - LAG])
        do_work()
    cap_out.start()
    for at in range(LAG):
        weights.stage_b(order[len(order) - LAG + at])
        complete(order[len(order) - LAG - 1 + at])
        do_work()
    complete(order[-1])
    while do_work():
        pass
    cap_out.wait()
    weights.end()
    for move in sent:
        move.wait_send()


def forward_all(buckets, seq, tokens, captions, small, slim, cond, w_mod, masks, shards, kinds):
    any_spec = pl.BlockSpec(memory_space=pl.ANY)
    vmem = pl.BlockSpec(memory_space=pltpu.VMEM)
    smem = pl.BlockSpec(memory_space=pltpu.SMEM)
    fulls = []
    for shard, kind in zip(shards, kinds, strict=True):
        rows, wide = shard.shape
        shape = (buckets, rows, wide) if kind in ("row", "stay") else (buckets, seq, rows, wide // seq)
        fulls.append(jax.ShapeDtypeStruct(shape, BF16))
    near = [pltpu.VMEM(full.shape, BF16) for full in fulls]
    width = tokens.shape[1]
    mod_lanes = w_mod.shape[1] // 8
    span, cap_span, share = seq * tokens.shape[0], seq * captions.shape[0], width // seq
    f32_rows = jax.ShapeDtypeStruct((span, share), F32)
    low_rows = jax.ShapeDtypeStruct((span, share), BF16)
    cap_low = jax.ShapeDtypeStruct((cap_span, share), BF16)
    inner = [
        jax.ShapeDtypeStruct((8, width), F32),
        jax.ShapeDtypeStruct((8, width), F32),
        jax.ShapeDtypeStruct((span, width), BF16),
        f32_rows,
        f32_rows,
        jax.ShapeDtypeStruct((cap_span, share), F32),
        low_rows,
        low_rows,
        low_rows,
        cap_low,
        cap_low,
        f32_rows,
        low_rows,
    ]
    n_sems = 64 + 16 * buckets + len(shards) * (seq + 2 * buckets)
    outs = pl.pallas_call(
        functools.partial(forward_kernel, buckets, seq, tuple(kinds), slim),
        out_shape=[jax.ShapeDtypeStruct((seq,) + captions.shape, BF16), *fulls, *inner],
        in_specs=[any_spec, any_spec, any_spec, vmem, vmem, smem, smem]
        + [vmem if kind == "cut" else any_spec for kind in kinds],
        out_specs=[any_spec] * (1 + len(shards)) + [vmem] * len(inner),
        scratch_shapes=[
            pltpu.VMEM((buckets, 8, mod_lanes), F32),
            pltpu.VMEM((buckets, 8, mod_lanes), F32),
            pltpu.VMEM((seq, 8, mod_lanes), F32),
            pltpu.VMEM((8, mod_lanes), F32),
            pltpu.VMEM((buckets, seq) + small.shape, F32),
            pltpu.VMEM((seq,) + tokens.shape, BF16),
            pltpu.VMEM((seq,) + captions.shape, BF16),
            pltpu.VMEM((span, share), F32),
            *near,
            pltpu.VMEM((span, 128), BF16),
            pltpu.VMEM((cap_span, 128), BF16),
            pltpu.SemaphoreType.DMA((n_sems,)),
            pltpu.SemaphoreType.DMA((n_sems,)),
            *(
                pltpu.VMEM((seq,) + full.shape[2:], BF16)
                for full, kind in zip(fulls, kinds, strict=True)
                if kind == "cut"
            ),
        ],
        compiler_params=pltpu.CompilerParams(
            collective_id=9, has_side_effects=True, vmem_limit_bytes=62 * 2**20
        ),
    )(tokens, captions, small, cond, w_mod, *masks, *shards)
    at = 1 + len(shards)
    return outs[0], outs[1:at], outs[at:]


def middle_kernel(buckets, seq, chunks, kinds, *refs):
    mixed, w_out, tokens, cotangent, counts, gain_rows, mod_rows = refs[:7]
    far_weights, refs = refs[7:10], refs[10:]
    block_out, d_tokens, d_attn, row_sums = refs[:4]
    outs, refs = refs[4:7], refs[7:]
    w_gate, w_up, w_down, ffn_all, d_ffn, act, d_gate, d_up = refs[:8]
    gate_keep, up_keep, attn_keep, resid_keep, got, parts, from_left, from_right = refs[8:16]
    row_scale, send, recv = refs[16:19]
    grads, refs = refs[19:22], refs[22:]
    b, s = lax.axis_index("bucket"), lax.axis_index("seq")
    copies = Copies(send, recv)
    sums = GradSums(copies, b, s, buckets, seq, kinds, grads, outs, refs, near=True)
    shards = (w_gate, w_up, w_down)
    weights = Gather(copies, b, s, buckets, seq, ("cut", "cut", "stay"), far_weights, shards)
    peers = greet_all(b, s, buckets, seq) + weights.greet_source()
    pl.semaphore_wait(pltpu.get_barrier_semaphore(), peers)
    loads = [copies.local(far_weights[w], shards[w]) for w in range(3) if w not in MOVED]
    for load in loads:
        load.start()
    if MOVED:
        weights.depart(MOVED[0])

    rows, width = tokens.shape
    live = sum(counts[k] for k in range(buckets))
    factor = buckets * seq * rows / jnp.full((rows, 128), live, jnp.int32).astype(F32)
    row = lax.broadcasted_iota(jnp.int32, (rows, 128), 0) + s * rows
    row_scale[...] = jnp.where(row < counts[b], factor, 0.0)
    thin = rows // chunks
    tall = seq * thin
    hidden = act.shape[-1]
    wide = 512
    gate_post = jnp.tanh(mod_rows[1:2, :]) * gain_rows[1:2, :]
    gain_ffn = gain_rows[2:3, :] * (1.0 + mod_rows[2:3, :])
    gate_last = jnp.tanh(mod_rows[3:4, :]) * gain_rows[3:4, :]
    row_sums[...] = jnp.zeros_like(row_sums)

    def of(c):
        return pl.ds(c * thin, thin)

    def chunk_of(ref, c, cols=slice(None)):
        whole = ref[:, of(c), cols]
        return whole.reshape(tall, whole.shape[-1])

    def mean(values):
        return jnp.mean(values, axis=-1, keepdims=True)

    def over_rows(c, body):
        step = 16

        def one(i, carry):
            return body(pl.ds(pl.multiple_of(c * thin + i * step, step), step), carry)

        return lax.fori_loop(0, thin // step, one, jnp.zeros((1, width), F32), unroll=2)

    def weighted(at):
        return cotangent[at, :].astype(F32) * row_scale[at, 0:1]

    def after_attn(c):
        def body(at, carry):
            out = got[at, :]
            attn_keep[at, :] = out
            resid = out * lax.rsqrt(mean(out * out) + 1e-05) * gate_post
            resid = tokens[at, :].astype(F32) + resid
            resid_keep[at, :] = resid
            normed = resid * lax.rsqrt(mean(resid * resid) + 1e-05)
            ffn_all[s, at, :] = (normed * gain_ffn).astype(BF16)
            return carry

        over_rows(c, body)

    def after_ffn(c):
        def body(at, total):
            out, resid, grad = got[at, :], resid_keep[at, :], weighted(at)
            size = lax.rsqrt(mean(out * out) + 1e-05)
            normed = out * size
            block_out[at, :] = (resid + gate_last * normed).astype(BF16)
            inner = grad * gate_last
            d_ffn[s, at, :] = (size * (inner - normed * mean(inner * normed))).astype(BF16)
            return total + jnp.sum(grad * normed, axis=0, keepdims=True)

        row_sums[2:3, :] += over_rows(c, body)

    def after_ffn_back(c):
        def body(at, totals):
            first, second = totals
            d_pre, resid, out = got[at, :], resid_keep[at, :], attn_keep[at, :]
            size = lax.rsqrt(mean(resid * resid) + 1e-05)
            normed, inner = resid * size, d_pre * gain_ffn
            second = second + jnp.sum(d_pre * normed, axis=0, keepdims=True)
            grad = weighted(at) + size * (inner - normed * mean(inner * normed))
            d_tokens[at, :] = grad
            size = lax.rsqrt(mean(out * out) + 1e-05)
            normed, inner = out * size, grad * gate_post
            first = first + jnp.sum(grad * normed, axis=0, keepdims=True)
            d_attn[s, at, :] = (size * (inner - normed * mean(inner * normed))).astype(BF16)
            return first, second

        step, zero = 16, jnp.zeros((1, width), F32)

        def one(i, carry):
            return body(pl.ds(pl.multiple_of(c * thin + i * step, step), step), carry)

        first, second = lax.fori_loop(0, thin // step, one, (zero, zero), unroll=2)
        row_sums[0:1, :] += first
        row_sums[1:2, :] += second

    def flat(values):
        return values.reshape(-1, values.shape[-1])

    def put_parts(c, cols, total):
        parts[c, :, :, cols] = total.astype(BF16).reshape(seq, thin, total.shape[-1])

    def attn_product(c):
        left = chunk_of(mixed, c)
        for at in range(0, width, wide):
            cols = slice(at, at + wide)
            put_parts(c, cols, bf_dot(left, w_out[:, cols]))

    def ffn_product(c):
        for at in range(0, hidden, wide):
            cols = slice(at, at + wide)
            left = chunk_of(ffn_all, c)
            gate = bf_dot(left, flat(w_gate[:, :, :, cols]))
            up = bf_dot(left, flat(w_up[:, :, :, cols]))
            gate_keep[c, :, cols], up_keep[c, :, cols] = gate, up
            value = (gate * jax.nn.sigmoid(gate) * up).astype(BF16)
            act[:, of(c), cols] = value.reshape(seq, thin, wide)
        left = chunk_of(act, c)
        for at in range(0, width, wide):
            cols = slice(at, at + wide)
            put_parts(c, cols, bf_dot(left, flat(w_down[:, :, cols])))

    def ffn_back_product(c):
        block = w_down.shape[1]
        for at in range(0, hidden, wide):
            cols = slice(at, at + wide)
            d_act = right_dot(chunk_of(d_ffn, c), flat(w_down[at // block : (at + wide) // block]))
            gate, up = gate_keep[c, :, cols], up_keep[c, :, cols]
            sig = jax.nn.sigmoid(gate)
            silu = gate * sig
            d_g = (d_act * up * (sig + silu * (1.0 - sig))).astype(BF16)
            d_u = (d_act * silu).astype(BF16)
            d_gate[:, of(c), cols] = d_g.reshape(seq, thin, wide)
            d_up[:, of(c), cols] = d_u.reshape(seq, thin, wide)
        left_g, left_u = chunk_of(d_gate, c), chunk_of(d_up, c)
        half = buckets // 2
        for at in range(0, buckets, half):
            cols = slice(at * width // buckets, (at + half) * width // buckets)
            total = right_dot(left_g, flat(w_gate[at : at + half]))
            total = total + right_dot(left_u, flat(w_up[at : at + half]))
            put_parts(c, cols, total)

    def pour_of(c, turn):
        left, right = from_left.at[turn * chunks + c], from_right.at[turn * chunks + c]
        return Pour(copies, parts.at[c], left, right, b, s, seq)

    gathered = (ffn_all, d_ffn, d_attn)
    after = (after_attn, after_ffn, after_ffn_back)
    products = (attn_product, ffn_product, ffn_back_product)

    def all_rows(ref, cols=slice(None)):
        whole = ref[:, :, cols]
        return whole.reshape(seq * rows, whole.shape[-1])

    def down_grad():
        chips, part = buckets // 2, hidden // buckets
        for i in range(chips):
            turned = all_rows(act, slice(2 * i * part, 2 * (i + 1) * part)).T
            total = bf_dot(turned, all_rows(d_ffn)).astype(BF16)
            for half in range(2):
                grads[2][i, half] = total[half * part : (half + 1) * part]
        sums.begin(2)

    def weight_grads():
        chips, part = buckets // 2, width // (buckets // 2)
        for i in range(chips):
            turned = all_rows(ffn_all, slice(i * part, (i + 1) * part)).T
            for grad, d in zip(grads[:2], (d_gate, d_up), strict=True):
                total = bf_dot(turned, all_rows(d))
                grad[i] = total.astype(BF16).reshape(2, part // 2, hidden)
            if i == 1:
                sums.stage_a(2)
            yield
        sums.begin(0)
        sums.begin(1)
        sums.stage_b(2)
        yield
        sums.stage_a(0)
        yield
        sums.stage_c(2)
        sums.stage_a(1)
        yield
        sums.stage_b(0)
        yield
        sums.stage_b(1)
        yield
        sums.stage_c(0)
        sums.stage_d(2)
        sums.stage_c(1)
        sums.stage_d(0)
        sums.stage_d(1)

    extra = weight_grads()
    plan = [(turn, c) for turn in range(3) for c in range(chunks)]
    gathers, open_gather = {}, []

    def finish_gather():
        turn, c = open_gather.pop(0)
        gathers[turn, c].start(seq - 1)
        for j in range(seq - 1):
            gathers[turn, c].sent(j)
        return turn, c

    def weights_come():
        count = len(MOVED)
        for n in range(count + 3):
            if n < count:
                weights.arrived(MOVED[n])
                if n + 1 < count:
                    weights.depart(MOVED[n + 1])
                weights.stage_a(MOVED[n])
                yield
            if 1 <= n <= count:
                weights.stage_b(MOVED[n - 1])
                yield
            if 2 <= n <= count + 1:
                weights.stage_c(MOVED[n - 2])
            if 3 <= n:
                weights.stage_d(MOVED[n - 3])
            yield

    coming = weights_come()
    attn_product(0)
    pours = {(0, 0): pour_of(0, 0)}
    ready = pours[0, 0].cuts
    for q in range(ready):
        pours[0, 0].step(q)
    for c in range(1, chunks):
        attn_product(c)
    for load in loads:
        load.wait()
    for at, (turn, c) in enumerate(plan):
        pour = pours[turn, c]
        mate = gathers[open_gather[0]] if open_gather else None
        per = pour.count // (seq - 1)
        final = at == len(plan) - 1
        for j in range(2, seq):
            if mate is not None and j < seq - 1:
                mate.start(j)
            if final:
                next(extra, None)
            for q in range((j - 1) * per, j * per):
                pour.step(q)
                next(coming, None)
            if final:
                next(extra, None)
        pour.end(got.at[of(c)])
        after[turn](c)
        gathers[turn, c] = Relay(copies, None, gathered[turn], b, s, seq, of(c))
        gathers[turn, c].start(0)
        if mate is not None:
            done_turn, done_c = finish_gather()
            if (done_turn, done_c) == (1, chunks - 1):
                down_grad()
            for _ in coming:
                pass
            if done_turn < 2:
                products[done_turn + 1](done_c)
        open_gather.append((turn, c))
        gathers[turn, c].start(1)
        if at + 1 < len(plan):
            nxt = plan[at + 1]
            pours[nxt] = pour_of(nxt[1], nxt[0])
            for q in range(ready):
                pours[nxt].step(q)
            if at + 2 == len(plan):
                for _ in range(AHEAD):
                    next(extra)
    turn, c = open_gather[0]
    for j in range(2, seq - 1):
        next(extra, None)
        gathers[turn, c].start(j)
    next(extra, None)
    finish_gather()
    for _ in extra:
        pass
    sums.end()
    weights.end()


def middle_all(buckets, seq, mixed, weights, tokens, cotangent, counts, gain_rows, mod_rows):
    any_spec = pl.BlockSpec(memory_space=pl.ANY)
    vmem = pl.BlockSpec(memory_space=pltpu.VMEM)
    smem = pl.BlockSpec(memory_space=pltpu.SMEM)
    chunks = CHUNKS
    w_out, w_gate, w_up, w_down = weights
    rows, width = tokens.shape
    hidden = w_down.shape[-2] * buckets if 2 in MOVED else w_down.shape[0] * w_down.shape[1]
    part = width // (buckets * seq)
    tall, thin = (seq, rows, width), rows // chunks
    flat = (seq, rows, hidden)
    blocks = pltpu.VMEM((3 * chunks, seq - 1, thin, width), BF16)
    kinds = ("hold", "hold", "stay")
    shapes, sums_out, scratch, n_sems = sums_shapes(
        buckets, seq, [(width, hidden), (width, hidden), (hidden, width)], kinds, near=True
    )
    n_sems += 64 + 3 * chunks * (2 * CUTS + 2) * seq
    results = pl.pallas_call(
        functools.partial(middle_kernel, buckets, seq, chunks, kinds),
        out_shape=[
            jax.ShapeDtypeStruct((rows, width), BF16),
            jax.ShapeDtypeStruct((rows, width), F32),
            jax.ShapeDtypeStruct(tall, BF16),
            jax.ShapeDtypeStruct((8, width), F32),
            *sums_out,
        ],
        in_specs=[vmem] * 4 + [smem] + [vmem] * 2 + [any_spec] * 3,
        out_specs=[vmem] * 7,
        scratch_shapes=[
            pltpu.VMEM((buckets, seq, part, hidden), BF16),
            pltpu.VMEM((buckets, seq, part, hidden), BF16),
            pltpu.VMEM((buckets, hidden // buckets, width), BF16),
            pltpu.VMEM(tall, BF16),
            pltpu.VMEM(tall, BF16),
            *([pltpu.VMEM(flat, BF16)] * 3),
            pltpu.VMEM((chunks, seq * thin, hidden), F32),
            pltpu.VMEM((chunks, seq * thin, hidden), F32),
            pltpu.VMEM((rows, width), F32),
            pltpu.VMEM((rows, width), F32),
            pltpu.VMEM((rows, width), F32),
            pltpu.VMEM((chunks, seq, thin, width), BF16),
            blocks,
            blocks,
            pltpu.VMEM((rows, 128), F32),
            pltpu.SemaphoreType.DMA((n_sems,)),
            pltpu.SemaphoreType.DMA((n_sems,)),
            *[pltpu.VMEM(shape, BF16) for shape in shapes],
            *scratch,
        ],
        compiler_params=pltpu.CompilerParams(
            collective_id=11, has_side_effects=True, vmem_limit_bytes=62 * 2**20
        ),
    )(
        mixed.reshape(seq, rows, mixed.shape[1]),
        w_out,
        tokens,
        cotangent,
        counts,
        gain_rows,
        mod_rows,
        w_gate,
        w_up,
        w_down,
    )
    return results[:4], (results[4], results[5], results[6].reshape(-1, results[6].shape[-1]))


LATE = (1, 2, 3, 11, 12, 19, 20, 21, 22)


def backward_kernel(buckets, seq, kinds, *refs):
    count = len(kinds)
    (
        d_attn,
        w_query,
        w_key,
        w_value,
        w_out,
        query,
        key,
        value,
        cap_key,
        cap_value,
        cross_out,
        query_raw,
        key_raw,
        cap_raw,
        gain_rows,
        mod_rows,
        counts,
        cap_lens,
        mixed,
        hidden,
        captions,
        tokens,
        d_tokens,
        row_sums,
    ) = refs[:24]
    holds, strip_outs = refs[24:26], refs[29:31]
    tokens_grad, mod_all, small_out, refs = refs[26], refs[27], refs[28], refs[31:]
    outs, refs = refs[:count], refs[count:]
    mixed_low, cross_low, query_acc, key_acc, value_acc, cap_key_acc, cap_value_acc = refs[:7]
    d_query, d_key, d_value, d_cap_key, d_cap_value, d_hidden, vec = refs[7:14]
    mod_give, mod_got, mod_sum, wide_give, wide_got, slim_give, slim_got = refs[14:21]
    key_bias, cap_bias, parts, from_left, from_right, send, recv = refs[21:28]
    late, refs = refs[28 : 28 + len(LATE)], refs[28 + len(LATE) :]
    strips, refs = refs[:2], refs[2:]
    grads, refs = refs[:count], refs[count:]
    b, s = lax.axis_index("bucket"), lax.axis_index("seq")
    copies = Copies(send, recv)
    far = (w_query, w_key, w_value, query_raw, key_raw, hidden, captions, tokens, d_tokens)
    loads = [copies.local(src, dst) for src, dst in zip(far, late, strict=True)]
    for at in (6, 3, 4, 0, 1, 2, 5, 7, 8):
        loads[at].start()
    w_query, w_key, w_value, query_raw, key_raw, hidden, captions, tokens, d_tokens = late
    sums = GradSums(copies, b, s, buckets, seq, kinds, grads, outs, refs, near=True)
    peers = greet_all(b, s, buckets, seq)

    rows, share = query.shape
    width = parts.shape[-1]
    pairs = share // 128
    chips = buckets // 2
    span_block = 256
    scale = HEAD_DIM**-0.5

    def gain_of(row, pair):
        at = pl.multiple_of(s * share + pair * 128, 128)
        return gain_rows[row : row + 1, pl.ds(at, 128)]

    vec[...] = jnp.zeros_like(vec)
    mod_give[...] = jnp.zeros_like(mod_give)
    wide_give[...] = jnp.zeros_like(wide_give)
    slim_give[...] = jnp.zeros_like(slim_give)
    fill_rows(key_bias, counts[b], 0, 0.0, -1e30)
    fill_rows(cap_bias, cap_lens[b], 0, 0.0, -1e30)
    mixed_low[...] = right_dot(d_attn[...], w_out[...]).astype(BF16)

    def own_sum(row, pair, total):
        vec[row : row + 1, pl.ds(pl.multiple_of(s * share + pair * 128, 128), 128)] = total

    def cross_part(pair):
        lane = slice(pair * 128, (pair + 1) * 128)
        gate = jnp.tanh(gain_of(7, pair))

        def body(i, total):
            at = pl.ds(pl.multiple_of(i * 128, 128), 128)
            d = mixed_low[at, lane].astype(F32)
            cross_low[at, lane] = (gate * d).astype(BF16)
            return total + jnp.sum(d * cross_out[at, lane], axis=0, keepdims=True)

        total = lax.fori_loop(0, rows // 128, body, jnp.zeros((1, 128), F32))
        own_sum(7, pair, total * (1.0 - gate * gate))

    def attend_back(pair, k_ref, v_ref, bias, d_ref, k_acc, v_acc, add):
        lane = slice(pair * 128, (pair + 1) * 128)
        low = low_half((span_block, 128))
        k_turned = k_ref[:, lane].T
        k_acc[:, lane] = jnp.zeros((k_acc.shape[0], 128), F32)
        v_acc[:, lane] = jnp.zeros((v_acc.shape[0], 128), F32)

        def body(i, carry):
            at = pl.ds(pl.multiple_of(i * span_block, span_block), span_block)
            q = query[at, lane] * jnp.asarray(scale, BF16)
            d = d_ref[at, lane]
            found = []
            for keep in (low, jnp.logical_not(low)):
                q_half = jnp.where(keep, q, jnp.zeros_like(q))
                d_half = jnp.where(keep, d, jnp.zeros_like(d))
                scores = right_dot(k_ref[:, lane], q_half)
                scores = scores + jnp.concatenate([bias[...], bias[...]], axis=1)
                weights = jnp.exp(scores)
                probs = weights * (1.0 / jnp.sum(weights, axis=0, keepdims=True))
                d_probs = right_dot(v_ref[:, lane], d_half)
                delta = jnp.sum(probs * d_probs, axis=0, keepdims=True)
                d_scores = (probs * (d_probs - delta)).astype(BF16)
                k_acc[:, lane] += bf_dot(d_scores, q_half)
                v_acc[:, lane] += bf_dot(probs.astype(BF16), d_half)
                found.append(bf_dot(k_turned, d_scores))
            turned = jnp.concatenate([found[0][:HEAD_DIM], found[1][HEAD_DIM:]], axis=0)
            d_q = turned.T * scale
            query_acc[at, lane] = query_acc[at, lane] + d_q if add else d_q
            return carry

        lax.fori_loop(0, rows // span_block, body, 0)

    def norm_back(raw, d_norm, out, row, sum_row):
        for pair in range(pairs):
            lane = slice(pair * 128, (pair + 1) * 128)
            gain = gain_of(row, pair)

            def body(i, total):
                at = pl.ds(pl.multiple_of(i * 128, 128), 128)
                x, d = raw[at, lane], d_norm[at, lane]
                size = pair_scale(x, 1e-06)
                normed, inner = x * size, d * gain
                mean = pair_sums(inner * normed) * (1.0 / HEAD_DIM)
                out[at, lane] = (size * (inner - normed * mean)).astype(BF16)
                return total + jnp.sum(d * normed, axis=0, keepdims=True)

            total = lax.fori_loop(0, raw.shape[0] // 128, body, jnp.zeros((1, 128), F32))
            own_sum(sum_row, pair, total)

    def weight_grads(left, chosen):
        part = left.shape[1] // chips
        for i in range(chips):
            turned = left[:, i * part : (i + 1) * part].T
            for w, right in chosen:
                total = bf_dot(turned, right[...])
                grads[w][i] = total.astype(BF16).reshape(2, part // 2, total.shape[-1])
            yield
        for w, _ in chosen:
            sums.begin(w)

    def out_grad():
        total = bf_dot(mixed[...].T, d_attn[...]).astype(BF16)
        part = share // buckets
        for block, p in enumerate(spread(buckets)):
            grads[0][p // 2, p % 2] = total[block * part : (block + 1) * part]
        sums.begin(0)

    pl.semaphore_wait(pltpu.get_barrier_semaphore(), peers)
    strip_moves = []
    for hold, strip in zip(holds, strips, strict=True):
        strip[s] = hold[s]
        for j in range(1, seq):
            peer = lax.rem(s + j, seq)
            strip_moves.append(sums.go(copies.remote(hold.at[peer], strip.at[s], b, peer)))
    for pair in range(pairs):
        cross_part(pair)
        attend_back(pair, cap_key, cap_value, cap_bias, cross_low, cap_key_acc, cap_value_acc, False)
    norm_back(cap_raw, cap_key_acc, d_cap_key, 6, 6)
    d_cap_value[...] = cap_value_acc[...].astype(BF16)
    loads[6].wait()
    for _ in weight_grads(captions, ((1, d_cap_key), (2, d_cap_value))):
        pass
    def deal_back():
        for move in strip_moves:
            move.wait_recv()
        for strip, out in zip(strips, strip_outs, strict=True):
            for j in range(seq):
                for part in range(strip.shape[2] // 128):
                    cols = slice((part * seq + j) * 128, (part * seq + j + 1) * 128)
                    out[:, cols] = strip[j, :, part * 128 : (part + 1) * 128].astype(F32)

    steps = (lambda: sums.stage_a(1), lambda: sums.stage_a(2), lambda: sums.stage_b(1))
    for pair in range(pairs):
        attend_back(pair, key, value, key_bias, mixed_low, key_acc, value_acc, True)
        steps[pair]()
    for at in (3, 4, 0, 1, 2, 5, 7, 8):
        loads[at].wait()
    norm_back(query_raw, query_acc, d_query, 4, 4)
    norm_back(key_raw, key_acc, d_key, 5, 5)
    d_value[...] = value_acc[...].astype(BF16)
    pour = Pour(copies, parts, from_left, from_right, b, s, seq)
    wide = 512
    for at in range(0, width, wide):
        cols = slice(at, at + wide)
        total = right_dot(d_query[...], w_query[cols, :]) + right_dot(d_key[...], w_key[cols, :])
        total = total + right_dot(d_value[...], w_value[cols, :])
        parts[:, :, cols] = total.astype(BF16).reshape(seq, rows // seq, wide)
    pieces = weight_grads(hidden, ((3, d_query), (4, d_key), (5, d_value)))
    between = {1: out_grad, 2: lambda: sums.stage_b(2)}
    for q in range(pour.count):
        pour.step(q)
        if q in between:
            between[q]()
        elif q > 2:
            next(pieces, None)
    for _ in pieces:
        pass
    deal_back()
    sums.stage_a(0)
    sums.stage_c(1)
    sums.stage_c(2)
    pour.end(d_hidden)

    factor = gain_rows[0:1, :] * (1.0 + mod_rows[0:1, :])

    def body(i, total):
        at = pl.ds(pl.multiple_of(i * 16, 16), 16)
        x, d = tokens[at, :].astype(F32), d_hidden[at, :]
        size = lax.rsqrt(jnp.mean(x * x, axis=-1, keepdims=True) + 1e-05)
        normed, inner = x * size, d * factor
        mean = jnp.mean(inner * normed, axis=-1, keepdims=True)
        tokens_grad[at, :] = d_tokens[at, :] + size * (inner - normed * mean)
        return total + jnp.sum(d * normed, axis=0, keepdims=True)

    total = lax.fori_loop(0, tokens.shape[0] // 16, body, jnp.zeros((1, width), F32))
    post, last = jnp.tanh(mod_rows[1:2, :]), jnp.tanh(mod_rows[3:4, :])
    vec[8:9, :] = total * gain_rows[0:1, :]
    vec[9:10, :] = row_sums[0:1, :] * gain_rows[1:2, :] * (1.0 - post * post)
    vec[10:11, :] = row_sums[1:2, :] * gain_rows[2:3, :]
    vec[11:12, :] = row_sums[2:3, :] * gain_rows[3:4, :] * (1.0 - last * last)
    vec[0:1, :] = total * (1.0 + mod_rows[0:1, :])
    vec[1:2, :] = row_sums[0:1, :] * post
    vec[2:3, :] = row_sums[1:2, :] * (1.0 + mod_rows[2:3, :])
    vec[3:4, :] = row_sums[2:3, :] * last
    piece, wide = width // 4, width // buckets
    slim = wide // seq
    for t in range(seq):
        for j in range(4):
            mod_give[t, j : j + 1, :] = vec[8 + t : 9 + t, j * piece : (j + 1) * piece]
    for t in range(buckets):
        wide_give[t, :, :wide] = vec[0:8, t * wide : (t + 1) * wide]
    mod_moves, wide_moves = [], []
    for j in range(1, seq):
        peer = lax.rem(s + j, seq)
        mod_moves.append(sums.go(copies.remote(mod_give.at[peer], mod_got.at[j], b, peer)))
    for j in range(1, buckets):
        peer = lax.rem(b + j, buckets)
        wide_moves.append(sums.go(copies.remote(wide_give.at[peer], wide_got.at[j], peer, s)))
    sums.stage_a(3)
    sums.stage_a(4)
    sums.stage_a(5)
    total = mod_give[s]
    for j, move in enumerate(mod_moves, 1):
        move.wait_recv()
        total = total + mod_got[j]
    mod_sum[...] = total
    mod_next, slim_next = [], []
    for j in range(1, buckets):
        peer = lax.rem(b + j, buckets)
        mod_next.append(sums.go(copies.remote(mod_sum, mod_all.at[b], peer, s)))
    mod_own = copies.local(mod_sum, mod_all.at[b])
    mod_own.start()
    total = wide_give[b]
    for j, move in enumerate(wide_moves, 1):
        move.wait_recv()
        total = total + wide_got[j]
    for t in range(seq):
        slim_give[t, :, :slim] = total[:, t * slim : (t + 1) * slim]
    for j in range(1, seq):
        peer = lax.rem(s + j, seq)
        slim_next.append(sums.go(copies.remote(slim_give.at[peer], slim_got.at[j], b, peer)))
    for w in (0, 3, 4, 5):
        sums.stage_b(w)
    sums.stage_c(0)
    for w in (3, 4, 5):
        sums.stage_c(w)
    sums.stage_d(0)
    total = slim_give[s]
    for j, move in enumerate(slim_next, 1):
        move.wait_recv()
        total = total + slim_got[j]
    small_out[...] = total
    for move in mod_next:
        move.wait_recv()
    mod_own.wait()
    sums.end()


def backward_all(buckets, seq, inputs, shapes, kinds):
    any_spec = pl.BlockSpec(memory_space=pl.ANY)
    vmem = pl.BlockSpec(memory_space=pltpu.VMEM)
    smem = pl.BlockSpec(memory_space=pltpu.SMEM)
    shapes, outs, scratch, n_sems = sums_shapes(buckets, seq, shapes, kinds, near=True)
    query, cap_key, tokens = inputs[5], inputs[8], inputs[21]
    rows, width = tokens.shape
    vec = (16, width)
    n_sems += 12 * seq + 4 * buckets + len(LATE) + 2 * seq
    results = pl.pallas_call(
        functools.partial(backward_kernel, buckets, seq, tuple(kinds)),
        out_shape=[
            jax.ShapeDtypeStruct((rows, width), F32),
            jax.ShapeDtypeStruct((buckets, 8, width // 4), F32),
            jax.ShapeDtypeStruct((8, 128), F32),
            *[jax.ShapeDtypeStruct((x.shape[1], x.shape[2] * seq), F32) for x in inputs[24:26]],
            *outs,
        ],
        in_specs=[
            smem if at in (16, 17) else any_spec if at in LATE else vmem for at in range(len(inputs))
        ],
        out_specs=[vmem, any_spec] + [vmem] * (3 + len(outs)),
        scratch_shapes=[
            pltpu.VMEM(query.shape, BF16),
            pltpu.VMEM(query.shape, BF16),
            pltpu.VMEM(query.shape, F32),
            pltpu.VMEM(query.shape, F32),
            pltpu.VMEM(query.shape, F32),
            pltpu.VMEM(cap_key.shape, F32),
            pltpu.VMEM(cap_key.shape, F32),
            pltpu.VMEM(query.shape, BF16),
            pltpu.VMEM(query.shape, BF16),
            pltpu.VMEM(query.shape, BF16),
            pltpu.VMEM(cap_key.shape, BF16),
            pltpu.VMEM(cap_key.shape, BF16),
            pltpu.VMEM((rows, width), F32),
            pltpu.VMEM(vec, F32),
            pltpu.VMEM((seq, 8, width // 4), F32),
            pltpu.VMEM((seq, 8, width // 4), F32),
            pltpu.VMEM((8, width // 4), F32),
            pltpu.VMEM((buckets, 8, 256), F32),
            pltpu.VMEM((buckets, 8, 256), F32),
            pltpu.VMEM((seq, 8, 128), F32),
            pltpu.VMEM((seq, 8, 128), F32),
            pltpu.VMEM((query.shape[0], 128), F32),
            pltpu.VMEM((cap_key.shape[0], 128), F32),
            pltpu.VMEM((seq, rows, width), BF16),
            pltpu.VMEM((seq - 1, rows, width), BF16),
            pltpu.VMEM((seq - 1, rows, width), BF16),
            pltpu.SemaphoreType.DMA((n_sems,)),
            pltpu.SemaphoreType.DMA((n_sems,)),
            *[pltpu.VMEM(inputs[at].shape, inputs[at].dtype) for at in LATE],
            *[pltpu.VMEM(x.shape, BF16) for x in inputs[24:26]],
            *[pltpu.VMEM(shape, BF16) for shape in shapes],
            *scratch,
        ],
        compiler_params=pltpu.CompilerParams(
            collective_id=10, has_side_effects=True, vmem_limit_bytes=62 * 2**20
        ),
    )(*inputs)
    sums = [*results[3:5], *(out.reshape(-1, out.shape[-1]) for out in results[5:])]
    return results[0], results[1], results[2], sums


def last_kernel(buckets, seq, slim, *refs):
    cond, mod_all, small = refs[:3]
    count = (len(refs) - 7) // 2
    sources, refs = refs[3 : 3 + count], refs[3 + count :]
    mod_grad, gains, cross = refs[:3]
    targets, sems = refs[3 : 3 + count], refs[3 + count]
    copies = [
        pltpu.make_async_copy(a, b, sems.at[i])
        for i, (a, b) in enumerate(zip(sources, targets, strict=True))
    ]
    for copy in copies:
        copy.start()
    piece = mod_all.shape[2]
    for j in range(4):
        total = None
        for k in range(buckets):
            term = cond[:, k : k + 1] * mod_all[k, j : j + 1, :]
            total = term if total is None else total + term
        mod_grad[:, j * piece : (j + 1) * piece] = total
    gains[...] = small[0:7, :slim]
    cross[...] = small[7:8, :slim]
    for copy in copies:
        copy.wait()


def last_all(buckets, seq, slim, cond, mod_all, small, results):
    any_spec = pl.BlockSpec(memory_space=pl.ANY)
    vmem = pl.BlockSpec(memory_space=pltpu.VMEM)
    outs = pl.pallas_call(
        functools.partial(last_kernel, buckets, seq, slim),
        out_shape=[
            jax.ShapeDtypeStruct((cond.shape[0], 4 * mod_all.shape[2]), F32),
            jax.ShapeDtypeStruct((7, slim), F32),
            jax.ShapeDtypeStruct((1, slim), F32),
            *[jax.ShapeDtypeStruct(x.shape, x.dtype) for x in results],
        ],
        in_specs=[vmem] * 3 + [any_spec] * len(results),
        out_specs=[vmem] * (3 + len(results)),
        scratch_shapes=[pltpu.SemaphoreType.DMA((len(results),))],
        compiler_params=pltpu.CompilerParams(vmem_limit_bytes=62 * 2**20),
    )(cond, mod_all, small, *results)
    return outs[0], outs[1], outs[2].reshape(slim), outs[3:]


def on_device(
    tokens,
    captions,
    cotangent,
    counts,
    cap_lens,
    steps_t,
    w_query,
    w_key,
    w_value,
    w_out,
    w_cap_key,
    w_cap_value,
    w_gate,
    w_up,
    w_down,
    w_mod,
    gains,
    cross_gate,
):
    buckets, seq = lax.axis_size("bucket"), lax.axis_size("seq")
    b, s = lax.axis_index("bucket"), lax.axis_index("seq")
    place = b * seq + s
    rows, width = tokens.shape
    span = rows * seq
    share = width // seq

    cond_size = w_mod.shape[0] * buckets * seq
    cond = jax.nn.silu(time_embed(steps_t, cond_size)).astype(BF16)
    cond_part = lax.dynamic_slice_in_dim(cond, place * w_mod.shape[0], w_mod.shape[0], 1)
    slim = gains.shape[1]
    small = jnp.concatenate([gains, cross_gate[None]], axis=0).astype(F32)
    small = jnp.pad(small, ((0, 0), (0, 128 - slim)))
    feed = [w_gate, w_up, w_down]
    early = [w for w in range(3) if w not in MOVED]
    cap_all, weights, inner = forward_all(
        buckets,
        seq,
        tokens,
        captions,
        small,
        slim,
        cond_part,
        w_mod,
        [counts, cap_lens],
        [w_query, w_key, w_value, w_cap_key, w_cap_value, w_out, *(feed[w] for w in early)],
        ["col", "col", "col", "col", "col", "row", *(("cut", "cut", "stay")[w] for w in early)],
    )
    wq, wk, wv, wck, wcv, wo = (x.reshape(-1, x.shape[-1]) for x in weights[:6])
    for w, full in zip(early, weights[6:], strict=True):
        feed[w] = full
    caps = cap_all.reshape(-1, captions.shape[1])
    small_rows, mod, hidden, query_proj, key_proj, cap_proj = inner[:6]
    query, key, value, cap_key, cap_value = inner[6:11]
    cross_out, mixed_low = inner[11:]
    (block_out, d_tokens, d_attn_all, row_sums), (h_gate, h_up, s_down) = middle_all(
        buckets,
        seq,
        mixed_low,
        (wo, *feed),
        tokens,
        cotangent,
        counts,
        small_rows,
        mod,
    )
    tokens_grad, mod_all, small_sums, sums = backward_all(
        buckets,
        seq,
        [
            d_attn_all.reshape(span, width),
            wq,
            wk,
            wv,
            wo,
            query,
            key,
            value,
            cap_key,
            cap_value,
            cross_out,
            query_proj,
            key_proj,
            cap_proj,
            small_rows,
            mod,
            counts,
            cap_lens,
            mixed_low,
            hidden,
            caps,
            tokens,
            d_tokens,
            row_sums,
            h_gate,
            h_up,
        ],
        [x.shape for x in (wo, wck, wcv, wq, wk, wv)],
        ["row", "col", "col", "col", "col", "col"],
    )
    s_gate, s_up, s_out, s_cap_key, s_cap_value, s_query, s_key, s_value = sums

    cond_size = cond.shape[1] // buckets
    cond_cols = lax.dynamic_slice_in_dim(cond, b * cond_size, cond_size, 1).astype(F32).T
    results = [block_out, tokens_grad, s_query, s_key, s_value, s_out]
    results += [s_cap_key, s_cap_value, s_gate, s_up, s_down]
    s_mod, s_gains, s_cross, results = last_all(
        buckets, seq, slim, cond_cols, mod_all, small_sums, results
    )
    return (*results, s_mod, s_gains, s_cross)


def solution(mesh):
    spread = P(("bucket", "seq"), None)
    in_specs = (
        *([spread] * 3),
        *([P()] * 3),
        *([spread] * 10),
        P(None, ("bucket", "seq")),
        P(("bucket", "seq")),
    )
    out_specs = (
        spread,
        spread,
        *([P("bucket", "seq")] * 10),
        P(None, ("bucket", "seq")),
        P(("bucket", "seq")),
    )
    buckets, seq = mesh.shape["bucket"], mesh.shape["seq"]

    def step(*args):
        tokens, weight = args[0], args[6]
        tiled = weight.shape[0] % 16 == 0 and weight.shape[1] // seq % 128 == 0
        fits = buckets == 8 and seq == 4 and tokens.shape[0] % 64 == 0
        return (on_device if tiled and fits else on_device_general)(*args)

    return jax.shard_map(
        step, mesh=mesh, in_specs=in_specs, out_specs=out_specs, check_vma=False
    )
```

```python
import functools
import math

import jax
import jax.numpy as jnp
from jax import lax
from jax.experimental import pallas as pl
from jax.experimental.pallas import tpu as pltpu
from jax.sharding import PartitionSpec as P

HEAD_DIM = 64
MESH = pl.DeviceIdType.MESH
F32, BF16 = jnp.float32, jnp.bfloat16
CHUNKS, CUTS, FLIGHT = 2, 2, 2


def rms_rows(values):
    return values * lax.rsqrt(jnp.mean(values * values, axis=-1, keepdims=True) + 1e-05)


def head_rms(values):
    shaped = values.reshape(values.shape[:-1] + (values.shape[-1] // HEAD_DIM, HEAD_DIM))
    shaped = shaped * lax.rsqrt(jnp.mean(shaped * shaped, axis=-1, keepdims=True) + 1e-06)
    return shaped.reshape(values.shape)


def time_embed(steps, width):
    half_width = width // 2
    freqs = jnp.exp(-math.log(10000.0) * jnp.arange(half_width, dtype=F32) / half_width)
    angles = steps.astype(F32)[:, None] * freqs
    return jnp.concatenate([jnp.cos(angles), jnp.sin(angles)], axis=1)


def pick_entry(table, index):
    return jnp.sum(jnp.where(jnp.arange(table.shape[0]) == index, table, 0))


def bf_dot(left, right):
    return jnp.dot(left, right, preferred_element_type=F32)


def left_dot(rows_left, rows_right):
    return lax.dot_general(
        rows_left, rows_right, (((0,), (0,)), ((), ())), preferred_element_type=F32
    )


def right_dot(left, right):
    return lax.dot_general(left, right, (((1,), (1,)), ((), ())), preferred_element_type=F32)


def pre_attn(tokens_in, gain_pre, scale_attn):
    return rms_rows(tokens_in) * gain_pre * (1.0 + scale_attn)


def qk_norm(query_in, key_in, gain_query, gain_key):
    return (head_rms(query_in) * gain_query, head_rms(key_in) * gain_key)


def cap_norm(key_in, gain_cap):
    return head_rms(key_in) * gain_cap


def middle(tokens_in, attn_out, gain_post, gate_attn, gain_ffn, scale_ffn):
    resid_one = tokens_in + jnp.tanh(gate_attn) * rms_rows(attn_out) * gain_post
    return (resid_one, rms_rows(resid_one) * gain_ffn * (1.0 + scale_ffn))


def activate(gate_proj, up_proj):
    return jax.nn.silu(gate_proj) * up_proj


def finish(resid_one, ffn_out, gain_last, gate_ffn):
    return resid_one + jnp.tanh(gate_ffn) * rms_rows(ffn_out) * gain_last


def flip(index, bit):
    return index + bit - 2 * bit * lax.rem(lax.div(index, bit), 2)


def slot(index, buckets):
    if buckets != 8:
        return index
    high, low = lax.div(index, 4), lax.rem(index, 4)
    return 4 * high + 2 * lax.rem(low, 2) + lax.div(low, 2)


class Copies:
    def __init__(self, send, recv):
        self.send, self.recv, self.used = send, recv, 0

    def take(self, count=1):
        first = self.used
        self.used += count
        assert self.used <= self.send.shape[0], self.used
        return first

    def remote(self, src, dst, b, s, at=None):
        at = self.take() if at is None else at
        return pltpu.make_async_remote_copy(
            src_ref=src,
            dst_ref=dst,
            send_sem=self.send.at[at],
            recv_sem=self.recv.at[at],
            device_id={"bucket": b, "seq": s},
            device_id_type=MESH,
        )

    def local(self, src, dst):
        return pltpu.make_async_copy(src, dst, self.send.at[self.take()])


def greet(b, s):
    pl.semaphore_signal(
        pltpu.get_barrier_semaphore(),
        inc=1,
        device_id={"bucket": b, "seq": s},
        device_id_type=MESH,
    )


class Relay:
    def __init__(self, copies, own, out, b, s, seq, part=None):
        self.copies, self.own, self.out, self.b, self.s, self.seq = copies, own, out, b, s, seq
        self.part = part
        self.base = {1: copies.take(seq - 1), -1: copies.take(seq - 1)}
        self.up = jnp.where(s < seq - 1, s + 1, s - 1)
        self.down = jnp.where(s > 0, s - 1, s + 1)
        self.kept = None if own is None else copies.local(own, out.at[s])

    def packet(self, way, j):
        at = self.s - way * j
        block = self.out.at[at] if self.part is None else self.out.at[at, self.part]
        return self.copies.remote(
            self.own if j == 0 and self.own is not None else block,
            block,
            self.b,
            self.up if way > 0 else self.down,
            self.base[way] + j,
        )

    def sends(self, way):
        return self.s < self.seq - 1 if way > 0 else self.s > 0

    def has(self, way, j):
        return self.s >= j if way > 0 else self.s + j <= self.seq - 1

    def start(self, j):
        if j == 0 and self.kept is not None:
            self.kept.start()
        for way in (1, -1):
            if j == self.seq - 1:

                @pl.when(jnp.logical_not(self.sends(way)))
                def _():
                    for k in range(self.seq - 1):
                        self.packet(way, k).wait_recv()

                continue

            @pl.when(jnp.logical_and(self.sends(way), self.has(way, j)))
            def _():
                if j > 0:
                    self.packet(way, j - 1).wait_recv()
                self.packet(way, j).start()

    def sent(self, j):
        for way in (1, -1):

            @pl.when(jnp.logical_and(self.sends(way), self.has(way, j)))
            def _():
                self.packet(way, j).wait_send()

        if j == 0 and self.kept is not None:
            self.kept.wait()


def greet_line(b, s, seq):
    @pl.when(s > 0)
    def _():
        greet(b, s - 1)

    @pl.when(s < seq - 1)
    def _():
        greet(b, s + 1)

    peers = jnp.where(s > 0, 1, 0) + jnp.where(s < seq - 1, 1, 0)
    pl.semaphore_wait(pltpu.get_barrier_semaphore(), peers)


def halves_of(shape):
    if len(shape) == 3:
        return shape[0] // 2
    return (shape[0] // 32) * 16 if shape[0] >= 32 else shape[0] // 2


def gather_kernel(buckets, seq, kinds, *refs):
    count = len(kinds)
    tokens, captions, small, cond, w_mod = refs[:5]
    shards = refs[5 : 5 + count]
    tok_all, cap_all, small_all, mod_out = refs[5 + count : 9 + count]
    fulls = refs[9 + count : 9 + 2 * count]
    part, got_bucket, got_seq, mod_sum, send, recv = refs[9 + 2 * count :]
    b, s = lax.axis_index("bucket"), lax.axis_index("seq")
    copies = Copies(send, recv)
    chips = buckets // 2
    place = b * seq + s
    to_b, to_s = lax.rem(place, buckets), lax.div(place, buckets)
    back = s * buckets + b
    from_b, from_s = lax.div(back, seq), lax.rem(back, seq)
    stays = jnp.logical_and(to_b == b, to_s == s)

    lanes = part.shape[2]
    for j in range(part.shape[1]):
        part[:, j, :] = bf_dot(cond[...], w_mod[:, j * lanes : (j + 1) * lanes])

    for k in range(1, buckets):
        greet(lax.rem(b + k, buckets), s)
    for k in range(1, seq):
        greet(b, lax.rem(s + k, seq))

    @pl.when(jnp.logical_not(stays))
    def _():
        greet(from_b, from_s)

    peers = buckets - 1 + seq - 1 + jnp.where(stays, 0, 1)
    pl.semaphore_wait(pltpu.get_barrier_semaphore(), peers)

    sent = []

    def go(copy):
        copy.start()
        sent.append(copy)
        return copy

    mod_moves = []
    for k in range(1, buckets):
        peer = lax.rem(b + k, buckets)
        mod_moves.append(go(copies.remote(part.at[peer], got_bucket.at[k], peer, s)))
    small_moves = []
    for k in range(1, seq):
        peer = lax.rem(s + k, seq)
        small_moves.append(go(copies.remote(small, small_all.at[b, s], b, peer)))
    small_own = copies.local(small, small_all.at[b, s])
    small_own.start()

    tok = Relay(copies, tokens, tok_all, b, s, seq)
    cap = Relay(copies, captions, cap_all, b, s, seq)
    queue = [(tok, j) for j in range(seq)] + [(cap, j) for j in range(seq)]
    ahead = [(None, at) for at in range(count)]
    items = []
    while queue or ahead:
        items += queue[:1] + ahead[:1]
        queue, ahead = queue[1:], ahead[1:]

    first = [None] * count

    def depart(at):
        kind, shard, full = kinds[at], shards[at], fulls[at]
        if kind == "row":
            move = copies.remote(shard, full.at[to_b], to_b, to_s)
            keep = copies.local(shard, full.at[b])

            @pl.when(jnp.logical_not(stays))
            def _():
                move.start()

            @pl.when(stays)
            def _():
                keep.start()

            first[at] = (move, keep)
            return
        wide = full.shape[-1]

        def columns(peer):
            if kind == "cut":
                return shard.at[peer]
            return shard.at[:, pl.ds(pl.multiple_of(peer * wide, 128), wide)]

        moves = []
        for k in range(1, seq):
            peer = lax.rem(s + k, seq)
            move = copies.remote(columns(peer), full.at[b, s], b, peer)
            move.start()
            moves.append(move)
        keep = copies.local(columns(s), full.at[b, s])
        keep.start()
        first[at] = (moves, keep)

    def arrived(at):
        moves, keep = first[at]
        if kinds[at] == "row":

            @pl.when(jnp.logical_not(stays))
            def _():
                moves.wait()

            @pl.when(stays)
            def _():
                keep.wait()

            return
        for move in moves:
            move.wait()
        keep.wait()

    twin = flip(b, 1)
    second = [None] * count
    if chips == 4:
        near_x, near_y = flip(b, 2), flip(b, 4)
        far = flip(near_x, 4)

        def stage_a(at):
            full = fulls[at]
            second[at] = {
                "x": go(copies.remote(full.at[b], full.at[b], near_x, s)),
                "y": go(copies.remote(full.at[b], full.at[b], near_y, s)),
                "twin": [go(copies.remote(full.at[b], full.at[b], twin, s))],
            }

        def stage_b(at):
            full, now = fulls[at], second[at]
            cut = halves_of(full.shape[1:])
            now["x"].wait_recv()
            block = full.at[near_x, pl.ds(0, cut)]
            now["dy"] = go(copies.remote(block, block, near_y, s))
            block = full.at[near_x]
            now["twin"].append(go(copies.remote(block, block, twin, s)))
            now["y"].wait_recv()
            block = full.at[near_y, pl.ds(cut, full.shape[1] - cut)]
            now["dx"] = go(copies.remote(block, block, near_x, s))
            block = full.at[near_y]
            now["twin"].append(go(copies.remote(block, block, twin, s)))

        def stage_c(at):
            full, now = fulls[at], second[at]
            now["dy"].wait_recv()
            now["dx"].wait_recv()
            block = full.at[far]
            now["twin"].append(go(copies.remote(block, block, twin, s)))

    else:

        def stage_a(at):
            full = fulls[at]
            second[at] = {"far": [], "twin": []}
            for k in range(1, chips):
                peer = lax.rem(b + 2 * k, buckets)
                second[at]["far"].append(go(copies.remote(full.at[b], full.at[b], peer, s)))
            second[at]["twin"].append(go(copies.remote(full.at[b], full.at[b], twin, s)))

        def stage_b(at):
            full = fulls[at]
            for k, copy in enumerate(second[at]["far"], 1):
                copy.wait_recv()
                block = full.at[lax.rem(b + buckets - 2 * k, buckets)]
                second[at]["twin"].append(go(copies.remote(block, block, twin, s)))

        def stage_c(at):
            pass

    def begin(i):
        relay, j = items[i]
        if relay is None:
            depart(j)
        else:
            relay.start(j)

    begin(0)
    begin(1)
    for move in small_moves:
        move.wait_recv()
    small_own.wait()
    small_next = []
    for k in range(1, buckets):
        peer = lax.rem(b + k, buckets)
        small_next.append(go(copies.remote(small_all.at[b], small_all.at[b], peer, s)))
    total = part[b]
    for k, move in enumerate(mod_moves, 1):
        move.wait_recv()
        total = total + got_bucket[k]
    mod_sum[...] = total
    mod_next = []
    for k in range(1, seq):
        peer = lax.rem(s + k, seq)
        mod_next.append(go(copies.remote(mod_sum, got_seq.at[k], b, peer)))

    for i, (relay, j) in enumerate(items):
        if relay is None:
            arrived(j)
        elif j <= seq - 2:
            relay.sent(j)
        if i + 2 < len(items):
            begin(i + 2)
        if relay is None:
            stage_a(j)
            if j >= 1:
                stage_b(j - 1)
            if j >= 2:
                stage_c(j - 2)
    stage_b(count - 1)
    if count >= 2:
        stage_c(count - 2)
    stage_c(count - 1)

    total = mod_sum[...]
    for k, move in enumerate(mod_next, 1):
        move.wait_recv()
        total = total + got_seq[k]
    mod_out[...] = total
    for move in small_next:
        move.wait_recv()
    for now in second:
        for move in now["twin"]:
            move.wait_recv()
    for move in sent:
        move.wait_send()


def gather_all(buckets, seq, tokens, captions, small, cond, w_mod, shards, kinds):
    any_spec = pl.BlockSpec(memory_space=pl.ANY)
    vmem = pl.BlockSpec(memory_space=pltpu.VMEM)
    fulls, inputs, names = [], [], []
    for shard, kind in zip(shards, kinds, strict=True):
        rows, wide = shard.shape
        if kind == "row":
            fulls.append(jax.ShapeDtypeStruct((buckets, rows, wide), BF16))
        else:
            part = wide // seq
            fulls.append(jax.ShapeDtypeStruct((buckets, seq, rows, part), BF16))
            if part % 128:
                kind = "cut"
                shard = shard.reshape(rows, seq, part).transpose(1, 0, 2)
        inputs.append(shard)
        names.append(kind)
    mod_lanes = w_mod.shape[1] // 8
    n_sems = 64 + 16 * buckets + len(shards) * (seq + 2 * buckets)
    outs = pl.pallas_call(
        functools.partial(gather_kernel, buckets, seq, tuple(names)),
        out_shape=[
            jax.ShapeDtypeStruct((seq,) + tokens.shape, BF16),
            jax.ShapeDtypeStruct((seq,) + captions.shape, BF16),
            jax.ShapeDtypeStruct((buckets, seq) + small.shape, F32),
            jax.ShapeDtypeStruct((8, mod_lanes), F32),
            *fulls,
        ],
        in_specs=[any_spec, any_spec, any_spec, vmem, vmem] + [any_spec] * len(shards),
        out_specs=[any_spec, any_spec, any_spec, vmem] + [any_spec] * len(shards),
        scratch_shapes=[
            pltpu.VMEM((buckets, 8, mod_lanes), F32),
            pltpu.VMEM((buckets, 8, mod_lanes), F32),
            pltpu.VMEM((seq, 8, mod_lanes), F32),
            pltpu.VMEM((8, mod_lanes), F32),
            pltpu.SemaphoreType.DMA((n_sems,)),
            pltpu.SemaphoreType.DMA((n_sems,)),
        ],
        compiler_params=pltpu.CompilerParams(
            collective_id=0, has_side_effects=True, vmem_limit_bytes=24 * 2**20
        ),
    )(tokens, captions, small, cond, w_mod, *inputs)
    weights = []
    for full, kind in zip(outs[4:], names, strict=True):
        weights.append(full.reshape(-1, full.shape[-1]))
    return outs[0], outs[1], outs[2], outs[3], weights


def line_gather_kernel(seq, own, out, send, recv):
    b, s = lax.axis_index("bucket"), lax.axis_index("seq")
    greet_line(b, s, seq)
    relay = Relay(Copies(send, recv), own, out, b, s, seq)
    for j in range(seq):
        relay.start(j)
    for j in range(seq - 1):
        relay.sent(j)


def line_gather(seq, own, collective_id):
    return pl.pallas_call(
        functools.partial(line_gather_kernel, seq),
        out_shape=jax.ShapeDtypeStruct((seq,) + own.shape, own.dtype),
        in_specs=[pl.BlockSpec(memory_space=pl.ANY)],
        out_specs=pl.BlockSpec(memory_space=pl.ANY),
        scratch_shapes=[pltpu.SemaphoreType.DMA((2 * seq + 2,))] * 2,
        compiler_params=pltpu.CompilerParams(collective_id=collective_id, has_side_effects=True),
    )(own).reshape(-1, own.shape[-1])


def add_rows(out, terms):
    rows = out.shape[0]
    step = 16 if rows % 16 == 0 else rows

    def body(i, carry):
        at = pl.ds(pl.multiple_of(i * step, step), step)
        total = terms[0][at, :].astype(F32)
        for term in terms[1:]:
            total = total + term[at, :].astype(F32)
        out[at, :] = total.astype(out.dtype)
        return carry

    lax.fori_loop(0, rows // step, body, 0)


class Pour:
    def __init__(self, copies, parts, from_left, from_right, b, s, seq):
        self.copies, self.parts, self.b, self.s, self.seq = copies, parts, b, s, seq
        self.got = {1: from_left, -1: from_right}
        rows = parts.shape[1]
        self.cuts = CUTS if rows % (16 * CUTS) == 0 else 1
        self.thin = rows // self.cuts
        self.count = (seq - 1) * self.cuts
        self.base = {1: copies.take(self.count), -1: copies.take(self.count)}
        self.next = {
            1: jnp.where(s < seq - 1, s + 1, s - 1),
            -1: jnp.where(s > 0, s - 1, s + 1),
        }

    def block(self, way, q):
        j, at = q // self.cuts, pl.ds(q % self.cuts * self.thin, self.thin)
        return self.parts.at[self.seq - 1 - j if way > 0 else j, at], self.got[way].at[j, at]

    def packet(self, way, q):
        src, dst = self.block(way, q)
        return self.copies.remote(src, dst, self.b, self.next[way], self.base[way] + q)

    def on(self, way, q):
        j = q // self.cuts
        return self.s < self.seq - 1 - j if way > 0 else self.s > j

    def behind(self, way):
        return self.s > 0 if way > 0 else self.s < self.seq - 1

    def one(self, way, q):
        src, dst = self.block(way, q)

        @pl.when(jnp.logical_and(self.behind(way), self.on(way, q)))
        def _():
            self.packet(way, q).wait_recv()
            add_rows(src, [src, dst])

        @pl.when(self.on(way, q))
        def _():
            if q >= FLIGHT:
                self.packet(way, q - FLIGHT).wait_send()
            self.packet(way, q).start()

    def step(self, q):
        @pl.when(self.s < self.seq // 2)
        def _():
            self.one(1, q)
            self.one(-1, q)

        @pl.when(self.s >= self.seq // 2)
        def _():
            self.one(-1, q)
            self.one(1, q)

    def end(self, out):
        seq, cuts = self.seq, self.cuts
        for t in range(seq):

            @pl.when(self.s == t)
            def _():
                terms = [self.parts.at[t]]
                for way, j in ((1, seq - 1 - t), (-1, t)):
                    if j < seq - 1:
                        for c in range(cuts):
                            self.packet(way, j * cuts + c).wait_recv()
                        terms.append(self.got[way].at[j])
                add_rows(out, terms)

        for q in range(self.count):
            more = q + FLIGHT < self.count
            for way in (1, -1):
                last = jnp.logical_not(self.on(way, q + FLIGHT)) if more else True

                @pl.when(jnp.logical_and(self.on(way, q), last))
                def _():
                    self.packet(way, q).wait_send()


def line_scatter_kernel(seq, parts, out, from_left, from_right, send, recv):
    b, s = lax.axis_index("bucket"), lax.axis_index("seq")
    greet_line(b, s, seq)
    pour = Pour(Copies(send, recv), parts, from_left, from_right, b, s, seq)
    for q in range(pour.count):
        pour.step(q)
    pour.end(out)


def line_scatter(seq, parts, collective_id):
    rows, wide = parts.shape[0] // seq, parts.shape[1]
    vmem = pl.BlockSpec(memory_space=pltpu.VMEM)
    return pl.pallas_call(
        functools.partial(line_scatter_kernel, seq),
        out_shape=jax.ShapeDtypeStruct((rows, wide), F32),
        in_specs=[vmem],
        out_specs=vmem,
        input_output_aliases={},
        scratch_shapes=[
            pltpu.VMEM((seq - 1, rows, wide), BF16),
            pltpu.VMEM((seq - 1, rows, wide), BF16),
            pltpu.SemaphoreType.DMA((4 * seq,)),
            pltpu.SemaphoreType.DMA((4 * seq,)),
        ],
        compiler_params=pltpu.CompilerParams(
            collective_id=collective_id, has_side_effects=True, vmem_limit_bytes=24 * 2**20
        ),
    )(parts.astype(BF16).reshape(seq, rows, wide))


class GradSums:
    def __init__(self, copies, b, s, buckets, seq, kinds, grads, outs, scratch, near=False):
        self.near = near
        self.copies, self.b, self.s, self.buckets, self.seq = copies, b, s, buckets, seq
        self.kinds, self.grads, self.outs = kinds, grads, outs
        self.scratch = [scratch[8 * w : 8 * w + 8] for w in range(len(kinds))]
        self.chips = buckets // 2
        self.chip, self.core = lax.div(b, 2), lax.rem(b, 2)
        self.place = s * buckets + slot(b, buckets)
        self.to_b = lax.div(self.place, seq)
        self.twin = flip(b, 1)
        self.begun, self.state, self.last = {}, {}, {}
        self.sent = []

    def go(self, copy):
        copy.start()
        self.sent.append(copy)
        return copy

    def own(self, w, chip, rows=None):
        where = (chip,) if rows is None else (chip, rows)
        if self.near:
            return self.grads[w].at[(chip, self.core, *where[1:])]
        return self.scratch[w][0].at[where]

    def begin(self, w):
        own, other = self.scratch[w][:2]
        grad = self.grads[w]
        swap = self.copies.remote(grad.at[:, 1 - self.core], other, self.twin, self.s)
        swap.start()
        self.begun[w] = [swap]
        if not self.near:
            keep = self.copies.local(grad.at[:, self.core], own)
            keep.start()
            self.begun[w].append(keep)

    def stage_a(self, w):
        _, other, half_x, half_y, got, _ = self.scratch[w][:6]
        for copy in self.begun[w]:
            copy.wait()
        if not self.near and w + 2 in range(len(self.kinds)) and w + 2 not in self.begun:
            self.begin(w + 2)
        rows = other.shape[1]
        if self.chips != 4:
            moves = []
            for k in range(1, self.chips):
                to = lax.rem(self.chip + k, self.chips)
                own = self.own(w, to)
                add_rows(own, [own, other.at[to]])
                move = self.copies.remote(own, got.at[k], 2 * to + self.core, self.s)
                moves.append(self.go(move))
            self.state[w] = moves
            return
        far = flip(flip(self.chip, 1), 2)
        add_rows(self.own(w, far), [self.own(w, far), other.at[far]])
        cut = halves_of(other.shape[1:])
        near_x, near_y = flip(self.b, 2), flip(self.b, 4)
        top, low = self.own(w, far, pl.ds(0, cut)), self.own(w, far, pl.ds(cut, rows - cut))
        self.state[w] = [
            self.go(self.copies.remote(top, half_x, near_x, self.s)),
            self.go(self.copies.remote(low, half_y, near_y, self.s)),
        ]

    def stage_b(self, w):
        if self.chips != 4:
            return
        _, other, half_x, half_y, got_x, got_y = self.scratch[w][:6]
        rows = other.shape[1]
        cut = halves_of(other.shape[1:])
        top, low = pl.ds(0, cut), pl.ds(cut, rows - cut)
        mx, my = flip(self.chip, 1), flip(self.chip, 2)
        move_x, move_y = self.state[w]
        move_x.wait_recv()
        block = self.own(w, my, top)
        add_rows(block, [block, other.at[my, top], half_x])
        block = self.own(w, my, low)
        add_rows(block, [block, other.at[my, low]])
        block = self.own(w, my)
        next_y = self.go(self.copies.remote(block, got_y, flip(self.b, 4), self.s))
        move_y.wait_recv()
        block = self.own(w, mx, low)
        add_rows(block, [block, other.at[mx, low], half_y])
        block = self.own(w, mx, top)
        add_rows(block, [block, other.at[mx, top]])
        block = self.own(w, mx)
        next_x = self.go(self.copies.remote(block, got_x, flip(self.b, 2), self.s))
        self.state[w] = [next_x, next_y]

    def stage_c(self, w):
        _, other, _, _, got_x, got_y, done, landed = self.scratch[w]
        for move in self.state[w]:
            move.wait_recv()
        terms = [self.own(w, self.chip), other.at[self.chip]]
        if self.chips == 4:
            terms += [got_x, got_y]
        else:
            terms += [got_x.at[k] for k in range(1, self.chips)]
        if self.kinds[w] == "col":
            add_rows(self.outs[w], terms)
            return
        seq, send, recv = self.seq, self.copies.send, self.copies.recv
        hold = self.kinds[w] == "hold"
        if hold:
            done = self.outs[w]
        wide = done.shape[-1]
        far = self.kinds[w] == "row"
        to_b, me = (self.to_b, lax.rem(self.place, seq)) if far else (self.b, self.s)
        base = 0 if hold else self.copies.take(2 * seq)
        rows = terms[0].shape[0]
        step = 16 if rows % 16 == 0 else rows

        def body(i, carry):
            at = pl.ds(pl.multiple_of(i * step, step), step)
            total = terms[0][at, :].astype(F32)
            for term in terms[1:]:
                total = total + term[at, :].astype(F32)
            for t in range(seq):
                done[t, at, :] = total[:, t * wide : (t + 1) * wide].astype(BF16)
            return carry

        lax.fori_loop(0, rows // step, body, 0)
        if hold:
            return
        moves = []
        for t in range(seq):
            move = pltpu.make_async_remote_copy(
                src_ref=done.at[t],
                dst_ref=landed.at[me],
                send_sem=send.at[base + t],
                recv_sem=recv.at[base + me],
                device_id={"bucket": to_b, "seq": t},
                device_id_type=MESH,
            )
            keep = pltpu.make_async_copy(done.at[t], landed.at[me], send.at[base + seq + t])
            here = jnp.logical_and(to_b == self.b, self.s == t) if far else self.s == t

            @pl.when(jnp.logical_not(here))
            def _():
                move.start()

            @pl.when(here)
            def _():
                keep.start()

            moves.append((move, keep, here))
        self.last[w] = (base, moves)

    def stage_d(self, w):
        if self.kinds[w] in ("col", "hold"):
            return
        done, landed = self.scratch[w][6:]
        base, moves = self.last[w]
        out, seq, buckets = self.outs[w], self.seq, self.buckets
        for j in range(seq):
            d = self.b * seq + j
            from_b = slot(lax.rem(d, buckets), buckets)
            here = jnp.logical_and(from_b == self.b, lax.div(d, buckets) == self.s)
            if self.kinds[w] != "row":
                here = self.s == j

            @pl.when(jnp.logical_not(here))
            def _():
                pltpu.make_async_remote_copy(
                    src_ref=done.at[j],
                    dst_ref=landed.at[j],
                    send_sem=self.copies.send.at[base + j],
                    recv_sem=self.copies.recv.at[base + j],
                    device_id={"bucket": self.twin, "seq": self.s},
                    device_id_type=MESH,
                ).wait_recv()

        for move, keep, here in moves:

            @pl.when(jnp.logical_not(here))
            def _():
                move.wait_send()

            @pl.when(here)
            def _():
                keep.wait()

        for j in range(seq):
            add_rows(out.at[j], [landed.at[j]])

    def steps(self):
        count = len(self.kinds)
        for w in range(count + 2):
            if w < count:
                yield lambda w=w: self.stage_a(w)
            if 1 <= w <= count:
                yield lambda w=w: self.stage_b(w - 1)
            if w >= 2:
                yield lambda w=w: self.stage_c(w - 2)
        yield lambda: [self.stage_d(w) for w in range(count)]

    def end(self):
        for move in self.sent:
            move.wait_send()


def greet_all(b, s, buckets, seq):
    for k in range(1, buckets):
        greet(lax.rem(b + k, buckets), s)
    for k in range(1, seq):
        greet(b, lax.rem(s + k, seq))
    for j in range(seq):
        d = b * seq + j
        src_b, src_s = slot(lax.rem(d, buckets), buckets), lax.div(d, buckets)

        @pl.when(jnp.logical_not(jnp.logical_and(src_b == b, src_s == s)))
        def _():
            greet(src_b, src_s)

    to_b = lax.div(s * buckets + slot(b, buckets), seq)
    return buckets - 1 + seq - 1 + seq - jnp.where(to_b == b, 1, 0)


def sums_shapes(buckets, seq, shapes, kinds, near=False):
    chips = buckets // 2
    inputs, outs, scratch = [], [], []
    tiny = pltpu.VMEM((16, 128), BF16)
    for (rows, wide), kind in zip(shapes, kinds, strict=True):
        rows = rows // buckets
        inputs.append((chips, 2, rows, wide))
        cut = halves_of((rows, wide))
        scratch += [tiny if near else pltpu.VMEM((chips, rows, wide), BF16)]
        scratch += [pltpu.VMEM((chips, rows, wide), BF16)]
        if chips == 4:
            scratch += [pltpu.VMEM((cut, wide), BF16), pltpu.VMEM((rows - cut, wide), BF16)]
            scratch += [pltpu.VMEM((rows, wide), BF16)] * 2
        else:
            scratch += [tiny, tiny, pltpu.VMEM((chips, rows, wide), BF16), tiny]
        split = (seq, rows, wide // seq)
        kept = BF16 if kind == "hold" else F32
        outs.append(jax.ShapeDtypeStruct((rows, wide) if kind == "col" else split, kept))
        scratch += [tiny if kind in ("col", "hold") else pltpu.VMEM(split, BF16)] * 2
    n_sems = 32 + 2 * buckets + len(shapes) * (8 + 3 * seq + buckets)
    return inputs, outs, scratch, n_sems


def place_grads(buckets, grads, kinds, shapes):
    inputs = []
    for grad, kind, shape in zip(grads, kinds, shapes, strict=True):
        grad = grad.astype(BF16)
        if kind == "row" and buckets == 8:
            grad = grad.reshape((2, 2, 2) + shape[2:]).transpose(0, 2, 1, 3, 4)
        inputs.append(grad.reshape(shape))
    return inputs


def spread(buckets):
    if buckets != 8:
        return tuple(range(buckets))
    return tuple(4 * (p // 4) + 2 * (p % 2) + p // 2 % 2 for p in range(buckets))


def scatter_kernel(buckets, seq, kinds, *refs):
    count = len(kinds)
    vec, grads = refs[0], refs[1 : 1 + count]
    vec_all, outs = refs[1 + count], refs[2 + count : 2 + 2 * count]
    at = 2 + 2 * count
    vec_seq, vec_sum, send, recv = refs[at : at + 4]
    b, s = lax.axis_index("bucket"), lax.axis_index("seq")
    copies = Copies(send, recv)
    sums = GradSums(copies, b, s, buckets, seq, kinds, grads, outs, refs[at + 4 :])
    peers = greet_all(b, s, buckets, seq)
    pl.semaphore_wait(pltpu.get_barrier_semaphore(), peers)
    vec_moves = []
    for k in range(1, seq):
        vec_moves.append(sums.go(copies.remote(vec, vec_seq.at[k], b, lax.rem(s + k, seq))))
    for w in range(min(2, count)):
        sums.begin(w)
    for move in vec_moves:
        move.wait_recv()
    add_rows(vec_sum, [vec] + [vec_seq.at[k] for k in range(1, seq)])
    vec_next = []
    for k in range(1, buckets):
        peer = lax.rem(b + k, buckets)
        vec_next.append(sums.go(copies.remote(vec_sum, vec_all.at[b], peer, s)))
    vec_own = copies.local(vec_sum, vec_all.at[b])
    vec_own.start()
    for step in sums.steps():
        step()
    for move in vec_next:
        move.wait_recv()
    vec_own.wait()
    sums.end()


def scatter_all(buckets, seq, vec, grads, kinds, collective_id=1):
    any_spec = pl.BlockSpec(memory_space=pl.ANY)
    vmem = pl.BlockSpec(memory_space=pltpu.VMEM)
    shapes, outs, scratch, n_sems = sums_shapes(buckets, seq, [g.shape for g in grads], kinds)
    inputs = place_grads(buckets, grads, kinds, shapes)
    results = pl.pallas_call(
        functools.partial(scatter_kernel, buckets, seq, tuple(kinds)),
        out_shape=[jax.ShapeDtypeStruct((buckets,) + vec.shape, F32), *outs],
        in_specs=[vmem] + [any_spec] * len(grads),
        out_specs=[any_spec] + [vmem] * len(grads),
        scratch_shapes=[
            pltpu.VMEM((seq,) + vec.shape, F32),
            pltpu.VMEM(vec.shape, F32),
            pltpu.SemaphoreType.DMA((n_sems,)),
            pltpu.SemaphoreType.DMA((n_sems,)),
            *scratch,
        ],
        compiler_params=pltpu.CompilerParams(
            collective_id=collective_id, has_side_effects=True, vmem_limit_bytes=60 * 2**20
        ),
    )(vec, *inputs)
    return results[0], [out.reshape(-1, out.shape[-1]) for out in results[1:]]


def attention(queries, keys, values, live, scale):
    scores = jnp.einsum("qhd,khd->hqk", queries, keys, preferred_element_type=F32) * scale
    scores = jnp.where(live[None, None, :], scores, -1e30)
    probs = jax.nn.softmax(scores, axis=-1)
    mixed = jnp.einsum("hqk,khd->qhd", probs.astype(BF16), values, preferred_element_type=F32)
    return probs, mixed


def attention_back(probs, queries, keys, values, d_out, scale):
    d_probs = jnp.einsum("qhd,khd->hqk", d_out, values, preferred_element_type=F32)
    d_scores = probs * (d_probs - jnp.sum(probs * d_probs, axis=-1, keepdims=True))
    d_low = d_scores.astype(BF16)
    d_query = jnp.einsum("hqk,khd->qhd", d_low, keys, preferred_element_type=F32) * scale
    d_key = jnp.einsum("hqk,qhd->khd", d_low, queries, preferred_element_type=F32) * scale
    d_value = jnp.einsum("hqk,qhd->khd", probs.astype(BF16), d_out, preferred_element_type=F32)
    return d_query, d_key, d_value


def on_device_general(
    tokens,
    captions,
    cotangent,
    counts,
    cap_lens,
    steps_t,
    w_query,
    w_key,
    w_value,
    w_out,
    w_cap_key,
    w_cap_value,
    w_gate,
    w_up,
    w_down,
    w_mod,
    gains,
    cross_gate,
):
    buckets, seq = lax.axis_size("bucket"), lax.axis_size("seq")
    b, s = lax.axis_index("bucket"), lax.axis_index("seq")
    place = b * seq + s
    rows, width = tokens.shape
    span = rows * seq
    share = width // seq
    heads = share // HEAD_DIM
    scale = HEAD_DIM ** (-0.5)
    live_rows, cap_len = pick_entry(counts, b), pick_entry(cap_lens, b)
    token_total = jnp.sum(counts).astype(F32)

    cond_size = w_mod.shape[0] * buckets * seq
    cond = jax.nn.silu(time_embed(steps_t, cond_size)).astype(BF16)
    cond_part = lax.dynamic_slice_in_dim(cond, place * w_mod.shape[0], w_mod.shape[0], 1)
    slim = gains.shape[1]
    small = jnp.concatenate([gains, cross_gate[None]], axis=0).astype(F32)
    small = jnp.pad(small, ((0, 0), (0, 128 - slim)))
    tok_all, cap_all, small_all, mod, weights = gather_all(
        buckets,
        seq,
        tokens,
        captions,
        small,
        cond_part,
        w_mod,
        [w_query, w_key, w_value, w_cap_key, w_cap_value, w_out, w_gate, w_up, w_down],
        ["col", "col", "col", "col", "col", "row", "col", "col", "row"],
    )
    wq, wk, wv, wck, wcv, wo, wg, wu, wd = weights
    caps = cap_all.reshape(-1, captions.shape[1])
    small_rows = small_all[..., :slim].transpose(2, 0, 1, 3).reshape(8, width)
    gain_f = small_rows[:7]
    own_cols = lax.dynamic_slice_in_dim(small_rows, s * share, share, 1)
    gate_cross = jnp.tanh(own_cols[7])
    scale_attn, gate_attn, scale_ffn, gate_ffn = mod.reshape(4, width)

    hidden = pre_attn(tok_all.astype(F32), gain_f[0], scale_attn).astype(BF16).reshape(span, width)
    query_proj, key_proj = bf_dot(hidden, wq), bf_dot(hidden, wk)
    value_low = bf_dot(hidden, wv).astype(BF16)
    (query_f, key_f), norm_back = jax.vjp(qk_norm, query_proj, key_proj, own_cols[4], own_cols[5])
    cap_key_f, cap_back = jax.vjp(cap_norm, bf_dot(caps, wck), own_cols[6])

    def by_head(values):
        return values.astype(BF16).reshape(values.shape[0], heads, HEAD_DIM)

    query, key, value = by_head(query_f), by_head(key_f), by_head(value_low)
    cap_key, cap_value = by_head(cap_key_f), by_head(bf_dot(caps, wcv))
    probs, self_out = attention(query, key, value, jnp.arange(span) < live_rows, scale)
    cap_live = jnp.arange(caps.shape[0]) < cap_len
    cap_probs, cross_out = attention(query, cap_key, cap_value, cap_live, scale)
    self_out, cross_out = self_out.reshape(span, share), cross_out.reshape(span, share)
    mixed_low = (self_out + gate_cross * cross_out).astype(BF16)
    attn_out = line_scatter(seq, bf_dot(mixed_low, wo), 2)

    tokens_f = tokens.astype(F32)
    (resid_one, ffn_pre), middle_back = jax.vjp(
        middle, tokens_f, attn_out, gain_f[1], gate_attn, gain_f[2], scale_ffn
    )
    ffn_all = line_gather(seq, ffn_pre.astype(BF16), 3)
    act_pre, act_back = jax.vjp(activate, bf_dot(ffn_all, wg), bf_dot(ffn_all, wu))
    act_low = act_pre.astype(BF16)
    ffn_out = line_scatter(seq, bf_dot(act_low, wd), 4)
    out_f, finish_back = jax.vjp(finish, resid_one, ffn_out, gain_f[3], gate_ffn)
    block_out = out_f.astype(BF16)

    row_live = (s * rows + jnp.arange(rows) < live_rows).astype(F32)
    weighted = cotangent.astype(F32) * row_live[:, None] * (buckets * span / token_total)
    d_resid, d_ffn_out, d_gain_last, d_gate_ffn = finish_back(weighted)
    d_ffn_all = line_gather(seq, d_ffn_out.astype(BF16), 5)
    d_gate, d_up = act_back(right_dot(d_ffn_all, wd))
    d_gate, d_up = d_gate.astype(BF16), d_up.astype(BF16)
    d_hidden_ffn = line_scatter(seq, right_dot(d_gate, wg) + right_dot(d_up, wu), 6)
    d_tokens_one, d_attn_out, d_gain_post, d_gate_attn, d_gain_ffn, d_scale_ffn = middle_back(
        (d_resid, d_hidden_ffn)
    )
    d_attn_all = line_gather(seq, d_attn_out.astype(BF16), 7)
    d_mixed_low = right_dot(d_attn_all, wo).astype(BF16)
    d_mixed = d_mixed_low.astype(F32)
    d_cross_low = (gate_cross * d_mixed).astype(BF16)
    grad_cross = jnp.sum(d_mixed * cross_out, axis=0) * (1.0 - gate_cross * gate_cross)

    d_query_cross, d_cap_key, d_cap_value = attention_back(
        cap_probs, query, cap_key, cap_value, by_head(d_cross_low), scale
    )
    d_query, d_key, d_value = attention_back(probs, query, key, value, by_head(d_mixed_low), scale)
    d_cap_key, d_gain_cap = cap_back(d_cap_key.reshape(-1, share))
    d_query, d_key, d_gain_query, d_gain_key = norm_back(
        ((d_query + d_query_cross).reshape(span, share), d_key.reshape(span, share))
    )
    d_query, d_key, d_cap_key = d_query.astype(BF16), d_key.astype(BF16), d_cap_key.astype(BF16)
    d_value = d_value.reshape(span, share).astype(BF16)
    d_cap_value = d_cap_value.reshape(-1, share).astype(BF16)
    d_hidden = line_scatter(
        seq, right_dot(d_query, wq) + right_dot(d_key, wk) + right_dot(d_value, wv), 8
    )
    _, pre_back = jax.vjp(pre_attn, tokens_f, gain_f[0], scale_attn)
    d_tokens_two, d_gain_pre, d_scale_attn = pre_back(d_hidden)
    tokens_grad = d_tokens_one + d_tokens_two

    own_sums = jnp.stack([d_gain_query, d_gain_key, d_gain_cap, grad_cross])
    own_wide = lax.dynamic_update_slice(jnp.zeros((4, width), F32), own_sums, (0, s * share))
    vec = jnp.concatenate(
        [
            jnp.stack([d_scale_attn, d_gate_attn, d_scale_ffn, d_gate_ffn]),
            jnp.stack([d_gain_pre, d_gain_post, d_gain_ffn, d_gain_last]),
            own_wide,
            jnp.zeros((4, width), F32),
        ]
    )
    grads = [
        left_dot(ffn_all, d_gate),
        left_dot(ffn_all, d_up),
        left_dot(act_low, d_ffn_all),
        left_dot(mixed_low, d_attn_all),
        left_dot(caps, d_cap_key),
        left_dot(caps, d_cap_value),
        left_dot(hidden, d_query),
        left_dot(hidden, d_key),
        left_dot(hidden, d_value),
    ]
    kinds = ["col", "col", "row", "row", "col", "col", "col", "col", "col"]
    vec_all, sums = scatter_all(buckets, seq, vec, grads, kinds)
    s_gate, s_up, s_down, s_out, s_cap_key, s_cap_value, s_query, s_key, s_value = sums

    quarter = 4 * width // seq
    mod_rows = vec_all[:, :4].reshape(buckets, -1, quarter)
    mod_rows = lax.dynamic_slice_in_dim(mod_rows, s, 1, 1)[:, 0]
    cond_size = cond.shape[1] // buckets
    cond_cols = lax.dynamic_slice_in_dim(cond, b * cond_size, cond_size, 1).astype(F32)
    s_mod = jnp.sum(cond_cols[:, :, None] * mod_rows[:, None, :], axis=0)
    tail = lax.dynamic_slice(vec_all, (0, 4, place * slim), (buckets, 8, slim))
    tail = jnp.sum(tail, axis=0)
    return (
        block_out,
        tokens_grad,
        s_query,
        s_key,
        s_value,
        s_out,
        s_cap_key,
        s_cap_value,
        s_gate,
        s_up,
        s_down,
        s_mod,
        tail[:7],
        tail[7],
    )


def low_half(shape):
    return lax.broadcasted_iota(jnp.int32, shape, len(shape) - 1) < HEAD_DIM


def pair_sums(values):
    row = lax.broadcasted_iota(jnp.int32, (128, 128), 0) < HEAD_DIM
    same = (row == low_half((128, 128))).astype(BF16)
    high = values.astype(BF16)
    rest = (values - high.astype(F32)).astype(BF16)
    return bf_dot(high, same) + bf_dot(rest, same)


def pair_scale(values, eps):
    return lax.rsqrt(pair_sums(values * values) * (1.0 / HEAD_DIM) + eps)


def fill_rows(out, live, first, yes, no):
    row = lax.broadcasted_iota(jnp.int32, out.shape, 0) + first
    out[...] = jnp.where(row < live, yes, no).astype(out.dtype)


FORWARD_ORDER = (8, "tok", 0, "tok", 1, "tok", 2, "tok", 6, 7, "cap", 3, "cap", 4, "cap", 5, "cap")
MOVED = ()
AHEAD = 4
LAG = 1
WINDOW = 2


class Gather:
    def __init__(self, copies, b, s, buckets, seq, kinds, shards, fulls, keep_at=None):
        self.copies, self.b, self.s, self.buckets, self.seq = copies, b, s, buckets, seq
        self.kinds, self.shards, self.fulls, self.keep_at = kinds, shards, fulls, keep_at
        place = b * seq + s
        self.to_slot, self.to_s = lax.rem(place, buckets), lax.div(place, buckets)
        self.to_b = slot(self.to_slot, buckets)
        back = s * buckets + slot(b, buckets)
        self.from_b, self.from_s = lax.div(back, seq), lax.rem(back, seq)
        self.stays = jnp.logical_and(self.to_b == b, self.to_s == s)
        self.twin, self.near_x, self.near_y = flip(b, 1), flip(b, 2), flip(b, 4)
        self.far = flip(self.near_x, 4)
        self.first, self.second, self.kept, self.sent = {}, {}, [], []

    def greet_source(self):
        @pl.when(jnp.logical_not(self.stays))
        def _():
            greet(self.from_b, self.from_s)

        return jnp.where(self.stays, 0, 1)

    def go(self, src, dst, b):
        copy = self.copies.remote(src, dst, b, self.s)
        copy.start()
        self.sent.append(copy)
        return copy

    def depart(self, at):
        copies, b, s, seq = self.copies, self.b, self.s, self.seq
        shard, full = self.shards[at], self.fulls[at]
        if self.kinds[at] == "stay":
            keep = copies.local(shard, full.at[b])
            keep.start()
            self.first[at] = ((), keep)
            return
        if self.kinds[at] == "row":
            move = copies.remote(shard, full.at[self.to_slot], self.to_b, self.to_s)
            keep = copies.local(shard, full.at[slot(b, self.buckets)])

            @pl.when(jnp.logical_not(self.stays))
            def _():
                move.start()

            @pl.when(self.stays)
            def _():
                keep.start()

            self.first[at] = (move, keep)
            return
        wide = full.shape[-1]

        def columns(peer):
            if self.kinds[at] == "cut":
                return shard.at[peer]
            return shard.at[:, pl.ds(pl.multiple_of(peer * wide, 128), wide)]

        moves = []
        for k in range(1, seq):
            peer = lax.rem(s + k, seq)
            move = copies.remote(columns(peer), full.at[b, s], b, peer)
            move.start()
            moves.append(move)
        keep = copies.local(columns(s), full.at[b, s])
        keep.start()
        self.first[at] = (moves, keep)

    def arrived(self, at):
        moves, keep = self.first[at]
        if self.kinds[at] == "row":

            @pl.when(jnp.logical_not(self.stays))
            def _():
                moves.wait()

            @pl.when(self.stays)
            def _():
                keep.wait()

            return
        for move in moves:
            move.wait()
        keep.wait()

    def index(self, at, device):
        return slot(device, self.buckets) if self.kinds[at] == "row" else device

    def stage_a(self, at):
        block = self.fulls[at].at[self.index(at, self.b)]
        self.second[at] = {
            "x": self.go(block, block, self.near_x),
            "y": self.go(block, block, self.near_y),
            "twin": [self.go(block, block, self.twin)],
        }

    def stage_b(self, at):
        full, now = self.fulls[at], self.second[at]
        cut = halves_of(full.shape[1:])
        now["x"].wait_recv()
        block = full.at[self.index(at, self.near_x), pl.ds(0, cut)]
        now["dy"] = self.go(block, block, self.near_y)
        block = full.at[self.index(at, self.near_x)]
        now["twin"].append(self.go(block, block, self.twin))
        now["y"].wait_recv()
        block = full.at[self.index(at, self.near_y), pl.ds(cut, full.shape[1] - cut)]
        now["dx"] = self.go(block, block, self.near_x)
        block = full.at[self.index(at, self.near_y)]
        now["twin"].append(self.go(block, block, self.twin))

    def stage_c(self, at):
        full, now = self.fulls[at], self.second[at]
        now["dy"].wait_recv()
        now["dx"].wait_recv()
        block = full.at[self.index(at, self.far)]
        now["twin"].append(self.go(block, block, self.twin))

    def stage_d(self, at):
        for move in self.second[at]["twin"]:
            move.wait_recv()
        if self.keep_at is not None:
            copy = self.copies.local(self.fulls[at], self.keep_at[at])
            copy.start()
            self.kept.append(copy)

    def end(self):
        for copy in self.kept:
            copy.wait()
        for move in self.sent:
            move.wait_send()


def forward_kernel(buckets, seq, kinds, slim, *refs):
    count = len(kinds)
    tokens, captions, small, cond, w_mod, counts, cap_lens = refs[:7]
    shards = refs[7 : 7 + count]
    refs = refs[7 + count :]
    cap_all = refs[0]
    far_fulls = refs[1 : 1 + count]
    refs = refs[1 + count :]
    (
        gain_rows,
        mod_rows,
        hidden,
        query_raw,
        key_raw,
        cap_raw,
        query,
        key,
        value,
        cap_key,
        cap_value,
        cross_out,
        mixed,
    ) = refs[:13]
    refs = refs[13:]
    part, got_bucket, got_seq, mod_sum, small_all, tok_all, cap_near, own_out = refs[:8]
    fulls = refs[8 : 8 + count]
    key_mask, cap_mask, send, recv = refs[8 + count : 12 + count]
    strips = refs[12 + count :]
    b, s = lax.axis_index("bucket"), lax.axis_index("seq")
    copies = Copies(send, recv)
    shards = list(shards)
    cuts = [at for at in range(count) if kinds[at] == "cut"]
    for at, strip in zip(cuts, strips, strict=True):
        for t in range(seq):
            for j in range(strip.shape[2] // 128):
                cols = slice((j * seq + t) * 128, (j * seq + t + 1) * 128)
                strip[t, :, j * 128 : (j + 1) * 128] = shards[at][:, cols]
        shards[at] = strip
    weights = Gather(copies, b, s, buckets, seq, kinds, shards, fulls, far_fulls)
    for k in range(1, buckets):
        greet(lax.rem(b + k, buckets), s)
    for k in range(1, seq):
        greet(b, lax.rem(s + k, seq))
    peers = buckets - 1 + seq - 1 + weights.greet_source()

    fill_rows(key_mask, counts[b], 0, 1.0, 0.0)
    fill_rows(cap_mask, cap_lens[b], 0, 1.0, 0.0)
    lanes = part.shape[2]
    for j in range(part.shape[1]):
        part[:, j, :] = bf_dot(cond[...], w_mod[:, j * lanes : (j + 1) * lanes])

    pl.semaphore_wait(pltpu.get_barrier_semaphore(), peers)

    sent = []

    def go(copy):
        copy.start()
        sent.append(copy)
        return copy

    mod_moves = []
    for k in range(1, buckets):
        peer = lax.rem(b + k, buckets)
        mod_moves.append(go(copies.remote(part.at[peer], got_bucket.at[k], peer, s)))
    small_moves = []
    for k in range(1, seq):
        peer = lax.rem(s + k, seq)
        small_moves.append(go(copies.remote(small, small_all.at[b, s], b, peer)))
    small_own = copies.local(small, small_all.at[b, s])
    small_own.start()

    tok = Relay(copies, tokens, tok_all, b, s, seq)
    cap = Relay(copies, captions, cap_near, b, s, seq)
    items, step = [], {"tok": 0, "cap": 0}
    for what in FORWARD_ORDER:
        if isinstance(what, str):
            items.append((tok if what == "tok" else cap, step[what]))
            step[what] += 1
        else:
            items.append((None, what))

    def fetch(at):
        whole = fulls[at][...]
        return whole.reshape(-1, whole.shape[-1])


    rows = seq * tok_all.shape[1]
    width = tok_all.shape[2]
    cap_rows = seq * cap_near.shape[1]
    share = query.shape[1]
    pairs = share // 128
    block_rows = tok_all.shape[1]

    def small_sums():
        for move in small_next:
            move.wait_recv()
        strips = [None] * (width // 128)
        lane = lax.broadcasted_iota(jnp.int32, (8, 128), 1)
        for d in range(buckets * seq):
            at, shift = divmod(d * slim, 128)
            piece = small_all[d // seq, d % seq]
            turned = pltpu.roll(piece, shift, 1) if shift else piece
            for index, keep in ((at, lane >= shift), (at + 1, lane < shift)):
                if index == at + 1 and shift + slim <= 128:
                    continue
                add = jnp.where(keep, turned, 0.0)
                strips[index] = add if strips[index] is None else strips[index] + add
        for at, strip in enumerate(strips):
            gain_rows[:, at * 128 : (at + 1) * 128] = strip
        total = mod_sum[...]
        for k, move in enumerate(mod_next, 1):
            move.wait_recv()
            total = total + got_seq[k]
        for j in range(8):
            at, lane_at = divmod(j * lanes, width)
            mod_rows[at : at + 1, lane_at : lane_at + lanes] = total[j : j + 1, :]
        mod_rows[4:8, :] = jnp.zeros((4, width), F32)

    def make_hidden():
        factor = gain_rows[0:1, :] * (1.0 + mod_rows[0:1, :])
        for t in range(seq):

            def body(i, carry):
                at = pl.ds(pl.multiple_of(i * 32, 32), 32)
                x = tok_all[t, at, :].astype(F32)
                x = x * lax.rsqrt(jnp.mean(x * x, axis=-1, keepdims=True) + 1e-05) * factor
                to = pl.ds(pl.multiple_of(t * block_rows + i * 32, 32), 32)
                hidden[to, :] = x.astype(BF16)
                return carry

            lax.fori_loop(0, block_rows // 32, body, 0)

    def gain_of(row, pair):
        at = pl.multiple_of(s * share + pair * 128, 128)
        return gain_rows[row : row + 1, pl.ds(at, 128)]

    def make_normed(raw, out, row, scale):
        def body(i, carry):
            at = pl.ds(pl.multiple_of(i * 64, 64), 64)
            for pair in range(pairs):
                lane = slice(pair * 128, (pair + 1) * 128)
                x = raw[at, lane]
                x = x * pair_scale(x, 1e-06) * gain_of(row, pair)
                out[at, lane] = x.astype(BF16)
            return carry

        del scale
        lax.fori_loop(0, raw.shape[0] // 64, body, 0)

    def make_query():
        query_raw[...] = bf_dot(hidden[...], fetch(0))
        make_normed(query_raw, query, 4, None)

    def make_key():
        key_raw[...] = bf_dot(hidden[...], fetch(1))
        make_normed(key_raw, key, 5, None)

    def make_value():
        value[...] = bf_dot(hidden[...], fetch(2)).astype(BF16)

    def cap_near_rows():
        whole = cap_near[...]
        return whole.reshape(cap_rows, whole.shape[-1])

    def make_cap_key():
        cap_raw[...] = bf_dot(cap_near_rows(), fetch(3))
        make_normed(cap_raw, cap_key, 6, None)

    def make_cap_value():
        cap_value[...] = bf_dot(cap_near_rows(), fetch(4)).astype(BF16)

    def attend(pair, k_ref, v_ref, mask, store):
        lane = slice(pair * 128, (pair + 1) * 128)
        low = low_half((128, 128))
        keys = k_ref[:, lane]
        values = jnp.concatenate([v_ref[:, lane] * mask[...], mask[...]], axis=1)

        def body(i, carry):
            at = pl.ds(pl.multiple_of(i * 128, 128), 128)
            q = query[at, lane] * jnp.asarray(HEAD_DIM**-0.5, BF16)
            outs = []
            for half in (jnp.where(low, q, jnp.zeros_like(q)), jnp.where(low, jnp.zeros_like(q), q)):
                weights = jnp.exp(right_dot(half, keys))
                outs.append(bf_dot(weights.astype(BF16), values))
            out = jnp.where(low, outs[0][:, :128], outs[1][:, :128])
            store(at, lane, out / jnp.where(low, outs[0][:, 128:], outs[1][:, 128:]))
            return carry

        lax.fori_loop(0, rows // 128, body, 0)

    def make_own(pair):
        def store(at, lane, out):
            own_out[at, lane] = out

        attend(pair, key, value, key_mask, store)

    def make_mixed(pair):
        gate = jnp.tanh(gain_of(7, pair))

        def store(at, lane, out):
            cross_out[at, lane] = out
            mixed[at, lane] = (own_out[at, lane] + gate * out).astype(BF16)

        attend(pair, cap_key, cap_value, cap_mask, store)

    work = [
        (lambda: (small_sums(), make_hidden()), "h", {"tok"}),
        (make_query, "q", {"h", 0}),
        (make_key, "k", {"h", 1}),
        (make_value, "v", {"h", 2}),
        (make_cap_key, "ck", {"cap", 3}),
        (make_cap_value, "cv", {"cap", 4}),
        *((functools.partial(make_own, p), ("own", p), {"q", "k", "v"}) for p in range(pairs)),
        *(
            (functools.partial(make_mixed, p), ("all", p), {"q", "ck", "cv", ("own", p)})
            for p in range(pairs)
        ),
    ]

    def do_work():
        for at, (piece, name, needs) in enumerate(work):
            if needs <= done:
                piece()
                done.add(name)
                del work[at]
                return True
        return False


    done = set()

    def begin(i):
        relay, j = items[i]
        if relay is None:
            weights.depart(j)
        else:
            relay.start(j)
            if j == seq - 1:
                done.add("tok" if relay is tok else "cap")

    def complete(at):
        weights.stage_c(at)
        weights.stage_d(at)
        done.add(at)

    window = WINDOW
    for i in range(window):
        begin(i)
    for move in small_moves:
        move.wait_recv()
    small_own.wait()
    small_next = []
    for k in range(1, buckets):
        peer = lax.rem(b + k, buckets)
        small_next.append(go(copies.remote(small_all.at[b], small_all.at[b], peer, s)))
    total = part[b]
    for k, move in enumerate(mod_moves, 1):
        move.wait_recv()
        total = total + got_bucket[k]
    mod_sum[...] = total
    mod_next = []
    for k in range(1, seq):
        peer = lax.rem(s + k, seq)
        mod_next.append(go(copies.remote(mod_sum, got_seq.at[k], b, peer)))

    cap_out = copies.local(cap_near, cap_all)
    order = []
    for i, (relay, j) in enumerate(items):
        if relay is None:
            weights.arrived(j)
        elif j <= seq - 2:
            relay.sent(j)
        if i + window < len(items):
            begin(i + window)
        if relay is None:
            order.append(j)
            weights.stage_a(j)
            if len(order) > LAG:
                weights.stage_b(order[-1 - LAG])
            if len(order) > LAG + 1:
                complete(order[-2 - LAG])
        do_work()
    cap_out.start()
    for at in range(LAG):
        weights.stage_b(order[len(order) - LAG + at])
        complete(order[len(order) - LAG - 1 + at])
        do_work()
    complete(order[-1])
    while do_work():
        pass
    cap_out.wait()
    weights.end()
    for move in sent:
        move.wait_send()


def forward_all(buckets, seq, tokens, captions, small, slim, cond, w_mod, masks, shards, kinds):
    any_spec = pl.BlockSpec(memory_space=pl.ANY)
    vmem = pl.BlockSpec(memory_space=pltpu.VMEM)
    smem = pl.BlockSpec(memory_space=pltpu.SMEM)
    fulls = []
    for shard, kind in zip(shards, kinds, strict=True):
        rows, wide = shard.shape
        shape = (buckets, rows, wide) if kind in ("row", "stay") else (buckets, seq, rows, wide // seq)
        fulls.append(jax.ShapeDtypeStruct(shape, BF16))
    near = [pltpu.VMEM(full.shape, BF16) for full in fulls]
    width = tokens.shape[1]
    mod_lanes = w_mod.shape[1] // 8
    span, cap_span, share = seq * tokens.shape[0], seq * captions.shape[0], width // seq
    f32_rows = jax.ShapeDtypeStruct((span, share), F32)
    low_rows = jax.ShapeDtypeStruct((span, share), BF16)
    cap_low = jax.ShapeDtypeStruct((cap_span, share), BF16)
    inner = [
        jax.ShapeDtypeStruct((8, width), F32),
        jax.ShapeDtypeStruct((8, width), F32),
        jax.ShapeDtypeStruct((span, width), BF16),
        f32_rows,
        f32_rows,
        jax.ShapeDtypeStruct((cap_span, share), F32),
        low_rows,
        low_rows,
        low_rows,
        cap_low,
        cap_low,
        f32_rows,
        low_rows,
    ]
    n_sems = 64 + 16 * buckets + len(shards) * (seq + 2 * buckets)
    outs = pl.pallas_call(
        functools.partial(forward_kernel, buckets, seq, tuple(kinds), slim),
        out_shape=[jax.ShapeDtypeStruct((seq,) + captions.shape, BF16), *fulls, *inner],
        in_specs=[any_spec, any_spec, any_spec, vmem, vmem, smem, smem]
        + [vmem if kind == "cut" else any_spec for kind in kinds],
        out_specs=[any_spec] * (1 + len(shards)) + [vmem] * len(inner),
        scratch_shapes=[
            pltpu.VMEM((buckets, 8, mod_lanes), F32),
            pltpu.VMEM((buckets, 8, mod_lanes), F32),
            pltpu.VMEM((seq, 8, mod_lanes), F32),
            pltpu.VMEM((8, mod_lanes), F32),
            pltpu.VMEM((buckets, seq) + small.shape, F32),
            pltpu.VMEM((seq,) + tokens.shape, BF16),
            pltpu.VMEM((seq,) + captions.shape, BF16),
            pltpu.VMEM((span, share), F32),
            *near,
            pltpu.VMEM((span, 128), BF16),
            pltpu.VMEM((cap_span, 128), BF16),
            pltpu.SemaphoreType.DMA((n_sems,)),
            pltpu.SemaphoreType.DMA((n_sems,)),
            *(
                pltpu.VMEM((seq,) + full.shape[2:], BF16)
                for full, kind in zip(fulls, kinds, strict=True)
                if kind == "cut"
            ),
        ],
        compiler_params=pltpu.CompilerParams(
            collective_id=9, has_side_effects=True, vmem_limit_bytes=62 * 2**20
        ),
    )(tokens, captions, small, cond, w_mod, *masks, *shards)
    at = 1 + len(shards)
    return outs[0], outs[1:at], outs[at:]


def middle_kernel(buckets, seq, chunks, kinds, *refs):
    mixed, w_out, tokens, cotangent, counts, gain_rows, mod_rows = refs[:7]
    far_weights, refs = refs[7:10], refs[10:]
    block_out, d_tokens, d_attn, row_sums = refs[:4]
    outs, refs = refs[4:7], refs[7:]
    w_gate, w_up, w_down, ffn_all, d_ffn, act, d_gate, d_up = refs[:8]
    gate_keep, up_keep, attn_keep, resid_keep, got, parts, from_left, from_right = refs[8:16]
    row_scale, send, recv = refs[16:19]
    grads, refs = refs[19:22], refs[22:]
    b, s = lax.axis_index("bucket"), lax.axis_index("seq")
    copies = Copies(send, recv)
    sums = GradSums(copies, b, s, buckets, seq, kinds, grads, outs, refs, near=True)
    shards = (w_gate, w_up, w_down)
    weights = Gather(copies, b, s, buckets, seq, ("cut", "cut", "stay"), far_weights, shards)
    peers = greet_all(b, s, buckets, seq) + weights.greet_source()
    pl.semaphore_wait(pltpu.get_barrier_semaphore(), peers)
    loads = [copies.local(far_weights[w], shards[w]) for w in range(3) if w not in MOVED]
    for load in loads:
        load.start()
    if MOVED:
        weights.depart(MOVED[0])

    rows, width = tokens.shape
    live = sum(counts[k] for k in range(buckets))
    factor = buckets * seq * rows / jnp.full((rows, 128), live, jnp.int32).astype(F32)
    row = lax.broadcasted_iota(jnp.int32, (rows, 128), 0) + s * rows
    row_scale[...] = jnp.where(row < counts[b], factor, 0.0)
    thin = rows // chunks
    tall = seq * thin
    hidden = act.shape[-1]
    wide = 512
    gate_post = jnp.tanh(mod_rows[1:2, :]) * gain_rows[1:2, :]
    gain_ffn = gain_rows[2:3, :] * (1.0 + mod_rows[2:3, :])
    gate_last = jnp.tanh(mod_rows[3:4, :]) * gain_rows[3:4, :]
    row_sums[...] = jnp.zeros_like(row_sums)

    def of(c):
        return pl.ds(c * thin, thin)

    def chunk_of(ref, c, cols=slice(None)):
        whole = ref[:, of(c), cols]
        return whole.reshape(tall, whole.shape[-1])

    def mean(values):
        return jnp.mean(values, axis=-1, keepdims=True)

    def over_rows(c, body):
        step = 16

        def one(i, carry):
            return body(pl.ds(pl.multiple_of(c * thin + i * step, step), step), carry)

        return lax.fori_loop(0, thin // step, one, jnp.zeros((1, width), F32), unroll=4)

    def weighted(at):
        return cotangent[at, :].astype(F32) * row_scale[at, 0:1]

    def after_attn(c):
        def body(at, carry):
            out = got[at, :]
            attn_keep[at, :] = out
            resid = out * lax.rsqrt(mean(out * out) + 1e-05) * gate_post
            resid = tokens[at, :].astype(F32) + resid
            resid_keep[at, :] = resid
            normed = resid * lax.rsqrt(mean(resid * resid) + 1e-05)
            ffn_all[s, at, :] = (normed * gain_ffn).astype(BF16)
            return carry

        over_rows(c, body)

    def after_ffn(c):
        def body(at, total):
            out, resid, grad = got[at, :], resid_keep[at, :], weighted(at)
            size = lax.rsqrt(mean(out * out) + 1e-05)
            normed = out * size
            block_out[at, :] = (resid + gate_last * normed).astype(BF16)
            inner = grad * gate_last
            d_ffn[s, at, :] = (size * (inner - normed * mean(inner * normed))).astype(BF16)
            return total + jnp.sum(grad * normed, axis=0, keepdims=True)

        row_sums[2:3, :] += over_rows(c, body)

    def after_ffn_back(c):
        def body(at, totals):
            first, second = totals
            d_pre, resid, out = got[at, :], resid_keep[at, :], attn_keep[at, :]
            size = lax.rsqrt(mean(resid * resid) + 1e-05)
            normed, inner = resid * size, d_pre * gain_ffn
            second = second + jnp.sum(d_pre * normed, axis=0, keepdims=True)
            grad = weighted(at) + size * (inner - normed * mean(inner * normed))
            d_tokens[at, :] = grad
            size = lax.rsqrt(mean(out * out) + 1e-05)
            normed, inner = out * size, grad * gate_post
            first = first + jnp.sum(grad * normed, axis=0, keepdims=True)
            d_attn[s, at, :] = (size * (inner - normed * mean(inner * normed))).astype(BF16)
            return first, second

        step, zero = 16, jnp.zeros((1, width), F32)

        def one(i, carry):
            return body(pl.ds(pl.multiple_of(c * thin + i * step, step), step), carry)

        first, second = lax.fori_loop(0, thin // step, one, (zero, zero), unroll=4)
        row_sums[0:1, :] += first
        row_sums[1:2, :] += second

    def flat(values):
        return values.reshape(-1, values.shape[-1])

    def put_parts(c, cols, total):
        parts[c, :, :, cols] = total.astype(BF16).reshape(seq, thin, total.shape[-1])

    def attn_product(c):
        left = chunk_of(mixed, c)
        for at in range(0, width, wide):
            cols = slice(at, at + wide)
            put_parts(c, cols, bf_dot(left, w_out[:, cols]))

    def ffn_product(c):
        for at in range(0, hidden, wide):
            cols = slice(at, at + wide)
            left = chunk_of(ffn_all, c)
            gate = bf_dot(left, flat(w_gate[:, :, :, cols]))
            up = bf_dot(left, flat(w_up[:, :, :, cols]))
            gate_keep[c, :, cols], up_keep[c, :, cols] = gate, up
            value = (gate * jax.nn.sigmoid(gate) * up).astype(BF16)
            act[:, of(c), cols] = value.reshape(seq, thin, wide)
        left = chunk_of(act, c)
        for at in range(0, width, wide):
            cols = slice(at, at + wide)
            put_parts(c, cols, bf_dot(left, flat(w_down[:, :, cols])))

    def ffn_back_product(c):
        block = w_down.shape[1]
        for at in range(0, hidden, wide):
            cols = slice(at, at + wide)
            d_act = right_dot(chunk_of(d_ffn, c), flat(w_down[at // block : (at + wide) // block]))
            gate, up = gate_keep[c, :, cols], up_keep[c, :, cols]
            sig = jax.nn.sigmoid(gate)
            silu = gate * sig
            d_g = (d_act * up * (sig + silu * (1.0 - sig))).astype(BF16)
            d_u = (d_act * silu).astype(BF16)
            d_gate[:, of(c), cols] = d_g.reshape(seq, thin, wide)
            d_up[:, of(c), cols] = d_u.reshape(seq, thin, wide)
        left_g, left_u = chunk_of(d_gate, c), chunk_of(d_up, c)
        half = buckets // 2
        for at in range(0, buckets, half):
            cols = slice(at * width // buckets, (at + half) * width // buckets)
            total = right_dot(left_g, flat(w_gate[at : at + half]))
            total = total + right_dot(left_u, flat(w_up[at : at + half]))
            put_parts(c, cols, total)

    def pour_of(c, turn):
        left, right = from_left.at[turn * chunks + c], from_right.at[turn * chunks + c]
        return Pour(copies, parts.at[c], left, right, b, s, seq)

    gathered = (ffn_all, d_ffn, d_attn)
    after = (after_attn, after_ffn, after_ffn_back)
    products = (attn_product, ffn_product, ffn_back_product)

    def all_rows(ref, cols=slice(None)):
        whole = ref[:, :, cols]
        return whole.reshape(seq * rows, whole.shape[-1])

    def down_grad():
        chips, part = buckets // 2, hidden // buckets
        for i in range(chips):
            turned = all_rows(act, slice(2 * i * part, 2 * (i + 1) * part)).T
            total = bf_dot(turned, all_rows(d_ffn)).astype(BF16)
            for half in range(2):
                grads[2][i, half] = total[half * part : (half + 1) * part]
        sums.begin(2)

    def weight_grads():
        chips, part = buckets // 2, width // (buckets // 2)
        for i in range(chips):
            turned = all_rows(ffn_all, slice(i * part, (i + 1) * part)).T
            for grad, d in zip(grads[:2], (d_gate, d_up), strict=True):
                total = bf_dot(turned, all_rows(d))
                grad[i] = total.astype(BF16).reshape(2, part // 2, hidden)
            if i == 1:
                sums.stage_a(2)
            yield
        sums.begin(0)
        sums.begin(1)
        sums.stage_b(2)
        yield
        sums.stage_a(0)
        yield
        sums.stage_c(2)
        sums.stage_a(1)
        yield
        sums.stage_b(0)
        yield
        sums.stage_b(1)
        yield
        sums.stage_c(0)
        sums.stage_d(2)
        sums.stage_c(1)
        sums.stage_d(0)
        sums.stage_d(1)

    extra = weight_grads()
    plan = [(turn, c) for turn in range(3) for c in range(chunks)]
    gathers, open_gather = {}, []

    def finish_gather():
        turn, c = open_gather.pop(0)
        gathers[turn, c].start(seq - 1)
        for j in range(seq - 1):
            gathers[turn, c].sent(j)
        return turn, c

    def weights_come():
        count = len(MOVED)
        for n in range(count + 3):
            if n < count:
                weights.arrived(MOVED[n])
                if n + 1 < count:
                    weights.depart(MOVED[n + 1])
                weights.stage_a(MOVED[n])
                yield
            if 1 <= n <= count:
                weights.stage_b(MOVED[n - 1])
                yield
            if 2 <= n <= count + 1:
                weights.stage_c(MOVED[n - 2])
            if 3 <= n:
                weights.stage_d(MOVED[n - 3])
            yield

    coming = weights_come()
    attn_product(0)
    pours = {(0, 0): pour_of(0, 0)}
    ready = pours[0, 0].cuts
    for q in range(ready):
        pours[0, 0].step(q)
    for c in range(1, chunks):
        attn_product(c)
    for load in loads:
        load.wait()
    for at, (turn, c) in enumerate(plan):
        pour = pours[turn, c]
        mate = gathers[open_gather[0]] if open_gather else None
        per = pour.count // (seq - 1)
        final = at == len(plan) - 1
        for j in range(2, seq):
            if mate is not None and j < seq - 1:
                mate.start(j)
            if final:
                next(extra, None)
            for q in range((j - 1) * per, j * per):
                pour.step(q)
                next(coming, None)
            if final:
                next(extra, None)
        pour.end(got.at[of(c)])
        after[turn](c)
        gathers[turn, c] = Relay(copies, None, gathered[turn], b, s, seq, of(c))
        gathers[turn, c].start(0)
        if mate is not None:
            done_turn, done_c = finish_gather()
            if (done_turn, done_c) == (1, chunks - 1):
                down_grad()
            for _ in coming:
                pass
            if done_turn < 2:
                products[done_turn + 1](done_c)
        open_gather.append((turn, c))
        gathers[turn, c].start(1)
        if at + 1 < len(plan):
            nxt = plan[at + 1]
            pours[nxt] = pour_of(nxt[1], nxt[0])
            for q in range(ready):
                pours[nxt].step(q)
            if at + 2 == len(plan):
                for _ in range(AHEAD):
                    next(extra)
    turn, c = open_gather[0]
    for j in range(2, seq - 1):
        next(extra, None)
        gathers[turn, c].start(j)
    next(extra, None)
    finish_gather()
    for _ in extra:
        pass
    sums.end()
    weights.end()


def middle_all(buckets, seq, mixed, weights, tokens, cotangent, counts, gain_rows, mod_rows):
    any_spec = pl.BlockSpec(memory_space=pl.ANY)
    vmem = pl.BlockSpec(memory_space=pltpu.VMEM)
    smem = pl.BlockSpec(memory_space=pltpu.SMEM)
    chunks = CHUNKS
    w_out, w_gate, w_up, w_down = weights
    rows, width = tokens.shape
    hidden = w_down.shape[-2] * buckets if 2 in MOVED else w_down.shape[0] * w_down.shape[1]
    part = width // (buckets * seq)
    tall, thin = (seq, rows, width), rows // chunks
    flat = (seq, rows, hidden)
    blocks = pltpu.VMEM((3 * chunks, seq - 1, thin, width), BF16)
    kinds = ("hold", "hold", "stay")
    shapes, sums_out, scratch, n_sems = sums_shapes(
        buckets, seq, [(width, hidden), (width, hidden), (hidden, width)], kinds, near=True
    )
    n_sems += 64 + 3 * chunks * (2 * CUTS + 2) * seq
    results = pl.pallas_call(
        functools.partial(middle_kernel, buckets, seq, chunks, kinds),
        out_shape=[
            jax.ShapeDtypeStruct((rows, width), BF16),
            jax.ShapeDtypeStruct((rows, width), F32),
            jax.ShapeDtypeStruct(tall, BF16),
            jax.ShapeDtypeStruct((8, width), F32),
            *sums_out,
        ],
        in_specs=[vmem] * 4 + [smem] + [vmem] * 2 + [any_spec] * 3,
        out_specs=[vmem] * 7,
        scratch_shapes=[
            pltpu.VMEM((buckets, seq, part, hidden), BF16),
            pltpu.VMEM((buckets, seq, part, hidden), BF16),
            pltpu.VMEM((buckets, hidden // buckets, width), BF16),
            pltpu.VMEM(tall, BF16),
            pltpu.VMEM(tall, BF16),
            *([pltpu.VMEM(flat, BF16)] * 3),
            pltpu.VMEM((chunks, seq * thin, hidden), F32),
            pltpu.VMEM((chunks, seq * thin, hidden), F32),
            pltpu.VMEM((rows, width), F32),
            pltpu.VMEM((rows, width), F32),
            pltpu.VMEM((rows, width), F32),
            pltpu.VMEM((chunks, seq, thin, width), BF16),
            blocks,
            blocks,
            pltpu.VMEM((rows, 128), F32),
            pltpu.SemaphoreType.DMA((n_sems,)),
            pltpu.SemaphoreType.DMA((n_sems,)),
            *[pltpu.VMEM(shape, BF16) for shape in shapes],
            *scratch,
        ],
        compiler_params=pltpu.CompilerParams(
            collective_id=11, has_side_effects=True, vmem_limit_bytes=62 * 2**20
        ),
    )(
        mixed.reshape(seq, rows, mixed.shape[1]),
        w_out,
        tokens,
        cotangent,
        counts,
        gain_rows,
        mod_rows,
        w_gate,
        w_up,
        w_down,
    )
    return results[:4], (results[4], results[5], results[6].reshape(-1, results[6].shape[-1]))


LATE = (1, 2, 3, 11, 12, 19, 20, 21, 22)


def backward_kernel(buckets, seq, kinds, *refs):
    count = len(kinds)
    (
        d_attn,
        w_query,
        w_key,
        w_value,
        w_out,
        query,
        key,
        value,
        cap_key,
        cap_value,
        cross_out,
        query_raw,
        key_raw,
        cap_raw,
        gain_rows,
        mod_rows,
        counts,
        cap_lens,
        mixed,
        hidden,
        captions,
        tokens,
        d_tokens,
        row_sums,
    ) = refs[:24]
    holds, strip_outs = refs[24:26], refs[29:31]
    tokens_grad, mod_all, small_out, refs = refs[26], refs[27], refs[28], refs[31:]
    outs, refs = refs[:count], refs[count:]
    mixed_low, cross_low, query_acc, key_acc, value_acc, cap_key_acc, cap_value_acc = refs[:7]
    d_query, d_key, d_value, d_cap_key, d_cap_value, d_hidden, vec = refs[7:14]
    mod_give, mod_got, mod_sum, wide_give, wide_got, slim_give, slim_got = refs[14:21]
    key_bias, cap_bias, parts, from_left, from_right, send, recv = refs[21:28]
    late, refs = refs[28 : 28 + len(LATE)], refs[28 + len(LATE) :]
    strips, refs = refs[:2], refs[2:]
    grads, refs = refs[:count], refs[count:]
    b, s = lax.axis_index("bucket"), lax.axis_index("seq")
    copies = Copies(send, recv)
    far = (w_query, w_key, w_value, query_raw, key_raw, hidden, captions, tokens, d_tokens)
    loads = [copies.local(src, dst) for src, dst in zip(far, late, strict=True)]
    for at in (6, 3, 4, 0, 1, 2, 5, 7, 8):
        loads[at].start()
    w_query, w_key, w_value, query_raw, key_raw, hidden, captions, tokens, d_tokens = late
    sums = GradSums(copies, b, s, buckets, seq, kinds, grads, outs, refs, near=True)
    peers = greet_all(b, s, buckets, seq)

    rows, share = query.shape
    width = parts.shape[-1]
    pairs = share // 128
    chips = buckets // 2
    span_block = 256
    scale = HEAD_DIM**-0.5

    def gain_of(row, pair):
        at = pl.multiple_of(s * share + pair * 128, 128)
        return gain_rows[row : row + 1, pl.ds(at, 128)]

    vec[...] = jnp.zeros_like(vec)
    mod_give[...] = jnp.zeros_like(mod_give)
    wide_give[...] = jnp.zeros_like(wide_give)
    slim_give[...] = jnp.zeros_like(slim_give)
    fill_rows(key_bias, counts[b], 0, 0.0, -1e30)
    fill_rows(cap_bias, cap_lens[b], 0, 0.0, -1e30)
    mixed_low[...] = right_dot(d_attn[...], w_out[...]).astype(BF16)

    def own_sum(row, pair, total):
        vec[row : row + 1, pl.ds(pl.multiple_of(s * share + pair * 128, 128), 128)] = total

    def cross_part(pair):
        lane = slice(pair * 128, (pair + 1) * 128)
        gate = jnp.tanh(gain_of(7, pair))

        def body(i, total):
            at = pl.ds(pl.multiple_of(i * 128, 128), 128)
            d = mixed_low[at, lane].astype(F32)
            cross_low[at, lane] = (gate * d).astype(BF16)
            return total + jnp.sum(d * cross_out[at, lane], axis=0, keepdims=True)

        total = lax.fori_loop(0, rows // 128, body, jnp.zeros((1, 128), F32))
        own_sum(7, pair, total * (1.0 - gate * gate))

    def attend_back(pair, k_ref, v_ref, bias, d_ref, k_acc, v_acc, add):
        lane = slice(pair * 128, (pair + 1) * 128)
        low = low_half((span_block, 128))
        k_turned = k_ref[:, lane].T
        k_acc[:, lane] = jnp.zeros((k_acc.shape[0], 128), F32)
        v_acc[:, lane] = jnp.zeros((v_acc.shape[0], 128), F32)

        def body(i, carry):
            at = pl.ds(pl.multiple_of(i * span_block, span_block), span_block)
            q = query[at, lane] * jnp.asarray(scale, BF16)
            d = d_ref[at, lane]
            found = []
            for keep in (low, jnp.logical_not(low)):
                q_half = jnp.where(keep, q, jnp.zeros_like(q))
                d_half = jnp.where(keep, d, jnp.zeros_like(d))
                scores = right_dot(k_ref[:, lane], q_half)
                scores = scores + jnp.concatenate([bias[...], bias[...]], axis=1)
                weights = jnp.exp(scores)
                probs = weights * (1.0 / jnp.sum(weights, axis=0, keepdims=True))
                d_probs = right_dot(v_ref[:, lane], d_half)
                delta = jnp.sum(probs * d_probs, axis=0, keepdims=True)
                d_scores = (probs * (d_probs - delta)).astype(BF16)
                k_acc[:, lane] += bf_dot(d_scores, q_half)
                v_acc[:, lane] += bf_dot(probs.astype(BF16), d_half)
                found.append(bf_dot(k_turned, d_scores))
            turned = jnp.concatenate([found[0][:HEAD_DIM], found[1][HEAD_DIM:]], axis=0)
            d_q = turned.T * scale
            query_acc[at, lane] = query_acc[at, lane] + d_q if add else d_q
            return carry

        lax.fori_loop(0, rows // span_block, body, 0)

    def norm_back(raw, d_norm, out, row, sum_row):
        for pair in range(pairs):
            lane = slice(pair * 128, (pair + 1) * 128)
            gain = gain_of(row, pair)

            def body(i, total):
                at = pl.ds(pl.multiple_of(i * 128, 128), 128)
                x, d = raw[at, lane], d_norm[at, lane]
                size = pair_scale(x, 1e-06)
                normed, inner = x * size, d * gain
                mean = pair_sums(inner * normed) * (1.0 / HEAD_DIM)
                out[at, lane] = (size * (inner - normed * mean)).astype(BF16)
                return total + jnp.sum(d * normed, axis=0, keepdims=True)

            total = lax.fori_loop(0, raw.shape[0] // 128, body, jnp.zeros((1, 128), F32))
            own_sum(sum_row, pair, total)

    def weight_grads(left, chosen):
        part = left.shape[1] // chips
        for i in range(chips):
            turned = left[:, i * part : (i + 1) * part].T
            for w, right in chosen:
                total = bf_dot(turned, right[...])
                grads[w][i] = total.astype(BF16).reshape(2, part // 2, total.shape[-1])
            yield
        for w, _ in chosen:
            sums.begin(w)

    def out_grad():
        total = bf_dot(mixed[...].T, d_attn[...]).astype(BF16)
        part = share // buckets
        for block, p in enumerate(spread(buckets)):
            grads[0][p // 2, p % 2] = total[block * part : (block + 1) * part]
        sums.begin(0)

    pl.semaphore_wait(pltpu.get_barrier_semaphore(), peers)
    strip_moves = []
    for hold, strip in zip(holds, strips, strict=True):
        strip[s] = hold[s]
        for j in range(1, seq):
            peer = lax.rem(s + j, seq)
            strip_moves.append(sums.go(copies.remote(hold.at[peer], strip.at[s], b, peer)))
    for pair in range(pairs):
        cross_part(pair)
        attend_back(pair, cap_key, cap_value, cap_bias, cross_low, cap_key_acc, cap_value_acc, False)
    norm_back(cap_raw, cap_key_acc, d_cap_key, 6, 6)
    d_cap_value[...] = cap_value_acc[...].astype(BF16)
    loads[6].wait()
    for _ in weight_grads(captions, ((1, d_cap_key), (2, d_cap_value))):
        pass
    def deal_back():
        for move in strip_moves:
            move.wait_recv()
        for strip, out in zip(strips, strip_outs, strict=True):
            for j in range(seq):
                for part in range(strip.shape[2] // 128):
                    cols = slice((part * seq + j) * 128, (part * seq + j + 1) * 128)
                    out[:, cols] = strip[j, :, part * 128 : (part + 1) * 128].astype(F32)

    steps = (lambda: sums.stage_a(1), lambda: sums.stage_a(2), lambda: sums.stage_b(1))
    for pair in range(pairs):
        attend_back(pair, key, value, key_bias, mixed_low, key_acc, value_acc, True)
        steps[pair]()
    for at in (3, 4, 0, 1, 2, 5, 7, 8):
        loads[at].wait()
    norm_back(query_raw, query_acc, d_query, 4, 4)
    norm_back(key_raw, key_acc, d_key, 5, 5)
    d_value[...] = value_acc[...].astype(BF16)
    pour = Pour(copies, parts, from_left, from_right, b, s, seq)
    wide = 512
    for at in range(0, width, wide):
        cols = slice(at, at + wide)
        total = right_dot(d_query[...], w_query[cols, :]) + right_dot(d_key[...], w_key[cols, :])
        total = total + right_dot(d_value[...], w_value[cols, :])
        parts[:, :, cols] = total.astype(BF16).reshape(seq, rows // seq, wide)
    pieces = weight_grads(hidden, ((3, d_query), (4, d_key), (5, d_value)))
    between = {1: out_grad, 2: lambda: sums.stage_b(2)}
    for q in range(pour.count):
        pour.step(q)
        if q in between:
            between[q]()
        elif q > 2:
            next(pieces, None)
    for _ in pieces:
        pass
    deal_back()
    sums.stage_a(0)
    sums.stage_c(1)
    sums.stage_c(2)
    pour.end(d_hidden)

    factor = gain_rows[0:1, :] * (1.0 + mod_rows[0:1, :])

    def body(i, total):
        at = pl.ds(pl.multiple_of(i * 16, 16), 16)
        x, d = tokens[at, :].astype(F32), d_hidden[at, :]
        size = lax.rsqrt(jnp.mean(x * x, axis=-1, keepdims=True) + 1e-05)
        normed, inner = x * size, d * factor
        mean = jnp.mean(inner * normed, axis=-1, keepdims=True)
        tokens_grad[at, :] = d_tokens[at, :] + size * (inner - normed * mean)
        return total + jnp.sum(d * normed, axis=0, keepdims=True)

    total = lax.fori_loop(0, tokens.shape[0] // 16, body, jnp.zeros((1, width), F32))
    post, last = jnp.tanh(mod_rows[1:2, :]), jnp.tanh(mod_rows[3:4, :])
    vec[8:9, :] = total * gain_rows[0:1, :]
    vec[9:10, :] = row_sums[0:1, :] * gain_rows[1:2, :] * (1.0 - post * post)
    vec[10:11, :] = row_sums[1:2, :] * gain_rows[2:3, :]
    vec[11:12, :] = row_sums[2:3, :] * gain_rows[3:4, :] * (1.0 - last * last)
    vec[0:1, :] = total * (1.0 + mod_rows[0:1, :])
    vec[1:2, :] = row_sums[0:1, :] * post
    vec[2:3, :] = row_sums[1:2, :] * (1.0 + mod_rows[2:3, :])
    vec[3:4, :] = row_sums[2:3, :] * last
    piece, wide = width // 4, width // buckets
    slim = wide // seq
    for t in range(seq):
        for j in range(4):
            mod_give[t, j : j + 1, :] = vec[8 + t : 9 + t, j * piece : (j + 1) * piece]
    for t in range(buckets):
        wide_give[t, :, :wide] = vec[0:8, t * wide : (t + 1) * wide]
    mod_moves, wide_moves = [], []
    for j in range(1, seq):
        peer = lax.rem(s + j, seq)
        mod_moves.append(sums.go(copies.remote(mod_give.at[peer], mod_got.at[j], b, peer)))
    for j in range(1, buckets):
        peer = lax.rem(b + j, buckets)
        wide_moves.append(sums.go(copies.remote(wide_give.at[peer], wide_got.at[j], peer, s)))
    sums.stage_a(3)
    sums.stage_a(4)
    sums.stage_a(5)
    total = mod_give[s]
    for j, move in enumerate(mod_moves, 1):
        move.wait_recv()
        total = total + mod_got[j]
    mod_sum[...] = total
    mod_next, slim_next = [], []
    for j in range(1, buckets):
        peer = lax.rem(b + j, buckets)
        mod_next.append(sums.go(copies.remote(mod_sum, mod_all.at[b], peer, s)))
    mod_own = copies.local(mod_sum, mod_all.at[b])
    mod_own.start()
    total = wide_give[b]
    for j, move in enumerate(wide_moves, 1):
        move.wait_recv()
        total = total + wide_got[j]
    for t in range(seq):
        slim_give[t, :, :slim] = total[:, t * slim : (t + 1) * slim]
    for j in range(1, seq):
        peer = lax.rem(s + j, seq)
        slim_next.append(sums.go(copies.remote(slim_give.at[peer], slim_got.at[j], b, peer)))
    for w in (0, 3, 4, 5):
        sums.stage_b(w)
    sums.stage_c(0)
    for w in (3, 4, 5):
        sums.stage_c(w)
    sums.stage_d(0)
    total = slim_give[s]
    for j, move in enumerate(slim_next, 1):
        move.wait_recv()
        total = total + slim_got[j]
    small_out[...] = total
    for move in mod_next:
        move.wait_recv()
    mod_own.wait()
    sums.end()


def backward_all(buckets, seq, inputs, shapes, kinds):
    any_spec = pl.BlockSpec(memory_space=pl.ANY)
    vmem = pl.BlockSpec(memory_space=pltpu.VMEM)
    smem = pl.BlockSpec(memory_space=pltpu.SMEM)
    shapes, outs, scratch, n_sems = sums_shapes(buckets, seq, shapes, kinds, near=True)
    query, cap_key, tokens = inputs[5], inputs[8], inputs[21]
    rows, width = tokens.shape
    vec = (16, width)
    n_sems += 12 * seq + 4 * buckets + len(LATE) + 2 * seq
    results = pl.pallas_call(
        functools.partial(backward_kernel, buckets, seq, tuple(kinds)),
        out_shape=[
            jax.ShapeDtypeStruct((rows, width), F32),
            jax.ShapeDtypeStruct((buckets, 8, width // 4), F32),
            jax.ShapeDtypeStruct((8, 128), F32),
            *[jax.ShapeDtypeStruct((x.shape[1], x.shape[2] * seq), F32) for x in inputs[24:26]],
            *outs,
        ],
        in_specs=[
            smem if at in (16, 17) else any_spec if at in LATE else vmem for at in range(len(inputs))
        ],
        out_specs=[vmem, any_spec] + [vmem] * (3 + len(outs)),
        scratch_shapes=[
            pltpu.VMEM(query.shape, BF16),
            pltpu.VMEM(query.shape, BF16),
            pltpu.VMEM(query.shape, F32),
            pltpu.VMEM(query.shape, F32),
            pltpu.VMEM(query.shape, F32),
            pltpu.VMEM(cap_key.shape, F32),
            pltpu.VMEM(cap_key.shape, F32),
            pltpu.VMEM(query.shape, BF16),
            pltpu.VMEM(query.shape, BF16),
            pltpu.VMEM(query.shape, BF16),
            pltpu.VMEM(cap_key.shape, BF16),
            pltpu.VMEM(cap_key.shape, BF16),
            pltpu.VMEM((rows, width), F32),
            pltpu.VMEM(vec, F32),
            pltpu.VMEM((seq, 8, width // 4), F32),
            pltpu.VMEM((seq, 8, width // 4), F32),
            pltpu.VMEM((8, width // 4), F32),
            pltpu.VMEM((buckets, 8, 256), F32),
            pltpu.VMEM((buckets, 8, 256), F32),
            pltpu.VMEM((seq, 8, 128), F32),
            pltpu.VMEM((seq, 8, 128), F32),
            pltpu.VMEM((query.shape[0], 128), F32),
            pltpu.VMEM((cap_key.shape[0], 128), F32),
            pltpu.VMEM((seq, rows, width), BF16),
            pltpu.VMEM((seq - 1, rows, width), BF16),
            pltpu.VMEM((seq - 1, rows, width), BF16),
            pltpu.SemaphoreType.DMA((n_sems,)),
            pltpu.SemaphoreType.DMA((n_sems,)),
            *[pltpu.VMEM(inputs[at].shape, inputs[at].dtype) for at in LATE],
            *[pltpu.VMEM(x.shape, BF16) for x in inputs[24:26]],
            *[pltpu.VMEM(shape, BF16) for shape in shapes],
            *scratch,
        ],
        compiler_params=pltpu.CompilerParams(
            collective_id=10, has_side_effects=True, vmem_limit_bytes=62 * 2**20
        ),
    )(*inputs)
    sums = [*results[3:5], *(out.reshape(-1, out.shape[-1]) for out in results[5:])]
    return results[0], results[1], results[2], sums


def last_kernel(buckets, seq, slim, *refs):
    cond, mod_all, small = refs[:3]
    count = (len(refs) - 7) // 2
    sources, refs = refs[3 : 3 + count], refs[3 + count :]
    mod_grad, gains, cross = refs[:3]
    targets, sems = refs[3 : 3 + count], refs[3 + count]
    copies = [
        pltpu.make_async_copy(a, b, sems.at[i])
        for i, (a, b) in enumerate(zip(sources, targets, strict=True))
    ]
    for copy in copies:
        copy.start()
    piece = mod_all.shape[2]
    for j in range(4):
        total = None
        for k in range(buckets):
            term = cond[:, k : k + 1] * mod_all[k, j : j + 1, :]
            total = term if total is None else total + term
        mod_grad[:, j * piece : (j + 1) * piece] = total
    gains[...] = small[0:7, :slim]
    cross[...] = small[7:8, :slim]
    for copy in copies:
        copy.wait()


def last_all(buckets, seq, slim, cond, mod_all, small, results):
    any_spec = pl.BlockSpec(memory_space=pl.ANY)
    vmem = pl.BlockSpec(memory_space=pltpu.VMEM)
    outs = pl.pallas_call(
        functools.partial(last_kernel, buckets, seq, slim),
        out_shape=[
            jax.ShapeDtypeStruct((cond.shape[0], 4 * mod_all.shape[2]), F32),
            jax.ShapeDtypeStruct((7, slim), F32),
            jax.ShapeDtypeStruct((1, slim), F32),
            *[jax.ShapeDtypeStruct(x.shape, x.dtype) for x in results],
        ],
        in_specs=[vmem] * 3 + [any_spec] * len(results),
        out_specs=[vmem] * (3 + len(results)),
        scratch_shapes=[pltpu.SemaphoreType.DMA((len(results),))],
        compiler_params=pltpu.CompilerParams(vmem_limit_bytes=62 * 2**20),
    )(cond, mod_all, small, *results)
    return outs[0], outs[1], outs[2].reshape(slim), outs[3:]


def on_device(
    tokens,
    captions,
    cotangent,
    counts,
    cap_lens,
    steps_t,
    w_query,
    w_key,
    w_value,
    w_out,
    w_cap_key,
    w_cap_value,
    w_gate,
    w_up,
    w_down,
    w_mod,
    gains,
    cross_gate,
):
    buckets, seq = lax.axis_size("bucket"), lax.axis_size("seq")
    b, s = lax.axis_index("bucket"), lax.axis_index("seq")
    place = b * seq + s
    rows, width = tokens.shape
    span = rows * seq
    share = width // seq

    cond_size = w_mod.shape[0] * buckets * seq
    cond = jax.nn.silu(time_embed(steps_t, cond_size)).astype(BF16)
    cond_part = lax.dynamic_slice_in_dim(cond, place * w_mod.shape[0], w_mod.shape[0], 1)
    slim = gains.shape[1]
    small = jnp.concatenate([gains, cross_gate[None]], axis=0).astype(F32)
    small = jnp.pad(small, ((0, 0), (0, 128 - slim)))
    feed = [w_gate, w_up, w_down]
    early = [w for w in range(3) if w not in MOVED]
    cap_all, weights, inner = forward_all(
        buckets,
        seq,
        tokens,
        captions,
        small,
        slim,
        cond_part,
        w_mod,
        [counts, cap_lens],
        [w_query, w_key, w_value, w_cap_key, w_cap_value, w_out, *(feed[w] for w in early)],
        ["col", "col", "col", "col", "col", "row", *(("cut", "cut", "stay")[w] for w in early)],
    )
    wq, wk, wv, wck, wcv, wo = (x.reshape(-1, x.shape[-1]) for x in weights[:6])
    for w, full in zip(early, weights[6:], strict=True):
        feed[w] = full
    caps = cap_all.reshape(-1, captions.shape[1])
    small_rows, mod, hidden, query_proj, key_proj, cap_proj = inner[:6]
    query, key, value, cap_key, cap_value = inner[6:11]
    cross_out, mixed_low = inner[11:]
    (block_out, d_tokens, d_attn_all, row_sums), (h_gate, h_up, s_down) = middle_all(
        buckets,
        seq,
        mixed_low,
        (wo, *feed),
        tokens,
        cotangent,
        counts,
        small_rows,
        mod,
    )
    tokens_grad, mod_all, small_sums, sums = backward_all(
        buckets,
        seq,
        [
            d_attn_all.reshape(span, width),
            wq,
            wk,
            wv,
            wo,
            query,
            key,
            value,
            cap_key,
            cap_value,
            cross_out,
            query_proj,
            key_proj,
            cap_proj,
            small_rows,
            mod,
            counts,
            cap_lens,
            mixed_low,
            hidden,
            caps,
            tokens,
            d_tokens,
            row_sums,
            h_gate,
            h_up,
        ],
        [x.shape for x in (wo, wck, wcv, wq, wk, wv)],
        ["row", "col", "col", "col", "col", "col"],
    )
    s_gate, s_up, s_out, s_cap_key, s_cap_value, s_query, s_key, s_value = sums

    cond_size = cond.shape[1] // buckets
    cond_cols = lax.dynamic_slice_in_dim(cond, b * cond_size, cond_size, 1).astype(F32).T
    results = [block_out, tokens_grad, s_query, s_key, s_value, s_out]
    results += [s_cap_key, s_cap_value, s_gate, s_up, s_down]
    s_mod, s_gains, s_cross, results = last_all(
        buckets, seq, slim, cond_cols, mod_all, small_sums, results
    )
    return (*results, s_mod, s_gains, s_cross)


def solution(mesh):
    spread = P(("bucket", "seq"), None)
    in_specs = (
        *([spread] * 3),
        *([P()] * 3),
        *([spread] * 10),
        P(None, ("bucket", "seq")),
        P(("bucket", "seq")),
    )
    out_specs = (
        spread,
        spread,
        *([P("bucket", "seq")] * 10),
        P(None, ("bucket", "seq")),
        P(("bucket", "seq")),
    )
    buckets, seq = mesh.shape["bucket"], mesh.shape["seq"]

    def step(*args):
        tokens, weight = args[0], args[6]
        tiled = weight.shape[0] % 16 == 0 and weight.shape[1] // seq % 128 == 0
        fits = buckets == 8 and seq == 4 and tokens.shape[0] % 64 == 0
        return (on_device if tiled and fits else on_device_general)(*args)

    return jax.shard_map(
        step, mesh=mesh, in_specs=in_specs, out_specs=out_specs, check_vma=False
    )
```
